32 devices in a mesh: dp: 16 (over z, x, core), tensor: 2 (over y).
Axes of the slice: x: 2, y: 2, z: 4, core: 2. Of those that a mesh axis runs over, the one named last changes fastest.
Arguments:
- tokens: bfloat16 [64, 256, 768], P('dp'), may hold values from -6 to 6
- segment_ids: int32 [64, 256], P('dp'), may hold values from 0 to 3, never falling along the last dimension, each value on 1 to 128 neighbouring positions
- pass_embed: float32 [768], replicated, may hold values from -5 to 5
- w_qkv: bfloat16 [3, 768, 768], P(None, None, 'tensor'), may hold values from -0.21875 to 0.21875
- w_out: bfloat16 [768, 768], P('tensor'), may hold values from -0.75 to 0.75
- w_up: bfloat16 [768, 3072], P(None, 'tensor'), may hold values from -0.21875 to 0.21875
- w_down: bfloat16 [3072, 768], P('tensor'), may hold values from -0.109375 to 0.109375
- ln_gain: float32 [2, 768], replicated, may hold values from 0.5 to 1.5
- ln_bias: float32 [2, 768], replicated, may hold values from -1.5 to 1.5
- cotangent: bfloat16 [64, 512, 768], P('dp'), may hold values from -6 to 6
Outputs:
- out: bfloat16 [64, 512, 768], P('dp')
- grad_tokens: float32 [64, 256, 768], P('dp')
- grad_qkv: float32 [3, 768, 768], P(None, None, 'tensor')
- grad_out: float32 [768, 768], P('tensor')
- grad_up: float32 [768, 3072], P(None, 'tensor')
- grad_down: float32 [3072, 768], P('tensor')
- grad_gain: float32 [2, 768], replicated
- grad_bias: float32 [2, 768], replicated
- grad_pass: float32 [768], replicated
The draws below stay inside these ranges and needn't reach their ends.
Inputs may be any that keep to these rules, and one draw needn't show every extreme that they name: `segment_ids`: along a row the ids never fall; a document holds at most 128 tokens and one in each row holds exactly 128.
All inputs are finite; a program needn't handle non-finite values.
Results may differ from the reference program's by a relative error of at most 0.019.
Values may be sent and summed in bfloat16 or wider, within the bound.
No kernel may reach another device: no remote copies, remote signals or barrier semaphores. Data moves between devices by JAX's collectives and lax.ppermute only.
A program may use at most 256 MiB of HBM per device.

```python
import math
import jax
import jax.numpy as jnp
import numpy as np
from jax import lax

D = 768
HEADS = 12
HD = 64
FF = 3072
SEQ = 256
DOCS = 4
MOST = 128
ROWS = 64


def levels(stream_key, shape, shards, smallest, high):
    factor_of = 1.0
    for position, blocks in shards:
        steps = jax.random.uniform(jax.random.fold_in(jax.random.fold_in(stream_key, 6), position), (blocks,), jnp.float32, smallest / len(shards), high / len(shards))
        factor_of = factor_of * jnp.repeat(jnp.exp(steps), shape[position] // blocks).reshape((-1,) + (1,) * (len(shape) - 1 - position))
    return factor_of


def split_up(amount, total, reach, skew):
    weights = [(1 << 20) // math.isqrt(grade ** skew) + 1 for grade in range(2, amount + 1)]
    spare, given = total - reach - (amount - 1), [1] * (amount - 1)
    while spare > 0:
        movable = [i for i in range(amount - 1) if given[i] < reach]
        pool, budget = sum([weights[i] for i in movable]), spare
        for i in movable:
            extra = min(reach - given[i], max(1, budget * weights[i] // pool), spare)
            given[i] = given[i] + extra
            spare = spare - extra
    return np.array([reach] + given)


def ragged(stream_key, number_of, total, bound, slope):
    if number_of == 2:
        one = jax.random.randint(stream_key, (), max(1, total - bound), min(bound, total - 1) + 1)
        return jnp.stack([one, total - one])
    lengths = jnp.asarray(split_up(number_of, total, bound, slope), jnp.int32)
    twos = (number_of - 1) // 2
    giver, sink = lengths[1:1 + 2 * twos:2], lengths[2:2 + 2 * twos:2]
    room = jnp.minimum(giver - 1, bound - sink)
    shifted = jax.random.randint(jax.random.fold_in(stream_key, 1), (twos,), 0, 1 << 20) % (room + 1)
    lengths = lengths.at[1:1 + 2 * twos:2].set(giver - shifted).at[2:2 + 2 * twos:2].set(sink + shifted)
    return lengths[jax.random.permutation(jax.random.fold_in(stream_key, 2), number_of)]


def noise(rng, shape, deviation, limit, pieces=(), kind=jnp.bfloat16):
    factor_of = levels(rng, shape, pieces, -0.22, 0.18) if pieces else 1.0
    array = jax.random.normal(rng, shape, jnp.float32) * deviation * factor_of
    return jnp.minimum(jnp.maximum(array, -limit), limit).astype(kind)


def setup_inputs(seed: int = 0) -> dict:
    streams_of = jax.random.split(jax.random.key(seed), 11)
    tokens = noise(streams_of[0], (ROWS, SEQ, D), 1.0, 6.0, ((0, 16),))
    segment_ids = jax.vmap(lambda own: jnp.searchsorted(jnp.cumsum(ragged(own, DOCS, SEQ, MOST, 1)), jnp.arange(SEQ), side="right"))(jax.random.split(streams_of[1], ROWS)).reshape((ROWS, SEQ)).astype(jnp.int32)
    pass_embed = noise(streams_of[2], (D,), 1.0, 5.0, (), jnp.float32)
    w_qkv = noise(streams_of[3], (3, D, D), D ** -0.5, 0.21875, ((2, 2),))
    w_out = noise(streams_of[4], (D, D), HD ** -0.5, 0.75, ((0, 2),))
    w_up = noise(streams_of[5], (D, FF), D ** -0.5, 0.21875, ((1, 2),))
    w_down = noise(streams_of[6], (FF, D), FF ** -0.5, 0.109375, ((0, 2),))
    ln_gain = jnp.clip(1.0 + 0.1 * jax.random.normal(streams_of[7], (2, D), jnp.float32), 0.5, 1.5)
    ln_bias = noise(streams_of[8], (2, D), 0.3, 1.5, (), jnp.float32)
    cotangent = noise(streams_of[9], (ROWS, 2 * SEQ, D), 1.0, 6.0, ((0, 16),))
    return dict(tokens=tokens, segment_ids=segment_ids, pass_embed=pass_embed, w_qkv=w_qkv, w_out=w_out, w_up=w_up, w_down=w_down, ln_gain=ln_gain, ln_bias=ln_bias, cotangent=cotangent)


eps_norm = 1e-05
neg_fill = -1000000000.0

@jax.custom_vjp
def low(v):
    return lax.optimization_barrier(v.astype(jnp.bfloat16)).astype(jnp.float32)

@jax.custom_vjp
def low_back(v):
    return v

def low_keep(v):
    return (low(v), None)

def low_pass(kept, grad):
    return (grad,)

def back_keep(v):
    return (v, None)

def back_low(kept, grad):
    return (low(grad),)
low.defvjp(low_keep, low_pass)
low_back.defvjp(back_keep, back_low)

def layer_norm(act_in, gain_row, bias_row):
    centred = act_in - lax.optimization_barrier(jnp.mean(act_in, axis=-1, keepdims=True))
    spread = lax.optimization_barrier(jnp.mean(centred * centred, axis=-1, keepdims=True))
    return centred * lax.rsqrt(spread + eps_norm) * gain_row + bias_row

def matmul(left, right):
    return jnp.dot(left, right, precision=lax.Precision.HIGHEST)

def build_mask(row_segments):
    place_ids = jnp.arange(row_segments.shape[0], dtype=jnp.int32)
    return (row_segments[:, None] == row_segments[None, :]) & (place_ids[:, None] >= place_ids[None, :])

def shared_block(act_in, visible, w_qkv, w_out, w_up, w_down, ln_gain, ln_bias):
    length = act_in.shape[0]
    normed = low(layer_norm(act_in, ln_gain[0], ln_bias[0]))
    projected = low(low_back(jnp.einsum('ld,kde->kle', normed, w_qkv, precision=lax.Precision.HIGHEST)))
    head_view = projected.reshape(3, length, HEADS, HD)
    raw_scores = jnp.einsum('qhe,khe->hqk', head_view[0], head_view[1], precision=lax.Precision.HIGHEST) * HD ** (-0.5)
    scores = jnp.where(visible[None], low_back(raw_scores), neg_fill)
    weights_soft = low(jax.nn.softmax(scores, axis=-1))
    mixed_heads = jnp.einsum('hqk,khe->qhe', weights_soft, head_view[2], precision=lax.Precision.HIGHEST).reshape(length, D)
    attended = low(low_back(mixed_heads))
    after_attn = act_in + low_back(matmul(attended, w_out))
    second = low(layer_norm(after_attn, ln_gain[1], ln_bias[1]))
    hidden = low(jax.nn.gelu(low_back(matmul(second, w_up)), approximate=True))
    return after_attn + low_back(matmul(hidden, w_down))

def row_forward(row_tokens, row_segments, pass_embed, w_qkv, w_out, w_up, w_down, ln_gain, ln_bias):
    weights = (w_qkv, w_out, w_up, w_down, ln_gain, ln_bias)
    first_out = shared_block(row_tokens, build_mask(row_segments), *weights)
    alternated = jnp.stack([row_tokens, first_out + pass_embed[None]], axis=1).reshape(2 * SEQ, D)
    return shared_block(alternated, build_mask(jnp.repeat(row_segments, 2)), *weights)

def reference(tokens, segment_ids, pass_embed, w_qkv, w_out, w_up, w_down, ln_gain, ln_bias, cotangent):
    params = tuple((item.astype(jnp.float32) for item in (pass_embed, w_qkv, w_out, w_up, w_down, ln_gain, ln_bias)))

    def one_row(totals, row_data):
        row_tokens, row_segments, row_cotangent = row_data

        def forward(tokens_in, *weights):
            return row_forward(tokens_in, row_segments, *weights)
        row_output, pull_back = jax.vjp(forward, row_tokens.astype(jnp.float32), *params)
        gradients = pull_back(row_cotangent.astype(jnp.float32))
        summed = tuple((total + piece for total, piece in zip(totals, gradients[1:])))
        return (summed, (row_output.astype(jnp.bfloat16), gradients[0]))
    zero_sums = tuple((jnp.zeros(item.shape, jnp.float32) for item in params))
    totals, (outputs, grad_tokens) = lax.scan(one_row, zero_sums, (tokens, segment_ids, cotangent))
    return (outputs, grad_tokens, totals[1], totals[2], totals[3], totals[4], totals[5], totals[6], totals[0])
```

```python
import jax
import jax.numpy as jnp
from jax import lax
from jax.sharding import Mesh
from jax.sharding import PartitionSpec as P

HD = 64
EPS = 1e-05
NEG = -1000000000.0
F32 = jnp.float32
BF16 = jnp.bfloat16
ROWS_OVER = ("o", "x", "core")
FLIP = ((0, 1), (1, 0))


def ordered(flag, mine, theirs):
    first = flag == 0
    return jnp.stack([jnp.where(first, mine, theirs), jnp.where(first, theirs, mine)])


def take_half(array, index):
    half = array.shape[0] // 2
    return lax.dynamic_slice_in_dim(array, index * half, half, 0)


def flip_bit(array, axis, size, bit):
    return lax.ppermute(array, axis, [(i, i ^ bit) for i in range(size)])


def steps_of(outer):
    steps = [("x", 2, 1)]
    bit = 1
    while bit < outer:
        steps.append(("o", outer, bit))
        bit *= 2
    return steps


def my_bit(axis, bit):
    return (lax.axis_index(axis) // bit) % 2


def fetch_half(own):
    shape = own.shape
    flat = own.reshape(-1, shape[-1])
    x, core = lax.axis_index("x"), lax.axis_index("core")
    piece = take_half(take_half(flat, core), x)
    got = lax.ppermute(piece, "tensor", FLIP)
    got = ordered(x, got, lax.ppermute(got, "x", FLIP)).reshape(-1, shape[-1])
    got = ordered(core, got, lax.ppermute(got, "core", FLIP)).reshape(shape)
    return got


def reduce_grad(own, other, outer):
    core = lax.axis_index("core")
    other_low = other.astype(BF16)
    own_low = own.astype(BF16)
    sent = lax.ppermute(take_half(other_low, 1 - core), "core", FLIP)
    other_sum = take_half(other, core) + sent.astype(F32)
    sent = lax.ppermute(take_half(own_low, 1 - core), "core", FLIP)
    total = take_half(own, core) + sent.astype(F32)
    total = total + lax.ppermute(other_sum.astype(BF16), "tensor", FLIP).astype(F32)
    steps = steps_of(outer)
    for axis, size, bit in steps:
        mine = my_bit(axis, bit)
        low = take_half(total.astype(BF16), 1 - mine)
        total = take_half(total, mine) + flip_bit(low, axis, size, bit).astype(F32)
    whole = total.astype(BF16)
    for axis, size, bit in reversed(steps):
        got = flip_bit(whole, axis, size, bit)
        whole = ordered(my_bit(axis, bit), whole, got).reshape(-1, whole.shape[-1])
    got = lax.ppermute(whole, "core", FLIP)
    whole = ordered(core, whole, got).reshape(-1, whole.shape[-1])
    return whole.astype(F32)


def sum_small(small, outer):
    for axis, size, bit in [("core", 2, 1), ("tensor", 2, 1)] + steps_of(outer):
        small = small + flip_bit(small, axis, size, bit)
    return small


def norm_parts(act, gain, bias):
    centred = act - jnp.mean(act, axis=-1, keepdims=True)
    inverse = lax.rsqrt(jnp.mean(centred * centred, axis=-1, keepdims=True) + EPS)
    normal = centred * inverse
    return (normal * gain + bias).astype(BF16), normal, inverse


def norm_back(grad, normal, inverse, gain):
    scaled = grad * gain
    centre = jnp.mean(scaled, axis=-1, keepdims=True)
    proj = jnp.mean(scaled * normal, axis=-1, keepdims=True)
    return inverse * (scaled - centre - normal * proj)


def mm(spec, a, b):
    return jnp.einsum(spec, a, b, preferred_element_type=F32)


def gelu(values):
    return jax.nn.gelu(values, approximate=True)


def attend(q, k, v, visible):
    s = mm("hrqe,hrke->hrqk", q, k) * HD**-0.5
    s = jnp.where(visible, s, NEG)
    top = jnp.max(s, axis=-1, keepdims=True)
    e = jnp.exp(s - top)
    mass = jnp.sum(e, axis=-1, keepdims=True)
    o = mm("hrqk,hrke->hrqe", (e / mass).astype(BF16), v)
    return o.astype(BF16), top + jnp.log(mass)


def attend_back(q, k, v, do, visible, lse):
    s = mm("hrqe,hrke->hrqk", q, k) * HD**-0.5
    s = jnp.where(visible, s, NEG)
    p = jnp.exp(s - lse)
    dv = mm("hrqk,hrqe->hrke", p.astype(BF16), do)
    dp = mm("hrqe,hrke->hrqk", do, v)
    ds = (p * (dp - jnp.sum(dp * p, axis=-1, keepdims=True))).astype(BF16)
    dq = mm("hrqk,hrke->hrqe", ds, k) * HD**-0.5
    dk = mm("hrqk,hrqe->hrke", ds, q) * HD**-0.5
    return dq, dk, dv


def split_heads(t):
    r, n, d = t.shape
    return t.reshape(r, n, d // HD, HD).transpose(2, 0, 1, 3)


def join_heads(t):
    h, r, n, e = t.shape
    return t.transpose(1, 2, 0, 3).reshape(r, n, h * e)


def shards(outer, tokens, segments, pass_embed, w_qkv, w_out, w_up, w_down, gain, bias, cotangent):
    ty = lax.axis_index("tensor")
    rows = tokens.shape[0] // 2
    seq, width = tokens.shape[1], tokens.shape[2]
    mine = lambda t: lax.dynamic_slice_in_dim(t, ty * rows, rows, 0)
    x = mine(tokens).astype(F32)
    seg = mine(segments)
    cot = mine(cotangent).reshape(rows, seq, 2, width).transpose(0, 2, 1, 3).reshape(rows, 2 * seq, width)
    wqkv = jnp.concatenate([w_qkv, fetch_half(w_qkv)], axis=2)
    wout = jnp.concatenate([w_out, fetch_half(w_out)], axis=0)
    wup = jnp.concatenate([w_up, fetch_half(w_up)], axis=1)
    wdown = jnp.concatenate([w_down, fetch_half(w_down)], axis=0)

    place = jnp.arange(seq, dtype=jnp.int32)
    same = seg[:, :, None] == seg[:, None, :]
    vis_one = (same & (place[:, None] >= place[None, :])[None])[None]
    place2 = jnp.concatenate([2 * place, 2 * place + 1])
    seg2 = jnp.concatenate([seg, seg], axis=1)
    vis_two = ((seg2[:, :, None] == seg2[:, None, :]) & (place2[:, None] >= place2[None, :])[None])[None]

    def project(a):
        return [split_heads(mm("rld,de->rle", a, wqkv[j]).astype(BF16)) for j in range(3)]

    def rest(h, o):
        h1 = h + mm("rle,ed->rld", o, wout)
        n2, hat2, inv2 = norm_parts(h1, gain[1], bias[1])
        u = mm("rld,df->rlf", n2, wup)
        g = gelu(u).astype(BF16)
        z = h1 + mm("rlf,fd->rld", g, wdown)
        return z, (o, n2, hat2, inv2, u, g)

    def rest_back(db, kept):
        o, n2, hat2, inv2, u, g = kept
        dm = db.astype(BF16)
        dg = mm("rld,fd->rlf", dm, wdown)
        du = jax.vjp(gelu, u)[1](dg)[0].astype(BF16)
        dn2 = mm("rlf,df->rld", du, wup)
        dh1 = db + norm_back(dn2, hat2, inv2, gain[1])
        dp = dh1.astype(BF16)
        do = split_heads(mm("rld,ed->rle", dp, wout).astype(BF16))
        grads = (jnp.sum(dn2 * hat2, axis=(0, 1)), jnp.sum(dn2, axis=(0, 1)))
        return dh1, do, (g, dm, n2, du, o, dp), grads

    a_e, hat_e, inv_e = norm_parts(x, gain[0], bias[0])
    qkv_e = project(a_e)
    o1, lse1 = attend(*qkv_e, vis_one)
    y, kept1 = rest(x, join_heads(o1))
    h_o = y + pass_embed
    a_o, hat_o, inv_o = norm_parts(h_o, gain[0], bias[0])
    qkv_o = project(a_o)
    both = [jnp.concatenate([e, o], axis=2) for e, o in zip(qkv_e, qkv_o)]
    o2, lse2 = attend(*both, vis_two)
    u2 = jnp.concatenate([x, h_o], axis=1)
    z, kept2 = rest(u2, join_heads(o2))
    out_mine = z.astype(BF16).reshape(rows, 2, seq, width).transpose(0, 2, 1, 3).reshape(rows, 2 * seq, width)
    out = ordered(ty, out_mine, lax.ppermute(out_mine, "tensor", FLIP)).reshape(cotangent.shape)

    dh1_2, do2, terms2, ln2 = rest_back(cot.astype(F32), kept2)
    dqkv2 = attend_back(*both, do2, vis_two, lse2)

    def back_project(d):
        return sum(mm("rle,de->rld", d[j], wqkv[j]) for j in range(3))

    d_o = [join_heads(t[:, :, seq:]).astype(BF16) for t in dqkv2]
    da_o = back_project(d_o)
    dy = dh1_2[:, seq:] + norm_back(da_o, hat_o, inv_o, gain[0])

    dh1_1, do1, terms1, ln1 = rest_back(dy, kept1)
    dqkv1 = attend_back(*qkv_e, do1, vis_one, lse1)
    d_e = [join_heads(t[:, :, :seq] + s).astype(BF16) for t, s in zip(dqkv2, dqkv1)]
    da_e = back_project(d_e)
    grad_tokens = dh1_1 + dh1_2[:, :seq] + norm_back(da_e, hat_e, inv_e, gain[0])
    gt = grad_tokens.astype(BF16)
    gt = ordered(ty, gt, lax.ppermute(gt, "tensor", FLIP)).reshape(tokens.shape).astype(F32)

    def wgrad(i, j):
        one = mm("rla,rlb->ab", terms1[i], terms1[j])
        return one + mm("rla,rlb->ab", terms2[i], terms2[j])

    half = lambda t, axis: jnp.split(t, 2, axis=axis)
    g_down = reduce_grad(*half(wgrad(0, 1), 0), outer)
    g_up = reduce_grad(*half(wgrad(2, 3), 1), outer)
    g_out = reduce_grad(*half(wgrad(4, 5), 0), outer)
    gq = jnp.stack([mm("rla,rlb->ab", a_e, e) + mm("rla,rlb->ab", a_o, o) for e, o in zip(d_e, d_o)])
    g_qkv = reduce_grad(*[t.reshape(3 * width, -1) for t in half(gq, 2)], outer).reshape(3, width, -1)

    small = jnp.stack(
        [
            jnp.sum(da_e * hat_e, axis=(0, 1)) + jnp.sum(da_o * hat_o, axis=(0, 1)),
            ln1[0] + ln2[0],
            jnp.sum(da_e, axis=(0, 1)) + jnp.sum(da_o, axis=(0, 1)),
            ln1[1] + ln2[1],
            jnp.sum(dy, axis=(0, 1)),
        ]
    )
    small = sum_small(small, outer)
    return out, gt, g_qkv, g_out, g_up, g_down, small[0:2], small[2:4], small[4]


def solution(mesh):
    outer = mesh.shape["dp"] // 4
    fine = Mesh(mesh.devices.reshape(outer, 2, 2, mesh.shape["tensor"]), ("o", "x", "core", "tensor"))
    rows = ROWS_OVER
    placed = (
        P(rows, None, None),
        P(rows, None),
        P(),
        P(None, None, "tensor"),
        P("tensor", None),
        P(None, "tensor"),
        P("tensor", None),
        P(),
        P(),
        P(rows, None, None),
    )

    def body(*args):
        return shards(outer, *args)

    return jax.shard_map(
        body,
        mesh=fine,
        in_specs=placed,
        out_specs=(
            P(rows, None, None),
            P(rows, None, None),
            P(None, None, "tensor"),
            P("tensor", None),
            P(None, "tensor"),
            P("tensor", None),
            P(),
            P(),
            P(),
        ),
        check_vma=False,
    )
```

```python
import functools

import jax
import jax.numpy as jnp
from jax import lax
from jax.experimental import pallas as pl
from jax.experimental.pallas import tpu as pltpu
from jax.sharding import Mesh
from jax.sharding import PartitionSpec as P

HD = 64
EPS = 1e-05
NEG = -1000000000.0
F32 = jnp.float32
BF16 = jnp.bfloat16
ROWS_OVER = ("o", "x", "core")
FLIP = ((0, 1), (1, 0))
VMEM_LIMIT = 60 * 1024 * 1024


def ordered(flag, mine, theirs):
    first = flag == 0
    return jnp.stack([jnp.where(first, mine, theirs), jnp.where(first, theirs, mine)])


def take_half(array, index):
    half = array.shape[0] // 2
    return lax.dynamic_slice_in_dim(array, index * half, half, 0)


def flip_bit(array, axis, size, bit):
    return lax.ppermute(array, axis, [(i, i ^ bit) for i in range(size)])


def steps_of(outer):
    steps = [("x", 2, 1)]
    bit = 1
    while bit < outer:
        steps.append(("o", outer, bit))
        bit *= 2
    return steps


def my_bit(axis, bit):
    return (lax.axis_index(axis) // bit) % 2


def fetch_half(own):
    shape = own.shape
    flat = own.reshape(-1, shape[-1])
    x, core = lax.axis_index("x"), lax.axis_index("core")
    piece = take_half(take_half(flat, core), x)
    got = lax.ppermute(piece, "tensor", FLIP)
    got = ordered(x, got, lax.ppermute(got, "x", FLIP)).reshape(-1, shape[-1])
    got = ordered(core, got, lax.ppermute(got, "core", FLIP)).reshape(shape)
    return got


def reduce_grad(own, other, outer):
    core = lax.axis_index("core")
    other_low = other.astype(BF16)
    own_low = own.astype(BF16)
    sent = lax.ppermute(take_half(other_low, 1 - core), "core", FLIP)
    other_sum = take_half(other, core) + sent.astype(F32)
    sent = lax.ppermute(take_half(own_low, 1 - core), "core", FLIP)
    total = take_half(own, core) + sent.astype(F32)
    total = total + lax.ppermute(other_sum.astype(BF16), "tensor", FLIP).astype(F32)
    steps = steps_of(outer)
    for axis, size, bit in steps:
        mine = my_bit(axis, bit)
        low = take_half(total.astype(BF16), 1 - mine)
        total = take_half(total, mine) + flip_bit(low, axis, size, bit).astype(F32)
    whole = total.astype(BF16)
    for axis, size, bit in reversed(steps):
        got = flip_bit(whole, axis, size, bit)
        whole = ordered(my_bit(axis, bit), whole, got).reshape(-1, whole.shape[-1])
    got = lax.ppermute(whole, "core", FLIP)
    whole = ordered(core, whole, got).reshape(-1, whole.shape[-1])
    return whole.astype(F32)


def sum_small(small, outer):
    for axis, size, bit in [("core", 2, 1), ("tensor", 2, 1)] + steps_of(outer):
        small = small + flip_bit(small, axis, size, bit)
    return small


def dot(a, b):
    return lax.dot_general(a, b, (((1,), (0,)), ((), ())), preferred_element_type=F32)


def dot_nt(a, b):
    return lax.dot_general(a, b, (((1,), (1,)), ((), ())), preferred_element_type=F32)


def dot_tn(a, b):
    return lax.dot_general(a, b, (((0,), (0,)), ((), ())), preferred_element_type=F32)


def norm_stats(h):
    centred = h - jnp.mean(h, axis=-1, keepdims=True)
    inverse = lax.rsqrt(jnp.mean(centred * centred, axis=-1, keepdims=True) + EPS)
    return centred * inverse, inverse


def norm_back(grad, normal, inverse, gain):
    scaled = grad * gain
    centre = jnp.mean(scaled, axis=-1, keepdims=True)
    proj = jnp.mean(scaled * normal, axis=-1, keepdims=True)
    return inverse * (scaled - centre - normal * proj)


def gelu_parts(u):
    c = 0.7978845608028654
    a = 0.044715 * c
    square = u * u
    half = 0.5 + 0.5 * jnp.tanh(u * (c + a * square))
    g = u * half
    return g, half + g * (1.0 - half) * (2.0 * c + 6.0 * a * square)


def whole(shape):
    return pl.BlockSpec(shape, lambda *_: (0,) * len(shape))


def call(body, grid, ins, outs, scratch=(), cost=(0, 0), name=None):
    return pl.pallas_call(
        body,
        grid=grid,
        in_specs=[s for _, s in ins],
        out_specs=[s for _, s in outs],
        out_shape=[a for a, _ in outs],
        scratch_shapes=scratch,
        compiler_params=pltpu.CompilerParams(
            dimension_semantics=("arbitrary",) * len(grid), vmem_limit_bytes=VMEM_LIMIT
        ),
        cost_estimate=pl.CostEstimate(
            flops=int(cost[0]), bytes_accessed=int(cost[1]), transcendentals=0
        ),
        name=name,
    )(*[a for a, _ in ins])


def sds(shape, dtype):
    return jax.ShapeDtypeStruct(shape, dtype)


def head_mask(h):
    lane = lax.broadcasted_iota(jnp.int32, (1, 2 * HD), 1)
    return jnp.where((lane >= h * HD) & (lane < (h + 1) * HD), 1.0, 0.0)


def first_half_lanes(shape):
    return lax.broadcasted_iota(jnp.int32, shape, 1) < HD


def pair_column(t, h):
    return t[:, h * HD : h * HD + 1]


def attend_first_body(rows, seq, pairs, a_ref, w_ref, bias_ref, qkv_ref, o_ref, lse_ref):
    a = a_ref[...]
    for j in range(3):
        qkv_ref[j] = dot(a, w_ref[j]).astype(BF16)
    for r in range(rows):
        sl = slice(r * seq, (r + 1) * seq)
        bias = bias_ref[r]
        for p in range(pairs):
            ln = slice(p * 2 * HD, (p + 1) * 2 * HD)
            q, k, v = (qkv_ref[j, sl, ln] for j in range(3))
            got = []
            for h in range(2):
                qm = q * (head_mask(h) * HD**-0.5).astype(BF16)
                s = dot_nt(qm, k) + bias
                top = jnp.max(s, axis=1, keepdims=True)
                e = jnp.exp(s - top)
                mass = jnp.sum(e, axis=1, keepdims=True)
                got.append((dot(e.astype(BF16), v) * (1.0 / mass), top + jnp.log(mass)))
            first = first_half_lanes((seq, 2 * HD))
            o_ref[sl, ln] = jnp.where(first, got[0][0], got[1][0]).astype(BF16)
            lse_ref[sl, ln] = jnp.where(first, got[0][1], got[1][1])


def attend_first(a, w, bias):
    rows, seq = bias.shape[0], bias.shape[1]
    n, d = a.shape
    f = w.shape[2]
    return call(
        functools.partial(attend_first_body, rows, seq, f // (2 * HD)),
        (1,),
        [(a, whole(a.shape)), (w, whole(w.shape)), (bias, whole(bias.shape))],
        [
            (sds((3, n, f), BF16), whole((3, n, f))),
            (sds((n, f), BF16), whole((n, f))),
            (sds((n, f), F32), whole((n, f))),
        ],
        cost=(6 * n * d * f + 16 * n * seq * f, 0),
        name="attend_first",
    )


def mlp_first_body(
    x_ref, o_ref, wout_ref, gb_ref, wup_ref, wdown_ref,
    h1_ref, n2_ref, g_ref, d_ref, ho_ref, ao_ref,
):
    j = pl.program_id(0)

    @pl.when(j == 0)
    def _():
        h1 = x_ref[...].astype(F32) + dot(o_ref[...], wout_ref[...])
        h1_ref[...] = h1
        normal, _ = norm_stats(h1)
        n2_ref[...] = (normal * gb_ref[1:2] + gb_ref[3:4]).astype(BF16)
        ho_ref[...] = h1 + gb_ref[4:5]

    u = dot(n2_ref[...], wup_ref[...])
    g, d = gelu_parts(u)
    g = g.astype(BF16)
    g_ref[...] = g
    d_ref[...] = d.astype(BF16)
    ho_ref[...] += dot(g, wdown_ref[...])

    @pl.when(j == pl.num_programs(0) - 1)
    def _():
        normal, _ = norm_stats(ho_ref[...])
        ao_ref[...] = (normal * gb_ref[0:1] + gb_ref[2:3]).astype(BF16)


def mlp_first(x, o, wout, gb, wup, wdown):
    n, d = x.shape
    ff = wup.shape[1]
    c = 512
    return call(
        mlp_first_body,
        (ff // c,),
        [
            (x, whole(x.shape)),
            (o, whole(o.shape)),
            (wout, whole(wout.shape)),
            (gb, whole(gb.shape)),
            (wup, pl.BlockSpec((d, c), lambda j: (0, j))),
            (wdown, pl.BlockSpec((c, d), lambda j: (j, 0))),
        ],
        [
            (sds((n, d), F32), whole((n, d))),
            (sds((n, d), BF16), whole((n, d))),
            (sds((n, ff), BF16), pl.BlockSpec((n, c), lambda j: (0, j))),
            (sds((n, ff), BF16), pl.BlockSpec((n, c), lambda j: (0, j))),
            (sds((n, d), F32), whole((n, d))),
            (sds((n, d), BF16), whole((n, d))),
        ],
        cost=(2 * n * d * (2 * ff + d), 0),
        name="mlp_first",
    )


def attend_second_body(
    rows, seq, pairs, a_ref, w_ref, incl_ref, strict_ref, qkve_ref, o1_ref, lse1_ref,
    qkvo_ref, o2_ref, lse2_ref,
):
    a = a_ref[...]
    for j in range(3):
        qkvo_ref[j] = dot(a, w_ref[j]).astype(BF16)

    def row(r, _):
        sl = pl.ds(pl.multiple_of(r * seq, seq), seq)
        incl, strict = incl_ref[r], strict_ref[r]
        for p in range(pairs):
            ln = slice(p * 2 * HD, (p + 1) * 2 * HD)
            qe, ke, ve = (qkve_ref[j, sl, ln] for j in range(3))
            qo, ko, vo = (qkvo_ref[j, sl, ln] for j in range(3))
            o1 = o1_ref[sl, ln].astype(F32)
            lse1 = lse1_ref[sl, ln]
            even, odd = [], []
            for h in range(2):
                scale = (head_mask(h) * HD**-0.5).astype(BF16)
                s = dot_nt(qe * scale, ko) + strict
                old = pair_column(lse1, h)
                top = jnp.maximum(old, jnp.max(s, axis=1, keepdims=True))
                e = jnp.exp(s - top)
                kept = jnp.exp(old - top)
                mass = kept + jnp.sum(e, axis=1, keepdims=True)
                o = (kept * o1 + dot(e.astype(BF16), vo)) * (1.0 / mass)
                even.append((o, top + jnp.log(mass)))
                qm = qo * scale
                s1 = dot_nt(qm, ke) + incl
                s2 = dot_nt(qm, ko) + incl
                top = jnp.max(jnp.maximum(s1, s2), axis=1, keepdims=True)
                e1 = jnp.exp(s1 - top)
                e2 = jnp.exp(s2 - top)
                mass = jnp.sum(e1 + e2, axis=1, keepdims=True)
                o = (dot(e1.astype(BF16), ve) + dot(e2.astype(BF16), vo)) * (1.0 / mass)
                odd.append((o, top + jnp.log(mass)))
            first = first_half_lanes((seq, 2 * HD))
            for i, got in enumerate((even, odd)):
                o2_ref[i, sl, ln] = jnp.where(first, got[0][0], got[1][0]).astype(BF16)
                lse2_ref[i, sl, ln] = jnp.where(first, got[0][1], got[1][1])
        return 0

    lax.fori_loop(0, rows, row, 0)


def attend_second(a, w, incl, strict, qkve, o1, lse1):
    rows, seq = incl.shape[0], incl.shape[1]
    n, d = a.shape
    f = w.shape[2]
    b = 256
    col = lambda lead: pl.BlockSpec(lead + (b,), lambda i: (0,) * len(lead) + (i,))
    return call(
        functools.partial(attend_second_body, rows, seq, b // (2 * HD)),
        (f // b,),
        [
            (a, whole(a.shape)),
            (w, col((3, d))),
            (incl, whole(incl.shape)),
            (strict, whole(strict.shape)),
            (qkve, col((3, n))),
            (o1, col((n,))),
            (lse1, col((n,))),
        ],
        [
            (sds((3, n, f), BF16), col((3, n))),
            (sds((2, n, f), BF16), col((2, n))),
            (sds((2, n, f), F32), col((2, n))),
        ],
        cost=(6 * n * d * f + 48 * n * seq * f, 0),
        name="attend_second",
    )


def weave(seq):
    i = lax.broadcasted_iota(jnp.int32, (2 * seq, 2 * seq), 0)
    k = lax.broadcasted_iota(jnp.int32, (2 * seq, 2 * seq), 1)
    place = jnp.where(k < seq, 2 * k, 2 * (k - seq) + 1)
    return jnp.where(i == place, 1.0, 0.0).astype(BF16)


def mlp_second_body(
    rows, seq, x_ref, ho_ref, o_ref, cot_ref, wout_ref, gb_ref, wup_ref, wdown_ref,
    out_ref, n2_ref, g_ref, du_ref, dh1_ref, dp_ref, do_ref, sums_ref, dm_ref,
    h1_ref, z_ref, dn_ref,
):
    j = pl.program_id(0)
    n = rows * seq
    halves = (slice(0, n), slice(n, 2 * n))

    @pl.when(j == 0)
    def _():
        for i, sl in enumerate(halves):
            start = x_ref[...].astype(F32) if i == 0 else ho_ref[...]
            h1 = start + dot(o_ref[i], wout_ref[...])
            h1_ref[sl] = h1
            normal, _ = norm_stats(h1)
            n2_ref[sl] = (normal * gb_ref[1:2] + gb_ref[3:4]).astype(BF16)
        z_ref[...] = jnp.zeros_like(z_ref)
        dn_ref[...] = jnp.zeros_like(dn_ref)
        mix = weave(seq)
        for r in range(rows):
            parted = dot_tn(mix, cot_ref[r]).astype(BF16)
            for i in range(2):
                dm_ref[i * n + r * seq : i * n + (r + 1) * seq] = parted[i * seq : (i + 1) * seq]

    for sl in halves:
        u = dot(n2_ref[sl], wup_ref[...])
        dg = dot_nt(dm_ref[sl], wdown_ref[...])
        g, d = gelu_parts(u)
        g = g.astype(BF16)
        du = (dg * d).astype(BF16)
        g_ref[sl] = g
        du_ref[sl] = du
        z_ref[sl] += dot(g, wdown_ref[...])
        dn_ref[sl] += dot_nt(du, wup_ref[...])

    @pl.when(j == pl.num_programs(0) - 1)
    def _():
        mix = weave(seq)
        for r in range(rows):
            pair = [slice(i * n + r * seq, i * n + (r + 1) * seq) for i in range(2)]
            z = jnp.concatenate([(h1_ref[s] + z_ref[s]).astype(BF16) for s in pair], axis=0)
            out_ref[r] = dot(mix, z).astype(BF16)
        gain_sum = jnp.zeros_like(gb_ref[0:1])
        bias_sum = jnp.zeros_like(gb_ref[0:1])
        for i in range(2 * rows):
            sl = slice(i * seq, (i + 1) * seq)
            normal, inverse = norm_stats(h1_ref[sl])
            dn = dn_ref[sl]
            gain_sum += jnp.sum(dn * normal, axis=0, keepdims=True)
            bias_sum += jnp.sum(dn, axis=0, keepdims=True)
            dh1 = dm_ref[sl].astype(F32) + norm_back(dn, normal, inverse, gb_ref[1:2])
            dh1_ref[sl] = dh1
            dp = dh1.astype(BF16)
            dp_ref[sl] = dp
            do_ref[sl] = dot_nt(dp, wout_ref[...]).astype(BF16)
        sums_ref[0:1] = gain_sum
        sums_ref[1:2] = bias_sum


def mlp_second(x, ho, o2, cot, wout, gb, wup, wdown, seq):
    n, d = x.shape
    ff = wup.shape[1]
    rows = n // seq
    c = 512
    blk = pl.BlockSpec((2 * n, c), lambda j: (0, j))
    return call(
        functools.partial(mlp_second_body, rows, seq),
        (ff // c,),
        [
            (x, whole(x.shape)),
            (ho, whole(ho.shape)),
            (o2, whole(o2.shape)),
            (cot, whole(cot.shape)),
            (wout, whole(wout.shape)),
            (gb, whole(gb.shape)),
            (wup, pl.BlockSpec((d, c), lambda j: (0, j))),
            (wdown, pl.BlockSpec((c, d), lambda j: (j, 0))),
        ],
        [
            (sds((rows, 2 * seq, d), BF16), whole((rows, 2 * seq, d))),
            (sds((2 * n, d), BF16), whole((2 * n, d))),
            (sds((2 * n, ff), BF16), blk),
            (sds((2 * n, ff), BF16), blk),
            (sds((2 * n, d), F32), whole((2 * n, d))),
            (sds((2 * n, d), BF16), whole((2 * n, d))),
            (sds((2 * n, d), BF16), whole((2 * n, d))),
            (sds((2, d), F32), whole((2, d))),
            (sds((2 * n, d), BF16), whole((2 * n, d))),
        ],
        scratch=[pltpu.VMEM((2 * n, d), F32)] * 3,
        cost=(2 * n * d * (8 * ff + 4 * d), 0),
        name="mlp_second",
    )


def attend_back_body(
    rows, seq, pairs, w_ref, incl_ref, strict_ref, qkve_ref, qkvo_ref, o2_ref, lse2_ref, do_ref,
    dh1_ref, ho_ref, gb_ref,
    dqkvo_ref, dqkve_ref, dy_ref, sums_ref, da_ref,
):
    j = pl.program_id(0)

    def row(r, _):
        sl = pl.ds(pl.multiple_of(r * seq, seq), seq)
        incl, strict = incl_ref[r], strict_ref[r]
        for p in range(pairs):
            ln = slice(p * 2 * HD, (p + 1) * 2 * HD)
            qe, ke, ve = (qkve_ref[t, sl, ln] for t in range(3))
            qo, ko, vo = (qkvo_ref[t, sl, ln] for t in range(3))
            doe, doo = do_ref[0, sl, ln], do_ref[1, sl, ln]
            de = doe.astype(F32) * o2_ref[0, sl, ln].astype(F32)
            dd = doo.astype(F32) * o2_ref[1, sl, ln].astype(F32)
            lse_e, lse_o = lse2_ref[0, sl, ln], lse2_ref[1, sl, ln]
            acc = [None] * 6
            first = first_half_lanes((seq, 2 * HD))
            for h in range(2):
                on = head_mask(h)
                low = on.astype(BF16)
                scale = (on * HD**-0.5).astype(BF16)
                delta_e = jnp.sum(de * on, axis=1, keepdims=True)
                delta_o = jnp.sum(dd * on, axis=1, keepdims=True)
                le, lo = pair_column(lse_e, h), pair_column(lse_o, h)
                qme, qmo = qe * scale, qo * scale
                dme, dmo = doe * low, doo * low

                def block(qm, k, bias, lse, dm, v, delta):
                    pr = jnp.exp(dot_nt(qm, k) + bias - lse)
                    ds = (pr * (dot_nt(dm, v) - delta)).astype(BF16)
                    return pr.astype(BF16), ds

                p1, s1 = block(qme, ko, strict, le, dme, vo, delta_e)
                p2, s2 = block(qmo, ke, incl, lo, dmo, ve, delta_o)
                p3, s3 = block(qmo, ko, incl, lo, dmo, vo, delta_o)
                new = [
                    dot(s1, ko),
                    dot_tn(s2, qo),
                    dot_tn(p2, doo),
                    dot(s2, ke) + dot(s3, ko),
                    dot_tn(s1, qe) + dot_tn(s3, qo),
                    dot_tn(p1, doe) + dot_tn(p3, doo),
                ]
                acc = [t if o is None else jnp.where(first, o, t) for o, t in zip(acc, new)]
            sc = HD**-0.5
            for t in range(3):
                k = 1.0 if t == 2 else sc
                dqkve_ref[t, sl, ln] = acc[t] * k
                dqkvo_ref[t, sl, ln] = (acc[3 + t] * k).astype(BF16)
        return 0

    lax.fori_loop(0, rows, row, 0)
    da = dot_nt(dqkvo_ref[0], w_ref[0])
    da += dot_nt(dqkvo_ref[1], w_ref[1])
    da += dot_nt(dqkvo_ref[2], w_ref[2])

    @pl.when(j == 0)
    def _():
        da_ref[...] = da

    @pl.when(j > 0)
    def _():
        da_ref[...] += da

    @pl.when(j == pl.num_programs(0) - 1)
    def _():
        gain_sum = jnp.zeros_like(gb_ref[0:1])
        bias_sum = jnp.zeros_like(gb_ref[0:1])
        pass_sum = jnp.zeros_like(gb_ref[0:1])
        for i in range(rows):
            sl = slice(i * seq, (i + 1) * seq)
            normal, inverse = norm_stats(ho_ref[sl])
            da = da_ref[sl]
            gain_sum += jnp.sum(da * normal, axis=0, keepdims=True)
            bias_sum += jnp.sum(da, axis=0, keepdims=True)
            dy = dh1_ref[sl] + norm_back(da, normal, inverse, gb_ref[0:1])
            dy_ref[sl] = dy
            pass_sum += jnp.sum(dy, axis=0, keepdims=True)
        sums_ref[0:1] = gain_sum
        sums_ref[1:2] = bias_sum
        sums_ref[2:3] = pass_sum


def attend_back(w, incl, strict, qkve, qkvo, o2, lse2, do, dh1, ho, gb):
    rows, seq = incl.shape[0], incl.shape[1]
    n, d = ho.shape
    f = w.shape[2]
    b = 256
    col = lambda lead: pl.BlockSpec(lead + (b,), lambda i: (0,) * len(lead) + (i,))
    return call(
        functools.partial(attend_back_body, rows, seq, b // (2 * HD)),
        (f // b,),
        [
            (w, col((3, d))),
            (incl, whole(incl.shape)),
            (strict, whole(strict.shape)),
            (qkve, col((3, n))),
            (qkvo, col((3, n))),
            (o2, col((2, n))),
            (lse2, col((2, n))),
            (do.reshape(2, n, f), col((2, n))),
            (dh1, pl.BlockSpec((n, d), lambda i: (1, 0))),
            (ho, whole(ho.shape)),
            (gb, whole(gb.shape)),
        ],
        [
            (sds((3, n, f), BF16), col((3, n))),
            (sds((3, n, f), F32), col((3, n))),
            (sds((n, d), F32), whole((n, d))),
            (sds((3, d), F32), whole((3, d))),
        ],
        scratch=[pltpu.VMEM((n, d), F32)],
        cost=(6 * n * d * f + 120 * n * seq * f, 0),
        name="attend_back",
    )


def mlp_back_body(
    rows, seq, dy_ref, h1_ref, wout_ref, gb_ref, d_ref, wup_ref, wdown_ref,
    du_ref, dh1_ref, dp_ref, do_ref, sums_ref, dm_ref, dn_ref,
):
    j = pl.program_id(0)

    @pl.when(j == 0)
    def _():
        dm_ref[...] = dy_ref[...].astype(BF16)
        dn_ref[...] = jnp.zeros_like(dn_ref)

    dg = dot_nt(dm_ref[...], wdown_ref[...])
    du = (dg * d_ref[...].astype(F32)).astype(BF16)
    du_ref[...] = du
    dn_ref[...] += dot_nt(du, wup_ref[...])

    @pl.when(j == pl.num_programs(0) - 1)
    def _():
        gain_sum = jnp.zeros_like(gb_ref[0:1])
        bias_sum = jnp.zeros_like(gb_ref[0:1])
        for i in range(rows):
            sl = slice(i * seq, (i + 1) * seq)
            normal, inverse = norm_stats(h1_ref[sl])
            dn = dn_ref[sl]
            gain_sum += jnp.sum(dn * normal, axis=0, keepdims=True)
            bias_sum += jnp.sum(dn, axis=0, keepdims=True)
            dh1 = dy_ref[sl] + norm_back(dn, normal, inverse, gb_ref[1:2])
            dh1_ref[sl] = dh1
            dp = dh1.astype(BF16)
            dp_ref[sl] = dp
            do_ref[sl] = dot_nt(dp, wout_ref[...]).astype(BF16)
        sums_ref[0:1] = gain_sum
        sums_ref[1:2] = bias_sum


def mlp_back(dy, h1, wout, gb, dgelu, wup, wdown, seq):
    n, d = dy.shape
    ff = wup.shape[1]
    c = 512
    blk = pl.BlockSpec((n, c), lambda j: (0, j))
    return call(
        functools.partial(mlp_back_body, n // seq, seq),
        (ff // c,),
        [
            (dy, whole(dy.shape)),
            (h1, whole(h1.shape)),
            (wout, whole(wout.shape)),
            (gb, whole(gb.shape)),
            (dgelu, blk),
            (wup, pl.BlockSpec((d, c), lambda j: (0, j))),
            (wdown, pl.BlockSpec((c, d), lambda j: (j, 0))),
        ],
        [
            (sds((n, ff), BF16), blk),
            (sds((n, d), F32), whole((n, d))),
            (sds((n, d), BF16), whole((n, d))),
            (sds((n, d), BF16), whole((n, d))),
            (sds((2, d), F32), whole((2, d))),
            (sds((n, d), BF16), whole((n, d))),
        ],
        scratch=[pltpu.VMEM((n, d), F32)],
        cost=(2 * n * d * (2 * ff + d), 0),
        name="mlp_back",
    )


def attend_back_even_body(
    rows, seq, pairs, w_ref, incl_ref, qkve_ref, o1_ref, lse1_ref, do1_ref, o2_ref, lse2_ref, do2_ref,
    part_ref, dh1_ref, dh2_ref, x_ref, gb_ref,
    dqkv_ref, gt_ref, sums_ref, da_ref,
):
    j = pl.program_id(0)

    def row(r, _):
        sl = pl.ds(pl.multiple_of(r * seq, seq), seq)
        incl = incl_ref[r]
        for p in range(pairs):
            ln = slice(p * 2 * HD, (p + 1) * 2 * HD)
            q, k, v = (qkve_ref[t, sl, ln] for t in range(3))
            do1 = do1_ref[sl, ln].astype(F32)
            do2 = do2_ref[0, sl, ln].astype(F32)
            lse1 = lse1_ref[sl, ln]
            ratio = jnp.exp(lse1 - lse2_ref[0, sl, ln])
            do2 = do2 * ratio
            both = (do1 + do2).astype(BF16)
            dd = do1 * o1_ref[sl, ln].astype(F32) + do2 * o2_ref[0, sl, ln].astype(F32)
            acc = [None] * 3
            first = first_half_lanes((seq, 2 * HD))
            for h in range(2):
                on = head_mask(h)
                delta = jnp.sum(dd * on, axis=1, keepdims=True)
                qm = q * (on * HD**-0.5).astype(BF16)
                pr = jnp.exp(dot_nt(qm, k) + incl - pair_column(lse1, h))
                ds = (pr * (dot_nt(both * on.astype(BF16), v) - delta)).astype(BF16)
                new = [dot(ds, k), dot_tn(ds, q), dot_tn(pr.astype(BF16), both)]
                acc = [t if o is None else jnp.where(first, o, t) for o, t in zip(acc, new)]
            for t in range(3):
                sc = 1.0 if t == 2 else HD**-0.5
                dqkv_ref[t, sl, ln] = (acc[t] * sc + part_ref[t, sl, ln]).astype(BF16)
        return 0

    lax.fori_loop(0, rows, row, 0)
    da = dot_nt(dqkv_ref[0], w_ref[0])
    da += dot_nt(dqkv_ref[1], w_ref[1])
    da += dot_nt(dqkv_ref[2], w_ref[2])

    @pl.when(j == 0)
    def _():
        da_ref[...] = da

    @pl.when(j > 0)
    def _():
        da_ref[...] += da

    @pl.when(j == pl.num_programs(0) - 1)
    def _():
        gain_sum = jnp.zeros_like(gb_ref[0:1])
        bias_sum = jnp.zeros_like(gb_ref[0:1])
        for i in range(rows):
            sl = slice(i * seq, (i + 1) * seq)
            normal, inverse = norm_stats(x_ref[sl].astype(F32))
            da = da_ref[sl]
            gain_sum += jnp.sum(da * normal, axis=0, keepdims=True)
            bias_sum += jnp.sum(da, axis=0, keepdims=True)
            back = norm_back(da, normal, inverse, gb_ref[0:1])
            gt_ref[sl] = (dh1_ref[sl] + dh2_ref[sl] + back).astype(BF16)
        sums_ref[0:1] = gain_sum
        sums_ref[1:2] = bias_sum


def attend_back_even(w, incl, qkve, o1, lse1, do1, o2, lse2, do2, part, dh1, dh2, x, gb):
    rows, seq = incl.shape[0], incl.shape[1]
    n, d = x.shape
    f = w.shape[2]
    b = 256
    col = lambda lead: pl.BlockSpec(lead + (b,), lambda i: (0,) * len(lead) + (i,))
    return call(
        functools.partial(attend_back_even_body, rows, seq, b // (2 * HD)),
        (f // b,),
        [
            (w, col((3, d))),
            (incl, whole(incl.shape)),
            (qkve, col((3, n))),
            (o1, col((n,))),
            (lse1, col((n,))),
            (do1, col((n,))),
            (o2, col((1, n))),
            (lse2, col((1, n))),
            (do2.reshape(2, n, f), col((1, n))),
            (part, col((3, n))),
            (dh1, whole((n, d))),
            (dh2, whole((n, d))),
            (x, whole(x.shape)),
            (gb, whole(gb.shape)),
        ],
        [
            (sds((3, n, f), BF16), col((3, n))),
            (sds((n, d), BF16), whole((n, d))),
            (sds((2, d), F32), whole((2, d))),
        ],
        scratch=[pltpu.VMEM((n, d), F32)],
        cost=(6 * n * d * f + 40 * n * seq * f, 0),
        name="attend_back_even",
    )


def mask_biases(seg):
    seq = seg.shape[1]
    place = jnp.arange(seq, dtype=jnp.int32)
    same = seg[:, :, None] == seg[:, None, :]
    below = (place[:, None] > place[None, :])[None]
    incl = (place[:, None] >= place[None, :])[None]
    bias = lambda m: jnp.where(same & m, 0.0, NEG).astype(F32)
    return bias(incl), bias(below)


def mm(spec, a, b):
    return jnp.einsum(spec, a, b, preferred_element_type=F32)


def local_part(x, seg, cot, gb, fetch_qkv, fetch_rest, send_out):
    rows, seq = seg.shape
    width = x.shape[1]
    n = x.shape[0]
    incl, strict = mask_biases(seg)
    normal, _ = norm_stats(x.astype(F32))
    a_e = (normal * gb[0] + gb[2]).astype(BF16)
    wq_own, fetched = fetch_qkv()
    first = attend_first(a_e, wq_own, incl)
    second = attend_first(a_e, fetched, incl)
    qkv_e, o1, lse1 = (jnp.concatenate([s, t], axis=-1) for s, t in zip(first, second))
    wqkv = jnp.concatenate([wq_own, fetched], axis=2)
    wout, wup, wdown = fetch_rest()
    h1, n2_1, g1, d1, ho, a_o = mlp_first(x, o1, wout, gb, wup, wdown)
    qkv_o, o2, lse2 = attend_second(a_o, wqkv, incl, strict, qkv_e, o1, lse1)
    out, n2_2, g2, du2, dh1_2, dp2, do2, sums2, dm2 = mlp_second(x, ho, o2, cot, wout, gb, wup, wdown, seq)
    out = send_out(out)
    dqkv_o, part, dy, sums_o = attend_back(wqkv, incl, strict, qkv_e, qkv_o, o2, lse2, do2, dh1_2, ho, gb)
    du1, dh1_1, dp1, do1, sums1, dm1 = mlp_back(dy, h1, wout, gb, d1, wup, wdown, seq)
    dqkv_e, gt, sums_e = attend_back_even(wqkv, incl, qkv_e, o1, lse1, do1, o2, lse2, do2, part, dh1_1, dh1_2, x, gb)
    o2 = o2.reshape(2 * n, width)

    def wgrad(l1, r1, l2, r2):
        return mm("la,lb->ab", l1, r1) + mm("la,lb->ab", l2, r2)

    grads = (
        jnp.stack([wgrad(a_e, dqkv_e[j], a_o, dqkv_o[j]) for j in range(3)]),
        wgrad(o1, dp1, o2, dp2),
        wgrad(n2_1, du1, n2_2, du2),
        wgrad(g1, dm1, g2, dm2),
    )
    small = jnp.stack([sums_e[0] + sums_o[0], sums1[0] + sums2[0], sums_e[1] + sums_o[1], sums1[1] + sums2[1], sums_o[2]])
    return out, gt, grads, small


def shards(outer, tokens, segments, pass_embed, w_qkv, w_out, w_up, w_down, gain, bias, cotangent):
    ty = lax.axis_index("tensor")
    rows = tokens.shape[0] // 2
    width = tokens.shape[2]
    mine = lambda t: lax.dynamic_slice_in_dim(t, ty * rows, rows, 0)
    x = mine(tokens).reshape(-1, width)
    gb = jnp.concatenate([gain, bias, pass_embed[None]], axis=0)

    def fetch_qkv():
        return w_qkv, fetch_half(w_qkv)

    def fetch_rest():
        return (
            jnp.concatenate([w_out, fetch_half(w_out)], axis=0),
            jnp.concatenate([w_up, fetch_half(w_up)], axis=1),
            jnp.concatenate([w_down, fetch_half(w_down)], axis=0),
        )

    def send_out(t):
        return ordered(ty, t, lax.ppermute(t, "tensor", FLIP)).reshape(cotangent.shape)

    out, gt, grads, small = local_part(x, mine(segments), mine(cotangent), gb, fetch_qkv, fetch_rest, send_out)
    gt = ordered(ty, gt, lax.ppermute(gt, "tensor", FLIP)).reshape(tokens.shape).astype(F32)
    half = lambda t, axis: jnp.split(t, 2, axis=axis)
    g_down = reduce_grad(*half(grads[3], 0), outer)
    g_up = reduce_grad(*half(grads[2], 1), outer)
    g_out = reduce_grad(*half(grads[1], 0), outer)
    g_qkv = reduce_grad(*[t.reshape(3 * width, -1) for t in half(grads[0], 2)], outer).reshape(3, width, -1)
    small = sum_small(small, outer)
    return out, gt, g_qkv, g_out, g_up, g_down, small[0:2], small[2:4], small[4]


def solution(mesh):
    outer = mesh.shape["dp"] // 4
    fine = Mesh(mesh.devices.reshape(outer, 2, 2, mesh.shape["tensor"]), ("o", "x", "core", "tensor"))
    rows = ROWS_OVER
    placed = (
        P(rows, None, None),
        P(rows, None),
        P(),
        P(None, None, "tensor"),
        P("tensor", None),
        P(None, "tensor"),
        P("tensor", None),
        P(),
        P(),
        P(rows, None, None),
    )

    def body(*args):
        return shards(outer, *args)

    return jax.shard_map(
        body,
        mesh=fine,
        in_specs=placed,
        out_specs=(
            P(rows, None, None),
            P(rows, None, None),
            P(None, None, "tensor"),
            P("tensor", None),
            P(None, "tensor"),
            P("tensor", None),
            P(),
            P(),
            P(),
        ),
        check_vma=False,
    )
```

```python
import functools

import jax
import jax.numpy as jnp
from jax import lax
from jax.experimental import pallas as pl
from jax.experimental.pallas import tpu as pltpu
from jax.sharding import Mesh
from jax.sharding import PartitionSpec as P

HD = 64
EPS = 1e-05
NEG = -1000000000.0
F32 = jnp.float32
BF16 = jnp.bfloat16
ROWS_OVER = ("o", "x", "core")
FLIP = ((0, 1), (1, 0))
VMEM_LIMIT = 60 * 1024 * 1024


def ordered(flag, mine, theirs):
    first = flag == 0
    return jnp.stack([jnp.where(first, mine, theirs), jnp.where(first, theirs, mine)])


def take_half(array, index):
    half = array.shape[0] // 2
    return lax.dynamic_slice_in_dim(array, index * half, half, 0)


def flip_bit(array, axis, size, bit):
    return lax.ppermute(array, axis, [(i, i ^ bit) for i in range(size)])


def steps_of(outer):
    steps = [("x", 2, 1)]
    bit = 1
    while bit < outer:
        steps.append(("o", outer, bit))
        bit *= 2
    return steps


def my_bit(axis, bit):
    return (lax.axis_index(axis) // bit) % 2


def fetch_half(own):
    shape = own.shape
    flat = own.reshape(-1, shape[-1])
    x, core = lax.axis_index("x"), lax.axis_index("core")
    piece = take_half(take_half(flat, core), x)
    got = lax.ppermute(piece, "tensor", FLIP)
    got = ordered(x, got, lax.ppermute(got, "x", FLIP)).reshape(-1, shape[-1])
    got = ordered(core, got, lax.ppermute(got, "core", FLIP)).reshape(shape)
    return got


def sum_small(small, outer):
    for axis, size, bit in [("core", 2, 1), ("tensor", 2, 1)] + steps_of(outer):
        small = small + flip_bit(small, axis, size, bit)
    return small


def dot(a, b):
    return lax.dot_general(a, b, (((1,), (0,)), ((), ())), preferred_element_type=F32)


def dot_nt(a, b):
    return lax.dot_general(a, b, (((1,), (1,)), ((), ())), preferred_element_type=F32)


def dot_tn(a, b):
    return lax.dot_general(a, b, (((0,), (0,)), ((), ())), preferred_element_type=F32)


def norm_stats(h):
    centred = h - jnp.mean(h, axis=-1, keepdims=True)
    inverse = lax.rsqrt(jnp.mean(centred * centred, axis=-1, keepdims=True) + EPS)
    return centred * inverse, inverse


def norm_back(grad, normal, inverse, gain):
    scaled = grad * gain
    centre = jnp.mean(scaled, axis=-1, keepdims=True)
    proj = jnp.mean(scaled * normal, axis=-1, keepdims=True)
    return inverse * (scaled - centre - normal * proj)


def gelu_parts(u):
    c = 0.7978845608028654
    a = 0.044715 * c
    square = u * u
    half = 0.5 + 0.5 * jnp.tanh(u * (c + a * square))
    g = u * half
    return g, half + g * (1.0 - half) * (2.0 * c + 6.0 * a * square)


def whole(shape):
    return pl.BlockSpec(shape, lambda *_: (0,) * len(shape))


def call(body, grid, ins, outs, scratch=(), cost=(0, 0), name=None):
    return pl.pallas_call(
        body,
        grid=grid,
        in_specs=[s for _, s in ins],
        out_specs=[s for _, s in outs],
        out_shape=[a for a, _ in outs],
        scratch_shapes=scratch,
        compiler_params=pltpu.CompilerParams(
            dimension_semantics=("arbitrary",) * len(grid), vmem_limit_bytes=VMEM_LIMIT
        ),
        cost_estimate=pl.CostEstimate(
            flops=int(cost[0]), bytes_accessed=int(cost[1]), transcendentals=0
        ),
        name=name,
    )(*[a for a, _ in ins])


def sds(shape, dtype):
    return jax.ShapeDtypeStruct(shape, dtype)


def head_mask(h):
    lane = lax.broadcasted_iota(jnp.int32, (1, 2 * HD), 1)
    return jnp.where((lane >= h * HD) & (lane < (h + 1) * HD), 1.0, 0.0)


def first_half_lanes(shape):
    return lax.broadcasted_iota(jnp.int32, shape, 1) < HD


def pair_column(t, h):
    return t[:, h * HD : h * HD + 1]


def attend_first_body(rows, seq, pairs, a_ref, w_ref, bias_ref, qkv_ref, o_ref, lse_ref):
    a = a_ref[...]
    for j in range(3):
        qkv_ref[j] = dot(a, w_ref[j]).astype(BF16)
    for r in range(rows):
        sl = slice(r * seq, (r + 1) * seq)
        bias = bias_ref[r]
        for p in range(pairs):
            ln = slice(p * 2 * HD, (p + 1) * 2 * HD)
            q, k, v = (qkv_ref[j, sl, ln] for j in range(3))
            got = []
            for h in range(2):
                qm = q * (head_mask(h) * HD**-0.5).astype(BF16)
                s = dot_nt(qm, k) + bias
                top = jnp.max(s, axis=1, keepdims=True)
                e = jnp.exp(s - top)
                mass = jnp.sum(e, axis=1, keepdims=True)
                got.append((dot(e.astype(BF16), v) * (1.0 / mass), top + jnp.log(mass)))
            first = first_half_lanes((seq, 2 * HD))
            o_ref[sl, ln] = jnp.where(first, got[0][0], got[1][0]).astype(BF16)
            lse_ref[sl, ln] = jnp.where(first, got[0][1], got[1][1])


def attend_first(a, w, bias):
    rows, seq = bias.shape[0], bias.shape[1]
    n, d = a.shape
    f = w.shape[2]
    return call(
        functools.partial(attend_first_body, rows, seq, f // (2 * HD)),
        (1,),
        [(a, whole(a.shape)), (w, whole(w.shape)), (bias, whole(bias.shape))],
        [
            (sds((3, n, f), BF16), whole((3, n, f))),
            (sds((n, f), BF16), whole((n, f))),
            (sds((n, f), F32), whole((n, f))),
        ],
        cost=(6 * n * d * f + 16 * n * seq * f, 0),
        name="attend_first",
    )


def mlp_first_body(
    x_ref, o_ref, wout_ref, gb_ref, wup_ref, wdown_ref,
    h1_ref, n2_ref, g_ref, d_ref, ho_ref, ao_ref,
):
    j = pl.program_id(0)

    @pl.when(j == 0)
    def _():
        h1 = x_ref[...].astype(F32) + dot(o_ref[...], wout_ref[...])
        h1_ref[...] = h1
        normal, _ = norm_stats(h1)
        n2_ref[...] = (normal * gb_ref[1:2] + gb_ref[3:4]).astype(BF16)
        ho_ref[...] = h1 + gb_ref[4:5]

    u = dot(n2_ref[...], wup_ref[...])
    g, d = gelu_parts(u)
    g = g.astype(BF16)
    g_ref[...] = g
    d_ref[...] = d.astype(BF16)
    ho_ref[...] += dot(g, wdown_ref[...])

    @pl.when(j == pl.num_programs(0) - 1)
    def _():
        normal, _ = norm_stats(ho_ref[...])
        ao_ref[...] = (normal * gb_ref[0:1] + gb_ref[2:3]).astype(BF16)


def mlp_first(x, o, wout, gb, wup, wdown):
    n, d = x.shape
    ff = wup.shape[1]
    c = 512
    return call(
        mlp_first_body,
        (ff // c,),
        [
            (x, whole(x.shape)),
            (o, whole(o.shape)),
            (wout, whole(wout.shape)),
            (gb, whole(gb.shape)),
            (wup, pl.BlockSpec((d, c), lambda j: (0, j))),
            (wdown, pl.BlockSpec((c, d), lambda j: (j, 0))),
        ],
        [
            (sds((n, d), F32), whole((n, d))),
            (sds((n, d), BF16), whole((n, d))),
            (sds((n, ff), BF16), pl.BlockSpec((n, c), lambda j: (0, j))),
            (sds((n, ff), BF16), pl.BlockSpec((n, c), lambda j: (0, j))),
            (sds((n, d), F32), whole((n, d))),
            (sds((n, d), BF16), whole((n, d))),
        ],
        cost=(2 * n * d * (2 * ff + d), 0),
        name="mlp_first",
    )


def attend_second_body(
    rows, seq, pairs, a_ref, w_ref, incl_ref, strict_ref, qkve_ref, o1_ref, lse1_ref,
    qkvo_ref, o2_ref, lse2_ref,
):
    a = a_ref[...]
    for j in range(3):
        qkvo_ref[j] = dot(a, w_ref[j]).astype(BF16)

    def row(r, _):
        sl = pl.ds(pl.multiple_of(r * seq, seq), seq)
        incl, strict = incl_ref[r], strict_ref[r]
        for p in range(pairs):
            ln = slice(p * 2 * HD, (p + 1) * 2 * HD)
            qe, ke, ve = (qkve_ref[j, sl, ln] for j in range(3))
            qo, ko, vo = (qkvo_ref[j, sl, ln] for j in range(3))
            o1 = o1_ref[sl, ln].astype(F32)
            lse1 = lse1_ref[sl, ln]
            even, odd = [], []
            for h in range(2):
                scale = (head_mask(h) * HD**-0.5).astype(BF16)
                s = dot_nt(qe * scale, ko) + strict
                old = pair_column(lse1, h)
                top = jnp.maximum(old, jnp.max(s, axis=1, keepdims=True))
                e = jnp.exp(s - top)
                kept = jnp.exp(old - top)
                mass = kept + jnp.sum(e, axis=1, keepdims=True)
                o = (kept * o1 + dot(e.astype(BF16), vo)) * (1.0 / mass)
                even.append((o, top + jnp.log(mass)))
                qm = qo * scale
                s1 = dot_nt(qm, ke) + incl
                s2 = dot_nt(qm, ko) + incl
                top = jnp.max(jnp.maximum(s1, s2), axis=1, keepdims=True)
                e1 = jnp.exp(s1 - top)
                e2 = jnp.exp(s2 - top)
                mass = jnp.sum(e1 + e2, axis=1, keepdims=True)
                o = (dot(e1.astype(BF16), ve) + dot(e2.astype(BF16), vo)) * (1.0 / mass)
                odd.append((o, top + jnp.log(mass)))
            first = first_half_lanes((seq, 2 * HD))
            for i, got in enumerate((even, odd)):
                o2_ref[i, sl, ln] = jnp.where(first, got[0][0], got[1][0]).astype(BF16)
                lse2_ref[i, sl, ln] = jnp.where(first, got[0][1], got[1][1])
        return 0

    lax.fori_loop(0, rows, row, 0)


def attend_second(a, w, incl, strict, qkve, o1, lse1):
    rows, seq = incl.shape[0], incl.shape[1]
    n, d = a.shape
    f = w.shape[2]
    b = 256
    col = lambda lead: pl.BlockSpec(lead + (b,), lambda i: (0,) * len(lead) + (i,))
    return call(
        functools.partial(attend_second_body, rows, seq, b // (2 * HD)),
        (f // b,),
        [
            (a, whole(a.shape)),
            (w, col((3, d))),
            (incl, whole(incl.shape)),
            (strict, whole(strict.shape)),
            (qkve, col((3, n))),
            (o1, col((n,))),
            (lse1, col((n,))),
        ],
        [
            (sds((3, n, f), BF16), col((3, n))),
            (sds((2, n, f), BF16), col((2, n))),
            (sds((2, n, f), F32), col((2, n))),
        ],
        cost=(6 * n * d * f + 48 * n * seq * f, 0),
        name="attend_second",
    )


def weave(seq):
    i = lax.broadcasted_iota(jnp.int32, (2 * seq, 2 * seq), 0)
    k = lax.broadcasted_iota(jnp.int32, (2 * seq, 2 * seq), 1)
    place = jnp.where(k < seq, 2 * k, 2 * (k - seq) + 1)
    return jnp.where(i == place, 1.0, 0.0).astype(BF16)


def mlp_second_body(
    rows, seq, x_ref, ho_ref, o_ref, cot_ref, wout_ref, gb_ref, wup_ref, wdown_ref,
    out_ref, n2_ref, g_ref, du_ref, dh1_ref, dp_ref, do_ref, sums_ref, dm_ref,
    h1_ref, z_ref, dn_ref,
):
    j = pl.program_id(0)
    n = rows * seq
    halves = (slice(0, n), slice(n, 2 * n))

    @pl.when(j == 0)
    def _():
        for i, sl in enumerate(halves):
            start = x_ref[...].astype(F32) if i == 0 else ho_ref[...]
            h1 = start + dot(o_ref[i], wout_ref[...])
            h1_ref[sl] = h1
            normal, _ = norm_stats(h1)
            n2_ref[sl] = (normal * gb_ref[1:2] + gb_ref[3:4]).astype(BF16)
        z_ref[...] = jnp.zeros_like(z_ref)
        dn_ref[...] = jnp.zeros_like(dn_ref)
        mix = weave(seq)
        for r in range(rows):
            parted = dot_tn(mix, cot_ref[r]).astype(BF16)
            for i in range(2):
                dm_ref[i * n + r * seq : i * n + (r + 1) * seq] = parted[i * seq : (i + 1) * seq]

    for sl in halves:
        u = dot(n2_ref[sl], wup_ref[...])
        dg = dot_nt(dm_ref[sl], wdown_ref[...])
        g, d = gelu_parts(u)
        g = g.astype(BF16)
        du = (dg * d).astype(BF16)
        g_ref[sl] = g
        du_ref[sl] = du
        z_ref[sl] += dot(g, wdown_ref[...])
        dn_ref[sl] += dot_nt(du, wup_ref[...])

    @pl.when(j == pl.num_programs(0) - 1)
    def _():
        mix = weave(seq)
        for r in range(rows):
            pair = [slice(i * n + r * seq, i * n + (r + 1) * seq) for i in range(2)]
            z = jnp.concatenate([(h1_ref[s] + z_ref[s]).astype(BF16) for s in pair], axis=0)
            out_ref[r] = dot(mix, z).astype(BF16)
        gain_sum = jnp.zeros_like(gb_ref[0:1])
        bias_sum = jnp.zeros_like(gb_ref[0:1])
        for i in range(2 * rows):
            sl = slice(i * seq, (i + 1) * seq)
            normal, inverse = norm_stats(h1_ref[sl])
            dn = dn_ref[sl]
            gain_sum += jnp.sum(dn * normal, axis=0, keepdims=True)
            bias_sum += jnp.sum(dn, axis=0, keepdims=True)
            dh1 = dm_ref[sl].astype(F32) + norm_back(dn, normal, inverse, gb_ref[1:2])
            dh1_ref[sl] = dh1
            dp = dh1.astype(BF16)
            dp_ref[sl] = dp
            do_ref[sl] = dot_nt(dp, wout_ref[...]).astype(BF16)
        sums_ref[0:1] = gain_sum
        sums_ref[1:2] = bias_sum


def mlp_second(x, ho, o2, cot, wout, gb, wup, wdown, seq):
    n, d = x.shape
    ff = wup.shape[1]
    rows = n // seq
    c = 512
    blk = pl.BlockSpec((2 * n, c), lambda j: (0, j))
    return call(
        functools.partial(mlp_second_body, rows, seq),
        (ff // c,),
        [
            (x, whole(x.shape)),
            (ho, whole(ho.shape)),
            (o2, whole(o2.shape)),
            (cot, whole(cot.shape)),
            (wout, whole(wout.shape)),
            (gb, whole(gb.shape)),
            (wup, pl.BlockSpec((d, c), lambda j: (0, j))),
            (wdown, pl.BlockSpec((c, d), lambda j: (j, 0))),
        ],
        [
            (sds((rows, 2 * seq, d), BF16), whole((rows, 2 * seq, d))),
            (sds((2 * n, d), BF16), whole((2 * n, d))),
            (sds((2 * n, ff), BF16), blk),
            (sds((2 * n, ff), BF16), blk),
            (sds((2 * n, d), F32), whole((2 * n, d))),
            (sds((2 * n, d), BF16), whole((2 * n, d))),
            (sds((2 * n, d), BF16), whole((2 * n, d))),
            (sds((2, d), F32), whole((2, d))),
            (sds((2 * n, d), BF16), whole((2 * n, d))),
        ],
        scratch=[pltpu.VMEM((2 * n, d), F32)] * 3,
        cost=(2 * n * d * (8 * ff + 4 * d), 0),
        name="mlp_second",
    )


def attend_back_body(
    rows, seq, pairs, w_ref, incl_ref, strict_ref, qkve_ref, qkvo_ref, o2_ref, lse2_ref, do_ref,
    dh1_ref, ho_ref, gb_ref,
    dqkvo_ref, dqkve_ref, dy_ref, sums_ref, da_ref,
):
    j = pl.program_id(0)

    def row(r, _):
        sl = pl.ds(pl.multiple_of(r * seq, seq), seq)
        incl, strict = incl_ref[r], strict_ref[r]
        for p in range(pairs):
            ln = slice(p * 2 * HD, (p + 1) * 2 * HD)
            qe, ke, ve = (qkve_ref[t, sl, ln] for t in range(3))
            qo, ko, vo = (qkvo_ref[t, sl, ln] for t in range(3))
            doe, doo = do_ref[0, sl, ln], do_ref[1, sl, ln]
            de = doe.astype(F32) * o2_ref[0, sl, ln].astype(F32)
            dd = doo.astype(F32) * o2_ref[1, sl, ln].astype(F32)
            lse_e, lse_o = lse2_ref[0, sl, ln], lse2_ref[1, sl, ln]
            acc = [None] * 6
            first = first_half_lanes((seq, 2 * HD))
            for h in range(2):
                on = head_mask(h)
                low = on.astype(BF16)
                scale = (on * HD**-0.5).astype(BF16)
                delta_e = jnp.sum(de * on, axis=1, keepdims=True)
                delta_o = jnp.sum(dd * on, axis=1, keepdims=True)
                le, lo = pair_column(lse_e, h), pair_column(lse_o, h)
                qme, qmo = qe * scale, qo * scale
                dme, dmo = doe * low, doo * low

                def block(qm, k, bias, lse, dm, v, delta):
                    pr = jnp.exp(dot_nt(qm, k) + bias - lse)
                    ds = (pr * (dot_nt(dm, v) - delta)).astype(BF16)
                    return pr.astype(BF16), ds

                p1, s1 = block(qme, ko, strict, le, dme, vo, delta_e)
                p2, s2 = block(qmo, ke, incl, lo, dmo, ve, delta_o)
                p3, s3 = block(qmo, ko, incl, lo, dmo, vo, delta_o)
                new = [
                    dot(s1, ko),
                    dot_tn(s2, qo),
                    dot_tn(p2, doo),
                    dot(s2, ke) + dot(s3, ko),
                    dot_tn(s1, qe) + dot_tn(s3, qo),
                    dot_tn(p1, doe) + dot_tn(p3, doo),
                ]
                acc = [t if o is None else jnp.where(first, o, t) for o, t in zip(acc, new)]
            sc = HD**-0.5
            for t in range(3):
                k = 1.0 if t == 2 else sc
                dqkve_ref[t, sl, ln] = acc[t] * k
                dqkvo_ref[t, sl, ln] = (acc[3 + t] * k).astype(BF16)
        return 0

    lax.fori_loop(0, rows, row, 0)
    da = dot_nt(dqkvo_ref[0], w_ref[0])
    da += dot_nt(dqkvo_ref[1], w_ref[1])
    da += dot_nt(dqkvo_ref[2], w_ref[2])

    @pl.when(j == 0)
    def _():
        da_ref[...] = da

    @pl.when(j > 0)
    def _():
        da_ref[...] += da

    @pl.when(j == pl.num_programs(0) - 1)
    def _():
        gain_sum = jnp.zeros_like(gb_ref[0:1])
        bias_sum = jnp.zeros_like(gb_ref[0:1])
        pass_sum = jnp.zeros_like(gb_ref[0:1])
        for i in range(rows):
            sl = slice(i * seq, (i + 1) * seq)
            normal, inverse = norm_stats(ho_ref[sl])
            da = da_ref[sl]
            gain_sum += jnp.sum(da * normal, axis=0, keepdims=True)
            bias_sum += jnp.sum(da, axis=0, keepdims=True)
            dy = dh1_ref[sl] + norm_back(da, normal, inverse, gb_ref[0:1])
            dy_ref[sl] = dy
            pass_sum += jnp.sum(dy, axis=0, keepdims=True)
        sums_ref[0:1] = gain_sum
        sums_ref[1:2] = bias_sum
        sums_ref[2:3] = pass_sum


def attend_back(w, incl, strict, qkve, qkvo, o2, lse2, do, dh1, ho, gb):
    rows, seq = incl.shape[0], incl.shape[1]
    n, d = ho.shape
    f = w.shape[2]
    b = 256
    col = lambda lead: pl.BlockSpec(lead + (b,), lambda i: (0,) * len(lead) + (i,))
    return call(
        functools.partial(attend_back_body, rows, seq, b // (2 * HD)),
        (f // b,),
        [
            (w, col((3, d))),
            (incl, whole(incl.shape)),
            (strict, whole(strict.shape)),
            (qkve, col((3, n))),
            (qkvo, col((3, n))),
            (o2, col((2, n))),
            (lse2, col((2, n))),
            (do.reshape(2, n, f), col((2, n))),
            (dh1, pl.BlockSpec((n, d), lambda i: (1, 0))),
            (ho, whole(ho.shape)),
            (gb, whole(gb.shape)),
        ],
        [
            (sds((3, n, f), BF16), col((3, n))),
            (sds((3, n, f), F32), col((3, n))),
            (sds((n, d), F32), whole((n, d))),
            (sds((3, d), F32), whole((3, d))),
        ],
        scratch=[pltpu.VMEM((n, d), F32)],
        cost=(6 * n * d * f + 120 * n * seq * f, 0),
        name="attend_back",
    )


def mlp_back_body(
    rows, seq, dy_ref, h1_ref, wout_ref, gb_ref, d_ref, wup_ref, wdown_ref,
    du_ref, dh1_ref, dp_ref, do_ref, sums_ref, dm_ref, dn_ref,
):
    j = pl.program_id(0)

    @pl.when(j == 0)
    def _():
        dm_ref[...] = dy_ref[...].astype(BF16)
        dn_ref[...] = jnp.zeros_like(dn_ref)

    dg = dot_nt(dm_ref[...], wdown_ref[...])
    du = (dg * d_ref[...].astype(F32)).astype(BF16)
    du_ref[...] = du
    dn_ref[...] += dot_nt(du, wup_ref[...])

    @pl.when(j == pl.num_programs(0) - 1)
    def _():
        gain_sum = jnp.zeros_like(gb_ref[0:1])
        bias_sum = jnp.zeros_like(gb_ref[0:1])
        for i in range(rows):
            sl = slice(i * seq, (i + 1) * seq)
            normal, inverse = norm_stats(h1_ref[sl])
            dn = dn_ref[sl]
            gain_sum += jnp.sum(dn * normal, axis=0, keepdims=True)
            bias_sum += jnp.sum(dn, axis=0, keepdims=True)
            dh1 = dy_ref[sl] + norm_back(dn, normal, inverse, gb_ref[1:2])
            dh1_ref[sl] = dh1
            dp = dh1.astype(BF16)
            dp_ref[sl] = dp
            do_ref[sl] = dot_nt(dp, wout_ref[...]).astype(BF16)
        sums_ref[0:1] = gain_sum
        sums_ref[1:2] = bias_sum


def mlp_back(dy, h1, wout, gb, dgelu, wup, wdown, seq):
    n, d = dy.shape
    ff = wup.shape[1]
    c = 512
    blk = pl.BlockSpec((n, c), lambda j: (0, j))
    return call(
        functools.partial(mlp_back_body, n // seq, seq),
        (ff // c,),
        [
            (dy, whole(dy.shape)),
            (h1, whole(h1.shape)),
            (wout, whole(wout.shape)),
            (gb, whole(gb.shape)),
            (dgelu, blk),
            (wup, pl.BlockSpec((d, c), lambda j: (0, j))),
            (wdown, pl.BlockSpec((c, d), lambda j: (j, 0))),
        ],
        [
            (sds((n, ff), BF16), blk),
            (sds((n, d), F32), whole((n, d))),
            (sds((n, d), BF16), whole((n, d))),
            (sds((n, d), BF16), whole((n, d))),
            (sds((2, d), F32), whole((2, d))),
        ],
        scratch=[pltpu.VMEM((n, d), BF16), pltpu.VMEM((n, d), F32)],
        cost=(2 * n * d * (2 * ff + d), 0),
        name="mlp_back",
    )


def attend_back_even_body(
    rows, seq, pairs, w_ref, incl_ref, qkve_ref, o1_ref, lse1_ref, do1_ref, o2_ref, lse2_ref, do2_ref,
    part_ref, dh1_ref, dh2_ref, x_ref, gb_ref,
    dqkv_ref, gt_ref, sums_ref, da_ref,
):
    j = pl.program_id(0)

    def row(r, _):
        sl = pl.ds(pl.multiple_of(r * seq, seq), seq)
        incl = incl_ref[r]
        for p in range(pairs):
            ln = slice(p * 2 * HD, (p + 1) * 2 * HD)
            q, k, v = (qkve_ref[t, sl, ln] for t in range(3))
            do1 = do1_ref[sl, ln].astype(F32)
            do2 = do2_ref[0, sl, ln].astype(F32)
            lse1 = lse1_ref[sl, ln]
            ratio = jnp.exp(lse1 - lse2_ref[0, sl, ln])
            do2 = do2 * ratio
            both = (do1 + do2).astype(BF16)
            dd = do1 * o1_ref[sl, ln].astype(F32) + do2 * o2_ref[0, sl, ln].astype(F32)
            acc = [None] * 3
            first = first_half_lanes((seq, 2 * HD))
            for h in range(2):
                on = head_mask(h)
                delta = jnp.sum(dd * on, axis=1, keepdims=True)
                qm = q * (on * HD**-0.5).astype(BF16)
                pr = jnp.exp(dot_nt(qm, k) + incl - pair_column(lse1, h))
                ds = (pr * (dot_nt(both * on.astype(BF16), v) - delta)).astype(BF16)
                new = [dot(ds, k), dot_tn(ds, q), dot_tn(pr.astype(BF16), both)]
                acc = [t if o is None else jnp.where(first, o, t) for o, t in zip(acc, new)]
            for t in range(3):
                sc = 1.0 if t == 2 else HD**-0.5
                dqkv_ref[t, sl, ln] = (acc[t] * sc + part_ref[t, sl, ln]).astype(BF16)
        return 0

    lax.fori_loop(0, rows, row, 0)
    da = dot_nt(dqkv_ref[0], w_ref[0])
    da += dot_nt(dqkv_ref[1], w_ref[1])
    da += dot_nt(dqkv_ref[2], w_ref[2])

    @pl.when(j == 0)
    def _():
        da_ref[...] = da

    @pl.when(j > 0)
    def _():
        da_ref[...] += da

    @pl.when(j == pl.num_programs(0) - 1)
    def _():
        gain_sum = jnp.zeros_like(gb_ref[0:1])
        bias_sum = jnp.zeros_like(gb_ref[0:1])
        for i in range(rows):
            sl = slice(i * seq, (i + 1) * seq)
            normal, inverse = norm_stats(x_ref[sl].astype(F32))
            da = da_ref[sl]
            gain_sum += jnp.sum(da * normal, axis=0, keepdims=True)
            bias_sum += jnp.sum(da, axis=0, keepdims=True)
            back = norm_back(da, normal, inverse, gb_ref[0:1])
            gt_ref[sl] = (dh1_ref[sl] + dh2_ref[sl] + back).astype(BF16)
        sums_ref[0:1] = gain_sum
        sums_ref[1:2] = bias_sum


def attend_back_even(w, incl, qkve, o1, lse1, do1, o2, lse2, do2, part, dh1, dh2, x, gb):
    rows, seq = incl.shape[0], incl.shape[1]
    n, d = x.shape
    f = w.shape[2]
    b = 256
    col = lambda lead: pl.BlockSpec(lead + (b,), lambda i: (0,) * len(lead) + (i,))
    return call(
        functools.partial(attend_back_even_body, rows, seq, b // (2 * HD)),
        (f // b,),
        [
            (w, col((3, d))),
            (incl, whole(incl.shape)),
            (qkve, col((3, n))),
            (o1, col((n,))),
            (lse1, col((n,))),
            (do1, col((n,))),
            (o2, col((1, n))),
            (lse2, col((1, n))),
            (do2.reshape(2, n, f), col((1, n))),
            (part, col((3, n))),
            (dh1, whole((n, d))),
            (dh2, whole((n, d))),
            (x, whole(x.shape)),
            (gb, whole(gb.shape)),
        ],
        [
            (sds((3, n, f), BF16), col((3, n))),
            (sds((n, d), BF16), whole((n, d))),
            (sds((2, d), F32), whole((2, d))),
        ],
        scratch=[pltpu.VMEM((n, d), F32)],
        cost=(6 * n * d * f + 40 * n * seq * f, 0),
        name="attend_back_even",
    )


def packed_call(body, grid, me, ins, outs, scratch=(), flops=0, name=None):
    return pl.pallas_call(
        body,
        grid_spec=pltpu.PrefetchScalarGridSpec(
            num_scalar_prefetch=1,
            grid=grid,
            in_specs=[s for _, s in ins],
            out_specs=[s for _, s in outs],
            scratch_shapes=scratch,
        ),
        out_shape=[a for a, _ in outs],
        compiler_params=pltpu.CompilerParams(
            dimension_semantics=("arbitrary",) * len(grid), vmem_limit_bytes=VMEM_LIMIT
        ),
        cost_estimate=pl.CostEstimate(flops=int(flops), bytes_accessed=0, transcendentals=0),
        name=name,
    )(me, *[a for a, _ in ins])


def grad_down_body(me_ref, g1_ref, g2_ref, dm1_ref, dm2_ref, out_ref, acc_ref):
    low = me_ref[0] % 4
    acc = dot_tn(g1_ref[...], dm1_ref[...])
    acc += dot_tn(g2_ref[...], dm2_ref[...])
    acc_ref[...] = acc.reshape(acc_ref.shape)
    for s in range(4):
        out_ref[0, s] = acc_ref[s ^ low].astype(BF16)


def grad_down(me, side, g1, g2, dm1, dm2):
    n, d = dm1.shape
    ff = g1.shape[1]
    b = ff // 8
    pick = lambda y, h, me: (0, (1 - y) * 4 + ((me[0] // 8) ^ side) * 2 + h)
    const = lambda y, h, me: (0, 0)
    return packed_call(
        grad_down_body,
        (2, 2),
        me,
        [
            (g1, pl.BlockSpec((n, b), pick)),
            (g2, pl.BlockSpec((2 * n, b), pick)),
            (dm1, pl.BlockSpec((n, d), const)),
            (dm2, pl.BlockSpec((2 * n, d), const)),
        ],
        [
            (
                sds((2, 8, b // 4, d), BF16),
                pl.BlockSpec((1, 4, b // 4, d), lambda y, h, me: (y, h ^ ((me[0] // 4) % 2), 0, 0)),
            )
        ],
        scratch=[pltpu.VMEM((4, b // 4, d), F32)],
        flops=2 * 3 * n * d * ff // 2,
        name="grad_down",
    )[0]


def grad_up_body(me_ref, n1_ref, n2_ref, du1_ref, du2_ref, out_ref, t1_ref, t2_ref, acc_ref):
    low = me_ref[0] % 8

    @pl.when((pl.program_id(0) == 0) & (pl.program_id(1) == 0))
    def _():
        t1_ref[...] = n1_ref[...].T
        t2_ref[...] = n2_ref[...].T

    acc = dot(t1_ref[...], du1_ref[...])
    acc += dot(t2_ref[...], du2_ref[...])
    acc_ref[...] = acc.reshape(acc_ref.shape)
    for s in range(8):
        out_ref[0, s] = acc_ref[s ^ low].astype(BF16)


def grad_up(me, side, n1, n2, du1, du2):
    n, d = n1.shape
    ff = du1.shape[1]
    b, c, parts = d // 2, 512, ff // 2 // 512
    rows = lambda y, j, me: (0, (me[0] // 8) ^ side)
    cols = lambda y, j, me: (0, (1 - y) * parts + j)
    return packed_call(
        grad_up_body,
        (2, parts),
        me,
        [
            (n1, pl.BlockSpec((n, b), rows)),
            (n2, pl.BlockSpec((2 * n, b), rows)),
            (du1, pl.BlockSpec((n, c), cols)),
            (du2, pl.BlockSpec((2 * n, c), cols)),
        ],
        [
            (
                sds((2, 8, b // 8, ff // 2), BF16),
                pl.BlockSpec((1, 8, b // 8, c), lambda y, j, me: (y, 0, 0, j)),
            )
        ],
        scratch=[
            pltpu.VMEM((b, n), BF16),
            pltpu.VMEM((b, 2 * n), BF16),
            pltpu.VMEM((8, b // 8, c), F32),
        ],
        flops=2 * 3 * n * d * ff // 2,
        name="grad_up",
    )[0]


def grad_heads_body(
    me_ref, ae_ref, ao_ref, dp1_ref, dp2_ref, de_ref, do_ref, o1_ref, o2_ref, out_ref, acc_ref
):
    low = me_ref[0] % 8
    f = o1_ref.shape[1]
    for j in range(4):
        if j < 3:
            acc = dot_tn(ae_ref[...], de_ref[j])
            acc += dot_tn(ao_ref[...], do_ref[j])
        else:
            acc = dot_tn(dp1_ref[...], o1_ref[...])
            acc += dot_tn(dp2_ref[...], o2_ref[...])
        acc_ref[...] = acc.reshape(acc_ref.shape)
        for s in range(8):
            out_ref[0, s, :, j * f : (j + 1) * f] = acc_ref[s ^ low].astype(BF16)


def grad_heads(me, side, ae, ao, dp1, dp2, dqkv_e, dqkv_o, o1, o2):
    n, d = ae.shape
    b, f = d // 2, o1.shape[1] // 2
    rows = lambda y, me: (0, (me[0] // 8) ^ side)
    cols = lambda y, me: (0, 1 - y)
    cols3 = lambda y, me: (0, 0, 1 - y)
    return packed_call(
        grad_heads_body,
        (2,),
        me,
        [
            (ae, pl.BlockSpec((n, b), rows)),
            (ao, pl.BlockSpec((n, b), rows)),
            (dp1, pl.BlockSpec((n, b), rows)),
            (dp2, pl.BlockSpec((2 * n, b), rows)),
            (dqkv_e, pl.BlockSpec((3, n, f), cols3)),
            (dqkv_o, pl.BlockSpec((3, n, f), cols3)),
            (o1, pl.BlockSpec((n, f), cols)),
            (o2, pl.BlockSpec((2 * n, f), cols)),
        ],
        [
            (
                sds((2, 8, b // 8, 4 * f), BF16),
                pl.BlockSpec((1, 8, b // 8, 4 * f), lambda y, me: (y, 0, 0, 0)),
            )
        ],
        scratch=[pltpu.VMEM((8, b // 8, f), F32)],
        flops=2 * (2 * 3 + 3) * n * d * f,
        name="grad_heads",
    )[0]


def unpack_body(heads, me_ref, mine_ref, got_ref, *out_refs):
    low = me_ref[0] % 8
    other = pl.program_id(0) ^ (me_ref[0] // 8)
    rows = mine_ref.shape[1]

    def write(ref):
        for s in range(8):
            sl = slice(s * rows, (s + 1) * rows)
            if not heads:
                out_refs[0][sl] = ref[s ^ low].astype(F32)
            else:
                f = out_refs[0].shape[2]
                for j in range(3):
                    out_refs[0][j, sl] = ref[s ^ low, :, j * f : (j + 1) * f].astype(F32)
                out_refs[2][sl] = ref[s ^ low, :, 3 * f :].astype(F32)
        if heads:
            out_refs[1][...] = out_refs[2][...].T

    pl.when(other == 0)(lambda: write(mine_ref))
    pl.when(other != 0)(lambda: write(got_ref))


def unpack(me, mine, got, heads=False):
    _, r, w = mine.shape
    half = 8 * r
    ins = [(t, pl.BlockSpec(t.shape, lambda i, me: (0, 0, 0))) for t in (mine, got)]
    if heads:
        f = w // 4
        outs = [
            (sds((3, 2 * half, f), F32), pl.BlockSpec((3, half, f), lambda i, me: (0, i, 0))),
            (sds((f, 2 * half), F32), pl.BlockSpec((f, half), lambda i, me: (0, i))),
        ]
        scratch = [pltpu.VMEM((half, f), F32)]
    else:
        outs = [(sds((2 * half, w), F32), pl.BlockSpec((half, w), lambda i, me: (i, 0)))]
        scratch = []
    return packed_call(
        functools.partial(unpack_body, heads), (2,), me, ins, outs, scratch=scratch, name="unpack"
    )


def fold(*parts):
    return sum(p.astype(F32) for p in parts).astype(BF16)


def after(value, *first):
    return lax.optimization_barrier((value, first))[0]


def over_core(send):
    return lax.ppermute(send, "core", FLIP)


class Summing:
    def __init__(self, outer, keep, got):
        self.steps = [("x", 2, 1), ("o", outer, 1), ("o", outer, 2)]
        self.extra = [("o", outer, 1 << b) for b in range(2, outer.bit_length() - 1)]
        self.own = (keep[1], got[1])
        self.got = lax.ppermute(fold(keep[0], got[0]), "tensor", FLIP)
        self.total = None

    def step(self, axis, size, bit):
        if self.total is None:
            total = fold(*self.own, self.got)
        else:
            total = fold(self.total, self.got)
        half = total.shape[0] // 2
        self.total = total[:half]
        self.got = flip_bit(total[half:], axis, size, bit)

    def scatter(self):
        for s in self.steps:
            self.step(*s)

    def gather(self):
        total = fold(self.total, self.got)
        for s in self.extra:
            total = fold(total, flip_bit(total, *s))
        for s in reversed(self.steps):
            total = jnp.concatenate([total, flip_bit(total, *s)], axis=0)
        return total, over_core(total)


def mask_biases(seg):
    seq = seg.shape[1]
    place = jnp.arange(seq, dtype=jnp.int32)
    same = seg[:, :, None] == seg[:, None, :]
    below = (place[:, None] > place[None, :])[None]
    incl = (place[:, None] >= place[None, :])[None]
    bias = lambda m: jnp.where(same & m, 0.0, NEG).astype(F32)
    return bias(incl), bias(below)


class Link:
    def __init__(self, outer, w_qkv, w_out, w_up, w_down):
        self.outer = outer
        self.own = (w_qkv, w_out, w_up, w_down)
        core, x, o = (lax.axis_index(a) for a in ("core", "x", "o"))
        self.me = (core * 8 + x * 4 + (o % 2) * 2 + (o // 2) % 2).astype(jnp.int32).reshape(1)

    def fetch_qkv(self):
        return self.own[0], fetch_half(self.own[0])

    def fetch_rest(self):
        return (
            jnp.concatenate([self.own[1], fetch_half(self.own[1])], axis=0),
            jnp.concatenate([self.own[2], fetch_half(self.own[2])], axis=1),
            jnp.concatenate([self.own[3], fetch_half(self.own[3])], axis=0),
        )

    def partner(self, t):
        return lax.ppermute(t, "tensor", FLIP)

    def core(self, t):
        return over_core(t)

    def summing(self, keep, got):
        return Summing(self.outer, keep, got)

    def small(self, t):
        return sum_small(t, self.outer)


def local_part(x, seg, cot, gb, link):
    rows, seq = seg.shape
    n, width = x.shape
    me = link.me
    incl, strict = mask_biases(seg)
    normal, _ = norm_stats(x.astype(F32))
    a_e = (normal * gb[0] + gb[2]).astype(BF16)
    wq_own, fetched = link.fetch_qkv()
    first = attend_first(a_e, wq_own, incl)
    second = attend_first(a_e, fetched, incl)
    qkv_e, o1, lse1 = (jnp.concatenate([s, t], axis=-1) for s, t in zip(first, second))
    wqkv = jnp.concatenate([wq_own, fetched], axis=2)
    wout, wup, wdown = link.fetch_rest()
    h1, n2_1, g1, d1, ho, a_o = mlp_first(x, o1, wout, gb, wup, wdown)
    qkv_o, o2, lse2 = attend_second(a_o, wqkv, incl, strict, qkv_e, o1, lse1)
    out, n2_2, g2, du2, dh1_2, dp2, do2, sums2, dm2 = mlp_second(x, ho, o2, cot, wout, gb, wup, wdown, seq)
    out_got = link.partner(out)
    dqkv_o, part, dy, sums_o = attend_back(wqkv, incl, strict, qkv_e, qkv_o, o2, lse2, do2, dh1_2, ho, gb)
    o2_flat = o2.reshape(2 * n, width)

    dm1 = dy.astype(BF16)
    down_go = grad_down(me, 1, g1, g2, dm1, dm2)
    down_got = link.core(down_go)
    down_keep = grad_down(me, 0, g1, g2, dm1, after(dm2, down_go))
    dy = after(dy, down_keep)
    du1, dh1_1, dp1, do1, sums1 = mlp_back(dy, h1, wout, gb, d1, wup, wdown, seq)
    down = link.summing(down_keep, after(down_got, du1))
    up_go = grad_up(me, 1, n2_1, n2_2, du1, du2)
    up_got = link.core(up_go)
    up_keep = grad_up(me, 0, n2_1, n2_2, du1, after(du2, up_go))
    do1 = after(do1, up_keep)
    dqkv_e, gt, sums_e = attend_back_even(wqkv, incl, qkv_e, o1, lse1, do1, o2, lse2, do2, part, dh1_1, dh1_2, x, gb)
    up = link.summing(up_keep, after(up_got, dqkv_e))
    heads = (a_e, a_o, dp1, dp2, dqkv_e, dqkv_o, o1)
    heads_go = grad_heads(me, 1, *heads, o2_flat)
    heads_got = link.core(heads_go)
    heads_keep = grad_heads(me, 0, *heads, after(o2_flat, heads_go))
    head = link.summing(heads_keep, heads_got)
    gt_got = link.partner(gt)
    small = jnp.stack([sums_e[0] + sums_o[0], sums1[0] + sums2[0], sums_e[1] + sums_o[1], sums1[1] + sums2[1], sums_o[2]])
    small = link.small(small)
    for s in (down, up, head):
        s.scatter()
    g_down, g_up, g_head = (s.gather() for s in (down, up, head))
    (g_down,) = unpack(me, *g_down)
    (g_up,) = unpack(me, *g_up)
    g_qkv, g_out = unpack(me, *g_head, heads=True)
    return (out, out_got), (gt, gt_got), (g_qkv, g_out, g_up, g_down), small


def shards(outer, tokens, segments, pass_embed, w_qkv, w_out, w_up, w_down, gain, bias, cotangent):
    ty = lax.axis_index("tensor")
    rows = tokens.shape[0] // 2
    width = tokens.shape[2]
    mine = lambda t: lax.dynamic_slice_in_dim(t, ty * rows, rows, 0)
    x = mine(tokens).reshape(-1, width)
    gb = jnp.concatenate([gain, bias, pass_embed[None]], axis=0)
    link = Link(outer, w_qkv, w_out, w_up, w_down)
    out, gt, grads, small = local_part(x, mine(segments), mine(cotangent), gb, link)
    out = ordered(ty, *out).reshape(cotangent.shape)
    gt = ordered(ty, *gt).reshape(tokens.shape).astype(F32)
    return out, gt, *grads, small[0:2], small[2:4], small[4]


def solution(mesh):
    outer = mesh.shape["dp"] // 4
    fine = Mesh(mesh.devices.reshape(outer, 2, 2, mesh.shape["tensor"]), ("o", "x", "core", "tensor"))
    rows = ROWS_OVER
    placed = (
        P(rows, None, None),
        P(rows, None),
        P(),
        P(None, None, "tensor"),
        P("tensor", None),
        P(None, "tensor"),
        P("tensor", None),
        P(),
        P(),
        P(rows, None, None),
    )

    def body(*args):
        return shards(outer, *args)

    return jax.shard_map(
        body,
        mesh=fine,
        in_specs=placed,
        out_specs=(
            P(rows, None, None),
            P(rows, None, None),
            P(None, None, "tensor"),
            P("tensor", None),
            P(None, "tensor"),
            P("tensor", None),
            P(),
            P(),
            P(),
        ),
        check_vma=False,
    )
```

```python
import functools

import jax
import jax.numpy as jnp
from jax import lax
from jax.experimental import pallas as pl
from jax.experimental.pallas import tpu as pltpu
from jax.sharding import Mesh
from jax.sharding import PartitionSpec as P

HD = 64
EPS = 1e-05
NEG = -1000000000.0
F32 = jnp.float32
BF16 = jnp.bfloat16
ROWS_OVER = ("o", "x", "core")
FLIP = ((0, 1), (1, 0))
VMEM_LIMIT = 60 * 1024 * 1024


def ordered(flag, mine, theirs):
    first = flag == 0
    return jnp.stack([jnp.where(first, mine, theirs), jnp.where(first, theirs, mine)])


def take_half(array, index):
    half = array.shape[0] // 2
    return lax.dynamic_slice_in_dim(array, index * half, half, 0)


def flip_bit(array, axis, size, bit):
    return lax.ppermute(array, axis, [(i, i ^ bit) for i in range(size)])


def steps_of(outer):
    steps = [("x", 2, 1)]
    bit = 1
    while bit < outer:
        steps.append(("o", outer, bit))
        bit *= 2
    return steps


def my_bit(axis, bit):
    return (lax.axis_index(axis) // bit) % 2


def dot(a, b):
    return lax.dot_general(a, b, (((1,), (0,)), ((), ())), preferred_element_type=F32)


def dot_nt(a, b):
    return lax.dot_general(a, b, (((1,), (1,)), ((), ())), preferred_element_type=F32)


def dot_tn(a, b):
    return lax.dot_general(a, b, (((0,), (0,)), ((), ())), preferred_element_type=F32)


def norm_stats(h):
    centred = h - jnp.mean(h, axis=-1, keepdims=True)
    inverse = lax.rsqrt(jnp.mean(centred * centred, axis=-1, keepdims=True) + EPS)
    return centred * inverse, inverse


def norm_back(grad, normal, inverse, gain):
    scaled = grad * gain
    centre = jnp.mean(scaled, axis=-1, keepdims=True)
    proj = jnp.mean(scaled * normal, axis=-1, keepdims=True)
    return inverse * (scaled - centre - normal * proj)


def gelu_parts(u):
    c = 0.7978845608028654
    a = 0.044715 * c
    square = u * u
    half = 0.5 + 0.5 * jnp.tanh(u * (c + a * square))
    g = u * half
    return g, half + g * (1.0 - half) * (2.0 * c + 6.0 * a * square)


def whole(shape):
    return pl.BlockSpec(shape, lambda *_: (0,) * len(shape))


def call(body, grid, ins, outs, scratch=(), cost=(0, 0), name=None, vmem=VMEM_LIMIT):
    return pl.pallas_call(
        body,
        grid=grid,
        in_specs=[s for _, s in ins],
        out_specs=[s for _, s in outs],
        out_shape=[a for a, _ in outs],
        scratch_shapes=scratch,
        compiler_params=pltpu.CompilerParams(
            dimension_semantics=("arbitrary",) * len(grid), vmem_limit_bytes=vmem
        ),
        cost_estimate=pl.CostEstimate(
            flops=int(cost[0]) // 16, bytes_accessed=int(cost[1]), transcendentals=0
        ),
        name=name,
    )(*[a for a, _ in ins])


FAR = pl.BlockSpec(memory_space=pl.ANY)


def resident(body, ins, outs, scratch=(), flops=0, vmem=16, name=None):
    spec = pl.BlockSpec(memory_space=pltpu.VMEM)
    ins, outs = ([o if isinstance(o, tuple) else (o, spec) for o in t] for t in (ins, outs))
    ins = [(pltpu.with_memory_space_constraint(a, pltpu.HBM) if s is FAR else a, s) for a, s in ins]
    outs = [(pltpu.HBM(a.shape, a.dtype) if s is FAR else a, s) for a, s in outs]
    return pl.pallas_call(
        body,
        in_specs=[s for _, s in ins],
        out_specs=[s for _, s in outs],
        out_shape=[a for a, _ in outs],
        scratch_shapes=scratch,
        compiler_params=pltpu.CompilerParams(vmem_limit_bytes=vmem * 1024 * 1024),
        cost_estimate=pl.CostEstimate(flops=int(flops) // 16, bytes_accessed=0, transcendentals=0),
        name=name,
    )(*[a for a, _ in ins])


def sds(shape, dtype):
    return jax.ShapeDtypeStruct(shape, dtype)


QB = 128
GROUP = 256


def lanes_of(ref, g):
    return ref.at[(slice(None),) * (len(ref.shape) - 1) + (pl.ds(pl.multiple_of(g * GROUP, GROUP), GROUP),)]


class Moves:
    def __init__(self, sems):
        self.sems, self.used = sems, 0

    def whole(self, source, target):
        copy = pltpu.make_async_copy(source, target, self.sems.at[self.used])
        self.used += 1
        copy.start()
        return copy.wait

    def groups(self, source, target):
        first = self.used
        self.used += source.shape[-1] // GROUP

        def copy(g):
            return pltpu.make_async_copy(lanes_of(source, g), lanes_of(target, g), self.sems.at[first + g])

        return (lambda g: copy(g).start()), (lambda g: copy(g).wait())


def cat_heads(t, scale=1.0):
    lane = lax.broadcasted_iota(jnp.int32, (1, 2 * HD), 1)
    parts = [t * jnp.where((lane < HD) == (h == 0), scale, 0.0).astype(t.dtype) for h in range(2)]
    return jnp.concatenate(parts, axis=0)


def own_lanes(t, scale=None):
    if scale is not None:
        t = t * scale
    return jnp.concatenate([t[:HD, :QB], t[HD:, QB:]], axis=0)


def twice(t):
    return jnp.concatenate([t, t], axis=1)


def pair_row(rows, p):
    return jnp.concatenate([rows[2 * p : 2 * p + 1], rows[2 * p + 1 : 2 * p + 2]], axis=1)


def put_pair(ref, p, cols, value):
    ref[2 * p : 2 * p + 1, cols] = value[:, :QB]
    ref[2 * p + 1 : 2 * p + 2, cols] = value[:, QB:]


def columns(t, r, seq, qb):
    return t[:, pl.ds(pl.multiple_of(r * seq + qb * QB, QB), QB)]


def rows_of(r, seq, qb):
    return pl.ds(pl.multiple_of(r * seq + qb * QB, QB), QB)


def attend_first_body(rows, seq, pairs, a_ref, w_ref, bias_ref, qkv_ref, o_ref, lse_ref):
    a = a_ref[...]
    for j in range(3):
        qkv_ref[j] = dot(a, w_ref[j]).astype(BF16)
    for r in range(rows):
        work = []
        for p in range(pairs):
            ln = slice(p * 2 * HD, (p + 1) * 2 * HD)
            k = qkv_ref[1, r * seq : (r + 1) * seq, ln]
            for b in range(seq // QB):
                sl, n = slice(r * seq + b * QB, r * seq + (b + 1) * QB), (b + 1) * QB
                q = cat_heads(qkv_ref[0, sl, ln], HD**-0.5)
                s = dot_nt(k[:n], q) + twice(bias_ref[r, :n, b * QB : n])
                work.append((p, ln, sl, n, s))
        done = []
        for p, ln, sl, n, s in work:
            top = jnp.max(s, axis=0, keepdims=True)
            e = jnp.exp(s - top)
            mass = jnp.sum(e, axis=0, keepdims=True)
            put_pair(lse_ref, p, sl, top + jnp.log(mass))
            done.append((e.astype(BF16), 1.0 / mass))
        for (p, ln, sl, n, _), (e, inv) in zip(work, done):
            vt = qkv_ref[2, r * seq : (r + 1) * seq, ln].T
            o_ref[sl, ln] = own_lanes(dot(vt[:, :n], e), inv).T.astype(BF16)


def attend_first(a, w, bias):
    rows, seq = bias.shape[0], bias.shape[1]
    n, d = a.shape
    f = w.shape[2]
    return resident(
        functools.partial(attend_first_body, rows, seq, f // (2 * HD)),
        (a, w, bias),
        [sds((3, n, f), BF16), sds((n, f), BF16), sds((f // HD, n), F32)],
        flops=6 * n * d * f + 16 * n * seq * f,
        name="attend_first",
    )


def attend_second_body(
    rows, seq, a_far, w_far, incl_far, strict_far, qkve_far, o1_far, lse1_ref,
    qkvo_far, o2_far, lse2_ref,
    a_ref, w_ref, incl_ref, strict_ref, qkve_ref, o1_ref, qkvo_ref, o2_ref, sems,
):
    groups = lse1_ref.shape[0]
    moves = Moves(sems)
    ready = [moves.whole(a_far, a_ref)]
    ready += [moves.whole(w_far.at[j], w_ref.at[j]) for j in range(3)]
    masks = [moves.whole(*t) for t in ((incl_far, incl_ref), (strict_far, strict_ref))]
    arrive = [moves.groups(*t) for t in ((qkve_far, qkve_ref), (o1_far, o1_ref))]
    leave = moves.groups(o2_ref, o2_far)
    for g in range(groups):
        for start, _ in arrive:
            start(g)
    ready[0]()
    a = a_ref[...]
    sent = []
    for j in range(3):
        ready[1 + j]()
        qkvo_ref[j] = dot(a, w_ref[j]).astype(BF16)
        sent.append(moves.whole(qkvo_ref.at[j], qkvo_far.at[j]))
    for wait in masks:
        wait()

    def row(i, _):
        r, group = i % rows, i // rows
        lanes = pl.multiple_of(group * GROUP, GROUP)
        all_of = pl.ds(pl.multiple_of(r * seq, seq), seq)

        @pl.when(r == 0)
        def _():
            for _, wait in arrive:
                wait(group)

        for p in range(GROUP // (2 * HD)):
            ln = pl.ds(lanes + p * 2 * HD, 2 * HD)
            ke, ko = qkve_ref[1, all_of, ln], qkvo_ref[1, all_of, ln]
            vte, vto = qkve_ref[2, all_of, ln].T, qkvo_ref[2, all_of, ln].T
            work = []
            for b in range(seq // QB):
                sl, n = rows_of(r, seq, b), (b + 1) * QB
                cols = slice(b * QB, n)
                incl, strict = twice(incl_ref[r, :n, cols]), twice(strict_ref[r, :n, cols])
                q = cat_heads(qkve_ref[0, sl, ln], HD**-0.5)
                work.append([dot_nt(ko[:n], q) + strict])
                q = cat_heads(qkvo_ref[0, sl, ln], HD**-0.5)
                work.append([dot_nt(ko[:n], q) + incl, dot_nt(ke[:n], q) + incl])
            for b in range(seq // QB):
                sl, n = rows_of(r, seq, b), (b + 1) * QB
                (s,), (so, se) = work[2 * b : 2 * b + 2]
                old = pair_row(lse1_ref[group, :, sl], p)
                top = jnp.maximum(old, jnp.max(s, axis=0, keepdims=True))
                e = jnp.exp(s - top)
                kept = jnp.exp(old - top)
                mass = kept + jnp.sum(e, axis=0, keepdims=True)
                work[2 * b] = (e.astype(BF16), kept, 1.0 / mass)
                put_pair(lse2_ref.at[0, group], p, sl, top + jnp.log(mass))
                top = jnp.max(jnp.maximum(se, so), axis=0, keepdims=True)
                ee, eo = jnp.exp(se - top), jnp.exp(so - top)
                mass = jnp.sum(ee + eo, axis=0, keepdims=True)
                work[2 * b + 1] = (ee.astype(BF16), eo.astype(BF16), 1.0 / mass)
                put_pair(lse2_ref.at[1, group], p, sl, top + jnp.log(mass))
            for b in range(seq // QB):
                sl, n = rows_of(r, seq, b), (b + 1) * QB
                (e, kept, inv), (ee, eo, inv2) = work[2 * b : 2 * b + 2]
                o1 = o1_ref[sl, ln].astype(F32).T
                o = own_lanes(dot(vto[:, :n], e), inv) + own_lanes(twice(o1), kept * inv)
                o2_ref[0, sl, ln] = o.T.astype(BF16)
                o = dot(vte[:, :n], ee) + dot(vto[:, :n], eo)
                o2_ref[1, sl, ln] = own_lanes(o, inv2).T.astype(BF16)

        @pl.when(r == rows - 1)
        def _():
            leave[0](group)

        return 0

    lax.fori_loop(0, rows * groups, row, 0)
    for wait in sent:
        wait()
    for g in range(groups):
        leave[1](g)


def attend_second(a, w, incl, strict, qkve, o1, lse1):
    rows, seq = incl.shape[0], incl.shape[1]
    n, d = a.shape
    f = w.shape[2]
    qkv, o2 = sds((3, n, f), BF16), sds((2, n, f), BF16)
    near = (a, w, incl, strict, qkve, o1, qkv, o2)
    return resident(
        functools.partial(attend_second_body, rows, seq),
        [(t, FAR) for t in (a, w, incl, strict, qkve, o1)] + [lse1],
        [(qkv, FAR), (o2, FAR), sds((2, *lse1.shape), F32)],
        scratch=[pltpu.VMEM(t.shape, t.dtype) for t in near] + [pltpu.SemaphoreType.DMA((32,))],
        flops=6 * n * d * f + 48 * n * seq * f,
        vmem=32,
        name="attend_second",
    )


def row_products(a, b):
    prod = cat_heads((a * b).astype(BF16))
    return dot_nt(jnp.ones((8, 2 * HD), BF16), prod)[:1]


def query_parts(sl, ln, group, p, i, qkv_ref, o_ref, lse_ref, do_ref):
    do = do_ref[i, sl, ln]
    delta = row_products(do.astype(F32), o_ref[i, sl, ln].astype(F32))
    return cat_heads(qkv_ref[0, sl, ln], HD**-0.5), cat_heads(do), pair_row(lse_ref[i, group, :, sl], p), delta


def blocks_back(tasks):
    scores = [dot_nt(k, q) + bias - lse for k, _, _, bias, q, _, lse, _ in tasks]
    moved = [dot_nt(v, do) - delta for _, v, _, _, _, do, _, delta in tasks]
    probs = [jnp.exp(s) for s in scores]
    ds = [(p * m).astype(BF16) for p, m in zip(probs, moved)]
    return [
        (dot(p.astype(BF16), do), dot(d, q), dot(kt, d))
        for (_, _, kt, _, q, do, _, _), p, d in zip(tasks, probs, ds)
    ]


def add_rows(total, part):
    if total is None:
        return part
    n = part.shape[0]
    return jnp.concatenate([total[:n] + part, total[n:]], axis=0)


def attend_back_body(
    rows, seq, w_far, incl_far, strict_far, qkve_far, qkvo_far, o2_far, lse2_ref, do_far,
    dh1_far, ho_far, gb_ref,
    dqkvo_far, dqkve_far, dy_ref, sums_ref,
    w_ref, incl_ref, strict_ref, qkve_ref, qkvo_ref, o2_ref, do_ref, dh1_ref, ho_ref,
    dqkvo_ref, dqkve_ref, da_ref, sems,
):
    groups = lse2_ref.shape[1]
    moves = Moves(sems)
    arrive = [
        moves.groups(*t)
        for t in ((qkve_far, qkve_ref), (qkvo_far, qkvo_ref), (o2_far, o2_ref), (do_far, do_ref))
    ]
    leave = [moves.groups(*t) for t in ((dqkvo_ref, dqkvo_far), (dqkve_ref, dqkve_far))]
    for start, _ in arrive:
        start(0)
    masks = [moves.whole(*t) for t in ((incl_far, incl_ref), (strict_far, strict_ref))]
    for g in range(1, groups):
        for start, _ in arrive:
            start(g)
    odd = pl.ds(rows * seq, rows * seq)
    late = [moves.whole(*t) for t in ((w_far, w_ref), (dh1_far.at[odd], dh1_ref), (ho_far, ho_ref))]
    for wait in masks:
        wait()
    sc = HD**-0.5

    def row(i, _):
        r, group = i % rows, i // rows
        lanes = pl.multiple_of(group * GROUP, GROUP)
        all_of = pl.ds(pl.multiple_of(r * seq, seq), seq)

        @pl.when(r == 0)
        def _():
            for _, wait in arrive:
                wait(group)

        for p in range(GROUP // (2 * HD)):
            ln = pl.ds(lanes + p * 2 * HD, 2 * HD)
            ke, ve = qkve_ref[1, all_of, ln], qkve_ref[2, all_of, ln]
            ko, vo = qkvo_ref[1, all_of, ln], qkvo_ref[2, all_of, ln]
            kte, kto = ke.T, ko.T
            tasks = []
            for b in reversed(range(seq // QB)):
                sl, n = rows_of(r, seq, b), (b + 1) * QB
                cols = slice(b * QB, n)
                incl, strict = twice(incl_ref[r, :n, cols]), twice(strict_ref[r, :n, cols])
                even = query_parts(sl, ln, group, p, 0, qkve_ref, o2_ref, lse2_ref, do_ref)
                odd = query_parts(sl, ln, group, p, 1, qkvo_ref, o2_ref, lse2_ref, do_ref)
                tasks.append((ko[:n], vo[:n], kto[:, :n], strict, *even))
                tasks.append((ko[:n], vo[:n], kto[:, :n], incl, *odd))
                tasks.append((ke[:n], ve[:n], kte[:, :n], incl, *odd))
            done = blocks_back(tasks)
            dke = dve = dko = dvo = None
            for b in reversed(range(seq // QB)):
                sl = rows_of(r, seq, b)
                (dv, dk, dqe), (dv2, dk2, dqo), (dv3, dk3, dqo2) = done[:3]
                done = done[3:]
                dvo, dko = add_rows(dvo, dv + dv2), add_rows(dko, dk + dk2)
                dve, dke = add_rows(dve, dv3), add_rows(dke, dk3)
                dqkve_ref[0, sl, ln] = (own_lanes(dqe).T * sc).astype(BF16)
                dqkvo_ref[0, sl, ln] = (own_lanes(dqo + dqo2).T * sc).astype(BF16)
            dqkve_ref[1, all_of, ln] = dke.astype(BF16)
            dqkve_ref[2, all_of, ln] = dve.astype(BF16)
            dqkvo_ref[1, all_of, ln] = dko.astype(BF16)
            dqkvo_ref[2, all_of, ln] = dvo.astype(BF16)

        @pl.when(r == rows - 1)
        def _():
            for start, _ in leave:
                start(group)

        return 0

    lax.fori_loop(0, rows * groups, row, 0)
    for wait in late:
        wait()
    da = dot_nt(dqkvo_ref[0], w_ref[0])
    da += dot_nt(dqkvo_ref[1], w_ref[1])
    da += dot_nt(dqkvo_ref[2], w_ref[2])
    da_ref[...] = da
    gain_sum = jnp.zeros_like(gb_ref[0:1])
    bias_sum = jnp.zeros_like(gb_ref[0:1])
    pass_sum = jnp.zeros_like(gb_ref[0:1])
    for i in range(rows):
        sl = slice(i * seq, (i + 1) * seq)
        normal, inverse = norm_stats(ho_ref[sl])
        da = da_ref[sl]
        gain_sum += jnp.sum(da * normal, axis=0, keepdims=True)
        bias_sum += jnp.sum(da, axis=0, keepdims=True)
        dy = dh1_ref[sl] + norm_back(da, normal, inverse, gb_ref[0:1])
        dy_ref[sl] = dy
        pass_sum += jnp.sum(dy, axis=0, keepdims=True)
    sums_ref[0:1] = gain_sum
    sums_ref[1:2] = bias_sum
    sums_ref[2:3] = pass_sum
    for g in range(groups):
        for _, wait in leave:
            wait(g)


def attend_back(w, incl, strict, qkve, qkvo, o2, lse2, do, dh1, ho, gb):
    rows, seq = incl.shape[0], incl.shape[1]
    n, d = ho.shape
    f = w.shape[2]
    do = do.reshape(2, n, f)
    qkv = sds((3, n, f), BF16)
    near = (w, incl, strict, qkve, qkvo, o2, do, sds((n, d), F32), ho, qkv, qkv, sds((n, d), F32))
    return resident(
        functools.partial(attend_back_body, rows, seq),
        [(t, FAR) for t in (w, incl, strict, qkve, qkvo, o2)]
        + [lse2]
        + [(t, FAR) for t in (do, dh1, ho)]
        + [gb],
        [(qkv, FAR), (qkv, FAR), sds((n, d), F32), sds((3, d), F32)],
        scratch=[pltpu.VMEM(t.shape, t.dtype) for t in near] + [pltpu.SemaphoreType.DMA((32,))],
        flops=6 * n * d * f + 120 * n * seq * f,
        vmem=44,
        name="attend_back",
    )


def attend_back_even_body(
    rows, seq, w_far, incl_far, qkve_far, o1_far, lse1_ref, do1_far, o2_far, lse2_ref, do2_far,
    part_far, dh1_far, dh2_far, x_far, gb_ref,
    dqkv_far, gt_ref, sums_ref,
    w_ref, incl_ref, qkve_ref, o1_ref, do1_ref, o2_ref, do2_ref, part_ref, dh1_ref, dh2_ref, x_ref,
    dqkv_ref, da_ref, sems,
):
    groups = lse1_ref.shape[0]
    moves = Moves(sems)
    even = pl.ds(0, rows * seq)
    arrive = [
        moves.groups(*t)
        for t in (
            (qkve_far, qkve_ref), (o1_far, o1_ref), (do1_far, do1_ref), (o2_far.at[0], o2_ref),
            (do2_far.at[0], do2_ref), (part_far, part_ref),
        )
    ]
    leave = [moves.groups(dqkv_ref, dqkv_far)]
    for start, _ in arrive:
        start(0)
    mask = moves.whole(incl_far, incl_ref)
    for g in range(1, groups):
        for start, _ in arrive:
            start(g)
    late = [
        moves.whole(*t)
        for t in ((w_far, w_ref), (dh1_far, dh1_ref), (dh2_far.at[even], dh2_ref), (x_far, x_ref))
    ]
    mask()
    sc = HD**-0.5

    def row(i, _):
        r, group = i % rows, i // rows
        lanes = pl.multiple_of(group * GROUP, GROUP)
        all_of = pl.ds(pl.multiple_of(r * seq, seq), seq)

        @pl.when(r == 0)
        def _():
            for _, wait in arrive:
                wait(group)

        for p in range(GROUP // (2 * HD)):
            ln = pl.ds(lanes + p * 2 * HD, 2 * HD)
            k, v = qkve_ref[1, all_of, ln], qkve_ref[2, all_of, ln]
            kt = k.T
            tasks = []
            for b in reversed(range(seq // QB)):
                sl, n = rows_of(r, seq, b), (b + 1) * QB
                incl = twice(incl_ref[r, :n, b * QB : n])
                lse1 = pair_row(lse1_ref[group, :, sl], p)
                ratio = jnp.exp(lse1 - pair_row(lse2_ref[0, group, :, sl], p))
                do1, do2 = do1_ref[sl, ln].astype(F32), do2_ref[sl, ln].astype(F32)
                delta = row_products(do1, o1_ref[sl, ln].astype(F32))
                delta += ratio * row_products(do2, o2_ref[sl, ln].astype(F32))
                both = do1 + own_lanes(twice(do2.T), ratio).T
                q, do = cat_heads(qkve_ref[0, sl, ln], sc), cat_heads(both.astype(BF16))
                tasks.append((k[:n], v[:n], kt[:, :n], incl, q, do, lse1, delta))
            dka = dva = None
            for b, (dv, dk, dq) in zip(reversed(range(seq // QB)), blocks_back(tasks)):
                sl = rows_of(r, seq, b)
                dva, dka = add_rows(dva, dv), add_rows(dka, dk)
                dqkv_ref[0, sl, ln] = (own_lanes(dq).T * sc + part_ref[0, sl, ln].astype(F32)).astype(BF16)
            dqkv_ref[1, all_of, ln] = (dka + part_ref[1, all_of, ln].astype(F32)).astype(BF16)
            dqkv_ref[2, all_of, ln] = (dva + part_ref[2, all_of, ln].astype(F32)).astype(BF16)

        @pl.when(r == rows - 1)
        def _():
            for start, _ in leave:
                start(group)

        return 0

    lax.fori_loop(0, rows * groups, row, 0)
    for wait in late:
        wait()
    da = dot_nt(dqkv_ref[0], w_ref[0])
    da += dot_nt(dqkv_ref[1], w_ref[1])
    da += dot_nt(dqkv_ref[2], w_ref[2])
    da_ref[...] = da
    gain_sum = jnp.zeros_like(gb_ref[0:1])
    bias_sum = jnp.zeros_like(gb_ref[0:1])
    for i in range(rows):
        sl = slice(i * seq, (i + 1) * seq)
        normal, inverse = norm_stats(x_ref[sl].astype(F32))
        da = da_ref[sl]
        gain_sum += jnp.sum(da * normal, axis=0, keepdims=True)
        bias_sum += jnp.sum(da, axis=0, keepdims=True)
        back = norm_back(da, normal, inverse, gb_ref[0:1])
        gt_ref[sl] = (dh1_ref[sl] + dh2_ref[sl] + back).astype(BF16)
    sums_ref[0:1] = gain_sum
    sums_ref[1:2] = bias_sum
    for g in range(groups):
        for _, wait in leave:
            wait(g)


def attend_back_even(w, incl, qkve, o1, lse1, do1, o2, lse2, do2, part, dh1, dh2, x, gb):
    rows, seq = incl.shape[0], incl.shape[1]
    n, d = x.shape
    f = w.shape[2]
    qkv, one = sds((3, n, f), BF16), sds((n, f), BF16)
    near = (w, incl, qkv, one, one, one, one, qkv, dh1, dh1, x, qkv, sds((n, d), F32))
    far = lambda *ts: [(t, FAR) for t in ts]
    return resident(
        functools.partial(attend_back_even_body, rows, seq),
        far(w, incl, qkve, o1)
        + [lse1]
        + far(do1, o2)
        + [lse2]
        + far(do2.reshape(2, n, f), part, dh1, dh2, x)
        + [gb],
        [(qkv, FAR), sds((n, d), BF16), sds((2, d), F32)],
        scratch=[pltpu.VMEM(t.shape, t.dtype) for t in near] + [pltpu.SemaphoreType.DMA((32,))],
        flops=6 * n * d * f + 40 * n * seq * f,
        vmem=40,
        name="attend_back_even",
    )


def mlp_first_body(
    x_ref, o_ref, wout_ref, gb_ref, wup_ref, wdown_ref,
    h1_ref, n2_ref, g_ref, d_ref, ho_ref, ao_ref,
):
    j = pl.program_id(0)

    @pl.when(j == 0)
    def _():
        h1 = x_ref[...].astype(F32) + dot(o_ref[...], wout_ref[...])
        h1_ref[...] = h1
        normal, _ = norm_stats(h1)
        n2_ref[...] = (normal * gb_ref[1:2] + gb_ref[3:4]).astype(BF16)
        ho_ref[...] = h1 + gb_ref[4:5]

    u = dot(n2_ref[...], wup_ref[...])
    g, d = gelu_parts(u)
    g = g.astype(BF16)
    g_ref[...] = g
    d_ref[...] = d.astype(BF16)
    ho_ref[...] += dot(g, wdown_ref[...])

    @pl.when(j == pl.num_programs(0) - 1)
    def _():
        normal, _ = norm_stats(ho_ref[...])
        ao_ref[...] = (normal * gb_ref[0:1] + gb_ref[2:3]).astype(BF16)


def mlp_first(x, o, wout, gb, wup, wdown):
    n, d = x.shape
    ff = wup.shape[1]
    c = 512
    return call(
        mlp_first_body,
        (ff // c,),
        [
            (x, whole(x.shape)),
            (o, whole(o.shape)),
            (wout, whole(wout.shape)),
            (gb, whole(gb.shape)),
            (wup, pl.BlockSpec((d, c), lambda j: (0, j))),
            (wdown, pl.BlockSpec((c, d), lambda j: (j, 0))),
        ],
        [
            (sds((n, d), F32), whole((n, d))),
            (sds((n, d), BF16), whole((n, d))),
            (sds((n, ff), BF16), pl.BlockSpec((n, c), lambda j: (0, j))),
            (sds((n, ff), BF16), pl.BlockSpec((n, c), lambda j: (0, j))),
            (sds((n, d), F32), whole((n, d))),
            (sds((n, d), BF16), whole((n, d))),
        ],
        cost=(2 * n * d * (2 * ff + d), 0),
        name="mlp_first",
    )


def weave(seq):
    i = lax.broadcasted_iota(jnp.int32, (2 * seq, 2 * seq), 0)
    k = lax.broadcasted_iota(jnp.int32, (2 * seq, 2 * seq), 1)
    place = jnp.where(k < seq, 2 * k, 2 * (k - seq) + 1)
    return jnp.where(i == place, 1.0, 0.0).astype(BF16)


def mlp_second_body(
    rows, seq, x_ref, ho_ref, o_ref, cot_ref, wout_ref, gb_ref, wup_ref, wdown_ref,
    out_ref, n2_ref, g_ref, du_ref, dh1_ref, dp_ref, do_ref, sums_ref, dm_ref,
    h1_ref, z_ref, dn_ref,
):
    j = pl.program_id(0)
    n = rows * seq
    halves = (slice(0, n), slice(n, 2 * n))

    @pl.when(j == 0)
    def _():
        for i, sl in enumerate(halves):
            start = x_ref[...].astype(F32) if i == 0 else ho_ref[...]
            h1 = start + dot(o_ref[i], wout_ref[...])
            h1_ref[sl] = h1
            normal, _ = norm_stats(h1)
            n2_ref[sl] = (normal * gb_ref[1:2] + gb_ref[3:4]).astype(BF16)
        z_ref[...] = jnp.zeros_like(z_ref)
        dn_ref[...] = jnp.zeros_like(dn_ref)
        mix = weave(seq)
        for r in range(rows):
            parted = dot_tn(mix, cot_ref[r]).astype(BF16)
            for i in range(2):
                dm_ref[i * n + r * seq : i * n + (r + 1) * seq] = parted[i * seq : (i + 1) * seq]

    for sl in halves:
        u = dot(n2_ref[sl], wup_ref[...])
        dg = dot_nt(dm_ref[sl], wdown_ref[...])
        g, d = gelu_parts(u)
        g = g.astype(BF16)
        du = (dg * d).astype(BF16)
        g_ref[sl] = g
        du_ref[sl] = du
        z_ref[sl] += dot(g, wdown_ref[...])
        dn_ref[sl] += dot_nt(du, wup_ref[...])

    @pl.when(j == pl.num_programs(0) - 1)
    def _():
        mix = weave(seq)
        for r in range(rows):
            pair = [slice(i * n + r * seq, i * n + (r + 1) * seq) for i in range(2)]
            z = jnp.concatenate([(h1_ref[s] + z_ref[s]).astype(BF16) for s in pair], axis=0)
            out_ref[r] = dot(mix, z).astype(BF16)
        gain_sum = jnp.zeros_like(gb_ref[0:1])
        bias_sum = jnp.zeros_like(gb_ref[0:1])
        for i in range(2 * rows):
            sl = slice(i * seq, (i + 1) * seq)
            normal, inverse = norm_stats(h1_ref[sl])
            dn = dn_ref[sl]
            gain_sum += jnp.sum(dn * normal, axis=0, keepdims=True)
            bias_sum += jnp.sum(dn, axis=0, keepdims=True)
            dh1 = dm_ref[sl].astype(F32) + norm_back(dn, normal, inverse, gb_ref[1:2])
            dh1_ref[sl] = dh1
            dp = dh1.astype(BF16)
            dp_ref[sl] = dp
            do_ref[sl] = dot_nt(dp, wout_ref[...]).astype(BF16)
        sums_ref[0:1] = gain_sum
        sums_ref[1:2] = bias_sum


def mlp_second(x, ho, o2, cot, wout, gb, wup, wdown, seq):
    n, d = x.shape
    ff = wup.shape[1]
    rows = n // seq
    c = 512
    blk = pl.BlockSpec((2 * n, c), lambda j: (0, j))
    return call(
        functools.partial(mlp_second_body, rows, seq),
        (ff // c,),
        [
            (x, whole(x.shape)),
            (ho, whole(ho.shape)),
            (o2, whole(o2.shape)),
            (cot, whole(cot.shape)),
            (wout, whole(wout.shape)),
            (gb, whole(gb.shape)),
            (wup, pl.BlockSpec((d, c), lambda j: (0, j))),
            (wdown, pl.BlockSpec((c, d), lambda j: (j, 0))),
        ],
        [
            (sds((rows, 2 * seq, d), BF16), whole((rows, 2 * seq, d))),
            (sds((2 * n, d), BF16), whole((2 * n, d))),
            (sds((2 * n, ff), BF16), blk),
            (sds((2 * n, ff), BF16), blk),
            (sds((2 * n, d), F32), whole((2 * n, d))),
            (sds((2 * n, d), BF16), whole((2 * n, d))),
            (sds((2 * n, d), BF16), whole((2 * n, d))),
            (sds((2, d), F32), whole((2, d))),
            (sds((2 * n, d), BF16), whole((2 * n, d))),
        ],
        scratch=[pltpu.VMEM((2 * n, d), F32)] * 3,
        cost=(2 * n * d * (8 * ff + 4 * d), 0),
        name="mlp_second",
    )


def mlp_back_body(
    rows, seq, dy_ref, h1_ref, wout_ref, gb_ref, d_ref, wup_ref, wdown_ref,
    du_ref, dh1_ref, dp_ref, do_ref, sums_ref, dm_ref, dn_ref,
):
    j = pl.program_id(0)

    @pl.when(j == 0)
    def _():
        dm_ref[...] = dy_ref[...].astype(BF16)
        dn_ref[...] = jnp.zeros_like(dn_ref)

    dg = dot_nt(dm_ref[...], wdown_ref[...])
    du = (dg * d_ref[...].astype(F32)).astype(BF16)
    du_ref[...] = du
    dn_ref[...] += dot_nt(du, wup_ref[...])

    @pl.when(j == pl.num_programs(0) - 1)
    def _():
        gain_sum = jnp.zeros_like(gb_ref[0:1])
        bias_sum = jnp.zeros_like(gb_ref[0:1])
        for i in range(rows):
            sl = slice(i * seq, (i + 1) * seq)
            normal, inverse = norm_stats(h1_ref[sl])
            dn = dn_ref[sl]
            gain_sum += jnp.sum(dn * normal, axis=0, keepdims=True)
            bias_sum += jnp.sum(dn, axis=0, keepdims=True)
            dh1 = dy_ref[sl] + norm_back(dn, normal, inverse, gb_ref[1:2])
            dh1_ref[sl] = dh1
            dp = dh1.astype(BF16)
            dp_ref[sl] = dp
            do_ref[sl] = dot_nt(dp, wout_ref[...]).astype(BF16)
        sums_ref[0:1] = gain_sum
        sums_ref[1:2] = bias_sum


def mlp_back(dy, h1, wout, gb, dgelu, wup, wdown, seq):
    n, d = dy.shape
    ff = wup.shape[1]
    c = 512
    blk = pl.BlockSpec((n, c), lambda j: (0, j))
    return call(
        functools.partial(mlp_back_body, n // seq, seq),
        (ff // c,),
        [
            (dy, whole(dy.shape)),
            (h1, whole(h1.shape)),
            (wout, whole(wout.shape)),
            (gb, whole(gb.shape)),
            (dgelu, blk),
            (wup, pl.BlockSpec((d, c), lambda j: (0, j))),
            (wdown, pl.BlockSpec((c, d), lambda j: (j, 0))),
        ],
        [
            (sds((n, ff), BF16), blk),
            (sds((n, d), F32), whole((n, d))),
            (sds((n, d), BF16), whole((n, d))),
            (sds((n, d), BF16), whole((n, d))),
            (sds((2, d), F32), whole((2, d))),
        ],
        scratch=[pltpu.VMEM((n, d), BF16), pltpu.VMEM((n, d), F32)],
        cost=(2 * n * d * (2 * ff + d), 0),
        name="mlp_back",
    )


def packed_call(body, grid, me, ins, outs, scratch=(), flops=0, aliases={}, name=None):
    return pl.pallas_call(
        body,
        grid_spec=pltpu.PrefetchScalarGridSpec(
            num_scalar_prefetch=1,
            grid=grid,
            in_specs=[s for _, s in ins],
            out_specs=[s for _, s in outs],
            scratch_shapes=scratch,
        ),
        out_shape=[a for a, _ in outs],
        input_output_aliases=aliases,
        compiler_params=pltpu.CompilerParams(
            dimension_semantics=("arbitrary",) * len(grid), vmem_limit_bytes=VMEM_LIMIT
        ),
        cost_estimate=pl.CostEstimate(flops=int(flops) // 16, bytes_accessed=0, transcendentals=0),
        name=name,
    )(me, *[a for a, _ in ins])


def place_of(quarter, y, me):
    return jnp.where(y == 0, 4 + (quarter ^ me[1]), quarter)


def grad_down_body(me_ref, g1_ref, g2_ref, dm1_ref, dm2_ref, out_ref, acc_ref):
    low = me_ref[0] % 4
    acc = dot_tn(g1_ref[...], dm1_ref[...])
    acc += dot_tn(g2_ref[...], dm2_ref[...])
    acc_ref[...] = acc.reshape(acc_ref.shape)
    for s in range(4):
        out_ref[0, s] = acc_ref[s ^ low].astype(BF16)


def grad_down(me, side, g1, g2, dm1, dm2):
    n, d = dm1.shape
    ff = g1.shape[1]
    b = ff // 8
    pick = lambda y, h, me: (0, place_of((((me[0] // 8) ^ side) * 2 + h), y, me))
    const = lambda y, h, me: (0, 0)
    return packed_call(
        grad_down_body,
        (2, 2),
        me,
        [
            (g1, pl.BlockSpec((n, b), pick)),
            (g2, pl.BlockSpec((2 * n, b), pick)),
            (dm1, pl.BlockSpec((n, d), const)),
            (dm2, pl.BlockSpec((2 * n, d), const)),
        ],
        [
            (
                sds((2, 8, b // 4, d), BF16),
                pl.BlockSpec((1, 4, b // 4, d), lambda y, h, me: (y, h ^ ((me[0] // 4) % 2), 0, 0)),
            )
        ],
        scratch=[pltpu.VMEM((4, b // 4, d), F32)],
        flops=2 * 3 * n * d * ff // 2,
        name="grad_down",
    )[0]


def grad_up_body(
    me_ref, n1_ref, n2_ref, du1_ref, du2_ref, dp1_ref, dp2_ref, o1_ref, o2_ref, out_ref, t1_ref, t2_ref, acc_ref
):
    low = me_ref[0] % 8
    j, last = pl.program_id(1), pl.num_programs(1) - 1

    @pl.when((pl.program_id(0) == 0) & (j == 0))
    def _():
        t1_ref[...] = n1_ref[...].T
        t2_ref[...] = n2_ref[...].T

    def write(acc):
        acc_ref[...] = acc.reshape(acc_ref.shape)
        for s in range(8):
            out_ref[0, s] = acc_ref[s ^ low].astype(BF16)

    @pl.when(j < last)
    def _():
        write(dot(t1_ref[...], du1_ref[...]) + dot(t2_ref[...], du2_ref[...]))

    @pl.when(j == last)
    def _():
        write(dot_tn(dp1_ref[...], o1_ref[...]) + dot_tn(dp2_ref[...], o2_ref[...]))


def grad_up(me, side, n1, n2, du1, du2, dp1, dp2, o1, o2):
    n, d = n1.shape
    ff = du1.shape[1]
    b, c = d // 2, o1.shape[1] // 2
    parts = ff // 2 // c
    rows = lambda y, j, me: (0, (me[0] // 8) ^ side)
    cols = lambda y, j, me: (0, place_of(jnp.minimum(j, parts - 1), y, me))
    half = lambda y, j, me: (0, 1 - y)
    return packed_call(
        grad_up_body,
        (2, parts + 1),
        me,
        [
            (n1, pl.BlockSpec((n, b), rows)),
            (n2, pl.BlockSpec((2 * n, b), rows)),
            (du1, pl.BlockSpec((n, c), cols)),
            (du2, pl.BlockSpec((2 * n, c), cols)),
            (dp1, pl.BlockSpec((n, b), rows)),
            (dp2, pl.BlockSpec((2 * n, b), rows)),
            (o1, pl.BlockSpec((n, c), half)),
            (o2, pl.BlockSpec((2 * n, c), half)),
        ],
        [
            (
                sds((2, 8, b // 8, (parts + 1) * c), BF16),
                pl.BlockSpec((1, 8, b // 8, c), lambda y, j, me: (y, 0, 0, j)),
            )
        ],
        scratch=[
            pltpu.VMEM((b, n), BF16),
            pltpu.VMEM((b, 2 * n), BF16),
            pltpu.VMEM((8, b // 8, c), F32),
        ],
        flops=2 * 3 * n * d * (ff + d) // 2,
        name="grad_up",
    )[0]


def grad_qkv_body(me_ref, ae_ref, ao_ref, de_ref, do_ref, out_ref, acc_ref):
    low = me_ref[0] % 8
    f = de_ref.shape[2]
    for j in range(3):
        acc = dot_tn(ae_ref[...], de_ref[j])
        acc += dot_tn(ao_ref[...], do_ref[j])
        acc_ref[...] = acc.reshape(acc_ref.shape)
        for s in range(8):
            out_ref[0, s, :, j * f : (j + 1) * f] = acc_ref[s ^ low].astype(BF16)


def grad_qkv(me, side, ae, ao, dqkv_e, dqkv_o):
    n, d = ae.shape
    b, f = d // 2, dqkv_e.shape[2] // 2
    rows = lambda y, me: (0, (me[0] // 8) ^ side)
    cols3 = lambda y, me: (0, 0, 1 - y)
    return packed_call(
        grad_qkv_body,
        (2,),
        me,
        [
            (ae, pl.BlockSpec((n, b), rows)),
            (ao, pl.BlockSpec((n, b), rows)),
            (dqkv_e, pl.BlockSpec((3, n, f), cols3)),
            (dqkv_o, pl.BlockSpec((3, n, f), cols3)),
        ],
        [
            (
                sds((2, 8, b // 8, 3 * f), BF16),
                pl.BlockSpec((1, 8, b // 8, 3 * f), lambda y, me: (y, 0, 0, 0)),
            )
        ],
        scratch=[pltpu.VMEM((8, b // 8, f), F32)],
        flops=2 * 2 * 3 * n * d * f,
        name="grad_qkv",
    )[0]


def unpack_body(kind, me_ref, part_ref, *refs):
    low = me_ref[0] % 8
    rows, width = part_ref.shape[1:]
    first = refs[-2] if kind == "up" else refs[-1]
    if kind == "up":
        first, second, wide = refs[-3:]
    for s in range(8):
        sl = slice(s * rows, (s + 1) * rows)
        if kind == "down":
            first[sl] = part_ref[s ^ low].astype(F32)
        elif kind == "up":
            f = first.shape[1]
            first[sl] = part_ref[s ^ low, :, :f].astype(F32)
            wide[sl] = part_ref[s ^ low, :, f:].astype(F32)
        else:
            f = width // 3
            for j in range(3):
                first[j, sl] = part_ref[s ^ low, :, j * f : (j + 1) * f].astype(F32)
    if kind == "up":
        second[...] = wide[...].T


def unpack(kind, me, side, part, into=()):
    _, r, w = part.shape
    half = 8 * r
    at = lambda me: (me[0] // 8) ^ side
    scratch = []
    if kind == "down":
        outs = [(sds((2 * half, w), F32), pl.BlockSpec((half, w), lambda i, me: (at(me), 0)))]
    elif kind == "up":
        f = half
        outs = [
            (sds((2 * half, w - f), F32), pl.BlockSpec((half, w - f), lambda i, me: (at(me), 0))),
            (sds((f, 2 * half), F32), pl.BlockSpec((f, half), lambda i, me: (0, at(me)))),
        ]
        scratch = [pltpu.VMEM((half, f), F32)]
    else:
        f = w // 3
        outs = [(sds((3, 2 * half, f), F32), pl.BlockSpec((3, half, f), lambda i, me: (0, at(me), 0)))]
    ins = [(part, pl.BlockSpec(part.shape, lambda i, me: (0, 0, 0)))]
    ins += [(t, pl.BlockSpec(memory_space=pl.ANY)) for t in into]
    return packed_call(
        functools.partial(unpack_body, kind),
        (1,),
        me,
        ins,
        outs,
        scratch=scratch,
        aliases={2 + i: i for i in range(len(into))},
        name="unpack_" + kind,
    )


def fold(*parts):
    return sum(p.astype(F32) for p in parts).astype(BF16)


def after(value, *first):
    return lax.optimization_barrier((value, first))[0]


class Chunk:
    def __init__(self, outer, keep, got, order):
        every = {"x": ("x", 2, 1), "z": ("o", outer, 1), "w": ("o", outer, 2)}
        self.steps = [every[name] for name in order]
        self.extra = [("o", outer, 1 << b) for b in range(2, outer.bit_length() - 1)]
        self.keep, self.got = keep, got
        self.sent = None

    def wait(self, *also):
        self.got, also = lax.optimization_barrier((self.got, also))
        return also

    def to_partner(self):
        total = fold(self.keep, self.got)
        self.keep, self.sent = total[1], total[0]
        self.got = lax.ppermute(self.sent, "tensor", FLIP)

    def scatter(self, number):
        total = fold(self.keep, self.got)
        half = total.shape[-3] // 2
        self.keep, self.sent = total[..., :half, :, :], total[..., half:, :, :]
        self.got = flip_bit(self.sent, *self.steps[number])

    def all_summed(self):
        total = fold(self.keep, self.got)
        for s in self.extra:
            total = fold(total, flip_bit(total, *s))
        self.keep = self.sent = total

    def gather(self, number):
        self.got = flip_bit(self.keep, *self.steps[number])

    def joined(self):
        self.keep = self.sent = jnp.concatenate([self.keep, self.got], axis=0)

    def gather_core(self):
        self.got = lax.ppermute(self.keep, "core", FLIP)


def mask_biases(seg):
    seq = seg.shape[1]
    place = jnp.arange(seq, dtype=jnp.int32)
    same = seg[:, :, None] == seg[:, None, :]
    below = (place[:, None] < place[None, :])[None]
    incl = (place[:, None] <= place[None, :])[None]
    bias = lambda m: jnp.where(same & m, 0.0, NEG).astype(F32)
    return bias(incl), bias(below)


def sync(*values):
    return lax.optimization_barrier(values)


class Link:
    def __init__(self, outer, w_qkv, w_out, w_up, w_down):
        self.outer = outer
        self.own = (w_qkv, w_out, w_up, w_down)
        self.core_at, self.x_at, o = (lax.axis_index(a) for a in ("core", "x", "o"))
        bits = {"x": self.x_at, "z": o % 2, "w": (o // 2) % 2}
        self.fetch_bits = self.core_at * 2 + self.x_at
        self.me = {}
        for order in ("zxw", "xzw"):
            slot = self.core_at
            for name in order:
                slot = slot * 2 + bits[name]
            self.me[order] = jnp.stack([slot, self.fetch_bits]).astype(jnp.int32)

    def quarter(self, own):
        flat = own.reshape(-1, own.shape[-1])
        return take_half(take_half(flat, self.core_at), self.x_at)

    def over_x(self, t):
        return lax.ppermute(t, "x", FLIP)

    def fetch(self, own_work):
        own = self.own
        size = own[2].shape[1] // 4
        part = lambda t, axis, bits: lax.dynamic_slice_in_dim(t, bits * size, size, axis)
        pieces = [
            self.quarter(own[1]),
            part(own[2], 1, self.fetch_bits),
            jnp.concatenate([part(own[3], 0, self.fetch_bits), part(own[3], 0, self.fetch_bits ^ 1)], axis=0),
        ]
        qkv = self.partner(self.quarter(own[0]))
        up, out, down = (self.partner(pieces[i]) for i in (1, 0, 2))
        qkv, own_work = sync(qkv, own_work)
        qkv, out, up = sync(ordered(self.x_at, qkv, self.over_x(qkv)).reshape(-1, qkv.shape[-1]), out, up)
        qkv_core, out_x, up_x = self.core(qkv), self.over_x(out), self.over_x(up)
        qkv = ordered(self.core_at, qkv, qkv_core).reshape(own[0].shape)

        def rest(*work):
            nonlocal out, up, out_x, up_x, down
            work, out, up, out_x, up_x = lax.optimization_barrier((work, out, up, out_x, up_x))
            ups = jnp.concatenate([up, up_x], axis=1)
            ups_core = self.core(ups)
            out = ordered(self.x_at, out, out_x).reshape(-1, out.shape[-1])
            out = ordered(self.core_at, out, self.core(out)).reshape(own[1].shape)
            wout = jnp.concatenate([own[1], out], axis=0)
            wup = jnp.concatenate([own[2], ups, ups_core], axis=1)
            down = after(down, wout, wup)
            wdown = jnp.concatenate([own[3], down, self.core(down)], axis=0)
            return work, wout, wup, wdown

        return own_work, own[0], qkv, jnp.concatenate([own[0], qkv], axis=2), rest

    def partner(self, t):
        return lax.ppermute(t, "tensor", FLIP)

    def core(self, t):
        return lax.ppermute(t, "core", FLIP)

    def chunk(self, keep, got, order):
        return Chunk(self.outer, keep, got, order)

    def small_steps(self):
        return [("core", 2, 1), ("tensor", 2, 1)] + steps_of(self.outer)

    def flip(self, t, step):
        return flip_bit(t, *step)


def local_part(x, seg, cot, gb, link):
    rows, seq = seg.shape
    n, width = x.shape
    me_z, me_x = link.me["zxw"], link.me["xzw"]
    incl, strict = mask_biases(seg)
    normal, _ = norm_stats(x.astype(F32))
    a_e = (normal * gb[0] + gb[2]).astype(BF16)
    first = attend_first(a_e, link.own[0], incl)
    (a_e, first), wq_own, fetched, wqkv, rest = link.fetch((a_e, first))
    second = attend_first(a_e, fetched, incl)
    qkv_e, o1 = (jnp.concatenate([s, t], axis=-1) for s, t in zip(first[:2], second[:2]))
    lse1 = jnp.concatenate([first[2], second[2]], axis=0).reshape(-1, GROUP // HD, n)
    (qkv_e, o1, lse1, wqkv), wout, wup, wdown = rest(qkv_e, o1, lse1, wqkv)
    h1, n2_1, g1, d1, ho, a_o = mlp_first(x, o1, wout, gb, wup, wdown)
    qkv_o, o2, lse2 = attend_second(a_o, wqkv, incl, strict, qkv_e, o1, lse1)
    out, n2_2, g2, du2, dh1_2, dp2, do2, sums2, dm2 = mlp_second(x, ho, o2, cot, wout, gb, wup, wdown, seq)
    out_got = link.partner(out[: rows // 2])
    dqkv_o, part, dy, sums_o = attend_back(wqkv, incl, strict, qkv_e, qkv_o, o2, lse2, do2, dh1_2, ho, gb)
    o2_flat = o2.reshape(2 * n, width)

    dm1 = dy.astype(BF16)
    out_got, dm1 = sync(out_got, dm1)
    down_go = grad_down(me_z, 1, g1, g2, dm1, dm2)
    down_got = link.core(down_go)
    down_keep = grad_down(me_z, 0, g1, g2, dm1, after(dm2, down_go))
    down = link.chunk(down_keep, down_got, "zxw")
    (down.keep,) = down.wait(down_keep)
    down.to_partner()
    du1, dh1_1, dp1, do1, sums1 = mlp_back(after(dy, down.sent), h1, wout, gb, d1, wup, wdown, seq)
    parts = (n2_1, n2_2, du1, du2, dp1, dp2, o1)
    up_go = grad_up(me_x, 1, *parts, o2_flat)
    (up_go,) = down.wait(up_go)
    down.scatter(0)
    up_got = link.core(up_go)
    up_keep = grad_up(me_x, 0, *parts, after(o2_flat, up_go, down.sent))
    up = link.chunk(up_keep, up_got, "xzw")
    (up.keep,) = up.wait(up_keep)
    up.scatter(0)
    do1 = after(do1, up.sent)
    dqkv_e, gt, sums_e = attend_back_even(wqkv, incl, qkv_e, o1, lse1, do1, o2, lse2, do2, part, dh1_1, dh1_2, x, gb)
    dqkv_e, gt, sums_e = down.wait(dqkv_e, gt, sums_e)
    down.scatter(1)
    small = jnp.stack([sums_e[0] + sums_o[0], sums1[0] + sums2[0], sums_e[1] + sums_o[1], sums1[1] + sums2[1], sums_o[2]])
    qkv_go = grad_qkv(me_z, 1, a_e, a_o, after(dqkv_e, down.sent), dqkv_o)
    (qkv_go,) = up.wait(qkv_go)
    up.to_partner()
    qkv_got = link.core(qkv_go)
    small_steps = iter(link.small_steps())
    small_got = link.flip(after(small, qkv_go), next(small_steps))
    qkv_keep = grad_qkv(me_z, 0, a_e, a_o, after(dqkv_e, up.sent, qkv_go), dqkv_o)
    qkv = link.chunk(qkv_keep, qkv_got, "zxw")
    qkv.keep, down.got = qkv.wait(qkv_keep, down.got)
    qkv.to_partner()

    def small_hop(chunk):
        nonlocal small, small_got
        small = small + chunk.wait(small_got)[0]
        step = next(small_steps, None)
        small_got = None if step is None else link.flip(small, step)

    def then(chunk, previous, *what):
        chunk.wait(previous.sent)
        for name, *args in what:
            getattr(chunk, name)(*args)

    gt_got = link.partner(after(gt, qkv.sent))
    then(down, qkv, ("scatter", 2))
    small_hop(up)
    then(up, down, ("scatter", 1))
    small_hop(qkv)
    then(qkv, up, ("scatter", 0))
    out_last = link.partner(after(out[rows // 2 :], qkv.sent))
    small_hop(down)
    then(down, qkv, ("all_summed",), ("gather", 2))
    then(down, up, ("joined",), ("gather", 1))
    then(qkv, down, ("scatter", 1))
    then(up, qkv, ("scatter", 2))
    small_hop(down)
    then(down, up, ("joined",), ("gather", 0))
    then(qkv, down, ("scatter", 2))
    (gt_got,) = up.wait(gt_got)
    small_hop(up)
    while small_got is not None:
        small_hop(up)
    then(up, qkv, ("all_summed",), ("gather", 2))
    then(qkv, up, ("all_summed",), ("gather", 2))
    out, gt = link.finish(out, sync(jnp.concatenate([out_got, out_last], axis=0), qkv.sent)[0], gt, gt_got)
    then(down, qkv, ("joined",), ("gather_core",))
    then(up, down, ("joined",), ("gather", 1))
    then(qkv, up, ("joined",), ("gather", 1))
    (g_down,) = unpack("down", me_z, 0, after(down.keep, qkv.sent))
    out, gt, *_ = down.wait(out, gt, g_down)
    g_down, = unpack("down", me_z, 1, down.got, (g_down,))
    qkv.wait(g_down, out, gt)
    qkv.joined()
    qkv.gather(0)
    then(up, qkv, ("joined",), ("gather", 0))
    then(qkv, up, ("joined",), ("gather_core",))
    (g_qkv,) = unpack("qkv", me_z, 0, qkv.keep)
    (g_qkv,) = up.wait(g_qkv)
    up.joined()
    up.gather_core()
    g_up = unpack("up", me_x, 0, up.keep)
    qkv.wait(up.sent)
    (g_qkv,) = unpack("qkv", me_z, 1, qkv.got, (g_qkv,))
    up.wait(g_qkv, *g_up)
    g_up, g_out = unpack("up", me_x, 1, up.got, g_up)
    return out, gt, (g_qkv, g_out, g_up, g_down), small


def shards(outer, tokens, segments, pass_embed, w_qkv, w_out, w_up, w_down, gain, bias, cotangent):
    ty = lax.axis_index("tensor")
    rows = tokens.shape[0] // 2
    width = tokens.shape[2]
    mine = lambda t: lax.dynamic_slice_in_dim(t, ty * rows, rows, 0)
    x = mine(tokens).reshape(-1, width)
    gb = jnp.concatenate([gain, bias, pass_embed[None]], axis=0)
    link = Link(outer, w_qkv, w_out, w_up, w_down)
    link.finish = lambda out, out_got, gt, gt_got: (
        ordered(ty, out, out_got).reshape(cotangent.shape),
        ordered(ty, gt, gt_got).reshape(tokens.shape).astype(F32),
    )
    out, gt, grads, small = local_part(x, mine(segments), mine(cotangent), gb, link)
    return out, gt, *grads, small[0:2], small[2:4], small[4]


def solution(mesh):
    outer = mesh.shape["dp"] // 4
    fine = Mesh(mesh.devices.reshape(outer, 2, 2, mesh.shape["tensor"]), ("o", "x", "core", "tensor"))
    rows = ROWS_OVER
    placed = (
        P(rows, None, None),
        P(rows, None),
        P(),
        P(None, None, "tensor"),
        P("tensor", None),
        P(None, "tensor"),
        P("tensor", None),
        P(),
        P(),
        P(rows, None, None),
    )

    def body(*args):
        return shards(outer, *args)

    return jax.shard_map(
        body,
        mesh=fine,
        in_specs=placed,
        out_specs=(
            P(rows, None, None),
            P(rows, None, None),
            P(None, None, "tensor"),
            P("tensor", None),
            P(None, "tensor"),
            P("tensor", None),
            P(),
            P(),
            P(),
        ),
        check_vma=False,
    )
```

```python
import functools

import jax
import jax.numpy as jnp
from jax import lax
from jax.experimental import pallas as pl
from jax.experimental.pallas import tpu as pltpu
from jax.sharding import Mesh
from jax.sharding import PartitionSpec as P

HD = 64
EPS = 1e-05
NEG = -1000000000.0
F32 = jnp.float32
BF16 = jnp.bfloat16
ROWS_OVER = ("o", "x", "core")
FLIP = ((0, 1), (1, 0))
VMEM_LIMIT = 60 * 1024 * 1024


def ordered(flag, mine, theirs):
    first = flag == 0
    return jnp.stack([jnp.where(first, mine, theirs), jnp.where(first, theirs, mine)])


def take_half(array, index):
    half = array.shape[0] // 2
    return lax.dynamic_slice_in_dim(array, index * half, half, 0)


def flip_bit(array, axis, size, bit):
    return lax.ppermute(array, axis, [(i, i ^ bit) for i in range(size)])


def steps_of(outer):
    steps = [("x", 2, 1)]
    bit = 1
    while bit < outer:
        steps.append(("o", outer, bit))
        bit *= 2
    return steps


def my_bit(axis, bit):
    return (lax.axis_index(axis) // bit) % 2


def dot(a, b):
    return lax.dot_general(a, b, (((1,), (0,)), ((), ())), preferred_element_type=F32)


def dot_nt(a, b):
    return lax.dot_general(a, b, (((1,), (1,)), ((), ())), preferred_element_type=F32)


def dot_tn(a, b):
    return lax.dot_general(a, b, (((0,), (0,)), ((), ())), preferred_element_type=F32)


def norm_stats(h):
    centred = h - jnp.mean(h, axis=-1, keepdims=True)
    inverse = lax.rsqrt(jnp.mean(centred * centred, axis=-1, keepdims=True) + EPS)
    return centred * inverse, inverse


def norm_back(grad, normal, inverse, gain):
    scaled = grad * gain
    centre = jnp.mean(scaled, axis=-1, keepdims=True)
    proj = jnp.mean(scaled * normal, axis=-1, keepdims=True)
    return inverse * (scaled - centre - normal * proj)


def gelu_parts(u):
    c = 0.7978845608028654
    a = 0.044715 * c
    square = u * u
    half = 0.5 + 0.5 * jnp.tanh(u * (c + a * square))
    g = u * half
    return g, half + g * (1.0 - half) * (2.0 * c + 6.0 * a * square)


def whole(shape):
    return pl.BlockSpec(shape, lambda *_: (0,) * len(shape))


def call(body, grid, ins, outs, scratch=(), cost=(0, 0), name=None, vmem=VMEM_LIMIT):
    return pl.pallas_call(
        body,
        grid=grid,
        in_specs=[s for _, s in ins],
        out_specs=[s for _, s in outs],
        out_shape=[a for a, _ in outs],
        scratch_shapes=scratch,
        compiler_params=pltpu.CompilerParams(
            dimension_semantics=("arbitrary",) * len(grid), vmem_limit_bytes=vmem
        ),
        cost_estimate=pl.CostEstimate(
            flops=int(cost[0]) // 16, bytes_accessed=int(cost[1]), transcendentals=0
        ),
        name=name,
    )(*[a for a, _ in ins])


FAR = pl.BlockSpec(memory_space=pl.ANY)


def resident(body, ins, outs, scratch=(), flops=0, vmem=16, name=None):
    spec = pl.BlockSpec(memory_space=pltpu.VMEM)
    ins, outs = ([o if isinstance(o, tuple) else (o, spec) for o in t] for t in (ins, outs))
    ins = [(pltpu.with_memory_space_constraint(a, pltpu.HBM) if s is FAR else a, s) for a, s in ins]
    outs = [(pltpu.HBM(a.shape, a.dtype) if s is FAR else a, s) for a, s in outs]
    return pl.pallas_call(
        body,
        in_specs=[s for _, s in ins],
        out_specs=[s for _, s in outs],
        out_shape=[a for a, _ in outs],
        scratch_shapes=scratch,
        compiler_params=pltpu.CompilerParams(vmem_limit_bytes=vmem * 1024 * 1024),
        cost_estimate=pl.CostEstimate(flops=int(flops) // 16, bytes_accessed=0, transcendentals=0),
        name=name,
    )(*[a for a, _ in ins])


def sds(shape, dtype):
    return jax.ShapeDtypeStruct(shape, dtype)


QB = 128
GROUP = 256


def lanes_of(ref, g):
    return ref.at[(slice(None),) * (len(ref.shape) - 1) + (pl.ds(pl.multiple_of(g * GROUP, GROUP), GROUP),)]


class Moves:
    def __init__(self, sems):
        self.sems, self.used = sems, 0

    def take(self, number):
        self.used += number
        return self.used - number

    def whole(self, source, target):
        copy = pltpu.make_async_copy(source, target, self.sems.at[self.take(1)])
        copy.start()
        return copy.wait

    def later(self, source, target):
        sem = self.sems.at[self.take(1)]
        copy = lambda: pltpu.make_async_copy(source, target, sem)
        return (lambda: copy().start()), (lambda: copy().wait())

    def groups(self, source, target):
        first = self.take(source.shape[-1] // GROUP)

        def copy(g):
            return pltpu.make_async_copy(lanes_of(source, g), lanes_of(target, g), self.sems.at[first + g])

        return (lambda g: copy(g).start()), (lambda g: copy(g).wait())


def cat_heads(t, scale=1.0):
    lane = lax.broadcasted_iota(jnp.int32, (1, 2 * HD), 1)
    parts = [t * jnp.where((lane < HD) == (h == 0), scale, 0.0).astype(t.dtype) for h in range(2)]
    return jnp.concatenate(parts, axis=0)


def own_lanes(t, scale=None):
    if scale is not None:
        t = t * scale
    return jnp.concatenate([t[:HD, :QB], t[HD:, QB:]], axis=0)


def twice(t):
    return jnp.concatenate([t, t], axis=1)


def pair_row(rows, p):
    return jnp.concatenate([rows[2 * p : 2 * p + 1], rows[2 * p + 1 : 2 * p + 2]], axis=1)


def put_pair(ref, p, cols, value):
    ref[2 * p : 2 * p + 1, cols] = value[:, :QB]
    ref[2 * p + 1 : 2 * p + 2, cols] = value[:, QB:]


def columns(t, r, seq, qb):
    return t[:, pl.ds(pl.multiple_of(r * seq + qb * QB, QB), QB)]


def rows_of(r, seq, qb):
    return pl.ds(pl.multiple_of(r * seq + qb * QB, QB), QB)


def in_turn(arrive, group, groups):
    for _, wait in arrive:
        wait(group)

    @pl.when(group + 2 < groups)
    def _():
        for start, _ in arrive:
            start(group + 2)


def attend_first_body(rows, seq, pairs, a_ref, w_ref, bias_ref, qkv_ref, o_ref, lse_ref):
    a = a_ref[...]
    for j in range(3):
        qkv_ref[j] = dot(a, w_ref[j]).astype(BF16)
    for r in range(rows):
        work = []
        for p in range(pairs):
            ln = slice(p * 2 * HD, (p + 1) * 2 * HD)
            k = qkv_ref[1, r * seq : (r + 1) * seq, ln]
            for b in range(seq // QB):
                sl, n = slice(r * seq + b * QB, r * seq + (b + 1) * QB), (b + 1) * QB
                q = cat_heads(qkv_ref[0, sl, ln], HD**-0.5)
                s = dot_nt(k[:n], q) + twice(bias_ref[r, :n, b * QB : n])
                work.append((p, ln, sl, n, s))
        done = []
        for p, ln, sl, n, s in work:
            top = jnp.max(s, axis=0, keepdims=True)
            e = jnp.exp(s - top)
            mass = jnp.sum(e, axis=0, keepdims=True)
            put_pair(lse_ref, p, sl, top + jnp.log(mass))
            done.append((e.astype(BF16), 1.0 / mass))
        for (p, ln, sl, n, _), (e, inv) in zip(work, done):
            vt = qkv_ref[2, r * seq : (r + 1) * seq, ln].T
            o_ref[sl, ln] = own_lanes(dot(vt[:, :n], e), inv).T.astype(BF16)


def attend_first(a, w, bias):
    rows, seq = bias.shape[0], bias.shape[1]
    n, d = a.shape
    f = w.shape[2]
    return resident(
        functools.partial(attend_first_body, rows, seq, f // (2 * HD)),
        (a, w, bias),
        [sds((3, n, f), BF16), sds((n, f), BF16), sds((f // HD, n), F32)],
        flops=6 * n * d * f + 16 * n * seq * f,
        name="attend_first",
    )


def attend_second_body(
    rows, seq, a_far, w_far, incl_far, strict_far, qkve_far, o1_far, lse1_ref,
    qkvo_far, o2_far, lse2_ref,
    a_ref, w_ref, incl_ref, strict_ref, qkve_ref, o1_ref, qkvo_ref, o2_ref, sems,
):
    groups = lse1_ref.shape[0]
    moves = Moves(sems)
    ready = [moves.whole(a_far, a_ref), moves.whole(w_far.at[0], w_ref.at[0])]
    arrive = [moves.groups(*t) for t in ((qkve_far, qkve_ref), (o1_far, o1_ref))]
    leave = moves.groups(o2_ref, o2_far)
    for wait in ready:
        wait()
    ready = [moves.whole(w_far.at[j], w_ref.at[j]) for j in (1, 2)]
    a = a_ref[...]
    sent = []
    for j in range(3):
        if j:
            ready[j - 1]()
        if j == 1:
            masks = [moves.whole(*t) for t in ((incl_far, incl_ref), (strict_far, strict_ref))]
            for g in range(2):
                for start, _ in arrive:
                    start(g)
        qkvo_ref[j] = dot(a, w_ref[j]).astype(BF16)
        sent.append(moves.whole(qkvo_ref.at[j], qkvo_far.at[j]))
    for wait in masks:
        wait()

    def next_group(group):
        in_turn(arrive, group, groups)

    def row(i, _):
        r, group = i % rows, i // rows
        lanes = pl.multiple_of(group * GROUP, GROUP)
        all_of = pl.ds(pl.multiple_of(r * seq, seq), seq)

        @pl.when(r == 0)
        def _():
            next_group(group)

        for p in range(GROUP // (2 * HD)):
            ln = pl.ds(lanes + p * 2 * HD, 2 * HD)
            ke, ko = qkve_ref[1, all_of, ln], qkvo_ref[1, all_of, ln]
            vte, vto = qkve_ref[2, all_of, ln].T, qkvo_ref[2, all_of, ln].T
            work = []
            for b in range(seq // QB):
                sl, n = rows_of(r, seq, b), (b + 1) * QB
                cols = slice(b * QB, n)
                incl, strict = twice(incl_ref[r, :n, cols]), twice(strict_ref[r, :n, cols])
                q = cat_heads(qkve_ref[0, sl, ln], HD**-0.5)
                work.append([dot_nt(ko[:n], q) + strict])
                q = cat_heads(qkvo_ref[0, sl, ln], HD**-0.5)
                work.append([dot_nt(ko[:n], q) + incl, dot_nt(ke[:n], q) + incl])
            for b in range(seq // QB):
                sl, n = rows_of(r, seq, b), (b + 1) * QB
                (s,), (so, se) = work[2 * b : 2 * b + 2]
                old = pair_row(lse1_ref[group, :, sl], p)
                top = jnp.maximum(old, jnp.max(s, axis=0, keepdims=True))
                e = jnp.exp(s - top)
                kept = jnp.exp(old - top)
                mass = kept + jnp.sum(e, axis=0, keepdims=True)
                work[2 * b] = (e.astype(BF16), kept, 1.0 / mass)
                put_pair(lse2_ref.at[0, group], p, sl, top + jnp.log(mass))
                top = jnp.max(jnp.maximum(se, so), axis=0, keepdims=True)
                ee, eo = jnp.exp(se - top), jnp.exp(so - top)
                mass = jnp.sum(ee + eo, axis=0, keepdims=True)
                work[2 * b + 1] = (ee.astype(BF16), eo.astype(BF16), 1.0 / mass)
                put_pair(lse2_ref.at[1, group], p, sl, top + jnp.log(mass))
            for b in range(seq // QB):
                sl, n = rows_of(r, seq, b), (b + 1) * QB
                (e, kept, inv), (ee, eo, inv2) = work[2 * b : 2 * b + 2]
                o1 = o1_ref[sl, ln].astype(F32).T
                o = own_lanes(dot(vto[:, :n], e), inv) + own_lanes(twice(o1), kept * inv)
                o2_ref[0, sl, ln] = o.T.astype(BF16)
                o = dot(vte[:, :n], ee) + dot(vto[:, :n], eo)
                o2_ref[1, sl, ln] = own_lanes(o, inv2).T.astype(BF16)

        @pl.when(r == rows - 1)
        def _():
            leave[0](group)

        return 0

    lax.fori_loop(0, rows * groups, row, 0)
    for wait in sent:
        wait()
    for g in range(groups):
        leave[1](g)


def attend_second(a, w, incl, strict, qkve, o1, lse1):
    rows, seq = incl.shape[0], incl.shape[1]
    n, d = a.shape
    f = w.shape[2]
    qkv, o2 = sds((3, n, f), BF16), sds((2, n, f), BF16)
    near = (a, w, incl, strict, qkve, o1, qkv, o2)
    return resident(
        functools.partial(attend_second_body, rows, seq),
        [(t, FAR) for t in (a, w, incl, strict, qkve, o1)] + [lse1],
        [(qkv, FAR), (o2, FAR), sds((2, *lse1.shape), F32)],
        scratch=[pltpu.VMEM(t.shape, t.dtype) for t in near] + [pltpu.SemaphoreType.DMA((32,))],
        flops=6 * n * d * f + 48 * n * seq * f,
        vmem=32,
        name="attend_second",
    )


def row_products(a, b):
    prod = cat_heads((a * b).astype(BF16))
    return dot_nt(jnp.ones((8, 2 * HD), BF16), prod)[:1]


def query_parts(sl, ln, group, p, i, qkv_ref, o_ref, lse_ref, do_ref):
    do = do_ref[i, sl, ln]
    delta = row_products(do.astype(F32), o_ref[i, sl, ln].astype(F32))
    return cat_heads(qkv_ref[0, sl, ln], HD**-0.5), cat_heads(do), pair_row(lse_ref[i, group, :, sl], p), delta


def blocks_back(tasks):
    scores = [dot_nt(k, q) + bias - lse for k, _, _, bias, q, _, lse, _ in tasks]
    moved = [dot_nt(v, do) - delta for _, v, _, _, _, do, _, delta in tasks]
    probs = [jnp.exp(s) for s in scores]
    ds = [(p * m).astype(BF16) for p, m in zip(probs, moved)]
    return [
        (dot(p.astype(BF16), do), dot(d, q), dot(kt, d))
        for (_, _, kt, _, q, do, _, _), p, d in zip(tasks, probs, ds)
    ]


def add_rows(total, part):
    if total is None:
        return part
    n = part.shape[0]
    return jnp.concatenate([total[:n] + part, total[n:]], axis=0)


def attend_back_body(
    rows, seq, w_far, incl_far, strict_far, qkve_far, qkvo_far, o2_far, lse2_ref, do_far,
    dh1_far, ho_far, gb_ref,
    dqkvo_far, dqkve_far, dy_ref, sums_ref,
    w_ref, incl_ref, strict_ref, qkve_ref, qkvo_ref, o2_ref, do_ref, dh1_ref, ho_ref,
    dqkvo_ref, dqkve_ref, da_ref, sems,
):
    groups = lse2_ref.shape[1]
    moves = Moves(sems)
    arrive = [
        moves.groups(*t)
        for t in ((qkve_far, qkve_ref), (qkvo_far, qkvo_ref), (o2_far, o2_ref), (do_far, do_ref))
    ]
    leave = [moves.groups(*t) for t in ((dqkvo_ref, dqkvo_far), (dqkve_ref, dqkve_far))]
    for start, _ in arrive:
        start(0)
    masks = [moves.whole(*t) for t in ((incl_far, incl_ref), (strict_far, strict_ref))]
    for start, _ in arrive:
        start(1)
    odd = pl.ds(rows * seq, rows * seq)
    late = [moves.later(*t) for t in ((w_far, w_ref), (dh1_far.at[odd], dh1_ref), (ho_far, ho_ref))]
    for wait in masks:
        wait()

    def next_group(group):
        in_turn(arrive, group, groups)

        @pl.when(group == groups - 2)
        def _():
            for start, _ in late:
                start()

    sc = HD**-0.5

    def row(i, _):
        r, group = i % rows, i // rows
        lanes = pl.multiple_of(group * GROUP, GROUP)
        all_of = pl.ds(pl.multiple_of(r * seq, seq), seq)

        @pl.when(r == 0)
        def _():
            next_group(group)

        for p in range(GROUP // (2 * HD)):
            ln = pl.ds(lanes + p * 2 * HD, 2 * HD)
            ke, ve = qkve_ref[1, all_of, ln], qkve_ref[2, all_of, ln]
            ko, vo = qkvo_ref[1, all_of, ln], qkvo_ref[2, all_of, ln]
            kte, kto = ke.T, ko.T
            tasks = []
            for b in reversed(range(seq // QB)):
                sl, n = rows_of(r, seq, b), (b + 1) * QB
                cols = slice(b * QB, n)
                incl, strict = twice(incl_ref[r, :n, cols]), twice(strict_ref[r, :n, cols])
                even = query_parts(sl, ln, group, p, 0, qkve_ref, o2_ref, lse2_ref, do_ref)
                odd = query_parts(sl, ln, group, p, 1, qkvo_ref, o2_ref, lse2_ref, do_ref)
                tasks.append((ko[:n], vo[:n], kto[:, :n], strict, *even))
                tasks.append((ko[:n], vo[:n], kto[:, :n], incl, *odd))
                tasks.append((ke[:n], ve[:n], kte[:, :n], incl, *odd))
            done = blocks_back(tasks)
            dke = dve = dko = dvo = None
            for b in reversed(range(seq // QB)):
                sl = rows_of(r, seq, b)
                (dv, dk, dqe), (dv2, dk2, dqo), (dv3, dk3, dqo2) = done[:3]
                done = done[3:]
                dvo, dko = add_rows(dvo, dv + dv2), add_rows(dko, dk + dk2)
                dve, dke = add_rows(dve, dv3), add_rows(dke, dk3)
                dqkve_ref[0, sl, ln] = (own_lanes(dqe).T * sc).astype(BF16)
                dqkvo_ref[0, sl, ln] = (own_lanes(dqo + dqo2).T * sc).astype(BF16)
            dqkve_ref[1, all_of, ln] = dke.astype(BF16)
            dqkve_ref[2, all_of, ln] = dve.astype(BF16)
            dqkvo_ref[1, all_of, ln] = dko.astype(BF16)
            dqkvo_ref[2, all_of, ln] = dvo.astype(BF16)

        @pl.when(r == rows - 1)
        def _():
            for start, _ in leave:
                start(group)

        return 0

    lax.fori_loop(0, rows * groups, row, 0)
    for _, wait in late:
        wait()
    da = dot_nt(dqkvo_ref[0], w_ref[0])
    da += dot_nt(dqkvo_ref[1], w_ref[1])
    da += dot_nt(dqkvo_ref[2], w_ref[2])
    da_ref[...] = da
    gain_sum = jnp.zeros_like(gb_ref[0:1])
    bias_sum = jnp.zeros_like(gb_ref[0:1])
    pass_sum = jnp.zeros_like(gb_ref[0:1])
    for i in range(rows):
        sl = slice(i * seq, (i + 1) * seq)
        normal, inverse = norm_stats(ho_ref[sl])
        da = da_ref[sl]
        gain_sum += jnp.sum(da * normal, axis=0, keepdims=True)
        bias_sum += jnp.sum(da, axis=0, keepdims=True)
        dy = dh1_ref[sl] + norm_back(da, normal, inverse, gb_ref[0:1])
        dy_ref[sl] = dy
        pass_sum += jnp.sum(dy, axis=0, keepdims=True)
    sums_ref[0:1] = gain_sum
    sums_ref[1:2] = bias_sum
    sums_ref[2:3] = pass_sum
    for g in range(groups):
        for _, wait in leave:
            wait(g)


def attend_back(w, incl, strict, qkve, qkvo, o2, lse2, do, dh1, ho, gb):
    rows, seq = incl.shape[0], incl.shape[1]
    n, d = ho.shape
    f = w.shape[2]
    do = do.reshape(2, n, f)
    qkv = sds((3, n, f), BF16)
    near = (w, incl, strict, qkve, qkvo, o2, do, sds((n, d), F32), ho, qkv, qkv, sds((n, d), F32))
    return resident(
        functools.partial(attend_back_body, rows, seq),
        [(t, FAR) for t in (w, incl, strict, qkve, qkvo, o2)]
        + [lse2]
        + [(t, FAR) for t in (do, dh1, ho)]
        + [gb],
        [(qkv, FAR), (qkv, FAR), sds((n, d), F32), sds((3, d), F32)],
        scratch=[pltpu.VMEM(t.shape, t.dtype) for t in near] + [pltpu.SemaphoreType.DMA((32,))],
        flops=6 * n * d * f + 120 * n * seq * f,
        vmem=44,
        name="attend_back",
    )


def attend_back_even_body(
    rows, seq, w_far, incl_far, qkve_far, o1_far, lse1_ref, do1_far, o2_far, lse2_ref, do2_far,
    part_far, dh1_far, dh2_far, x_far, gb_ref,
    dqkv_far, gt_ref, sums_ref,
    w_ref, incl_ref, qkve_ref, o1_ref, do1_ref, o2_ref, do2_ref, part_ref, dh1_ref, dh2_ref, x_ref,
    dqkv_ref, da_ref, sems,
):
    groups = lse1_ref.shape[0]
    moves = Moves(sems)
    even = pl.ds(0, rows * seq)
    arrive = [
        moves.groups(*t)
        for t in (
            (qkve_far, qkve_ref), (o1_far, o1_ref), (do1_far, do1_ref), (o2_far.at[0], o2_ref),
            (do2_far.at[0], do2_ref), (part_far, part_ref),
        )
    ]
    leave = [moves.groups(dqkv_ref, dqkv_far)]
    for start, _ in arrive:
        start(0)
    mask = moves.whole(incl_far, incl_ref)
    for start, _ in arrive:
        start(1)
    late = [
        moves.later(*t)
        for t in ((w_far, w_ref), (dh1_far, dh1_ref), (dh2_far.at[even], dh2_ref), (x_far, x_ref))
    ]
    mask()

    def next_group(group):
        in_turn(arrive, group, groups)

        @pl.when(group == groups - 2)
        def _():
            for start, _ in late:
                start()

    sc = HD**-0.5

    def row(i, _):
        r, group = i % rows, i // rows
        lanes = pl.multiple_of(group * GROUP, GROUP)
        all_of = pl.ds(pl.multiple_of(r * seq, seq), seq)

        @pl.when(r == 0)
        def _():
            next_group(group)

        for p in range(GROUP // (2 * HD)):
            ln = pl.ds(lanes + p * 2 * HD, 2 * HD)
            k, v = qkve_ref[1, all_of, ln], qkve_ref[2, all_of, ln]
            kt = k.T
            tasks = []
            for b in reversed(range(seq // QB)):
                sl, n = rows_of(r, seq, b), (b + 1) * QB
                incl = twice(incl_ref[r, :n, b * QB : n])
                lse1 = pair_row(lse1_ref[group, :, sl], p)
                ratio = jnp.exp(lse1 - pair_row(lse2_ref[0, group, :, sl], p))
                do1, do2 = do1_ref[sl, ln].astype(F32), do2_ref[sl, ln].astype(F32)
                delta = row_products(do1, o1_ref[sl, ln].astype(F32))
                delta += ratio * row_products(do2, o2_ref[sl, ln].astype(F32))
                both = do1 + own_lanes(twice(do2.T), ratio).T
                q, do = cat_heads(qkve_ref[0, sl, ln], sc), cat_heads(both.astype(BF16))
                tasks.append((k[:n], v[:n], kt[:, :n], incl, q, do, lse1, delta))
            dka = dva = None
            for b, (dv, dk, dq) in zip(reversed(range(seq // QB)), blocks_back(tasks)):
                sl = rows_of(r, seq, b)
                dva, dka = add_rows(dva, dv), add_rows(dka, dk)
                dqkv_ref[0, sl, ln] = (own_lanes(dq).T * sc + part_ref[0, sl, ln].astype(F32)).astype(BF16)
            dqkv_ref[1, all_of, ln] = (dka + part_ref[1, all_of, ln].astype(F32)).astype(BF16)
            dqkv_ref[2, all_of, ln] = (dva + part_ref[2, all_of, ln].astype(F32)).astype(BF16)

        @pl.when(r == rows - 1)
        def _():
            for start, _ in leave:
                start(group)

        return 0

    lax.fori_loop(0, rows * groups, row, 0)
    for _, wait in late:
        wait()
    da = dot_nt(dqkv_ref[0], w_ref[0])
    da += dot_nt(dqkv_ref[1], w_ref[1])
    da += dot_nt(dqkv_ref[2], w_ref[2])
    da_ref[...] = da
    gain_sum = jnp.zeros_like(gb_ref[0:1])
    bias_sum = jnp.zeros_like(gb_ref[0:1])
    for i in range(rows):
        sl = slice(i * seq, (i + 1) * seq)
        normal, inverse = norm_stats(x_ref[sl].astype(F32))
        da = da_ref[sl]
        gain_sum += jnp.sum(da * normal, axis=0, keepdims=True)
        bias_sum += jnp.sum(da, axis=0, keepdims=True)
        back = norm_back(da, normal, inverse, gb_ref[0:1])
        gt_ref[sl] = (dh1_ref[sl] + dh2_ref[sl] + back).astype(BF16)
    sums_ref[0:1] = gain_sum
    sums_ref[1:2] = bias_sum
    for g in range(groups):
        for _, wait in leave:
            wait(g)


def attend_back_even(w, incl, qkve, o1, lse1, do1, o2, lse2, do2, part, dh1, dh2, x, gb):
    rows, seq = incl.shape[0], incl.shape[1]
    n, d = x.shape
    f = w.shape[2]
    qkv, one = sds((3, n, f), BF16), sds((n, f), BF16)
    near = (w, incl, qkv, one, one, one, one, qkv, dh1, dh1, x, qkv, sds((n, d), F32))
    far = lambda *ts: [(t, FAR) for t in ts]
    return resident(
        functools.partial(attend_back_even_body, rows, seq),
        far(w, incl, qkve, o1)
        + [lse1]
        + far(do1, o2)
        + [lse2]
        + far(do2.reshape(2, n, f), part, dh1, dh2, x)
        + [gb],
        [(qkv, FAR), sds((n, d), BF16), sds((2, d), F32)],
        scratch=[pltpu.VMEM(t.shape, t.dtype) for t in near] + [pltpu.SemaphoreType.DMA((32,))],
        flops=6 * n * d * f + 40 * n * seq * f,
        vmem=40,
        name="attend_back_even",
    )


CHUNK = 512


def chunk_of(ref, j, axis):
    at = pl.ds(pl.multiple_of(j * CHUNK, CHUNK), CHUNK)
    return ref.at[:, at] if axis else ref.at[at]


class Chunks:
    def __init__(self, moves, far, near, axis, ring=False, leave=False):
        self.first = moves.take(far.shape[axis] // CHUNK)
        self.sems, self.far, self.near = moves.sems, far, near
        self.axis, self.ring, self.leave = axis, ring, leave

    def copy(self, j):
        near = self.near.at[j % self.near.shape[0]] if self.ring else chunk_of(self.near, j, self.axis)
        ends = (chunk_of(self.far, j, self.axis), near)
        return pltpu.make_async_copy(*(ends[::-1] if self.leave else ends), self.sems.at[self.first + j])

    def start(self, j):
        self.copy(j).start()

    def wait(self, j):
        self.copy(j).wait()


def mlp_first_body(
    x_far, o_far, wout_far, gb_ref, wup_far, wdown_far,
    h1_far, n2_far, g_far, d_far, ho_ref, ao_ref,
    x_ref, o_ref, wout_ref, wup_ref, wdown_ref, h1_ref, n2_ref, g_buf, d_buf, sems,
):
    moves = Moves(sems)
    first = [moves.whole(*t) for t in ((o_far, o_ref), (wout_far, wout_ref), (x_far, x_ref))]
    ups, downs = Chunks(moves, wup_far, wup_ref, 1), Chunks(moves, wdown_far, wdown_ref, 0)
    gs, ds = (Chunks(moves, f, b, 1, True, True) for f, b in ((g_far, g_buf), (d_far, d_buf)))
    number = wup_far.shape[1] // CHUNK
    for wait in first:
        wait()
    for j in range(2):
        ups.start(j)
        downs.start(j)
    h1 = x_ref[...].astype(F32) + dot(o_ref[...], wout_ref[...])
    h1_ref[...] = h1
    normal, _ = norm_stats(h1)
    n2_ref[...] = (normal * gb_ref[1:2] + gb_ref[3:4]).astype(BF16)
    ho_ref[...] = h1 + gb_ref[4:5]
    kept = [moves.whole(*t) for t in ((h1_ref, h1_far), (n2_ref, n2_far))]

    def step(j, _):
        ups.wait(j)
        downs.wait(j)

        @pl.when(j + 2 < number)
        def _():
            ups.start(j + 2)
            downs.start(j + 2)

        @pl.when(j >= 2)
        def _():
            gs.wait(j - 2)
            ds.wait(j - 2)

        half = n2_ref.shape[0] // 2
        parts = []
        for sl in (slice(0, half), slice(half, 2 * half)):
            g, d = gelu_parts(dot(n2_ref[sl], chunk_of(wup_ref, j, 1)[...]))
            parts.append(g.astype(BF16))
            g_buf[j % 2, sl] = parts[-1]
            d_buf[j % 2, sl] = d.astype(BF16)
        gs.start(j)
        ds.start(j)
        for i, g in enumerate(parts):
            ho_ref[i * half : (i + 1) * half] += dot(g, chunk_of(wdown_ref, j, 0)[...])
        return 0

    lax.fori_loop(0, number, step, 0, unroll=2)
    normal, _ = norm_stats(ho_ref[...])
    ao_ref[...] = (normal * gb_ref[0:1] + gb_ref[2:3]).astype(BF16)
    for wait in kept:
        wait()
    for j in range(number - 2, number):
        gs.wait(j)
        ds.wait(j)


def near_of(*arrays):
    return [pltpu.VMEM(t.shape, t.dtype) for t in arrays]


def far_of(*arrays):
    return [(t, FAR) for t in arrays]


def mlp_first(x, o, wout, gb, wup, wdown):
    n, d = x.shape
    ff = wup.shape[1]
    h1, low, wide = sds((n, d), F32), sds((n, d), BF16), sds((n, ff), BF16)
    return resident(
        mlp_first_body,
        far_of(x, o, wout) + [gb] + far_of(wup, wdown),
        far_of(h1, low, wide, wide) + [h1, low],
        scratch=near_of(x, o, wout, wup, wdown, h1, low)
        + [pltpu.VMEM((2, n, CHUNK), BF16)] * 2
        + [pltpu.SemaphoreType.DMA((40,))],
        vmem=40,
        name="mlp_first",
    )


def weave(seq):
    i = lax.broadcasted_iota(jnp.int32, (2 * seq, 2 * seq), 0)
    k = lax.broadcasted_iota(jnp.int32, (2 * seq, 2 * seq), 1)
    place = jnp.where(k < seq, 2 * k, 2 * (k - seq) + 1)
    return jnp.where(i == place, 1.0, 0.0).astype(BF16)


def after_norm_back(
    moves, size, h1_ref, dn_ref, db_ref, wout_ref, gb_ref, sums_ref, dp_ref, do_ref, dh1_far, dp_far, do_far
):
    gain_sum = jnp.zeros_like(gb_ref[0:1])
    bias_sum = jnp.zeros_like(gb_ref[0:1])
    waits = []
    for i in range(h1_ref.shape[0] // size):
        sl = slice(i * size, (i + 1) * size)
        normal, inverse = norm_stats(h1_ref[sl])
        dn = dn_ref[sl]
        gain_sum += jnp.sum(dn * normal, axis=0, keepdims=True)
        bias_sum += jnp.sum(dn, axis=0, keepdims=True)
        dh1 = db_ref[sl].astype(F32) + norm_back(dn, normal, inverse, gb_ref[1:2])
        dn_ref[sl] = dh1
        dp = dh1.astype(BF16)
        dp_ref[sl] = dp
        do_ref[sl] = dot_nt(dp, wout_ref[...]).astype(BF16)
        at = pl.ds(i * size, size)
        waits += [moves.whole(a.at[at], b.at[at]) for a, b in ((dn_ref, dh1_far), (dp_ref, dp_far), (do_ref, do_far))]
    sums_ref[0:1] = gain_sum
    sums_ref[1:2] = bias_sum
    return waits


def mlp_second_body(
    rows, seq, x_far, ho_far, o_far, cot_far, wout_far, gb_ref, wup_far, wdown_far,
    out_far, n2_far, g_far, du_far, dh1_far, dp_far, do_far, sums_ref, dm_far,
    x_ref, ho_ref, o_ref, cot_ref, wout_ref, wup_ref, wdown_ref, n2_ref, dm_ref,
    h1_ref, z_ref, dn_ref, dp_ref, do_ref, g_buf, du_buf, sems,
):
    n = rows * seq
    moves = Moves(sems)
    halves = (slice(0, n), slice(n, 2 * n))
    first = [moves.whole(*t) for t in ((o_far, o_ref), (wout_far, wout_ref), (x_far, x_ref))]
    ups, downs = Chunks(moves, wup_far, wup_ref, 1), Chunks(moves, wdown_far, wdown_ref, 0)
    gs, dus = (Chunks(moves, f, b, 1, True, True) for f, b in ((g_far, g_buf), (du_far, du_buf)))
    number = wup_far.shape[1] // CHUNK
    for wait in first:
        wait()
    then = [moves.whole(*t) for t in ((ho_far, ho_ref), (cot_far, cot_ref))]
    for j in range(2):
        ups.start(j)
        downs.start(j)
    for i, sl in enumerate(halves):
        if i:
            for wait in then:
                wait()
        start = x_ref[...].astype(F32) if i == 0 else ho_ref[...]
        h1 = start + dot(o_ref[i], wout_ref[...])
        h1_ref[sl] = h1
        normal, _ = norm_stats(h1)
        n2_ref[sl] = (normal * gb_ref[1:2] + gb_ref[3:4]).astype(BF16)
    mix = weave(seq)
    for r in range(rows):
        parted = dot_tn(mix, cot_ref[r]).astype(BF16)
        for i in range(2):
            dm_ref[i * n + r * seq : i * n + (r + 1) * seq] = parted[i * seq : (i + 1) * seq]
    kept = [moves.whole(*t) for t in ((n2_ref, n2_far), (dm_ref, dm_far))]
    z_ref[...] = jnp.zeros_like(z_ref)
    dn_ref[...] = jnp.zeros_like(dn_ref)

    def step(j, _):
        ups.wait(j)
        downs.wait(j)

        @pl.when(j + 2 < number)
        def _():
            ups.start(j + 2)
            downs.start(j + 2)

        @pl.when(j >= 2)
        def _():
            gs.wait(j - 2)
            dus.wait(j - 2)

        for sl in halves:
            u = dot(n2_ref[sl], chunk_of(wup_ref, j, 1)[...])
            dg = dot_nt(dm_ref[sl], chunk_of(wdown_ref, j, 0)[...])
            g, d = gelu_parts(u)
            g = g.astype(BF16)
            du = (dg * d).astype(BF16)
            g_buf[j % 2, sl] = g
            du_buf[j % 2, sl] = du
            z_ref[sl] += dot(g, chunk_of(wdown_ref, j, 0)[...])
            dn_ref[sl] += dot_nt(du, chunk_of(wup_ref, j, 1)[...])
        gs.start(j)
        dus.start(j)
        return 0

    lax.fori_loop(0, number, step, 0)
    for r in range(rows):
        pair = [slice(i * n + r * seq, i * n + (r + 1) * seq) for i in range(2)]
        z = jnp.concatenate([(h1_ref[s] + z_ref[s]).astype(BF16) for s in pair], axis=0)
        cot_ref[r] = dot(mix, z).astype(BF16)
    kept.append(moves.whole(cot_ref, out_far))
    kept += after_norm_back(
        moves, seq, h1_ref, dn_ref, dm_ref, wout_ref, gb_ref, sums_ref, dp_ref, do_ref, dh1_far, dp_far, do_far
    )
    for wait in kept:
        wait()
    for j in range(number - 2, number):
        gs.wait(j)
        dus.wait(j)


def mlp_second(x, ho, o2, cot, wout, gb, wup, wdown, seq):
    n, d = x.shape
    ff = wup.shape[1]
    rows = n // seq
    low, wide, full = sds((2 * n, d), BF16), sds((2 * n, ff), BF16), sds((2 * n, d), F32)
    return resident(
        functools.partial(mlp_second_body, rows, seq),
        far_of(x, ho, o2, cot, wout) + [gb] + far_of(wup, wdown),
        far_of(cot, low, wide, wide, full, low, low) + [sds((2, d), F32)] + far_of(low),
        scratch=near_of(x, ho, o2, cot, wout, wup, wdown, low, low, full, full, full, low, low)
        + [pltpu.VMEM((2, 2 * n, CHUNK), BF16)] * 2
        + [pltpu.SemaphoreType.DMA((64,))],
        vmem=60,
        name="mlp_second",
    )


def mlp_back_body(
    rows, seq, dy_far, h1_far, wout_far, gb_ref, d_far, wup_far, wdown_far,
    du_far, dh1_far, dp_far, do_far, sums_ref,
    dy_ref, h1_ref, wout_ref, wup_ref, wdown_ref, d_ref, dm_ref, dn_ref, dp_ref, do_ref, du_buf, sems,
):
    moves = Moves(sems)
    first = moves.whole(dy_far, dy_ref)
    ups, downs = Chunks(moves, wup_far, wup_ref, 1), Chunks(moves, wdown_far, wdown_ref, 0)
    ds, dus = Chunks(moves, d_far, d_ref, 1), Chunks(moves, du_far, du_buf, 1, True, True)
    number = wup_far.shape[1] // CHUNK
    for j in range(2):
        for chunks in (downs, ds, ups):
            chunks.start(j)
    then = [moves.later(*t) for t in ((wout_far, wout_ref), (h1_far, h1_ref))]
    first()
    dm_ref[...] = dy_ref[...].astype(BF16)
    dn_ref[...] = jnp.zeros_like(dn_ref)

    def step(j, _):
        for chunks in (downs, ds, ups):
            chunks.wait(j)

        @pl.when(j + 2 < number)
        def _():
            for chunks in (downs, ds, ups):
                chunks.start(j + 2)

        @pl.when(j + 2 == number)
        def _():
            for start, _ in then:
                start()

        @pl.when(j >= 2)
        def _():
            dus.wait(j - 2)

        dg = dot_nt(dm_ref[...], chunk_of(wdown_ref, j, 0)[...])
        du = (dg * chunk_of(d_ref, j, 1)[...].astype(F32)).astype(BF16)
        du_buf[j % 2] = du
        dus.start(j)
        dn_ref[...] += dot_nt(du, chunk_of(wup_ref, j, 1)[...])
        return 0

    lax.fori_loop(0, number, step, 0, unroll=2)
    for _, wait in then:
        wait()
    kept = after_norm_back(
        moves, seq, h1_ref, dn_ref, dy_ref, wout_ref, gb_ref, sums_ref, dp_ref, do_ref, dh1_far, dp_far, do_far
    )
    for wait in kept:
        wait()
    for j in range(number - 2, number):
        dus.wait(j)


def mlp_back(dy, h1, wout, gb, dgelu, wup, wdown, seq):
    n, d = dy.shape
    low = sds((n, d), BF16)
    return resident(
        functools.partial(mlp_back_body, n // seq, seq),
        far_of(dy, h1, wout) + [gb] + far_of(dgelu, wup, wdown),
        far_of(dgelu, h1, low, low) + [sds((2, d), F32)],
        scratch=near_of(dy, h1, wout, wup, wdown, dgelu, low, dy, low, low)
        + [pltpu.VMEM((2, n, CHUNK), BF16)]
        + [pltpu.SemaphoreType.DMA((48,))],
        vmem=48,
        name="mlp_back",
    )


def lanes_at(ref, start, size):
    return ref.at[:, pl.ds(pl.multiple_of(start, 128), size)]


def stack_rows(moves, pairs, target, start, size):
    copies, row = [], 0
    for far in pairs:
        copies.append(moves.later(lanes_at(far, start, size), target.at[pl.ds(row, far.shape[0])]))
        row += far.shape[0]
    return (lambda: [s() for s, _ in copies]), (lambda: [w() for _, w in copies])


def all_of(*parts):
    return (lambda: [s() for s, _ in parts]), (lambda: [w() for _, w in parts])


class InTurn:
    def __init__(self, *tiles):
        self.tiles, self.at = tiles, 0
        for start, _ in tiles[:2]:
            start()

    def next(self):
        self.tiles[self.at][1]()
        self.at += 1
        if self.at + 1 < len(self.tiles):
            self.tiles[self.at + 1][0]()


def place_of(quarter, y, me_ref):
    return quarter if y else 4 + (quarter ^ me_ref[1])


def packed(body, me, arrays, shape, scratch, flops, vmem, name):
    smem = pl.BlockSpec(memory_space=pltpu.SMEM)
    out = sds(shape, BF16)
    return resident(
        body,
        [(me, smem)] + far_of(*arrays),
        far_of(out, out),
        scratch=near_of(sds((2,) + shape, BF16)) + scratch + [pltpu.SemaphoreType.DMA((64,))],
        flops=flops,
        vmem=vmem,
        name=name,
    )


def grad_down_body(
    me_ref, g1_far, g2_far, dm1_far, dm2_far, keep_far, go_far, out_ref, dm_ref, g_ref, acc_ref, sems
):
    moves = Moves(sems)
    low, group = me_ref[0] % 4, (me_ref[0] // 4) % 2
    ring, n, b = g_ref.shape[0], g1_far.shape[0], g_ref.shape[2]
    order = [(side, y, h) for side in (1, 0) for y in range(2) for h in range(2)]
    tiles = []
    for i, (side, y, h) in enumerate(order):
        at = place_of(((me_ref[0] // 8) ^ side) * 2 + h, y, me_ref) * b
        near = g_ref.at[i % ring]
        tiles += [stack_rows(moves, (g1_far,), near, at, b), stack_rows(moves, (g2_far,), near.at[pl.ds(n, 2 * n)], at, b)]
    tiles[0] = all_of(tiles[0], stack_rows(moves, (dm1_far,), dm_ref, 0, dm1_far.shape[1]))
    tiles[1] = all_of(tiles[1], stack_rows(moves, (dm2_far,), dm_ref.at[pl.ds(n, 2 * n)], 0, dm1_far.shape[1]))
    loads = InTurn(*tiles)
    sent = []
    for i, (side, y, h) in enumerate(order):
        loads.next()
        acc = dot_tn(g_ref[i % ring, :n], dm_ref[:n])
        loads.next()
        acc += dot_tn(g_ref[i % ring, n:], dm_ref[n:])
        acc_ref[h] = acc.reshape(acc_ref.shape[1:])
        for s in range(4):
            out_ref[side, y, (h ^ group) * 4 + s] = acc_ref[h, s ^ low].astype(BF16)
        if h:
            sent.append(moves.whole(out_ref.at[side, y], (go_far if side else keep_far).at[y]))
    for wait in sent:
        wait()


def grad_down(me, g1, g2, dm1, dm2):
    n, d = dm1.shape
    ff = g1.shape[1]
    b = ff // 8
    return packed(
        grad_down_body,
        me,
        (g1, g2, dm1, dm2),
        (2, 8, b // 4, d),
        [
            pltpu.VMEM((3 * n, d), BF16),
            pltpu.VMEM((3, 3 * n, b), BF16),
            pltpu.VMEM((2, 4, b // 4, d), F32),
        ],
        2 * 3 * n * d * ff,
        40,
        "grad_down",
    )


CUT = 1024


def put_slots(out_ref, y, start, acc_ref, me_ref):
    stop = start + acc_ref.shape[2]
    for lanes, me in ((slice(start, min(stop, CUT)), me_ref[0]), (slice(max(start, CUT), stop), me_ref[2])):
        if lanes.start < lanes.stop:
            for s in range(16):
                block = acc_ref[s ^ me, :, lanes.start - start : lanes.stop - start]
                out_ref[s // 8, y, s % 8, :, lanes] = block.astype(BF16)


def grad_up_body(
    me_ref, n1_far, n2_far, du1_far, du2_far, dp1_far, dp2_far, o1_far, o2_far, keep_far, go_far,
    out_ref, n_ref, t_ref, du_ref, dp_ref, o_ref, acc_ref, acc2_ref, sems,
):
    moves = Moves(sems)
    d, f = n_ref.shape[1], o_ref.shape[2]
    ring, c = du_ref.shape[0], du_ref.shape[2]
    ready = stack_rows(moves, (n1_far, n2_far), n_ref, 0, d)
    tiles = [
        all_of(
            *[
                stack_rows(
                    moves,
                    (du1_far, du2_far),
                    lanes_at(du_ref.at[(2 * y + t) % ring], k * f, f),
                    place_of(2 * t + k, y, me_ref) * f,
                    f,
                )
                for k in range(2)
            ]
        )
        for y in range(2)
        for t in range(2)
    ]
    last = [stack_rows(moves, (dp1_far, dp2_far), dp_ref, 0, d)]
    last += [stack_rows(moves, (o1_far, o2_far), o_ref.at[y], (1 - y) * f, f) for y in range(2)]
    loads = InTurn(ready, tiles[0], tiles[1], all_of(*last), tiles[2], tiles[3])
    loads.next()
    t_ref[...] = n_ref[...].T
    sent = []
    for y in range(2):
        for t in range(2):
            loads.next()
            acc_ref[...] = dot(t_ref[...], du_ref[(2 * y + t) % ring]).reshape(acc_ref.shape)
            put_slots(out_ref, y, t * c, acc_ref, me_ref)
        if y == 0:
            loads.next()
        acc2_ref[...] = dot_tn(dp_ref[...], o_ref[y]).reshape(acc2_ref.shape)
        put_slots(out_ref, y, 2 * c, acc2_ref, me_ref)
        sent += [moves.whole(out_ref.at[i, y], far.at[y]) for i, far in enumerate((keep_far, go_far))]
    for wait in sent:
        wait()


def grad_up(me, n1, n2, du1, du2, dp1, dp2, o1, o2):
    n, d = n1.shape
    ff = du1.shape[1]
    f, c = o1.shape[1] // 2, ff // 4
    return packed(
        grad_up_body,
        me,
        (n1, n2, du1, du2, dp1, dp2, o1, o2),
        (2, 8, d // 16, 2 * c + f),
        [
            pltpu.VMEM((3 * n, d), BF16),
            pltpu.VMEM((d, 3 * n), BF16),
            pltpu.VMEM((3, 3 * n, c), BF16),
            pltpu.VMEM((3 * n, d), BF16),
            pltpu.VMEM((2, 3 * n, f), BF16),
            pltpu.VMEM((16, d // 16, c), F32),
            pltpu.VMEM((16, d // 16, f), F32),
        ],
        2 * 3 * n * d * (ff + d),
        56,
        "grad_up",
    )


def grad_qkv_body(me_ref, ae_far, ao_far, de_far, do_far, keep_far, go_far, out_ref, a_ref, t_ref, d_ref, acc_ref, sems):
    moves = Moves(sems)
    d = a_ref.shape[1]
    f = de_far.shape[2] // 2
    ready = stack_rows(moves, (ae_far, ao_far), a_ref, 0, d)
    tiles = [stack_rows(moves, (de_far.at[j], do_far.at[j]), d_ref.at[j], 0, 2 * f) for j in range(3)]
    loads = InTurn(ready, *tiles)
    loads.next()
    t_ref[...] = a_ref[...].T
    for j in range(3):
        loads.next()
        acc_ref[...] = dot(t_ref[...], d_ref[j]).reshape(acc_ref.shape)
        for s in range(16):
            block = acc_ref[s ^ me_ref[0]].astype(BF16)
            lanes = slice(j * f, (j + 1) * f)
            out_ref[s // 8, 1, s % 8, :, lanes] = block[:, :f]
            out_ref[s // 8, 0, s % 8, :, lanes] = block[:, f:]
    sent = [moves.whole(out_ref.at[i], far) for i, far in ((1, go_far), (0, keep_far))]
    for wait in sent:
        wait()


def grad_qkv(me, ae, ao, dqkv_e, dqkv_o):
    n, d = ae.shape
    f = dqkv_e.shape[2] // 2
    return packed(
        grad_qkv_body,
        me,
        (ae, ao, dqkv_e, dqkv_o),
        (2, 8, d // 16, 3 * f),
        [
            pltpu.VMEM((2 * n, d), BF16),
            pltpu.VMEM((d, 2 * n), BF16),
            pltpu.VMEM((3, 2 * n, 2 * f), BF16),
            pltpu.VMEM((16, d // 16, 2 * f), F32),
        ],
        2 * 2 * 3 * n * d * 2 * f,
        40,
        "grad_qkv",
    )


def packed_call(body, grid, me, ins, outs, scratch=(), flops=0, aliases={}, name=None):
    return pl.pallas_call(
        body,
        grid_spec=pltpu.PrefetchScalarGridSpec(
            num_scalar_prefetch=1,
            grid=grid,
            in_specs=[s for _, s in ins],
            out_specs=[s for _, s in outs],
            scratch_shapes=scratch,
        ),
        out_shape=[a for a, _ in outs],
        input_output_aliases=aliases,
        compiler_params=pltpu.CompilerParams(
            dimension_semantics=("arbitrary",) * len(grid), vmem_limit_bytes=VMEM_LIMIT
        ),
        cost_estimate=pl.CostEstimate(flops=int(flops) // 16, bytes_accessed=0, transcendentals=0),
        name=name,
    )(me, *[a for a, _ in ins])


def unpack_body(kind, me_ref, part_ref, *refs):
    low = me_ref[0] % 8
    rows, width = part_ref.shape[1:]
    first = refs[-2] if kind == "up" else refs[-1]
    if kind == "up":
        first, second, wide = refs[-3:]
    for s in range(8):
        sl = slice(s * rows, (s + 1) * rows)
        if kind == "down":
            first[sl] = part_ref[s ^ low].astype(F32)
        elif kind == "up":
            f = first.shape[1]
            other = s ^ (me_ref[2] % 8)
            first[sl, :CUT] = part_ref[s ^ low, :, :CUT].astype(F32)
            first[sl, CUT:] = part_ref[other, :, CUT:f].astype(F32)
            wide[sl] = part_ref[other, :, f:].astype(F32)
        else:
            f = width // 3
            for j in range(3):
                first[j, sl] = part_ref[s ^ low, :, j * f : (j + 1) * f].astype(F32)
    if kind == "up":
        second[...] = wide[...].T


def unpack(kind, me, side, part, into=()):
    _, r, w = part.shape
    half = 8 * r
    at = lambda me: (me[0] // 8) ^ side
    scratch = []
    if kind == "down":
        outs = [(sds((2 * half, w), F32), pl.BlockSpec((half, w), lambda i, me: (at(me), 0)))]
    elif kind == "up":
        f = half
        outs = [
            (sds((2 * half, w - f), F32), pl.BlockSpec((half, w - f), lambda i, me: (at(me), 0))),
            (sds((f, 2 * half), F32), pl.BlockSpec((f, half), lambda i, me: (0, at(me)))),
        ]
        scratch = [pltpu.VMEM((half, f), F32)]
    else:
        f = w // 3
        outs = [(sds((3, 2 * half, f), F32), pl.BlockSpec((3, half, f), lambda i, me: (0, at(me), 0)))]
    ins = [(part, pl.BlockSpec(part.shape, lambda i, me: (0, 0, 0)))]
    ins += [(t, pl.BlockSpec(memory_space=pl.ANY)) for t in into]
    return packed_call(
        functools.partial(unpack_body, kind),
        (1,),
        me,
        ins,
        outs,
        scratch=scratch,
        aliases={2 + i: i for i in range(len(into))},
        name="unpack_" + kind,
    )


def fold(*parts):
    return sum(p.astype(F32) for p in parts).astype(BF16)


def after(value, *first):
    return lax.optimization_barrier((value, first))[0]


class Chunk:
    def __init__(self, keep, got):
        self.keep, self.got = keep, got
        self.sent = None

    def wait(self, *also):
        self.got, also = lax.optimization_barrier((self.got, also))
        return also

    def to_partner(self):
        total = fold(self.keep, self.got)
        self.keep, self.sent = total[1], total[0]
        self.got = lax.ppermute(self.sent, "tensor", FLIP)

    def gather_core(self):
        self.got = lax.ppermute(self.keep, "core", FLIP)


class Hops(Chunk):
    def __init__(self, outer, keep, got):
        super().__init__(keep, got)
        self.axes = {"x": ("x", 2, 1), "z": ("o", outer, 1), "w": ("o", outer, 2)}
        self.extra = [("o", outer, 1 << b) for b in range(2, outer.bit_length() - 1)]

    def send(self, *parts):
        self.keep, self.sent, self.got = [], [], []
        for total, way in parts:
            if way == "partner":
                keep, sent = total[1], total[0]
                got = lax.ppermute(sent, "tensor", FLIP)
            else:
                half = total.shape[-3] // 2
                keep, sent = total[..., :half, :, :], total[..., half:, :, :]
                got = flip_bit(sent, *self.axes[way])
            self.keep.append(keep)
            self.sent.append(sent)
            self.got.append(got)

    def folded(self):
        return [fold(k, g) for k, g in zip(self.keep, self.got)]

    def first(self):
        total = fold(self.keep, self.got)
        self.send((total[..., :CUT], "x"), (total[..., CUT:], "z"))

    def hop(self, *ways):
        self.send(*zip(self.folded(), ways))

    def first_hop(self, way):
        self.send((fold(self.keep, self.got), way))

    def last_hop(self):
        self.send((jnp.concatenate(self.folded(), axis=-1), "w"))

    def back(self, *ways):
        self.sent = self.keep
        self.got = [flip_bit(k, *self.axes[w]) for k, w in zip(self.keep, ways)]

    def back_first(self):
        (total,) = self.folded()
        for s in self.extra:
            total = fold(total, flip_bit(total, *s))
        self.keep = [total]
        self.back("w")

    def joined(self, parts=1):
        self.keep = [jnp.concatenate([k, g], axis=0) for k, g in zip(self.keep, self.got)]
        if parts == 2:
            (total,) = self.keep
            self.keep = [total[..., :CUT], total[..., CUT:]]

    def back_core(self):
        self.joined()
        self.keep = self.sent = jnp.concatenate(self.keep, axis=-1)
        self.gather_core()


def mask_biases(seg):
    seq = seg.shape[1]
    place = jnp.arange(seq, dtype=jnp.int32)
    same = seg[:, :, None] == seg[:, None, :]
    below = (place[:, None] < place[None, :])[None]
    incl = (place[:, None] <= place[None, :])[None]
    bias = lambda m: jnp.where(same & m, 0.0, NEG).astype(F32)
    return bias(incl), bias(below)


def sync(*values):
    return lax.optimization_barrier(values)


class Link:
    def __init__(self, outer, w_qkv, w_out, w_up, w_down):
        self.outer = outer
        self.own = (w_qkv, w_out, w_up, w_down)
        self.core_at, self.x_at, o = (lax.axis_index(a) for a in ("core", "x", "o"))
        bits = {"x": self.x_at, "z": o % 2, "w": (o // 2) % 2}
        self.fetch_bits = self.core_at * 2 + self.x_at
        slots = []
        for order in ("xzw", "zxw"):
            slot = self.core_at
            for name in order:
                slot = slot * 2 + bits[name]
            slots.append(slot)
        self.me = jnp.stack([slots[0], self.fetch_bits, slots[1]]).astype(jnp.int32)
        self.me_z = self.me[2:0:-1]

    def quarter(self, own):
        flat = own.reshape(-1, own.shape[-1])
        return take_half(take_half(flat, self.core_at), self.x_at)

    def over_x(self, t):
        return lax.ppermute(t, "x", FLIP)

    def fetch(self, own_work):
        own = self.own
        size = own[2].shape[1] // 4
        part = lambda t, axis, bits: lax.dynamic_slice_in_dim(t, bits * size, size, axis)
        pieces = [
            self.quarter(own[1]),
            part(own[2], 1, self.fetch_bits),
            jnp.concatenate([part(own[3], 0, self.fetch_bits), part(own[3], 0, self.fetch_bits ^ 1)], axis=0),
        ]
        qkv = self.partner(self.quarter(own[0]))
        up, out, down = (self.partner(pieces[i]) for i in (1, 0, 2))
        qkv, own_work = sync(qkv, own_work)
        qkv, out, up = sync(ordered(self.x_at, qkv, self.over_x(qkv)).reshape(-1, qkv.shape[-1]), out, up)
        qkv_core, out_x, up_x = self.core(qkv), self.over_x(out), self.over_x(up)
        qkv = ordered(self.core_at, qkv, qkv_core).reshape(own[0].shape)

        def rest(*work):
            nonlocal out, up, out_x, up_x, down
            work, out, up, out_x, up_x = lax.optimization_barrier((work, out, up, out_x, up_x))
            ups = jnp.concatenate([up, up_x], axis=1)
            ups_core = self.core(ups)
            out = ordered(self.x_at, out, out_x).reshape(-1, out.shape[-1])
            out = ordered(self.core_at, out, self.core(out)).reshape(own[1].shape)
            wout = jnp.concatenate([own[1], out], axis=0)
            wup = jnp.concatenate([own[2], ups, ups_core], axis=1)
            down = after(down, wout, wup)
            wdown = jnp.concatenate([own[3], down, self.core(down)], axis=0)
            return work, wout, wup, wdown

        return own_work, own[0], qkv, jnp.concatenate([own[0], qkv], axis=2), rest

    def partner(self, t):
        return lax.ppermute(t, "tensor", FLIP)

    def core(self, t):
        return lax.ppermute(t, "core", FLIP)

    def chunk(self, keep, got):
        return Chunk(keep, got)

    def hops(self, keep, got):
        return Hops(self.outer, keep, got)

    def small_steps(self):
        return [("core", 2, 1), ("tensor", 2, 1)] + steps_of(self.outer)

    def flip(self, t, step):
        return flip_bit(t, *step)


def local_part(x, seg, cot, gb, link):
    rows, seq = seg.shape
    n, width = x.shape
    me, me_z = link.me, link.me_z
    incl, strict = mask_biases(seg)
    normal, _ = norm_stats(x.astype(F32))
    a_e = (normal * gb[0] + gb[2]).astype(BF16)
    first = attend_first(a_e, link.own[0], incl)
    (a_e, first), wq_own, fetched, wqkv, rest = link.fetch((a_e, first))
    second = attend_first(a_e, fetched, incl)
    qkv_e, o1 = (jnp.concatenate([s, t], axis=-1) for s, t in zip(first[:2], second[:2]))
    lse1 = jnp.concatenate([first[2], second[2]], axis=0).reshape(-1, GROUP // HD, n)
    (qkv_e, o1, lse1, wqkv), wout, wup, wdown = rest(qkv_e, o1, lse1, wqkv)
    h1, n2_1, g1, d1, ho, a_o = mlp_first(x, o1, wout, gb, wup, wdown)
    qkv_o, o2, lse2 = attend_second(a_o, wqkv, incl, strict, qkv_e, o1, lse1)
    out, n2_2, g2, du2, dh1_2, dp2, do2, sums2, dm2 = mlp_second(x, ho, o2, cot, wout, gb, wup, wdown, seq)
    out_got = link.partner(out[: rows // 2])
    dqkv_o, part, dy, sums_o = attend_back(wqkv, incl, strict, qkv_e, qkv_o, o2, lse2, do2, dh1_2, ho, gb)
    o2_flat = o2.reshape(2 * n, width)

    dm1 = dy.astype(BF16)
    out_got, dm1 = sync(out_got, dm1)
    out_last = link.partner(after(out[rows // 2 :], out_got))
    down_keep, down_go = grad_down(me_z, g1, g2, dm1, dm2)
    down_keep, down_go, out_last = sync(down_keep, down_go, out_last)
    down = link.hops(down_keep, link.core(down_go))
    dy = after(dy, down_go)
    du1, dh1_1, dp1, do1, sums1 = mlp_back(dy, h1, wout, gb, d1, wup, wdown, seq)
    du1, dp1, do1 = down.wait(du1, dp1, do1)
    down.to_partner()
    up_keep, up_go = grad_up(me, n2_1, n2_2, after(du1, down.sent), du2, dp1, dp2, o1, o2_flat)
    do1 = after(do1, up_go)
    dqkv_e, gt, sums_e = attend_back_even(wqkv, incl, qkv_e, o1, lse1, do1, o2, lse2, do2, part, dh1_1, dh1_2, x, gb)
    dqkv_e, gt, sums_e, up_go = down.wait(dqkv_e, gt, sums_e, up_go)
    up = link.hops(up_keep, link.core(up_go))
    down.first_hop("z")
    small = jnp.stack([sums_e[0] + sums_o[0], sums1[0] + sums2[0], sums_e[1] + sums_o[1], sums1[1] + sums2[1], sums_o[2]])
    qkv_keep, qkv_go = grad_qkv(me_z, a_e, a_o, after(dqkv_e, *down.sent), dqkv_o)
    qkv_keep, qkv_go, down.got = up.wait(qkv_keep, qkv_go, down.got)
    qkv = link.hops(qkv_keep, link.core(qkv_go))
    small_steps = iter(link.small_steps())
    small_got = link.flip(after(small, qkv_go), next(small_steps))

    def wait_all(with_down=True):
        nonlocal small, small_got
        (qkv.got, small_got, *rest) = up.wait(qkv.got, small_got, *([down.got] if with_down else []))
        if rest:
            (down.got,) = rest
        if small_got is not None:
            small = small + small_got
            step = next(small_steps, None)
            small_got = None if step is None else link.flip(small, step)

    wait_all(False)
    up.first()
    qkv.first_hop("partner")
    down.hop("x")
    wait_all()
    up.hop("partner", "x")
    qkv.hop("z")
    down.hop("w")
    wait_all()
    up.hop("z", "partner")
    qkv.hop("x")
    down.back_first()
    half = gt.shape[0] // 2
    gt_got = [link.partner(after(gt[:half], *up.sent))]
    wait_all()
    up.last_hop()
    qkv.hop("w")
    down.joined()
    down.back("x")
    gt_got.append(link.partner(after(gt[half:], *up.sent)))
    (gt_got[0],) = up.wait(gt_got[0])
    wait_all()
    up.back_first()
    qkv.back_first()
    down.joined()
    down.back("z")
    (gt_got[1],) = up.wait(gt_got[1])
    wait_all()
    while small_got is not None:
        wait_all()
    up.joined(2)
    up.back("z", "x")
    qkv.joined()
    qkv.back("x")
    down.back_core()
    out, gt, *_ = link.finish(out, jnp.concatenate([out_got, out_last], axis=0), gt, jnp.concatenate(gt_got, axis=0))
    out, gt = up.wait(out, gt)
    wait_all()
    up.joined()
    up.back("x", "z")
    qkv.joined()
    qkv.back("z")
    (g_down,) = unpack("down", me_z, 0, after(down.keep, up.sent, qkv.sent))
    (g_down,) = unpack("down", me_z, 1, down.got, (g_down,))
    g_down, qkv.got = up.wait(g_down, qkv.got)
    up.back_core()
    qkv.back_core()
    g_up = unpack("up", me, 0, after(up.keep, qkv.sent))
    (g_qkv,) = unpack("qkv", me_z, 0, after(qkv.keep, g_up))
    (g_qkv,) = up.wait(g_qkv)
    g_up, g_out = unpack("up", me, 1, up.got, g_up)
    qkv.wait(g_up)
    (g_qkv,) = unpack("qkv", me_z, 1, qkv.got, (g_qkv,))
    return out, gt, (g_qkv, g_out, g_up, g_down), small


def shards(outer, tokens, segments, pass_embed, w_qkv, w_out, w_up, w_down, gain, bias, cotangent):
    ty = lax.axis_index("tensor")
    rows = tokens.shape[0] // 2
    width = tokens.shape[2]
    mine = lambda t: lax.dynamic_slice_in_dim(t, ty * rows, rows, 0)
    x = mine(tokens).reshape(-1, width)
    gb = jnp.concatenate([gain, bias, pass_embed[None]], axis=0)
    link = Link(outer, w_qkv, w_out, w_up, w_down)
    link.finish = lambda out, out_got, gt, gt_got: (
        ordered(ty, out, out_got).reshape(cotangent.shape),
        ordered(ty, gt, gt_got).reshape(tokens.shape).astype(F32),
    )
    out, gt, grads, small = local_part(x, mine(segments), mine(cotangent), gb, link)
    return out, gt, *grads, small[0:2], small[2:4], small[4]


def solution(mesh):
    outer = mesh.shape["dp"] // 4
    fine = Mesh(mesh.devices.reshape(outer, 2, 2, mesh.shape["tensor"]), ("o", "x", "core", "tensor"))
    rows = ROWS_OVER
    placed = (
        P(rows, None, None),
        P(rows, None),
        P(),
        P(None, None, "tensor"),
        P("tensor", None),
        P(None, "tensor"),
        P("tensor", None),
        P(),
        P(),
        P(rows, None, None),
    )

    def body(*args):
        return shards(outer, *args)

    return jax.shard_map(
        body,
        mesh=fine,
        in_specs=placed,
        out_specs=(
            P(rows, None, None),
            P(rows, None, None),
            P(None, None, "tensor"),
            P("tensor", None),
            P(None, "tensor"),
            P("tensor", None),
            P(),
            P(),
            P(),
        ),
        check_vma=False,
    )
```

```python
import functools

import jax
import jax.numpy as jnp
from jax import lax
from jax.experimental import pallas as pl
from jax.experimental.pallas import tpu as pltpu
from jax.sharding import Mesh
from jax.sharding import PartitionSpec as P

HD = 64
EPS = 1e-05
NEG = -1000000000.0
F32 = jnp.float32
BF16 = jnp.bfloat16
ROWS_OVER = ("o", "x", "core")
FLIP = ((0, 1), (1, 0))
VMEM_LIMIT = 60 * 1024 * 1024


def ordered(flag, mine, theirs):
    first = flag == 0
    return jnp.stack([jnp.where(first, mine, theirs), jnp.where(first, theirs, mine)])


def take_half(array, index):
    half = array.shape[0] // 2
    return lax.dynamic_slice_in_dim(array, index * half, half, 0)


def flip_bit(array, axis, size, bit):
    return lax.ppermute(array, axis, [(i, i ^ bit) for i in range(size)])


def steps_of(outer):
    steps = [("x", 2, 1)]
    bit = 1
    while bit < outer:
        steps.append(("o", outer, bit))
        bit *= 2
    return steps


def my_bit(axis, bit):
    return (lax.axis_index(axis) // bit) % 2


def dot(a, b):
    return lax.dot_general(a, b, (((1,), (0,)), ((), ())), preferred_element_type=F32)


def dot_nt(a, b):
    return lax.dot_general(a, b, (((1,), (1,)), ((), ())), preferred_element_type=F32)


def dot_tn(a, b):
    return lax.dot_general(a, b, (((0,), (0,)), ((), ())), preferred_element_type=F32)


def norm_stats(h):
    centred = h - jnp.mean(h, axis=-1, keepdims=True)
    inverse = lax.rsqrt(jnp.mean(centred * centred, axis=-1, keepdims=True) + EPS)
    return centred * inverse, inverse


def norm_back(grad, normal, inverse, gain):
    scaled = grad * gain
    centre = jnp.mean(scaled, axis=-1, keepdims=True)
    proj = jnp.mean(scaled * normal, axis=-1, keepdims=True)
    return inverse * (scaled - centre - normal * proj)


def gelu_parts(u):
    c = 0.7978845608028654
    a = 0.044715 * c
    square = u * u
    half = 0.5 + 0.5 * jnp.tanh(u * (c + a * square))
    g = u * half
    return g, half + g * (1.0 - half) * (2.0 * c + 6.0 * a * square)


def whole(shape):
    return pl.BlockSpec(shape, lambda *_: (0,) * len(shape))


def call(body, grid, ins, outs, scratch=(), cost=(0, 0), name=None, vmem=VMEM_LIMIT):
    return pl.pallas_call(
        body,
        grid=grid,
        in_specs=[s for _, s in ins],
        out_specs=[s for _, s in outs],
        out_shape=[a for a, _ in outs],
        scratch_shapes=scratch,
        compiler_params=pltpu.CompilerParams(
            dimension_semantics=("arbitrary",) * len(grid), vmem_limit_bytes=vmem
        ),
        cost_estimate=pl.CostEstimate(
            flops=int(cost[0]) // 16, bytes_accessed=int(cost[1]), transcendentals=0
        ),
        name=name,
    )(*[a for a, _ in ins])


FAR = pl.BlockSpec(memory_space=pl.ANY)


def resident(body, ins, outs, scratch=(), flops=0, vmem=16, aliases={}, name=None):
    spec = pl.BlockSpec(memory_space=pltpu.VMEM)
    ins, outs = ([o if isinstance(o, tuple) else (o, spec) for o in t] for t in (ins, outs))
    ins = [(pltpu.with_memory_space_constraint(a, pltpu.HBM) if s is FAR else a, s) for a, s in ins]
    outs = [(pltpu.HBM(a.shape, a.dtype) if s is FAR else a, s) for a, s in outs]
    return pl.pallas_call(
        body,
        in_specs=[s for _, s in ins],
        out_specs=[s for _, s in outs],
        out_shape=[a for a, _ in outs],
        scratch_shapes=scratch,
        input_output_aliases=aliases,
        compiler_params=pltpu.CompilerParams(vmem_limit_bytes=vmem * 1024 * 1024),
        cost_estimate=pl.CostEstimate(flops=int(flops) // 16, bytes_accessed=0, transcendentals=0),
        name=name,
    )(*[a for a, _ in ins])


def sds(shape, dtype):
    return jax.ShapeDtypeStruct(shape, dtype)


QB = 128
GROUP = 256


def lanes_of(ref, g):
    return ref.at[(slice(None),) * (len(ref.shape) - 1) + (pl.ds(pl.multiple_of(g * GROUP, GROUP), GROUP),)]


class Moves:
    def __init__(self, sems):
        self.sems, self.used = sems, 0

    def take(self, number):
        self.used += number
        return self.used - number

    def whole(self, source, target):
        copy = pltpu.make_async_copy(source, target, self.sems.at[self.take(1)])
        copy.start()
        return copy.wait

    def later(self, source, target):
        sem = self.sems.at[self.take(1)]
        copy = lambda: pltpu.make_async_copy(source, target, sem)
        return (lambda: copy().start()), (lambda: copy().wait())

    def groups(self, source, target):
        first = self.take(source.shape[-1] // GROUP)

        def copy(g):
            return pltpu.make_async_copy(lanes_of(source, g), lanes_of(target, g), self.sems.at[first + g])

        return (lambda g: copy(g).start()), (lambda g: copy(g).wait())


def cat_heads(t, scale=1.0):
    lane = lax.broadcasted_iota(jnp.int32, (1, 2 * HD), 1)
    parts = [t * jnp.where((lane < HD) == (h == 0), scale, 0.0).astype(t.dtype) for h in range(2)]
    return jnp.concatenate(parts, axis=0)


def own_lanes(t, scale=None):
    if scale is not None:
        t = t * scale
    return jnp.concatenate([t[:HD, :QB], t[HD:, QB:]], axis=0)


def twice(t):
    return jnp.concatenate([t, t], axis=1)


def pair_row(rows, p):
    return jnp.concatenate([rows[2 * p : 2 * p + 1], rows[2 * p + 1 : 2 * p + 2]], axis=1)


def put_pair(ref, p, cols, value):
    ref[2 * p : 2 * p + 1, cols] = value[:, :QB]
    ref[2 * p + 1 : 2 * p + 2, cols] = value[:, QB:]


def columns(t, r, seq, qb):
    return t[:, pl.ds(pl.multiple_of(r * seq + qb * QB, QB), QB)]


def rows_of(r, seq, qb):
    return pl.ds(pl.multiple_of(r * seq + qb * QB, QB), QB)


def in_turn(arrive, group, groups):
    for _, wait in arrive:
        wait(group)

    @pl.when(group + 2 < groups)
    def _():
        for start, _ in arrive:
            start(group + 2)


def attend_first_body(rows, seq, pairs, a_ref, w_ref, bias_ref, qkv_ref, o_ref, lse_ref):
    a = a_ref[...]
    for j in range(3):
        qkv_ref[j] = dot(a, w_ref[j]).astype(BF16)
    for r in range(rows):
        work = []
        for p in range(pairs):
            ln = slice(p * 2 * HD, (p + 1) * 2 * HD)
            k = qkv_ref[1, r * seq : (r + 1) * seq, ln]
            for b in range(seq // QB):
                sl, n = slice(r * seq + b * QB, r * seq + (b + 1) * QB), (b + 1) * QB
                q = cat_heads(qkv_ref[0, sl, ln], HD**-0.5)
                s = dot_nt(k[:n], q) + twice(bias_ref[r, :n, b * QB : n])
                work.append((p, ln, sl, n, s))
        done = []
        for p, ln, sl, n, s in work:
            top = jnp.max(s, axis=0, keepdims=True)
            e = jnp.exp(s - top)
            mass = jnp.sum(e, axis=0, keepdims=True)
            put_pair(lse_ref, p, sl, top + jnp.log(mass))
            done.append((e.astype(BF16), 1.0 / mass))
        for (p, ln, sl, n, _), (e, inv) in zip(work, done):
            vt = qkv_ref[2, r * seq : (r + 1) * seq, ln].T
            o_ref[sl, ln] = own_lanes(dot(vt[:, :n], e), inv).T.astype(BF16)


def attend_first(a, w, bias):
    rows, seq = bias.shape[0], bias.shape[1]
    n, d = a.shape
    f = w.shape[2]
    return resident(
        functools.partial(attend_first_body, rows, seq, f // (2 * HD)),
        (a, w, bias),
        [sds((3, n, f), BF16), sds((n, f), BF16), sds((f // HD, n), F32)],
        flops=6 * n * d * f + 16 * n * seq * f,
        name="attend_first",
    )


def attend_second_body(
    rows, seq, a_far, w_far, incl_far, strict_far, qkve_far, o1_far, lse1_ref,
    qkvo_far, o2_far, lse2_ref,
    a_ref, w_ref, incl_ref, strict_ref, qkve_ref, o1_ref, qkvo_ref, o2_ref, sems,
):
    groups = lse1_ref.shape[0]
    moves = Moves(sems)
    ready = [moves.whole(a_far, a_ref), moves.whole(w_far.at[0], w_ref.at[0])]
    arrive = [moves.groups(*t) for t in ((qkve_far, qkve_ref), (o1_far, o1_ref))]
    leave = moves.groups(o2_ref, o2_far)
    for wait in ready:
        wait()
    ready = [moves.whole(w_far.at[j], w_ref.at[j]) for j in (1, 2)]
    a = a_ref[...]
    sent = []
    for j in range(3):
        if j:
            ready[j - 1]()
        if j == 1:
            masks = [moves.whole(*t) for t in ((incl_far, incl_ref), (strict_far, strict_ref))]
            for g in range(2):
                for start, _ in arrive:
                    start(g)
        qkvo_ref[j] = dot(a, w_ref[j]).astype(BF16)
        sent.append(moves.whole(qkvo_ref.at[j], qkvo_far.at[j]))
    for wait in masks:
        wait()

    def next_group(group):
        in_turn(arrive, group, groups)

    def row(i, _):
        r, group = i % rows, i // rows
        lanes = pl.multiple_of(group * GROUP, GROUP)
        all_of = pl.ds(pl.multiple_of(r * seq, seq), seq)

        @pl.when(r == 0)
        def _():
            next_group(group)

        for p in range(GROUP // (2 * HD)):
            ln = pl.ds(lanes + p * 2 * HD, 2 * HD)
            ke, ko = qkve_ref[1, all_of, ln], qkvo_ref[1, all_of, ln]
            vte, vto = qkve_ref[2, all_of, ln].T, qkvo_ref[2, all_of, ln].T
            work = []
            for b in range(seq // QB):
                sl, n = rows_of(r, seq, b), (b + 1) * QB
                cols = slice(b * QB, n)
                incl, strict = twice(incl_ref[r, :n, cols]), twice(strict_ref[r, :n, cols])
                q = cat_heads(qkve_ref[0, sl, ln], HD**-0.5)
                work.append([dot_nt(ko[:n], q) + strict])
                q = cat_heads(qkvo_ref[0, sl, ln], HD**-0.5)
                work.append([dot_nt(ko[:n], q) + incl, dot_nt(ke[:n], q) + incl])
            for b in range(seq // QB):
                sl, n = rows_of(r, seq, b), (b + 1) * QB
                (s,), (so, se) = work[2 * b : 2 * b + 2]
                old = pair_row(lse1_ref[group, :, sl], p)
                top = jnp.maximum(old, jnp.max(s, axis=0, keepdims=True))
                e = jnp.exp(s - top)
                kept = jnp.exp(old - top)
                mass = kept + jnp.sum(e, axis=0, keepdims=True)
                work[2 * b] = (e.astype(BF16), kept, 1.0 / mass)
                put_pair(lse2_ref.at[0, group], p, sl, top + jnp.log(mass))
                top = jnp.max(jnp.maximum(se, so), axis=0, keepdims=True)
                ee, eo = jnp.exp(se - top), jnp.exp(so - top)
                mass = jnp.sum(ee + eo, axis=0, keepdims=True)
                work[2 * b + 1] = (ee.astype(BF16), eo.astype(BF16), 1.0 / mass)
                put_pair(lse2_ref.at[1, group], p, sl, top + jnp.log(mass))
            for b in range(seq // QB):
                sl, n = rows_of(r, seq, b), (b + 1) * QB
                (e, kept, inv), (ee, eo, inv2) = work[2 * b : 2 * b + 2]
                o1 = o1_ref[sl, ln].astype(F32).T
                o = own_lanes(dot(vto[:, :n], e), inv) + own_lanes(twice(o1), kept * inv)
                o2_ref[0, sl, ln] = o.T.astype(BF16)
                o = dot(vte[:, :n], ee) + dot(vto[:, :n], eo)
                o2_ref[1, sl, ln] = own_lanes(o, inv2).T.astype(BF16)

        @pl.when(r == rows - 1)
        def _():
            leave[0](group)

        return 0

    lax.fori_loop(0, rows * groups, row, 0)
    for wait in sent:
        wait()
    for g in range(groups):
        leave[1](g)


def attend_second(a, w, incl, strict, qkve, o1, lse1):
    rows, seq = incl.shape[0], incl.shape[1]
    n, d = a.shape
    f = w.shape[2]
    qkv, o2 = sds((3, n, f), BF16), sds((2, n, f), BF16)
    near = (a, w, incl, strict, qkve, o1, qkv, o2)
    return resident(
        functools.partial(attend_second_body, rows, seq),
        [(t, FAR) for t in (a, w, incl, strict, qkve, o1)] + [lse1],
        [(qkv, FAR), (o2, FAR), sds((2, *lse1.shape), F32)],
        scratch=[pltpu.VMEM(t.shape, t.dtype) for t in near] + [pltpu.SemaphoreType.DMA((32,))],
        flops=6 * n * d * f + 48 * n * seq * f,
        vmem=32,
        name="attend_second",
    )


def row_products(a, b):
    prod = cat_heads((a * b).astype(BF16))
    return dot_nt(jnp.ones((8, 2 * HD), BF16), prod)[:1]


def query_parts(sl, ln, group, p, i, qkv_ref, o_ref, lse_ref, do_ref):
    do = do_ref[i, sl, ln]
    delta = row_products(do.astype(F32), o_ref[i, sl, ln].astype(F32))
    return cat_heads(qkv_ref[0, sl, ln], HD**-0.5), cat_heads(do), pair_row(lse_ref[i, group, :, sl], p), delta


def blocks_back(tasks):
    scores = [dot_nt(k, q) + bias - lse for k, _, _, bias, q, _, lse, _ in tasks]
    moved = [dot_nt(v, do) - delta for _, v, _, _, _, do, _, delta in tasks]
    probs = [jnp.exp(s) for s in scores]
    ds = [(p * m).astype(BF16) for p, m in zip(probs, moved)]
    return [
        (dot(p.astype(BF16), do), dot(d, q), dot(kt, d))
        for (_, _, kt, _, q, do, _, _), p, d in zip(tasks, probs, ds)
    ]


def add_rows(total, part):
    if total is None:
        return part
    n = part.shape[0]
    return jnp.concatenate([total[:n] + part, total[n:]], axis=0)


def attend_back_body(
    rows, seq, w_far, incl_far, strict_far, qkve_far, qkvo_far, o2_far, lse2_ref, do_far,
    dh1_far, ho_far, gb_ref,
    dqkvo_far, dqkve_far, dy_far, sums_ref,
    w_ref, incl_ref, strict_ref, qkve_ref, qkvo_ref, o2_ref, do_ref, dh1_ref, ho_ref,
    dqkvo_ref, dqkve_ref, da_ref, dy_ref, sems,
):
    groups = lse2_ref.shape[1]
    moves = Moves(sems)
    arrive = [
        moves.groups(*t)
        for t in ((qkve_far, qkve_ref), (qkvo_far, qkvo_ref), (o2_far, o2_ref), (do_far, do_ref))
    ]
    leave = [moves.groups(*t) for t in ((dqkvo_ref, dqkvo_far), (dqkve_ref, dqkve_far))]
    for start, _ in arrive:
        start(0)
    masks = [moves.whole(*t) for t in ((incl_far, incl_ref), (strict_far, strict_ref))]
    for start, _ in arrive:
        start(1)
    odd = pl.ds(rows * seq, rows * seq)
    late = [moves.later(*t) for t in ((w_far, w_ref), (dh1_far.at[odd], dh1_ref), (ho_far, ho_ref))]
    for wait in masks:
        wait()

    def next_group(group):
        in_turn(arrive, group, groups)

        @pl.when(group == groups - 2)
        def _():
            for start, _ in late:
                start()

    sc = HD**-0.5

    def row(i, _):
        r, group = i % rows, i // rows
        lanes = pl.multiple_of(group * GROUP, GROUP)
        all_of = pl.ds(pl.multiple_of(r * seq, seq), seq)

        @pl.when(r == 0)
        def _():
            next_group(group)

        for p in range(GROUP // (2 * HD)):
            ln = pl.ds(lanes + p * 2 * HD, 2 * HD)
            ke, ve = qkve_ref[1, all_of, ln], qkve_ref[2, all_of, ln]
            ko, vo = qkvo_ref[1, all_of, ln], qkvo_ref[2, all_of, ln]
            kte, kto = ke.T, ko.T
            tasks = []
            for b in reversed(range(seq // QB)):
                sl, n = rows_of(r, seq, b), (b + 1) * QB
                cols = slice(b * QB, n)
                incl, strict = twice(incl_ref[r, :n, cols]), twice(strict_ref[r, :n, cols])
                even = query_parts(sl, ln, group, p, 0, qkve_ref, o2_ref, lse2_ref, do_ref)
                odd = query_parts(sl, ln, group, p, 1, qkvo_ref, o2_ref, lse2_ref, do_ref)
                tasks.append((ko[:n], vo[:n], kto[:, :n], strict, *even))
                tasks.append((ko[:n], vo[:n], kto[:, :n], incl, *odd))
                tasks.append((ke[:n], ve[:n], kte[:, :n], incl, *odd))
            done = blocks_back(tasks)
            dke = dve = dko = dvo = None
            for b in reversed(range(seq // QB)):
                sl = rows_of(r, seq, b)
                (dv, dk, dqe), (dv2, dk2, dqo), (dv3, dk3, dqo2) = done[:3]
                done = done[3:]
                dvo, dko = add_rows(dvo, dv + dv2), add_rows(dko, dk + dk2)
                dve, dke = add_rows(dve, dv3), add_rows(dke, dk3)
                dqkve_ref[0, sl, ln] = (own_lanes(dqe).T * sc).astype(BF16)
                dqkvo_ref[0, sl, ln] = (own_lanes(dqo + dqo2).T * sc).astype(BF16)
            dqkve_ref[1, all_of, ln] = dke.astype(BF16)
            dqkve_ref[2, all_of, ln] = dve.astype(BF16)
            dqkvo_ref[1, all_of, ln] = dko.astype(BF16)
            dqkvo_ref[2, all_of, ln] = dvo.astype(BF16)

        @pl.when(r == rows - 1)
        def _():
            for start, _ in leave:
                start(group)

        return 0

    lax.fori_loop(0, rows * groups, row, 0)
    for _, wait in late:
        wait()
    da = dot_nt(dqkvo_ref[0], w_ref[0])
    da += dot_nt(dqkvo_ref[1], w_ref[1])
    da += dot_nt(dqkvo_ref[2], w_ref[2])
    da_ref[...] = da
    sums_ref[...] = jnp.zeros_like(sums_ref)

    def finish(i, _):
        sl = pl.ds(pl.multiple_of(i * ROWS_AT_ONCE, ROWS_AT_ONCE), ROWS_AT_ONCE)
        normal, inverse = norm_stats(ho_ref[sl])
        da = da_ref[sl]
        dy = dh1_ref[sl] + norm_back(da, normal, inverse, gb_ref[0:1])
        dy_ref[sl] = dy
        for k, t in enumerate((da * normal, da, dy)):
            sums_ref[k : k + 1] += jnp.sum(t, axis=0, keepdims=True)
        return 0

    lax.fori_loop(0, rows * seq // ROWS_AT_ONCE, finish, 0)
    kept = [moves.whole(dy_ref, dy_far)]
    for g in range(groups):
        for _, wait in leave:
            wait(g)
    for wait in kept:
        wait()


def attend_back(w, incl, strict, qkve, qkvo, o2, lse2, do, dh1, ho, gb):
    rows, seq = incl.shape[0], incl.shape[1]
    n, d = ho.shape
    f = w.shape[2]
    do = do.reshape(2, n, f)
    qkv = sds((3, n, f), BF16)
    near = (w, incl, strict, qkve, qkvo, o2, do, sds((n, d), F32), ho, qkv, qkv, sds((n, d), F32))
    return resident(
        functools.partial(attend_back_body, rows, seq),
        [(t, FAR) for t in (w, incl, strict, qkve, qkvo, o2)]
        + [lse2]
        + [(t, FAR) for t in (do, dh1, ho)]
        + [gb],
        [(qkv, FAR), (qkv, FAR), (sds((n, d), F32), FAR), sds((3, d), F32)],
        scratch=[pltpu.VMEM(t.shape, t.dtype) for t in near + (sds((n, d), F32),)] + [pltpu.SemaphoreType.DMA((32,))],
        flops=6 * n * d * f + 120 * n * seq * f,
        vmem=44,
        name="attend_back",
    )


def attend_back_even_body(
    rows, seq, w_far, incl_far, qkve_far, o1_far, lse1_ref, do1_far, o2_far, lse2_ref, do2_far,
    part_far, dh1_far, dh2_far, x_far, gb_ref,
    dqkv_far, gt_ref, sums_ref,
    w_ref, incl_ref, qkve_ref, o1_ref, do1_ref, o2_ref, do2_ref, part_ref, dh1_ref, dh2_ref, x_ref,
    dqkv_ref, da_ref, sems,
):
    groups = lse1_ref.shape[0]
    moves = Moves(sems)
    even = pl.ds(0, rows * seq)
    arrive = [
        moves.groups(*t)
        for t in (
            (qkve_far, qkve_ref), (o1_far, o1_ref), (do1_far, do1_ref), (o2_far.at[0], o2_ref),
            (do2_far.at[0], do2_ref), (part_far, part_ref),
        )
    ]
    leave = [moves.groups(dqkv_ref, dqkv_far)]
    for start, _ in arrive:
        start(0)
    mask = moves.whole(incl_far, incl_ref)
    for start, _ in arrive:
        start(1)
    late = [
        moves.later(*t)
        for t in ((w_far, w_ref), (dh1_far, dh1_ref), (dh2_far.at[even], dh2_ref), (x_far, x_ref))
    ]
    mask()

    def next_group(group):
        in_turn(arrive, group, groups)

        @pl.when(group == groups - 2)
        def _():
            for start, _ in late:
                start()

    sc = HD**-0.5

    def row(i, _):
        r, group = i % rows, i // rows
        lanes = pl.multiple_of(group * GROUP, GROUP)
        all_of = pl.ds(pl.multiple_of(r * seq, seq), seq)

        @pl.when(r == 0)
        def _():
            next_group(group)

        for p in range(GROUP // (2 * HD)):
            ln = pl.ds(lanes + p * 2 * HD, 2 * HD)
            k, v = qkve_ref[1, all_of, ln], qkve_ref[2, all_of, ln]
            kt = k.T
            tasks = []
            for b in reversed(range(seq // QB)):
                sl, n = rows_of(r, seq, b), (b + 1) * QB
                incl = twice(incl_ref[r, :n, b * QB : n])
                lse1 = pair_row(lse1_ref[group, :, sl], p)
                ratio = jnp.exp(lse1 - pair_row(lse2_ref[0, group, :, sl], p))
                do1, do2 = do1_ref[sl, ln].astype(F32), do2_ref[sl, ln].astype(F32)
                delta = row_products(do1, o1_ref[sl, ln].astype(F32))
                delta += ratio * row_products(do2, o2_ref[sl, ln].astype(F32))
                both = do1 + own_lanes(twice(do2.T), ratio).T
                q, do = cat_heads(qkve_ref[0, sl, ln], sc), cat_heads(both.astype(BF16))
                tasks.append((k[:n], v[:n], kt[:, :n], incl, q, do, lse1, delta))
            dka = dva = None
            for b, (dv, dk, dq) in zip(reversed(range(seq // QB)), blocks_back(tasks)):
                sl = rows_of(r, seq, b)
                dva, dka = add_rows(dva, dv), add_rows(dka, dk)
                dqkv_ref[0, sl, ln] = (own_lanes(dq).T * sc + part_ref[0, sl, ln].astype(F32)).astype(BF16)
            dqkv_ref[1, all_of, ln] = (dka + part_ref[1, all_of, ln].astype(F32)).astype(BF16)
            dqkv_ref[2, all_of, ln] = (dva + part_ref[2, all_of, ln].astype(F32)).astype(BF16)

        @pl.when(r == rows - 1)
        def _():
            for start, _ in leave:
                start(group)

        return 0

    lax.fori_loop(0, rows * groups, row, 0)
    for _, wait in late:
        wait()
    da = dot_nt(dqkv_ref[0], w_ref[0])
    da += dot_nt(dqkv_ref[1], w_ref[1])
    da += dot_nt(dqkv_ref[2], w_ref[2])
    da_ref[...] = da
    sums_ref[...] = jnp.zeros_like(sums_ref)

    def finish(i, _):
        sl = pl.ds(pl.multiple_of(i * ROWS_AT_ONCE, ROWS_AT_ONCE), ROWS_AT_ONCE)
        normal, inverse = norm_stats(x_ref[sl].astype(F32))
        da = da_ref[sl]
        sums_ref[0:1] += jnp.sum(da * normal, axis=0, keepdims=True)
        sums_ref[1:2] += jnp.sum(da, axis=0, keepdims=True)
        back = norm_back(da, normal, inverse, gb_ref[0:1])
        gt_ref[sl] = (dh1_ref[sl] + dh2_ref[sl] + back).astype(BF16)
        return 0

    lax.fori_loop(0, rows * seq // ROWS_AT_ONCE, finish, 0)
    for g in range(groups):
        for _, wait in leave:
            wait(g)


def attend_back_even(w, incl, qkve, o1, lse1, do1, o2, lse2, do2, part, dh1, dh2, x, gb):
    rows, seq = incl.shape[0], incl.shape[1]
    n, d = x.shape
    f = w.shape[2]
    qkv, one = sds((3, n, f), BF16), sds((n, f), BF16)
    near = (w, incl, qkv, one, one, one, one, qkv, dh1, dh1, x, qkv, sds((n, d), F32))
    far = lambda *ts: [(t, FAR) for t in ts]
    return resident(
        functools.partial(attend_back_even_body, rows, seq),
        far(w, incl, qkve, o1)
        + [lse1]
        + far(do1, o2)
        + [lse2]
        + far(do2.reshape(2, n, f), part, dh1, dh2, x)
        + [gb],
        [(qkv, FAR), sds((n, d), BF16), sds((2, d), F32)],
        scratch=[pltpu.VMEM(t.shape, t.dtype) for t in near] + [pltpu.SemaphoreType.DMA((32,))],
        flops=6 * n * d * f + 40 * n * seq * f,
        vmem=40,
        name="attend_back_even",
    )


CHUNK = 512
ROWS_AT_ONCE = 256


def chunk_of(ref, j, axis):
    at = pl.ds(pl.multiple_of(j * CHUNK, CHUNK), CHUNK)
    return ref.at[:, at] if axis else ref.at[at]


class Chunks:
    def __init__(self, moves, far, near, axis, ring=False, leave=False):
        self.first = moves.take(far.shape[axis] // CHUNK)
        self.sems, self.far, self.near = moves.sems, far, near
        self.axis, self.ring, self.leave = axis, ring, leave

    def copy(self, j):
        near = self.near.at[j % self.near.shape[0]] if self.ring else chunk_of(self.near, j, self.axis)
        ends = (chunk_of(self.far, j, self.axis), near)
        return pltpu.make_async_copy(*(ends[::-1] if self.leave else ends), self.sems.at[self.first + j])

    def start(self, j):
        self.copy(j).start()

    def wait(self, j):
        self.copy(j).wait()


class Weight:
    def __init__(self, moves, pieces, near, axis):
        self.axis, self.near = axis, near
        self.own = Chunks(moves, pieces[0], near, axis) if pieces[0] is not None else None
        self.number = near.shape[axis] // CHUNK // 2
        self.others, start = [], near.shape[axis] // 2
        for far in pieces[1:]:
            at = pl.ds(start, far.shape[axis])
            self.others.append(moves.later(far, near.at[:, at] if axis else near.at[at]))
            start += far.shape[axis]

    def start_others(self):
        for start, _ in self.others:
            start()

    def wait_others(self):
        for _, wait in self.others:
            wait()


def load_in_turn(j, *weights):
    number = weights[0].number

    @pl.when(j < number)
    def _():
        for w in weights:
            w.own.wait(j)

    @pl.when(j + 2 < number)
    def _():
        for w in weights:
            w.own.start(j + 2)

    @pl.when(j + 2 == number)
    def _():
        for w in weights:
            w.start_others()

    @pl.when(j == number)
    def _():
        for w in weights:
            w.wait_others()


def start_loads(*weights):
    for j in range(2):
        for w in weights:
            w.own.start(j)


def feed_chunk(n2_ref, wup_ref, wdown_ref, j, g_buf, d_buf, ho_ref, gs, ds, first):
    @pl.when(first >= 2)
    def _():
        gs.wait(j - 2)
        ds.wait(j - 2)

    half = n2_ref.shape[0] // 2
    parts = []
    for sl in (slice(0, half), slice(half, 2 * half)):
        g, d = gelu_parts(dot(n2_ref[sl], chunk_of(wup_ref, j, 1)[...]))
        parts.append(g.astype(BF16))
        g_buf[j % 2, sl] = parts[-1]
        d_buf[j % 2, sl] = d.astype(BF16)
    gs.start(j)
    ds.start(j)
    for i, g in enumerate(parts):
        ho_ref[i * half : (i + 1) * half] += dot(g, chunk_of(wdown_ref, j, 0)[...])


def start_norm(x_ref, h1_ref, n2_ref, gb_ref, ho_ref=None):
    def part(k, _):
        sl = pl.ds(pl.multiple_of(k * ROWS_AT_ONCE, ROWS_AT_ONCE), ROWS_AT_ONCE)
        h1 = x_ref[sl].astype(F32) + h1_ref[sl]
        h1_ref[sl] = h1
        normal, _ = norm_stats(h1)
        n2_ref[sl] = (normal * gb_ref[1:2] + gb_ref[3:4]).astype(BF16)
        if ho_ref is not None:
            ho_ref[sl] = h1 + gb_ref[4:5]
        return 0

    lax.fori_loop(0, h1_ref.shape[0] // ROWS_AT_ONCE, part, 0)


def mlp_own_body(
    x_far, o_far, wout_far, gb_ref, wup_far, wdown_far,
    h1_far, n2_far, g_far, d_far, ho_far,
    x_ref, o_ref, wout_ref, wup_ref, wdown_ref, h1_ref, n2_ref, ho_ref, g_buf, d_buf, sems,
):
    moves = Moves(sems)
    first = [moves.whole(*t) for t in ((o_far, o_ref), (wout_far, wout_ref), (x_far, x_ref))]
    ups, downs = Chunks(moves, wup_far, wup_ref, 1), Chunks(moves, wdown_far, wdown_ref, 0)
    gs, ds = (Chunks(moves, f, b, 1, True, True) for f, b in ((g_far, g_buf), (d_far, d_buf)))
    number = wup_far.shape[1] // CHUNK
    for wait in first:
        wait()
    for j in range(number):
        ups.start(j)
        downs.start(j)
    h1_ref[...] = dot(o_ref[...], wout_ref[...])
    start_norm(x_ref, h1_ref, n2_ref, gb_ref, ho_ref)
    kept = [moves.whole(*t) for t in ((h1_ref, h1_far), (n2_ref, n2_far))]

    def step(j, _):
        ups.wait(j)
        downs.wait(j)
        feed_chunk(n2_ref, wup_ref, wdown_ref, j, g_buf, d_buf, ho_ref, gs, ds, j)
        return 0

    lax.fori_loop(0, number, step, 0)
    kept.append(moves.whole(ho_ref, ho_far))
    for wait in kept:
        wait()
    for j in range(number - 2, number):
        gs.wait(j)
        ds.wait(j)


def mlp_other_body(number_up, number_down, n2_far, part_far, g_in, d_in, gb_ref, *refs):
    ups_far, refs = refs[:number_up], refs[number_up:]
    downs_far, refs = refs[:number_down], refs[number_down:]
    g_far, d_far, ho_far, ao_far, n2_ref, wup_ref, wdown_ref, ho_ref, ao_ref, g_buf, d_buf, sems = refs
    moves = Moves(sems)
    up = Weight(moves, (None,) + ups_far, wup_ref, 1)
    down = Weight(moves, (None,) + downs_far, wdown_ref, 0)
    gs, ds = (Chunks(moves, f, b, 1, True, True) for f, b in ((g_far, g_buf), (d_far, d_buf)))
    ready = [moves.whole(*t) for t in ((n2_far, n2_ref), (part_far, ho_ref))]
    up.start_others()
    down.start_others()
    for wait in ready:
        wait()
    up.wait_others()
    down.wait_others()

    def step(i, _):
        feed_chunk(n2_ref, wup_ref, wdown_ref, up.number + i, g_buf, d_buf, ho_ref, gs, ds, i)
        return 0

    lax.fori_loop(0, up.number, step, 0)
    sent = moves.whole(ho_ref, ho_far)

    def norm(k, _):
        sl = pl.ds(pl.multiple_of(k * ROWS_AT_ONCE, ROWS_AT_ONCE), ROWS_AT_ONCE)
        normal, _ = norm_stats(ho_ref[sl])
        ao_ref[sl] = (normal * gb_ref[0:1] + gb_ref[2:3]).astype(BF16)
        return 0

    lax.fori_loop(0, ho_ref.shape[0] // ROWS_AT_ONCE, norm, 0)
    moves.whole(ao_ref, ao_far)()
    sent()
    for j in range(2 * up.number - 2, 2 * up.number):
        gs.wait(j)
        ds.wait(j)


def near_of(*arrays):
    return [pltpu.VMEM(t.shape, t.dtype) for t in arrays]


def far_of(*arrays):
    return [(t, FAR) for t in arrays]


def mlp_own(x, o, wout, gb, wup, wdown):
    n, d = x.shape
    ff = 2 * wup.shape[1]
    h1, low, wide = sds((n, d), F32), sds((n, d), BF16), sds((n, ff), BF16)
    return resident(
        mlp_own_body,
        far_of(x, o, wout) + [gb] + far_of(wup, wdown),
        far_of(h1, low, wide, wide, h1),
        scratch=near_of(x, o, wout, wup, wdown, h1, low, h1)
        + [pltpu.VMEM((2, n, CHUNK), BF16)] * 2
        + [pltpu.SemaphoreType.DMA((40,))],
        vmem=36,
        name="mlp_own",
    )


def mlp_other(n2, part, g, dgelu, gb, ups, downs):
    n, d = n2.shape
    ff = g.shape[1]
    return resident(
        functools.partial(mlp_other_body, len(ups), len(downs)),
        far_of(n2, part, g, dgelu) + [gb] + far_of(*ups, *downs),
        far_of(sds(g.shape, BF16), sds(g.shape, BF16), sds(part.shape, F32), sds(n2.shape, BF16)),
        scratch=near_of(n2, sds((d, ff), BF16), sds((ff, d), BF16), part, n2)
        + [pltpu.VMEM((2, n, CHUNK), BF16)] * 2
        + [pltpu.SemaphoreType.DMA((40,))],
        vmem=40,
        aliases={2: 0, 3: 1},
        name="mlp_other",
    )


def weave(seq):
    i = lax.broadcasted_iota(jnp.int32, (2 * seq, 2 * seq), 0)
    k = lax.broadcasted_iota(jnp.int32, (2 * seq, 2 * seq), 1)
    place = jnp.where(k < seq, 2 * k, 2 * (k - seq) + 1)
    return jnp.where(i == place, 1.0, 0.0).astype(BF16)


def after_norm_back(
    moves, size, h1_ref, dn_ref, db_ref, wout_ref, gb_ref, sums_ref, dp_ref, do_ref, dh1_far, dp_far, do_far
):
    gain_sum = jnp.zeros_like(gb_ref[0:1])
    bias_sum = jnp.zeros_like(gb_ref[0:1])
    waits = []
    for i in range(h1_ref.shape[0] // size):
        sl = slice(i * size, (i + 1) * size)
        normal, inverse = norm_stats(h1_ref[sl])
        dn = dn_ref[sl]
        gain_sum += jnp.sum(dn * normal, axis=0, keepdims=True)
        bias_sum += jnp.sum(dn, axis=0, keepdims=True)
        dh1 = db_ref[sl].astype(F32) + norm_back(dn, normal, inverse, gb_ref[1:2])
        dn_ref[sl] = dh1
        dp_ref[sl] = dh1.astype(BF16)
    sums_ref[0:1] = gain_sum
    sums_ref[1:2] = bias_sum
    waits += [moves.whole(dn_ref, dh1_far), moves.whole(dp_ref, dp_far)]
    do_ref[...] = dot_nt(dp_ref[...], wout_ref[...]).astype(BF16)
    return waits + [moves.whole(do_ref, do_far)]


def mlp_second_body(rows, seq, number_up, number_down, x_far, ho_far, o_far, cot_far, wout_far, gb_ref, *refs):
    mlp_second_work(rows, seq, x_far, ho_far, o_far, cot_far, wout_far, gb_ref, *in_pieces(refs, number_up, number_down))


def in_pieces(refs, *numbers):
    out = []
    for k in numbers:
        out.append(refs[:k])
        refs = refs[k:]
    return out + list(refs)


def mlp_second_work(
    rows, seq, x_far, ho_far, o_far, cot_far, wout_far, gb_ref, ups_far, downs_far,
    outs_far, outs2_far, n2_far, g_far, du_far, dh1_far, dp_far, do_far, sums_ref, dm_far,
    x_ref, ho_ref, o_ref, cot_ref, wout_ref, wup_ref, wdown_ref, n2_ref, dm_ref,
    h1_ref, z_ref, dn_ref, dp_ref, do_ref, g_buf, du_buf, sems,
):
    n = rows * seq
    moves = Moves(sems)
    halves = (slice(0, n), slice(n, 2 * n))
    cot_there = moves.whole(cot_far, cot_ref)
    first = [moves.whole(*t) for t in ((o_far, o_ref), (wout_far, wout_ref), (x_far, x_ref))]
    up, down = Weight(moves, ups_far, wup_ref, 1), Weight(moves, downs_far, wdown_ref, 0)
    gs, dus = (Chunks(moves, f, b, 1, True, True) for f, b in ((g_far, g_buf), (du_far, du_buf)))
    number = 2 * up.number
    mix = weave(seq)
    cot_there()
    for r in range(rows):
        parted = dot_tn(mix, cot_ref[r]).astype(BF16)
        for i in range(2):
            dm_ref[i * n + r * seq : i * n + (r + 1) * seq] = parted[i * seq : (i + 1) * seq]
    for wait in first:
        wait()
    then = moves.whole(ho_far, ho_ref)
    start_loads(up, down)
    for i, sl in enumerate(halves):
        if i:
            then()
        h1_ref[sl] = dot(o_ref[i], wout_ref[...])
        start_norm(x_ref if i == 0 else ho_ref, h1_ref.at[pl.ds(i * n, n)], n2_ref.at[pl.ds(i * n, n)], gb_ref)
    kept = [moves.whole(*t) for t in ((n2_ref, n2_far), (dm_ref, dm_far))]
    z_ref[...] = jnp.zeros_like(z_ref)
    dn_ref[...] = jnp.zeros_like(dn_ref)

    def step(j, _):
        load_in_turn(j, up, down)

        @pl.when(j >= 2)
        def _():
            gs.wait(j - 2)
            dus.wait(j - 2)

        for sl in halves:
            u = dot(n2_ref[sl], chunk_of(wup_ref, j, 1)[...])
            dg = dot_nt(dm_ref[sl], chunk_of(wdown_ref, j, 0)[...])
            g, d = gelu_parts(u)
            g = g.astype(BF16)
            du = (dg * d).astype(BF16)
            g_buf[j % 2, sl] = g
            du_buf[j % 2, sl] = du
            z_ref[sl] += dot(g, chunk_of(wdown_ref, j, 0)[...])
            dn_ref[sl] += dot_nt(du, chunk_of(wup_ref, j, 1)[...])
        gs.start(j)
        dus.start(j)
        return 0

    lax.fori_loop(0, number, step, 0)
    for r in range(rows):
        pair = [slice(i * n + r * seq, i * n + (r + 1) * seq) for i in range(2)]
        z = jnp.concatenate([(h1_ref[s] + z_ref[s]).astype(BF16) for s in pair], axis=0)
        cot_ref[r] = dot(mix, z).astype(BF16)
    half = rows // 2
    kept += [moves.whole(cot_ref.at[pl.ds(i * half, half)], far) for i, far in enumerate((outs_far, outs2_far))]
    kept += after_norm_back(
        moves, seq, h1_ref, dn_ref, dm_ref, wout_ref, gb_ref, sums_ref, dp_ref, do_ref, dh1_far, dp_far, do_far
    )
    for wait in kept:
        wait()
    for j in range(number - 2, number):
        gs.wait(j)
        dus.wait(j)


def mlp_second(x, ho, o2, cot, wout, gb, ups, downs, seq):
    n, d = x.shape
    ff = 2 * ups[0].shape[1]
    rows = n // seq
    low, wide, full = sds((2 * n, d), BF16), sds((2 * n, ff), BF16), sds((2 * n, d), F32)
    out = sds((rows // 2, 2 * seq, d), BF16)
    return resident(
        functools.partial(mlp_second_body, rows, seq, len(ups), len(downs)),
        far_of(x, ho, o2, cot, wout) + [gb] + far_of(*ups, *downs),
        far_of(out, out, low, wide, wide, full, low, low) + [sds((2, d), F32)] + far_of(low),
        scratch=near_of(x, ho, o2, cot, wout, sds((d, ff), BF16), sds((ff, d), BF16), low, low, full, full, full, low, low)
        + [pltpu.VMEM((2, 2 * n, CHUNK), BF16)] * 2
        + [pltpu.SemaphoreType.DMA((64,))],
        vmem=60,
        name="mlp_second",
    )


def mlp_back_body(rows, seq, number_up, number_down, dy_far, h1_far, wout_far, gb_ref, d_far, *refs):
    mlp_back_work(rows, seq, dy_far, h1_far, wout_far, gb_ref, d_far, *in_pieces(refs, number_up, number_down))


def mlp_back_work(
    rows, seq, dy_far, h1_far, wout_far, gb_ref, d_far, ups_far, downs_far,
    du_far, dh1_far, dp_far, do_far, sums_ref,
    dy_ref, h1_ref, wout_ref, wup_ref, wdown_ref, d_ref, dm_ref, dn_ref, dp_ref, do_ref, du_buf, sems,
):
    moves = Moves(sems)
    first = moves.whole(dy_far, dy_ref)
    up, down = Weight(moves, ups_far, wup_ref, 1), Weight(moves, downs_far, wdown_ref, 0)
    ds, dus = Chunks(moves, d_far, d_ref, 1), Chunks(moves, du_far, du_buf, 1, True, True)
    number = 2 * up.number
    start_loads(down, up)
    for j in range(2):
        ds.start(j)
    then = [moves.later(*t) for t in ((wout_far, wout_ref), (h1_far, h1_ref))]
    first()
    dm_ref[...] = dy_ref[...].astype(BF16)
    dn_ref[...] = jnp.zeros_like(dn_ref)

    def step(j, _):
        load_in_turn(j, down, up)
        ds.wait(j)

        @pl.when(j + 2 < number)
        def _():
            ds.start(j + 2)

        @pl.when(j + 2 == number)
        def _():
            for start, _ in then:
                start()

        @pl.when(j >= 2)
        def _():
            dus.wait(j - 2)

        dg = dot_nt(dm_ref[...], chunk_of(wdown_ref, j, 0)[...])
        du = (dg * chunk_of(d_ref, j, 1)[...].astype(F32)).astype(BF16)
        du_buf[j % 2] = du
        dus.start(j)
        dn_ref[...] += dot_nt(du, chunk_of(wup_ref, j, 1)[...])
        return 0

    lax.fori_loop(0, number, step, 0)
    for _, wait in then:
        wait()
    kept = after_norm_back(
        moves, seq, h1_ref, dn_ref, dy_ref, wout_ref, gb_ref, sums_ref, dp_ref, do_ref, dh1_far, dp_far, do_far
    )
    for wait in kept:
        wait()
    for j in range(number - 2, number):
        dus.wait(j)


def mlp_back(dy, h1, wout, gb, dgelu, ups, downs, seq):
    n, d = dy.shape
    ff = dgelu.shape[1]
    low = sds((n, d), BF16)
    return resident(
        functools.partial(mlp_back_body, n // seq, seq, len(ups), len(downs)),
        far_of(dy, h1, wout) + [gb] + far_of(dgelu, *ups, *downs),
        far_of(dgelu, h1, low, low) + [sds((2, d), F32)],
        scratch=near_of(dy, h1, wout, sds((d, ff), BF16), sds((ff, d), BF16), dgelu, low, dy, low, low)
        + [pltpu.VMEM((2, n, CHUNK), BF16)]
        + [pltpu.SemaphoreType.DMA((48,))],
        vmem=48,
        name="mlp_back",
    )


def lanes_at(ref, start, size):
    return ref.at[:, pl.ds(pl.multiple_of(start, 128), size)]


def stack_rows(moves, pairs, target, start, size):
    copies, row = [], 0
    for far in pairs:
        copies.append(moves.later(lanes_at(far, start, size), target.at[pl.ds(row, far.shape[0])]))
        row += far.shape[0]
    return (lambda: [s() for s, _ in copies]), (lambda: [w() for _, w in copies])


def all_of(*parts):
    return (lambda: [s() for s, _ in parts]), (lambda: [w() for _, w in parts])


class InTurn:
    def __init__(self, *tiles):
        self.tiles, self.at = tiles, 0
        for start, _ in tiles[:2]:
            start()

    def next(self):
        self.tiles[self.at][1]()
        self.at += 1
        if self.at + 1 < len(self.tiles):
            self.tiles[self.at + 1][0]()


def place_of(quarter, y, me_ref):
    return quarter if y else 4 + (quarter ^ me_ref[1])


def packed(body, me, arrays, shape, scratch, flops, vmem, name):
    smem = pl.BlockSpec(memory_space=pltpu.SMEM)
    out = sds(shape, BF16)
    return resident(
        body,
        [(me, smem)] + far_of(*arrays),
        far_of(out, out),
        scratch=near_of(sds((2,) + shape, BF16)) + scratch + [pltpu.SemaphoreType.DMA((64,))],
        flops=flops,
        vmem=vmem,
        name=name,
    )


def grad_down_body(
    me_ref, g1_far, g2_far, dy_far, dm2_far, keep_far, go_far, out_ref, dy_ref, dm_ref, g_ref, acc_ref, sems
):
    low, group = me_ref[0] % 4, (me_ref[0] // 4) % 2
    ring, n, b = g_ref.shape[0], g1_far.shape[0], g_ref.shape[2]
    moves = Moves(sems)
    first, last = moves.take(2 * ring), moves.take(4)

    def tile(i):
        side, y, h = 1 - i // 4, (i // 2) % 2, i % 2
        quarter = ((me_ref[0] // 8) ^ side) * 2 + h
        at = jnp.where(y == 0, 4 + (quarter ^ me_ref[1]), quarter) * b
        return side, y, h, at

    def loads(i):
        at, slot = tile(i)[3], i % ring
        near = g_ref.at[slot]
        ends = ((g1_far, near.at[pl.ds(0, n)]), (g2_far, near.at[pl.ds(n, 2 * n)]))
        return [pltpu.make_async_copy(lanes_at(f, at, b), t, sems.at[first + 2 * slot + k]) for k, (f, t) in enumerate(ends)]

    def store(far, side, y):
        return pltpu.make_async_copy(out_ref.at[side, y], far.at[y], sems.at[last + side * 2 + y])

    ready = [moves.whole(dy_far, dy_ref), moves.whole(dm2_far, dm_ref.at[pl.ds(n, 2 * n)])]
    for i in range(2):
        for c in loads(i):
            c.start()
    for wait in ready:
        wait()
    dm_ref[:n] = dy_ref[...].astype(BF16)

    def step(i, _):
        side, y, h, _ = tile(i)
        for c in loads(i):
            c.wait()

        @pl.when(i + 2 < 8)
        def _():
            for c in loads(i + 2):
                c.start()

        acc_ref[...] = dot_tn(g_ref[i % ring], dm_ref[...]).reshape(acc_ref.shape)
        for s in range(4):
            out_ref[side, y, (h ^ group) * 4 + s] = acc_ref[s ^ low].astype(BF16)

        @pl.when((h == 1) & (side == 1))
        def _():
            store(go_far, 1, y).start()

        @pl.when((h == 1) & (side == 0))
        def _():
            store(keep_far, 0, y).start()

        return 0

    lax.fori_loop(0, 8, step, 0)
    for y in range(2):
        store(go_far, 1, y).wait()
        store(keep_far, 0, y).wait()


def grad_down(me, g1, g2, dy, dm2):
    n, d = dy.shape
    ff = g1.shape[1]
    b = ff // 8
    return packed(
        grad_down_body,
        me,
        (g1, g2, dy, dm2),
        (2, 8, b // 4, d),
        [
            pltpu.VMEM((n, d), F32),
            pltpu.VMEM((3 * n, d), BF16),
            pltpu.VMEM((3, 3 * n, b), BF16),
            pltpu.VMEM((4, b // 4, d), F32),
        ],
        2 * 3 * n * d * ff,
        40,
        "grad_down",
    )


CUT = 768


def put_slots(out_ref, y, lanes, acc_ref, me):
    for s in range(16):
        out_ref[s // 8, y, s % 8, :, lanes] = acc_ref[s ^ me].astype(BF16)


def grad_up_body(
    me_ref, n1_far, n2_far, du1_far, du2_far, dp1_far, dp2_far, o1_far, o2_far, keep_far, go_far,
    out_ref, n_ref, t_ref, du_ref, dp_ref, o_ref, acc_ref, acc2_ref, sems,
):
    moves = Moves(sems)
    d, f = n_ref.shape[1], o_ref.shape[2]
    ring, c, n = du_ref.shape[0], du_ref.shape[2], du1_far.shape[0]
    first, last = moves.take(4 * ring), moves.take(4)

    def loads(i):
        y, t, slot = i // 2, i % 2, i % ring
        copies = []
        for k in range(2):
            quarter = 2 * t + k
            at = jnp.where(y == 0, 4 + (quarter ^ me_ref[1]), quarter) * f
            near = lanes_at(du_ref.at[slot], k * f, f)
            for far, rows in ((du1_far, pl.ds(0, n)), (du2_far, pl.ds(n, 2 * n))):
                copies.append((lanes_at(far, at, f), near.at[rows]))
        return [pltpu.make_async_copy(a, b, sems.at[first + 4 * slot + k]) for k, (a, b) in enumerate(copies)]

    def stores(y):
        return [
            pltpu.make_async_copy(out_ref.at[i, y], far.at[y], sems.at[last + 2 * y + i])
            for i, far in enumerate((keep_far, go_far))
        ]

    ready = stack_rows(moves, (n1_far, n2_far), n_ref, 0, d)
    ready[0]()
    for c0 in loads(0):
        c0.start()
    out_loads = [stack_rows(moves, (dp1_far, dp2_far), dp_ref, 0, d)]
    out_loads += [stack_rows(moves, (o1_far, o2_far), o_ref.at[y], (1 - y) * f, f) for y in range(2)]
    ready[1]()
    for c0 in loads(1):
        c0.start()
    t_ref[...] = n_ref[...].T

    def step(i, _):
        y, t = i // 2, i % 2
        for c0 in loads(i):
            c0.wait()

        @pl.when(i + 2 < 4)
        def _():
            for c0 in loads(i + 2):
                c0.start()

        @pl.when(i == 0)
        def _():
            for start, _ in out_loads:
                start()

        acc_ref[...] = dot(t_ref[...], du_ref[i % ring]).reshape(acc_ref.shape)
        put_slots(out_ref, y, pl.ds(pl.multiple_of(t * c, c), c), acc_ref, jnp.where(t == 0, me_ref[0], me_ref[2]))

        @pl.when(i == 1)
        def _():
            for _, wait in out_loads:
                wait()

        @pl.when(t == 1)
        def _():
            acc2_ref[...] = dot_tn(dp_ref[...], o_ref[y]).reshape(acc2_ref.shape)
            put_slots(out_ref, y, slice(2 * c, 2 * c + f), acc2_ref, me_ref[2])
            for s in stores(y):
                s.start()

        return 0

    lax.fori_loop(0, 4, step, 0)
    for y in range(2):
        for s in stores(y):
            s.wait()


def grad_up(me, n1, n2, du1, du2, dp1, dp2, o1, o2):
    n, d = n1.shape
    ff = du1.shape[1]
    f, c = o1.shape[1] // 2, ff // 4
    return packed(
        grad_up_body,
        me,
        (n1, n2, du1, du2, dp1, dp2, o1, o2),
        (2, 8, d // 16, 2 * c + f),
        [
            pltpu.VMEM((3 * n, d), BF16),
            pltpu.VMEM((d, 3 * n), BF16),
            pltpu.VMEM((3, 3 * n, c), BF16),
            pltpu.VMEM((3 * n, d), BF16),
            pltpu.VMEM((2, 3 * n, f), BF16),
            pltpu.VMEM((16, d // 16, c), F32),
            pltpu.VMEM((16, d // 16, f), F32),
        ],
        2 * 3 * n * d * (ff + d),
        56,
        "grad_up",
    )


def grad_qkv_body(me_ref, ae_far, ao_far, de_far, do_far, keep_far, go_far, out_ref, a_ref, t_ref, d_ref, acc_ref, sems):
    moves = Moves(sems)
    d = a_ref.shape[1]
    f = de_far.shape[2] // 2
    ready = stack_rows(moves, (ae_far, ao_far), a_ref, 0, d)
    tiles = [stack_rows(moves, (de_far.at[j], do_far.at[j]), d_ref.at[j], 0, 2 * f) for j in range(3)]
    ready[0]()
    for start, _ in tiles[:2]:
        start()
    ready[1]()
    tiles[2][0]()
    t_ref[...] = a_ref[...].T
    for _, wait in tiles:
        wait()

    def step(j, _):
        acc_ref[...] = dot(t_ref[...], d_ref[j]).reshape(acc_ref.shape)
        lanes = pl.ds(pl.multiple_of(j * f, f), f)
        for s in range(16):
            block = acc_ref[s ^ me_ref[0]].astype(BF16)
            out_ref[s // 8, 1, s % 8, :, lanes] = block[:, :f]
            out_ref[s // 8, 0, s % 8, :, lanes] = block[:, f:]
        return 0

    lax.fori_loop(0, 3, step, 0)
    sent = [moves.whole(out_ref.at[i], far) for i, far in ((1, go_far), (0, keep_far))]
    for wait in sent:
        wait()


def grad_qkv(me, ae, ao, dqkv_e, dqkv_o):
    n, d = ae.shape
    f = dqkv_e.shape[2] // 2
    return packed(
        grad_qkv_body,
        me,
        (ae, ao, dqkv_e, dqkv_o),
        (2, 8, d // 16, 3 * f),
        [
            pltpu.VMEM((2 * n, d), BF16),
            pltpu.VMEM((d, 2 * n), BF16),
            pltpu.VMEM((3, 2 * n, 2 * f), BF16),
            pltpu.VMEM((16, d // 16, 2 * f), F32),
        ],
        2 * 2 * 3 * n * d * 2 * f,
        40,
        "grad_qkv",
    )


def packed_call(body, grid, me, ins, outs, scratch=(), flops=0, aliases={}, name=None):
    return pl.pallas_call(
        body,
        grid_spec=pltpu.PrefetchScalarGridSpec(
            num_scalar_prefetch=1,
            grid=grid,
            in_specs=[s for _, s in ins],
            out_specs=[s for _, s in outs],
            scratch_shapes=scratch,
        ),
        out_shape=[a for a, _ in outs],
        input_output_aliases=aliases,
        compiler_params=pltpu.CompilerParams(
            dimension_semantics=("arbitrary",) * len(grid), vmem_limit_bytes=VMEM_LIMIT
        ),
        cost_estimate=pl.CostEstimate(flops=int(flops) // 16, bytes_accessed=0, transcendentals=0),
        name=name,
    )(me, *[a for a, _ in ins])


def unpack_body(kind, me_ref, part_ref, *refs):
    low = me_ref[0] % 8
    rows, width = part_ref.shape[1:]
    first = refs[-2] if kind == "up" else refs[-1]
    if kind == "up":
        first, second, wide = refs[-3:]
    for s in range(8):
        sl = slice(s * rows, (s + 1) * rows)
        if kind == "down":
            first[sl] = part_ref[s ^ low].astype(F32)
        elif kind == "up":
            f = first.shape[1]
            other = s ^ (me_ref[2] % 8)
            first[sl, :CUT] = part_ref[s ^ low, :, :CUT].astype(F32)
            first[sl, CUT:] = part_ref[other, :, CUT:f].astype(F32)
            wide[sl] = part_ref[other, :, f:].astype(F32)
        else:
            f = width // 3
            for j in range(3):
                first[j, sl] = part_ref[s ^ low, :, j * f : (j + 1) * f].astype(F32)
    if kind == "up":
        second[...] = wide[...].T


def unpack(kind, me, side, part, into=()):
    _, r, w = part.shape
    half = 8 * r
    at = lambda me: (me[0] // 8) ^ side
    scratch = []
    if kind == "down":
        outs = [(sds((2 * half, w), F32), pl.BlockSpec((half, w), lambda i, me: (at(me), 0)))]
    elif kind == "up":
        f = half
        outs = [
            (sds((2 * half, w - f), F32), pl.BlockSpec((half, w - f), lambda i, me: (at(me), 0))),
            (sds((f, 2 * half), F32), pl.BlockSpec((f, half), lambda i, me: (0, at(me)))),
        ]
        scratch = [pltpu.VMEM((half, f), F32)]
    else:
        f = w // 3
        outs = [(sds((3, 2 * half, f), F32), pl.BlockSpec((3, half, f), lambda i, me: (0, at(me), 0)))]
    ins = [(part, pl.BlockSpec(part.shape, lambda i, me: (0, 0, 0)))]
    ins += [(t, pl.BlockSpec(memory_space=pl.ANY)) for t in into]
    return packed_call(
        functools.partial(unpack_body, kind),
        (1,),
        me,
        ins,
        outs,
        scratch=scratch,
        aliases={2 + i: i for i in range(len(into))},
        name="unpack_" + kind,
    )


def fold(*parts):
    return sum(p.astype(F32) for p in parts).astype(BF16)


def after(value, *first):
    return lax.optimization_barrier((value, first))[0]


class Chunk:
    def __init__(self, keep, got):
        self.keep, self.got = keep, got
        self.sent = None

    def wait(self, *also):
        self.got, also = lax.optimization_barrier((self.got, also))
        return also

    def to_partner(self):
        total = fold(self.keep, self.got)
        self.keep, self.sent = total[1], total[0]
        self.got = lax.ppermute(self.sent, "tensor", FLIP)

    def gather_core(self):
        self.got = lax.ppermute(self.keep, "core", FLIP)


class Hops(Chunk):
    def __init__(self, outer, keep, got):
        super().__init__(keep, got)
        self.axes = {"x": ("x", 2, 1), "z": ("o", outer, 1), "w": ("o", outer, 2)}
        self.extra = [("o", outer, 1 << b) for b in range(2, outer.bit_length() - 1)]

    def send(self, *parts):
        self.keep, self.sent, self.got = [], [], []
        for total, way in parts:
            if way == "partner":
                keep, sent = total[1], total[0]
                got = lax.ppermute(sent, "tensor", FLIP)
            else:
                half = total.shape[-3] // 2
                keep, sent = total[..., :half, :, :], total[..., half:, :, :]
                got = flip_bit(sent, *self.axes[way])
            self.keep.append(keep)
            self.sent.append(sent)
            self.got.append(got)

    def folded(self):
        return [fold(k, g) for k, g in zip(self.keep, self.got)]

    def first(self):
        total = fold(self.keep, self.got)
        self.send((total[..., :CUT], "x"), (total[..., CUT:], "z"))

    def hop(self, *ways):
        self.send(*zip(self.folded(), ways))

    def first_hop(self, way):
        self.send((fold(self.keep, self.got), way))

    def last_hop(self):
        self.send((jnp.concatenate(self.folded(), axis=-1), "w"))

    def back(self, *ways):
        self.sent = self.keep
        self.got = [flip_bit(k, *self.axes[w]) for k, w in zip(self.keep, ways)]

    def back_first(self):
        (total,) = self.folded()
        for s in self.extra:
            total = fold(total, flip_bit(total, *s))
        self.keep = [total]
        self.back("w")

    def joined(self, parts=1):
        self.keep = [jnp.concatenate([k, g], axis=0) for k, g in zip(self.keep, self.got)]
        if parts == 2:
            (total,) = self.keep
            self.keep = [total[..., :CUT], total[..., CUT:]]

    def back_core(self):
        self.joined()
        self.keep = self.sent = jnp.concatenate(self.keep, axis=-1)
        self.gather_core()


def mask_biases(seg):
    seq = seg.shape[1]
    place = jnp.arange(seq, dtype=jnp.int32)
    same = seg[:, :, None] == seg[:, None, :]
    below = (place[:, None] < place[None, :])[None]
    incl = (place[:, None] <= place[None, :])[None]
    bias = lambda m: jnp.where(same & m, 0.0, NEG).astype(F32)
    return bias(incl), bias(below)


def sync(*values):
    return lax.optimization_barrier(values)


class Link:
    def __init__(self, outer, w_qkv, w_out, w_up, w_down):
        self.outer = outer
        self.own = (w_qkv, w_out, w_up, w_down)
        self.core_at, self.x_at, o = (lax.axis_index(a) for a in ("core", "x", "o"))
        bits = {"x": self.x_at, "z": o % 2, "w": (o // 2) % 2}
        self.fetch_bits = self.core_at * 2 + self.x_at
        slots = []
        for order in ("xzw", "zxw"):
            slot = self.core_at
            for name in order:
                slot = slot * 2 + bits[name]
            slots.append(slot)
        self.me = jnp.stack([slots[0], self.fetch_bits, slots[1]]).astype(jnp.int32)
        self.me_z = self.me[2:0:-1]

    def quarter(self, own):
        flat = own.reshape(-1, own.shape[-1])
        return take_half(take_half(flat, self.core_at), self.x_at)

    def over_x(self, t):
        return lax.ppermute(t, "x", FLIP)

    def fetch(self, own_work):
        own = self.own
        size = own[2].shape[1] // 4
        part = lambda t, axis, bits: lax.dynamic_slice_in_dim(t, bits * size, size, axis)
        pieces = [
            self.quarter(own[1]),
            part(own[2], 1, self.fetch_bits),
            jnp.concatenate([part(own[3], 0, self.fetch_bits), part(own[3], 0, self.fetch_bits ^ 1)], axis=0),
        ]
        qkv = self.partner(self.quarter(own[0]))
        up, out, down = (self.partner(pieces[i]) for i in (1, 0, 2))
        qkv, own_work = sync(qkv, own_work)
        qkv, out, up = sync(ordered(self.x_at, qkv, self.over_x(qkv)).reshape(-1, qkv.shape[-1]), out, up)
        qkv_core, out_x, up_x = self.core(qkv), self.over_x(out), self.over_x(up)
        qkv = ordered(self.core_at, qkv, qkv_core).reshape(own[0].shape)

        def join_out(*work):
            nonlocal out, out_x
            work, out, out_x = sync(work, out, out_x)
            out = ordered(self.x_at, out, out_x).reshape(-1, out.shape[-1])
            out = ordered(self.core_at, out, self.core(out)).reshape(own[1].shape)
            return work, jnp.concatenate([own[1], out], axis=0)

        def pieces_of(*work):
            up_there, down_there, work = sync(up_x, down, work)
            ups = (own[2], up, up_there, self.core(up), self.core(up_there))
            return ups, (own[3], down_there, self.core(down_there)), work

        return own_work, own[0], qkv, jnp.concatenate([own[0], qkv], axis=2), join_out, pieces_of

    def partner(self, t):
        return lax.ppermute(t, "tensor", FLIP)

    def core(self, t):
        return lax.ppermute(t, "core", FLIP)

    def chunk(self, keep, got):
        return Chunk(keep, got)

    def hops(self, keep, got):
        return Hops(self.outer, keep, got)

    def small_steps(self):
        return [("core", 2, 1), ("tensor", 2, 1)] + steps_of(self.outer)

    def flip(self, t, step):
        return flip_bit(t, *step)


def local_part(x, seg, cot, gb, link):
    rows, seq = seg.shape
    n, width = x.shape
    me, me_z = link.me, link.me_z
    incl, strict = mask_biases(seg)
    normal, _ = norm_stats(x.astype(F32))
    a_e = (normal * gb[0] + gb[2]).astype(BF16)
    first = attend_first(a_e, link.own[0], incl)
    (a_e, first, cot), wq_own, fetched, wqkv, join_out, pieces_of = link.fetch((a_e, first, cot))
    second = attend_first(a_e, fetched, incl)
    qkv_e, o1 = (jnp.concatenate([s, t], axis=-1) for s, t in zip(first[:2], second[:2]))
    lse1 = jnp.concatenate([first[2], second[2]], axis=0).reshape(-1, GROUP // HD, n)
    (qkv_e, o1, lse1, wqkv), wout = join_out(qkv_e, o1, lse1, wqkv)
    h1, n2_1, g1, d1, part_one = mlp_own(x, o1, wout, gb, link.own[2], link.own[3])
    ups, downs, (n2_1, part_one) = pieces_of(n2_1, part_one)
    g1, d1, ho, a_o = mlp_other(n2_1, part_one, g1, d1, gb, ups[1:], downs[1:])
    qkv_o, o2, lse2 = attend_second(a_o, wqkv, incl, strict, qkv_e, o1, lse1)
    out, out_two, n2_2, g2, du2, dh1_2, dp2, do2, sums2, dm2 = mlp_second(x, ho, o2, cot, wout, gb, ups, downs, seq)
    out_got = link.partner(out)
    dqkv_o, part, dy, sums_o = attend_back(wqkv, incl, strict, qkv_e, qkv_o, o2, lse2, do2, dh1_2, ho, gb)
    o2_flat = o2.reshape(2 * n, width)

    out_got, dy = sync(out_got, dy)
    out_last = link.partner(after(out_two, out_got))
    down_keep, down_go = grad_down(me_z, g1, g2, dy, dm2)
    down_keep, down_go, out_last = sync(down_keep, down_go, out_last)
    down = link.hops(down_keep, link.core(down_go))
    dy = after(dy, down_go)
    du1, dh1_1, dp1, do1, sums1 = mlp_back(dy, h1, wout, gb, d1, ups, downs, seq)
    du1, dp1, do1 = down.wait(du1, dp1, do1)
    down.to_partner()
    up_keep, up_go = grad_up(me, n2_1, n2_2, after(du1, down.sent), du2, dp1, dp2, o1, o2_flat)
    do1 = after(do1, up_go)
    dqkv_e, gt, sums_e = attend_back_even(wqkv, incl, qkv_e, o1, lse1, do1, o2, lse2, do2, part, dh1_1, dh1_2, x, gb)
    dqkv_e, gt, sums_e, up_go = down.wait(dqkv_e, gt, sums_e, up_go)
    up = link.hops(up_keep, link.core(up_go))
    down.first_hop("z")
    small = jnp.stack([sums_e[0] + sums_o[0], sums1[0] + sums2[0], sums_e[1] + sums_o[1], sums1[1] + sums2[1], sums_o[2]])
    qkv_keep, qkv_go = grad_qkv(me_z, a_e, a_o, after(dqkv_e, *down.sent), dqkv_o)
    qkv_keep, qkv_go, down.got = up.wait(qkv_keep, qkv_go, down.got)
    qkv = link.hops(qkv_keep, link.core(qkv_go))
    small_steps = iter(link.small_steps())
    small_got = link.flip(after(small, qkv_go), next(small_steps))

    def wait_all(with_down=True):
        nonlocal small, small_got
        (qkv.got, small_got, *rest) = up.wait(qkv.got, small_got, *([down.got] if with_down else []))
        if rest:
            (down.got,) = rest
        if small_got is not None:
            small = small + small_got
            step = next(small_steps, None)
            small_got = None if step is None else link.flip(small, step)

    wait_all(False)
    up.first()
    qkv.first_hop("partner")
    down.hop("x")
    wait_all()
    up.hop("partner", "x")
    qkv.hop("z")
    down.hop("w")
    wait_all()
    up.hop("z", "partner")
    qkv.hop("x")
    down.back_first()
    half = gt.shape[0] // 2
    gt_got = [link.partner(after(gt[:half], *up.sent))]
    wait_all()
    up.last_hop()
    qkv.hop("w")
    down.joined()
    down.back("x")
    gt_got.append(link.partner(after(gt[half:], *up.sent)))
    (gt_got[0],) = up.wait(gt_got[0])
    wait_all()
    up.back_first()
    qkv.back_first()
    down.joined()
    down.back("z")
    (gt_got[1],) = up.wait(gt_got[1])
    wait_all()
    while small_got is not None:
        wait_all()
    up.joined(2)
    up.back("z", "x")
    qkv.joined()
    qkv.back("x")
    down.back_core()
    out, gt, *_ = link.finish(jnp.concatenate([out, out_two], axis=0), jnp.concatenate([out_got, out_last], axis=0), gt, jnp.concatenate(gt_got, axis=0))
    out, gt = up.wait(out, gt)
    wait_all()
    up.joined()
    up.back("x", "z")
    qkv.joined()
    qkv.back("z")
    (g_down,) = unpack("down", me_z, 0, after(down.keep, up.sent, qkv.sent))
    (g_down,) = unpack("down", me_z, 1, down.got, (g_down,))
    g_down, qkv.got = up.wait(g_down, qkv.got)
    up.back_core()
    qkv.back_core()
    g_up = unpack("up", me, 0, after(up.keep, qkv.sent))
    (g_qkv,) = unpack("qkv", me_z, 0, after(qkv.keep, g_up))
    (g_qkv,) = up.wait(g_qkv)
    g_up, g_out = unpack("up", me, 1, up.got, g_up)
    qkv.wait(g_up)
    (g_qkv,) = unpack("qkv", me_z, 1, qkv.got, (g_qkv,))
    return out, gt, (g_qkv, g_out, g_up, g_down), small


def shards(outer, tokens, segments, pass_embed, w_qkv, w_out, w_up, w_down, gain, bias, cotangent):
    ty = lax.axis_index("tensor")
    rows = tokens.shape[0] // 2
    width = tokens.shape[2]
    mine = lambda t: lax.dynamic_slice_in_dim(t, ty * rows, rows, 0)
    x = mine(tokens).reshape(-1, width)
    gb = jnp.concatenate([gain, bias, pass_embed[None]], axis=0)
    link = Link(outer, w_qkv, w_out, w_up, w_down)
    link.finish = lambda out, out_got, gt, gt_got: (
        ordered(ty, out, out_got).reshape(cotangent.shape),
        ordered(ty, gt, gt_got).reshape(tokens.shape).astype(F32),
    )
    out, gt, grads, small = local_part(x, mine(segments), mine(cotangent), gb, link)
    return out, gt, *grads, small[0:2], small[2:4], small[4]


def solution(mesh):
    outer = mesh.shape["dp"] // 4
    fine = Mesh(mesh.devices.reshape(outer, 2, 2, mesh.shape["tensor"]), ("o", "x", "core", "tensor"))
    rows = ROWS_OVER
    placed = (
        P(rows, None, None),
        P(rows, None),
        P(),
        P(None, None, "tensor"),
        P("tensor", None),
        P(None, "tensor"),
        P("tensor", None),
        P(),
        P(),
        P(rows, None, None),
    )

    def body(*args):
        return shards(outer, *args)

    return jax.shard_map(
        body,
        mesh=fine,
        in_specs=placed,
        out_specs=(
            P(rows, None, None),
            P(rows, None, None),
            P(None, None, "tensor"),
            P("tensor", None),
            P(None, "tensor"),
            P("tensor", None),
            P(),
            P(),
            P(),
        ),
        check_vma=False,
    )
```

```python
import functools

import jax
import jax.numpy as jnp
from jax import lax
from jax.experimental import pallas as pl
from jax.experimental.pallas import tpu as pltpu
from jax.sharding import Mesh
from jax.sharding import PartitionSpec as P

HD = 64
EPS = 1e-05
NEG = -1000000000.0
F32 = jnp.float32
BF16 = jnp.bfloat16
ROWS_OVER = ("o", "x", "core")
FLIP = ((0, 1), (1, 0))
VMEM_LIMIT = 16 * 1024 * 1024


def ordered(flag, mine, theirs):
    first = flag == 0
    return jnp.stack([jnp.where(first, mine, theirs), jnp.where(first, theirs, mine)])


def take_half(array, index):
    half = array.shape[0] // 2
    return lax.dynamic_slice_in_dim(array, index * half, half, 0)


def flip_bit(array, axis, size, bit):
    return lax.ppermute(array, axis, [(i, i ^ bit) for i in range(size)])


def steps_of(outer):
    steps = [("x", 2, 1)]
    bit = 1
    while bit < outer:
        steps.append(("o", outer, bit))
        bit *= 2
    return steps


def my_bit(axis, bit):
    return (lax.axis_index(axis) // bit) % 2


def dot(a, b):
    return lax.dot_general(a, b, (((1,), (0,)), ((), ())), preferred_element_type=F32)


def dot_nt(a, b):
    return lax.dot_general(a, b, (((1,), (1,)), ((), ())), preferred_element_type=F32)


def dot_tn(a, b):
    return lax.dot_general(a, b, (((0,), (0,)), ((), ())), preferred_element_type=F32)


def norm_stats(h):
    centred = h - jnp.mean(h, axis=-1, keepdims=True)
    inverse = lax.rsqrt(jnp.mean(centred * centred, axis=-1, keepdims=True) + EPS)
    return centred * inverse, inverse


def norm_back(grad, normal, inverse, gain):
    scaled = grad * gain
    centre = jnp.mean(scaled, axis=-1, keepdims=True)
    proj = jnp.mean(scaled * normal, axis=-1, keepdims=True)
    return inverse * (scaled - centre - normal * proj)


def gelu_parts(u):
    c = 0.7978845608028654
    a = 0.044715 * c
    square = u * u
    half = 0.5 + 0.5 * jnp.tanh(u * (c + a * square))
    g = u * half
    return g, half + g * (1.0 - half) * (2.0 * c + 6.0 * a * square)


def whole(shape):
    return pl.BlockSpec(shape, lambda *_: (0,) * len(shape))


def call(body, grid, ins, outs, scratch=(), cost=(0, 0), name=None, vmem=VMEM_LIMIT):
    return pl.pallas_call(
        body,
        grid=grid,
        in_specs=[s for _, s in ins],
        out_specs=[s for _, s in outs],
        out_shape=[a for a, _ in outs],
        scratch_shapes=scratch,
        compiler_params=pltpu.CompilerParams(
            dimension_semantics=("arbitrary",) * len(grid), vmem_limit_bytes=vmem
        ),
        cost_estimate=pl.CostEstimate(
            flops=int(cost[0]) // 16, bytes_accessed=int(cost[1]), transcendentals=0
        ),
        name=name,
    )(*[a for a, _ in ins])


FAR = pl.BlockSpec(memory_space=pl.ANY)


def resident(body, ins, outs, scratch=(), flops=0, vmem=16, aliases={}, name=None):
    spec = pl.BlockSpec(memory_space=pltpu.VMEM)
    ins, outs = ([o if isinstance(o, tuple) else (o, spec) for o in t] for t in (ins, outs))
    ins = [(pltpu.with_memory_space_constraint(a, pltpu.HBM) if s is FAR else a, s) for a, s in ins]
    outs = [(pltpu.HBM(a.shape, a.dtype) if s is FAR else a, s) for a, s in outs]
    return pl.pallas_call(
        body,
        in_specs=[s for _, s in ins],
        out_specs=[s for _, s in outs],
        out_shape=[a for a, _ in outs],
        scratch_shapes=scratch,
        input_output_aliases=aliases,
        compiler_params=pltpu.CompilerParams(vmem_limit_bytes=vmem * 1024 * 1024),
        cost_estimate=pl.CostEstimate(flops=int(flops) // 16, bytes_accessed=0, transcendentals=0),
        name=name,
    )(*[a for a, _ in ins])


def sds(shape, dtype):
    return jax.ShapeDtypeStruct(shape, dtype)


QB = 128
GROUP = 256


def lanes_of(ref, g):
    return ref.at[(slice(None),) * (len(ref.shape) - 1) + (pl.ds(pl.multiple_of(g * GROUP, GROUP), GROUP),)]


class Moves:
    def __init__(self, sems):
        self.sems, self.used = sems, 0

    def take(self, number):
        self.used += number
        return self.used - number

    def whole(self, source, target):
        copy = pltpu.make_async_copy(source, target, self.sems.at[self.take(1)])
        copy.start()
        return copy.wait

    def later(self, source, target):
        sem = self.sems.at[self.take(1)]
        copy = lambda: pltpu.make_async_copy(source, target, sem)
        return (lambda: copy().start()), (lambda: copy().wait())

    def groups(self, source, target):
        first = self.take(source.shape[-1] // GROUP)

        def copy(g):
            return pltpu.make_async_copy(lanes_of(source, g), lanes_of(target, g), self.sems.at[first + g])

        return (lambda g: copy(g).start()), (lambda g: copy(g).wait())


def cat_heads(t, scale=1.0):
    lane = lax.broadcasted_iota(jnp.int32, (1, 2 * HD), 1)
    parts = [t * jnp.where((lane < HD) == (h == 0), scale, 0.0).astype(t.dtype) for h in range(2)]
    return jnp.concatenate(parts, axis=0)


def own_lanes(t, scale=None):
    if scale is not None:
        t = t * scale
    return jnp.concatenate([t[:HD, :QB], t[HD:, QB:]], axis=0)


def twice(t):
    return jnp.concatenate([t, t], axis=1)


def pair_row(rows, p):
    return jnp.concatenate([rows[2 * p : 2 * p + 1], rows[2 * p + 1 : 2 * p + 2]], axis=1)


def put_pair(ref, p, cols, value):
    ref[2 * p : 2 * p + 1, cols] = value[:, :QB]
    ref[2 * p + 1 : 2 * p + 2, cols] = value[:, QB:]


def columns(t, r, seq, qb):
    return t[:, pl.ds(pl.multiple_of(r * seq + qb * QB, QB), QB)]


def rows_of(r, seq, qb):
    return pl.ds(pl.multiple_of(r * seq + qb * QB, QB), QB)


def in_turn(arrive, group, groups):
    for _, wait in arrive:
        wait(group)

    @pl.when(group + 2 < groups)
    def _():
        for start, _ in arrive:
            start(group + 2)


def attend_first_body(rows, seq, pairs, a_ref, w_ref, bias_ref, qkv_ref, o_ref, lse_ref):
    a = a_ref[...]
    for j in range(3):
        qkv_ref[j] = dot(a, w_ref[j]).astype(BF16)
    for r in range(rows):
        work = []
        for p in range(pairs):
            ln = slice(p * 2 * HD, (p + 1) * 2 * HD)
            k = qkv_ref[1, r * seq : (r + 1) * seq, ln]
            for b in range(seq // QB):
                sl, n = slice(r * seq + b * QB, r * seq + (b + 1) * QB), (b + 1) * QB
                q = cat_heads(qkv_ref[0, sl, ln], HD**-0.5)
                s = dot_nt(k[:n], q) + twice(bias_ref[r, :n, b * QB : n])
                work.append((p, ln, sl, n, s))
        done = []
        for p, ln, sl, n, s in work:
            top = jnp.max(s, axis=0, keepdims=True)
            e = jnp.exp(s - top)
            mass = jnp.sum(e, axis=0, keepdims=True)
            put_pair(lse_ref, p, sl, top + jnp.log(mass))
            done.append((e.astype(BF16), 1.0 / mass))
        for (p, ln, sl, n, _), (e, inv) in zip(work, done):
            vt = qkv_ref[2, r * seq : (r + 1) * seq, ln].T
            o_ref[sl, ln] = own_lanes(dot(vt[:, :n], e), inv).T.astype(BF16)


def attend_first(a, w, bias):
    rows, seq = bias.shape[0], bias.shape[1]
    n, d = a.shape
    f = w.shape[2]
    return resident(
        functools.partial(attend_first_body, rows, seq, f // (2 * HD)),
        (a, w, bias),
        [sds((3, n, f), BF16), sds((n, f), BF16), sds((f // HD, n), F32)],
        flops=6 * n * d * f + 16 * n * seq * f,
        name="attend_first",
    )


def attend_second_body(
    rows, seq, a_far, w_far, incl_far, strict_far, qkve_far, o1_far, lse1_ref,
    qkvo_far, o2_far, lse2_ref,
    a_ref, w_ref, incl_ref, strict_ref, qkve_ref, o1_ref, qkvo_ref, o2_ref, sems,
):
    groups = lse1_ref.shape[0]
    moves = Moves(sems)
    ready = [moves.whole(a_far, a_ref), moves.whole(w_far.at[0], w_ref.at[0])]
    arrive = [moves.groups(*t) for t in ((qkve_far, qkve_ref), (o1_far, o1_ref))]
    leave = moves.groups(o2_ref, o2_far)
    for wait in ready:
        wait()
    ready = [moves.whole(w_far.at[j], w_ref.at[j]) for j in (1, 2)]
    a = a_ref[...]
    sent = []
    for j in range(3):
        if j:
            ready[j - 1]()
        if j == 1:
            masks = [moves.whole(*t) for t in ((incl_far, incl_ref), (strict_far, strict_ref))]
            for g in range(2):
                for start, _ in arrive:
                    start(g)
        qkvo_ref[j] = dot(a, w_ref[j]).astype(BF16)
        sent.append(moves.whole(qkvo_ref.at[j], qkvo_far.at[j]))
    for wait in masks:
        wait()

    def next_group(group):
        in_turn(arrive, group, groups)

    def row(i, _):
        r, group = i % rows, i // rows
        lanes = pl.multiple_of(group * GROUP, GROUP)
        all_of = pl.ds(pl.multiple_of(r * seq, seq), seq)

        @pl.when(r == 0)
        def _():
            next_group(group)

        for p in range(GROUP // (2 * HD)):
            ln = pl.ds(lanes + p * 2 * HD, 2 * HD)
            ke, ko = qkve_ref[1, all_of, ln], qkvo_ref[1, all_of, ln]
            vte, vto = qkve_ref[2, all_of, ln].T, qkvo_ref[2, all_of, ln].T
            work = []
            for b in range(seq // QB):
                sl, n = rows_of(r, seq, b), (b + 1) * QB
                cols = slice(b * QB, n)
                incl, strict = twice(incl_ref[r, :n, cols]), twice(strict_ref[r, :n, cols])
                q = cat_heads(qkve_ref[0, sl, ln], HD**-0.5)
                work.append([dot_nt(ko[:n], q) + strict])
                q = cat_heads(qkvo_ref[0, sl, ln], HD**-0.5)
                work.append([dot_nt(ko[:n], q) + incl, dot_nt(ke[:n], q) + incl])
            for b in range(seq // QB):
                sl, n = rows_of(r, seq, b), (b + 1) * QB
                (s,), (so, se) = work[2 * b : 2 * b + 2]
                old = pair_row(lse1_ref[group, :, sl], p)
                top = jnp.maximum(old, jnp.max(s, axis=0, keepdims=True))
                e = jnp.exp(s - top)
                kept = jnp.exp(old - top)
                mass = kept + jnp.sum(e, axis=0, keepdims=True)
                work[2 * b] = (e.astype(BF16), kept, 1.0 / mass)
                put_pair(lse2_ref.at[0, group], p, sl, top + jnp.log(mass))
                top = jnp.max(jnp.maximum(se, so), axis=0, keepdims=True)
                ee, eo = jnp.exp(se - top), jnp.exp(so - top)
                mass = jnp.sum(ee + eo, axis=0, keepdims=True)
                work[2 * b + 1] = (ee.astype(BF16), eo.astype(BF16), 1.0 / mass)
                put_pair(lse2_ref.at[1, group], p, sl, top + jnp.log(mass))
            for b in range(seq // QB):
                sl, n = rows_of(r, seq, b), (b + 1) * QB
                (e, kept, inv), (ee, eo, inv2) = work[2 * b : 2 * b + 2]
                o1 = o1_ref[sl, ln].astype(F32).T
                o = own_lanes(dot(vto[:, :n], e), inv) + own_lanes(twice(o1), kept * inv)
                o2_ref[0, sl, ln] = o.T.astype(BF16)
                o = dot(vte[:, :n], ee) + dot(vto[:, :n], eo)
                o2_ref[1, sl, ln] = own_lanes(o, inv2).T.astype(BF16)

        @pl.when(r == rows - 1)
        def _():
            leave[0](group)

        return 0

    lax.fori_loop(0, rows * groups, row, 0)
    for wait in sent:
        wait()
    for g in range(groups):
        leave[1](g)


def attend_second(a, w, incl, strict, qkve, o1, lse1):
    rows, seq = incl.shape[0], incl.shape[1]
    n, d = a.shape
    f = w.shape[2]
    qkv, o2 = sds((3, n, f), BF16), sds((2, n, f), BF16)
    near = (a, w, incl, strict, qkve, o1, qkv, o2)
    return resident(
        functools.partial(attend_second_body, rows, seq),
        [(t, FAR) for t in (a, w, incl, strict, qkve, o1)] + [lse1],
        [(qkv, FAR), (o2, FAR), sds((2, *lse1.shape), F32)],
        scratch=[pltpu.VMEM(t.shape, t.dtype) for t in near] + [pltpu.SemaphoreType.DMA((64,))],
        flops=6 * n * d * f + 48 * n * seq * f,
        vmem=32,
        name="attend_second",
    )


def row_products(a, b):
    prod = cat_heads((a * b).astype(BF16))
    return dot_nt(jnp.ones((8, 2 * HD), BF16), prod)[:1]


def query_parts(sl, ln, group, p, i, qkv_ref, o_ref, lse_ref, do_ref):
    do = do_ref[i, sl, ln]
    delta = row_products(do.astype(F32), o_ref[i, sl, ln].astype(F32))
    return cat_heads(qkv_ref[0, sl, ln], HD**-0.5), cat_heads(do), pair_row(lse_ref[i, group, :, sl], p), delta


def blocks_back(tasks):
    scores = [dot_nt(k, q) + bias - lse for k, _, _, bias, q, _, lse, _ in tasks]
    moved = [dot_nt(v, do) - delta for _, v, _, _, _, do, _, delta in tasks]
    probs = [jnp.exp(s) for s in scores]
    ds = [(p * m).astype(BF16) for p, m in zip(probs, moved)]
    return [
        (dot(p.astype(BF16), do), dot(d, q), dot(kt, d))
        for (_, _, kt, _, q, do, _, _), p, d in zip(tasks, probs, ds)
    ]


def add_rows(total, part):
    if total is None:
        return part
    n = part.shape[0]
    return jnp.concatenate([total[:n] + part, total[n:]], axis=0)


def attend_back_body(
    rows, seq, w_far, incl_far, strict_far, qkve_far, qkvo_far, o2_far, lse2_ref, do_far,
    dh1_far, ho_far, gb_ref,
    dqkvo_far, dqkve_far, dy_far, sums_ref,
    w_ref, incl_ref, strict_ref, qkve_ref, qkvo_ref, o2_ref, do_ref, dh1_ref, ho_ref,
    dqkvo_ref, dqkve_ref, da_ref, dy_ref, sems,
):
    groups = lse2_ref.shape[1]
    moves = Moves(sems)
    arrive = [
        moves.groups(*t)
        for t in ((qkve_far, qkve_ref), (qkvo_far, qkvo_ref), (o2_far, o2_ref), (do_far, do_ref))
    ]
    leave = [moves.groups(*t) for t in ((dqkvo_ref, dqkvo_far), (dqkve_ref, dqkve_far))]
    for start, _ in arrive:
        start(0)
    masks = [moves.whole(*t) for t in ((incl_far, incl_ref), (strict_far, strict_ref))]
    for start, _ in arrive:
        start(1)
    odd = pl.ds(rows * seq, rows * seq)
    late = [moves.later(*t) for t in ((w_far, w_ref), (dh1_far.at[odd], dh1_ref), (ho_far, ho_ref))]
    for wait in masks:
        wait()

    def next_group(group):
        in_turn(arrive, group, groups)

        @pl.when(group == groups - 2)
        def _():
            for start, _ in late:
                start()

    sc = HD**-0.5

    def row(i, _):
        r, group = i % rows, i // rows
        lanes = pl.multiple_of(group * GROUP, GROUP)
        all_of = pl.ds(pl.multiple_of(r * seq, seq), seq)

        @pl.when(r == 0)
        def _():
            next_group(group)

        for p in range(GROUP // (2 * HD)):
            ln = pl.ds(lanes + p * 2 * HD, 2 * HD)
            ke, ve = qkve_ref[1, all_of, ln], qkve_ref[2, all_of, ln]
            ko, vo = qkvo_ref[1, all_of, ln], qkvo_ref[2, all_of, ln]
            kte, kto = ke.T, ko.T
            tasks = []
            for b in reversed(range(seq // QB)):
                sl, n = rows_of(r, seq, b), (b + 1) * QB
                cols = slice(b * QB, n)
                incl, strict = twice(incl_ref[r, :n, cols]), twice(strict_ref[r, :n, cols])
                even = query_parts(sl, ln, group, p, 0, qkve_ref, o2_ref, lse2_ref, do_ref)
                odd = query_parts(sl, ln, group, p, 1, qkvo_ref, o2_ref, lse2_ref, do_ref)
                tasks.append((ko[:n], vo[:n], kto[:, :n], strict, *even))
                tasks.append((ko[:n], vo[:n], kto[:, :n], incl, *odd))
                tasks.append((ke[:n], ve[:n], kte[:, :n], incl, *odd))
            done = blocks_back(tasks)
            dke = dve = dko = dvo = None
            for b in reversed(range(seq // QB)):
                sl = rows_of(r, seq, b)
                (dv, dk, dqe), (dv2, dk2, dqo), (dv3, dk3, dqo2) = done[:3]
                done = done[3:]
                dvo, dko = add_rows(dvo, dv + dv2), add_rows(dko, dk + dk2)
                dve, dke = add_rows(dve, dv3), add_rows(dke, dk3)
                dqkve_ref[0, sl, ln] = (own_lanes(dqe).T * sc).astype(BF16)
                dqkvo_ref[0, sl, ln] = (own_lanes(dqo + dqo2).T * sc).astype(BF16)
            dqkve_ref[1, all_of, ln] = dke.astype(BF16)
            dqkve_ref[2, all_of, ln] = dve.astype(BF16)
            dqkvo_ref[1, all_of, ln] = dko.astype(BF16)
            dqkvo_ref[2, all_of, ln] = dvo.astype(BF16)

        @pl.when(r == rows - 1)
        def _():
            for start, _ in leave:
                start(group)

        return 0

    lax.fori_loop(0, rows * groups, row, 0)
    for _, wait in late:
        wait()
    da = dot_nt(dqkvo_ref[0], w_ref[0])
    da += dot_nt(dqkvo_ref[1], w_ref[1])
    da += dot_nt(dqkvo_ref[2], w_ref[2])
    da_ref[...] = da
    sums_ref[...] = jnp.zeros_like(sums_ref)

    def finish(i, _):
        sl = pl.ds(pl.multiple_of(i * ROWS_AT_ONCE, ROWS_AT_ONCE), ROWS_AT_ONCE)
        normal, inverse = norm_stats(ho_ref[sl])
        da = da_ref[sl]
        dy = dh1_ref[sl] + norm_back(da, normal, inverse, gb_ref[0:1])
        dy_ref[sl] = dy
        for k, t in enumerate((da * normal, da, dy)):
            sums_ref[k : k + 1] += jnp.sum(t, axis=0, keepdims=True)
        return 0

    lax.fori_loop(0, rows * seq // ROWS_AT_ONCE, finish, 0)
    kept = [moves.whole(dy_ref, dy_far)]
    for g in range(groups):
        for _, wait in leave:
            wait(g)
    for wait in kept:
        wait()


def attend_back(w, incl, strict, qkve, qkvo, o2, lse2, do, dh1, ho, gb):
    rows, seq = incl.shape[0], incl.shape[1]
    n, d = ho.shape
    f = w.shape[2]
    do = do.reshape(2, n, f)
    qkv = sds((3, n, f), BF16)
    near = (w, incl, strict, qkve, qkvo, o2, do, sds((n, d), F32), ho, qkv, qkv, sds((n, d), F32))
    return resident(
        functools.partial(attend_back_body, rows, seq),
        [(t, FAR) for t in (w, incl, strict, qkve, qkvo, o2)]
        + [lse2]
        + [(t, FAR) for t in (do, dh1, ho)]
        + [gb],
        [(qkv, FAR), (qkv, FAR), (sds((n, d), F32), FAR), sds((3, d), F32)],
        scratch=[pltpu.VMEM(t.shape, t.dtype) for t in near + (sds((n, d), F32),)] + [pltpu.SemaphoreType.DMA((64,))],
        flops=6 * n * d * f + 120 * n * seq * f,
        vmem=44,
        name="attend_back",
    )


def attend_back_even_body(
    rows, seq, w_far, incl_far, qkve_far, o1_far, lse1_ref, do1_far, o2_far, lse2_ref, do2_far,
    part_far, dh1_far, dh2_far, x_far, gb_ref,
    dqkv_far, gt_ref, sums_ref,
    w_ref, incl_ref, qkve_ref, o1_ref, do1_ref, o2_ref, do2_ref, part_ref, dh1_ref, dh2_ref, x_ref,
    dqkv_ref, da_ref, sems,
):
    groups = lse1_ref.shape[0]
    moves = Moves(sems)
    even = pl.ds(0, rows * seq)
    arrive = [
        moves.groups(*t)
        for t in (
            (qkve_far, qkve_ref), (o1_far, o1_ref), (do1_far, do1_ref), (o2_far.at[0], o2_ref),
            (do2_far.at[0], do2_ref), (part_far, part_ref),
        )
    ]
    leave = [moves.groups(dqkv_ref, dqkv_far)]
    for start, _ in arrive:
        start(0)
    mask = moves.whole(incl_far, incl_ref)
    for start, _ in arrive:
        start(1)
    late = [
        moves.later(*t)
        for t in ((w_far, w_ref), (dh1_far, dh1_ref), (dh2_far.at[even], dh2_ref), (x_far, x_ref))
    ]
    mask()

    def next_group(group):
        in_turn(arrive, group, groups)

        @pl.when(group == groups - 2)
        def _():
            for start, _ in late:
                start()

    sc = HD**-0.5

    def row(i, _):
        r, group = i % rows, i // rows
        lanes = pl.multiple_of(group * GROUP, GROUP)
        all_of = pl.ds(pl.multiple_of(r * seq, seq), seq)

        @pl.when(r == 0)
        def _():
            next_group(group)

        for p in range(GROUP // (2 * HD)):
            ln = pl.ds(lanes + p * 2 * HD, 2 * HD)
            k, v = qkve_ref[1, all_of, ln], qkve_ref[2, all_of, ln]
            kt = k.T
            tasks = []
            for b in reversed(range(seq // QB)):
                sl, n = rows_of(r, seq, b), (b + 1) * QB
                incl = twice(incl_ref[r, :n, b * QB : n])
                lse1 = pair_row(lse1_ref[group, :, sl], p)
                ratio = jnp.exp(lse1 - pair_row(lse2_ref[0, group, :, sl], p))
                do1, do2 = do1_ref[sl, ln].astype(F32), do2_ref[sl, ln].astype(F32)
                delta = row_products(do1, o1_ref[sl, ln].astype(F32))
                delta += ratio * row_products(do2, o2_ref[sl, ln].astype(F32))
                both = do1 + own_lanes(twice(do2.T), ratio).T
                q, do = cat_heads(qkve_ref[0, sl, ln], sc), cat_heads(both.astype(BF16))
                tasks.append((k[:n], v[:n], kt[:, :n], incl, q, do, lse1, delta))
            dka = dva = None
            for b, (dv, dk, dq) in zip(reversed(range(seq // QB)), blocks_back(tasks)):
                sl = rows_of(r, seq, b)
                dva, dka = add_rows(dva, dv), add_rows(dka, dk)
                dqkv_ref[0, sl, ln] = (own_lanes(dq).T * sc + part_ref[0, sl, ln].astype(F32)).astype(BF16)
            dqkv_ref[1, all_of, ln] = (dka + part_ref[1, all_of, ln].astype(F32)).astype(BF16)
            dqkv_ref[2, all_of, ln] = (dva + part_ref[2, all_of, ln].astype(F32)).astype(BF16)

        @pl.when(r == rows - 1)
        def _():
            for start, _ in leave:
                start(group)

        return 0

    lax.fori_loop(0, rows * groups, row, 0)
    for _, wait in late:
        wait()
    da = dot_nt(dqkv_ref[0], w_ref[0])
    da += dot_nt(dqkv_ref[1], w_ref[1])
    da += dot_nt(dqkv_ref[2], w_ref[2])
    da_ref[...] = da
    sums_ref[...] = jnp.zeros_like(sums_ref)

    def finish(i, _):
        sl = pl.ds(pl.multiple_of(i * ROWS_AT_ONCE, ROWS_AT_ONCE), ROWS_AT_ONCE)
        normal, inverse = norm_stats(x_ref[sl].astype(F32))
        da = da_ref[sl]
        sums_ref[0:1] += jnp.sum(da * normal, axis=0, keepdims=True)
        sums_ref[1:2] += jnp.sum(da, axis=0, keepdims=True)
        back = norm_back(da, normal, inverse, gb_ref[0:1])
        gt_ref[sl] = (dh1_ref[sl] + dh2_ref[sl] + back).astype(BF16)
        return 0

    lax.fori_loop(0, rows * seq // ROWS_AT_ONCE, finish, 0)
    for g in range(groups):
        for _, wait in leave:
            wait(g)


def attend_back_even(w, incl, qkve, o1, lse1, do1, o2, lse2, do2, part, dh1, dh2, x, gb):
    rows, seq = incl.shape[0], incl.shape[1]
    n, d = x.shape
    f = w.shape[2]
    qkv, one = sds((3, n, f), BF16), sds((n, f), BF16)
    near = (w, incl, qkv, one, one, one, one, qkv, dh1, dh1, x, qkv, sds((n, d), F32))
    far = lambda *ts: [(t, FAR) for t in ts]
    return resident(
        functools.partial(attend_back_even_body, rows, seq),
        far(w, incl, qkve, o1)
        + [lse1]
        + far(do1, o2)
        + [lse2]
        + far(do2.reshape(2, n, f), part, dh1, dh2, x)
        + [gb],
        [(qkv, FAR), sds((n, d), BF16), sds((2, d), F32)],
        scratch=[pltpu.VMEM(t.shape, t.dtype) for t in near] + [pltpu.SemaphoreType.DMA((64,))],
        flops=6 * n * d * f + 40 * n * seq * f,
        vmem=40,
        name="attend_back_even",
    )


CHUNK = 512
ROWS_AT_ONCE = 256


def chunk_of(ref, j, axis):
    at = pl.ds(pl.multiple_of(j * CHUNK, CHUNK), CHUNK)
    return ref.at[:, at] if axis else ref.at[at]


class Chunks:
    def __init__(self, moves, far, near, axis, ring=False, leave=False):
        self.first = moves.take(far.shape[axis] // CHUNK)
        self.sems, self.far, self.near = moves.sems, far, near
        self.axis, self.ring, self.leave = axis, ring, leave

    def copy(self, j):
        near = self.near.at[j % self.near.shape[0]] if self.ring else chunk_of(self.near, j, self.axis)
        ends = (chunk_of(self.far, j, self.axis), near)
        return pltpu.make_async_copy(*(ends[::-1] if self.leave else ends), self.sems.at[self.first + j])

    def start(self, j):
        self.copy(j).start()

    def wait(self, j):
        self.copy(j).wait()


class Weight:
    def __init__(self, moves, pieces, near, axis):
        self.axis, self.near = axis, near
        self.own = Chunks(moves, pieces[0], near, axis) if pieces[0] is not None else None
        self.number = near.shape[axis] // CHUNK // 2
        self.others, start = [], near.shape[axis] // 2
        for far in pieces[1:]:
            at = pl.ds(start, far.shape[axis])
            self.others.append(moves.later(far, near.at[:, at] if axis else near.at[at]))
            start += far.shape[axis]

    def start_others(self):
        for start, _ in self.others:
            start()

    def wait_others(self):
        for _, wait in self.others:
            wait()


def load_in_turn(j, *weights):
    number = weights[0].number

    @pl.when(j < number)
    def _():
        for w in weights:
            w.own.wait(j)

    @pl.when(j + 2 < number)
    def _():
        for w in weights:
            w.own.start(j + 2)

    @pl.when(j + 2 == number)
    def _():
        for w in weights:
            w.start_others()

    @pl.when(j == number)
    def _():
        for w in weights:
            w.wait_others()


def start_loads(*weights):
    for j in range(2):
        for w in weights:
            w.own.start(j)


def feed_chunk(n2_ref, wup_ref, wdown_ref, j, g_buf, d_buf, ho_ref, gs, ds, first):
    @pl.when(first >= 2)
    def _():
        gs.wait(j - 2)
        ds.wait(j - 2)

    half = n2_ref.shape[0] // 2
    parts = []
    for sl in (slice(0, half), slice(half, 2 * half)):
        g, d = gelu_parts(dot(n2_ref[sl], chunk_of(wup_ref, j, 1)[...]))
        parts.append(g.astype(BF16))
        g_buf[j % 2, sl] = parts[-1]
        d_buf[j % 2, sl] = d.astype(BF16)
    gs.start(j)
    ds.start(j)
    for i, g in enumerate(parts):
        ho_ref[i * half : (i + 1) * half] += dot(g, chunk_of(wdown_ref, j, 0)[...])


def start_norm(x_ref, h1_ref, n2_ref, gb_ref, ho_ref=None):
    def part(k, _):
        sl = pl.ds(pl.multiple_of(k * ROWS_AT_ONCE, ROWS_AT_ONCE), ROWS_AT_ONCE)
        h1 = x_ref[sl].astype(F32) + h1_ref[sl]
        h1_ref[sl] = h1
        normal, _ = norm_stats(h1)
        n2_ref[sl] = (normal * gb_ref[1:2] + gb_ref[3:4]).astype(BF16)
        if ho_ref is not None:
            ho_ref[sl] = h1 + gb_ref[4:5]
        return 0

    lax.fori_loop(0, h1_ref.shape[0] // ROWS_AT_ONCE, part, 0)


def mlp_own_body(
    x_far, o_far, wout_far, gb_ref, wup_far, wdown_far,
    h1_far, n2_far, g_far, d_far, ho_far,
    x_ref, o_ref, wout_ref, wup_ref, wdown_ref, h1_ref, n2_ref, ho_ref, g_buf, d_buf, sems,
):
    moves = Moves(sems)
    first = [moves.whole(*t) for t in ((o_far, o_ref), (wout_far, wout_ref), (x_far, x_ref))]
    ups, downs = Chunks(moves, wup_far, wup_ref, 1), Chunks(moves, wdown_far, wdown_ref, 0)
    gs, ds = (Chunks(moves, f, b, 1, True, True) for f, b in ((g_far, g_buf), (d_far, d_buf)))
    number = wup_far.shape[1] // CHUNK
    for wait in first:
        wait()
    for j in range(number):
        ups.start(j)
        downs.start(j)
    h1_ref[...] = dot(o_ref[...], wout_ref[...])
    start_norm(x_ref, h1_ref, n2_ref, gb_ref, ho_ref)
    kept = [moves.whole(*t) for t in ((h1_ref, h1_far), (n2_ref, n2_far))]

    def step(j, _):
        ups.wait(j)
        downs.wait(j)
        feed_chunk(n2_ref, wup_ref, wdown_ref, j, g_buf, d_buf, ho_ref, gs, ds, j)
        return 0

    lax.fori_loop(0, number, step, 0)
    kept.append(moves.whole(ho_ref, ho_far))
    for wait in kept:
        wait()
    for j in range(number - 2, number):
        gs.wait(j)
        ds.wait(j)


def mlp_other_body(number_up, number_down, n2_far, part_far, g_in, d_in, gb_ref, *refs):
    ups_far, refs = refs[:number_up], refs[number_up:]
    downs_far, refs = refs[:number_down], refs[number_down:]
    g_far, d_far, ho_far, ao_far, n2_ref, wup_ref, wdown_ref, ho_ref, ao_ref, g_buf, d_buf, sems = refs
    moves = Moves(sems)
    up = Weight(moves, (None,) + ups_far, wup_ref, 1)
    down = Weight(moves, (None,) + downs_far, wdown_ref, 0)
    gs, ds = (Chunks(moves, f, b, 1, True, True) for f, b in ((g_far, g_buf), (d_far, d_buf)))
    ready = [moves.whole(*t) for t in ((n2_far, n2_ref), (part_far, ho_ref))]
    up.start_others()
    down.start_others()
    for wait in ready:
        wait()
    up.wait_others()
    down.wait_others()

    def step(i, _):
        feed_chunk(n2_ref, wup_ref, wdown_ref, up.number + i, g_buf, d_buf, ho_ref, gs, ds, i)
        return 0

    lax.fori_loop(0, up.number, step, 0)
    sent = moves.whole(ho_ref, ho_far)

    def norm(k, _):
        sl = pl.ds(pl.multiple_of(k * ROWS_AT_ONCE, ROWS_AT_ONCE), ROWS_AT_ONCE)
        normal, _ = norm_stats(ho_ref[sl])
        ao_ref[sl] = (normal * gb_ref[0:1] + gb_ref[2:3]).astype(BF16)
        return 0

    lax.fori_loop(0, ho_ref.shape[0] // ROWS_AT_ONCE, norm, 0)
    moves.whole(ao_ref, ao_far)()
    sent()
    for j in range(2 * up.number - 2, 2 * up.number):
        gs.wait(j)
        ds.wait(j)


def near_of(*arrays):
    return [pltpu.VMEM(t.shape, t.dtype) for t in arrays]


def far_of(*arrays):
    return [(t, FAR) for t in arrays]


def mlp_own(x, o, wout, gb, wup, wdown):
    n, d = x.shape
    ff = 2 * wup.shape[1]
    h1, low, wide = sds((n, d), F32), sds((n, d), BF16), sds((n, ff), BF16)
    return resident(
        mlp_own_body,
        far_of(x, o, wout) + [gb] + far_of(wup, wdown),
        far_of(h1, low, wide, wide, h1),
        scratch=near_of(x, o, wout, wup, wdown, h1, low, h1)
        + [pltpu.VMEM((2, n, CHUNK), BF16)] * 2
        + [pltpu.SemaphoreType.DMA((40,))],
        vmem=36,
        name="mlp_own",
    )


def mlp_other(n2, part, g, dgelu, gb, ups, downs):
    n, d = n2.shape
    ff = g.shape[1]
    return resident(
        functools.partial(mlp_other_body, len(ups), len(downs)),
        far_of(n2, part, g, dgelu) + [gb] + far_of(*ups, *downs),
        far_of(sds(g.shape, BF16), sds(g.shape, BF16), sds(part.shape, F32), sds(n2.shape, BF16)),
        scratch=near_of(n2, sds((d, ff), BF16), sds((ff, d), BF16), part, n2)
        + [pltpu.VMEM((2, n, CHUNK), BF16)] * 2
        + [pltpu.SemaphoreType.DMA((40,))],
        vmem=40,
        aliases={2: 0, 3: 1},
        name="mlp_other",
    )


def weave(seq):
    i = lax.broadcasted_iota(jnp.int32, (2 * seq, 2 * seq), 0)
    k = lax.broadcasted_iota(jnp.int32, (2 * seq, 2 * seq), 1)
    place = jnp.where(k < seq, 2 * k, 2 * (k - seq) + 1)
    return jnp.where(i == place, 1.0, 0.0).astype(BF16)


def after_norm_back(
    moves, size, h1_ref, dn_ref, db_ref, wout_ref, gb_ref, sums_ref, dp_ref, do_ref, dh1_far, dp_far, do_far
):
    gain_sum = jnp.zeros_like(gb_ref[0:1])
    bias_sum = jnp.zeros_like(gb_ref[0:1])
    waits = []
    for i in range(h1_ref.shape[0] // size):
        sl = slice(i * size, (i + 1) * size)
        normal, inverse = norm_stats(h1_ref[sl])
        dn = dn_ref[sl]
        gain_sum += jnp.sum(dn * normal, axis=0, keepdims=True)
        bias_sum += jnp.sum(dn, axis=0, keepdims=True)
        dh1 = db_ref[sl].astype(F32) + norm_back(dn, normal, inverse, gb_ref[1:2])
        dn_ref[sl] = dh1
        dp_ref[sl] = dh1.astype(BF16)
    sums_ref[0:1] = gain_sum
    sums_ref[1:2] = bias_sum
    waits += [moves.whole(dn_ref, dh1_far), moves.whole(dp_ref, dp_far)]
    do_ref[...] = dot_nt(dp_ref[...], wout_ref[...]).astype(BF16)
    return waits + [moves.whole(do_ref, do_far)]


def mlp_second_body(rows, seq, number_up, number_down, x_far, ho_far, o_far, cot_far, wout_far, gb_ref, *refs):
    mlp_second_work(rows, seq, x_far, ho_far, o_far, cot_far, wout_far, gb_ref, *in_pieces(refs, number_up, number_down))


def in_pieces(refs, *numbers):
    out = []
    for k in numbers:
        out.append(refs[:k])
        refs = refs[k:]
    return out + list(refs)


def mlp_second_work(
    rows, seq, x_far, ho_far, o_far, cot_far, wout_far, gb_ref, ups_far, downs_far,
    outs_far, outs2_far, n2_far, g_far, du_far, dh1_far, dp_far, do_far, sums_ref, dm_far,
    x_ref, ho_ref, o_ref, cot_ref, wout_ref, wup_ref, wdown_ref, n2_ref, dm_ref,
    h1_ref, z_ref, dn_ref, dp_ref, do_ref, g_buf, du_buf, sems,
):
    n = rows * seq
    moves = Moves(sems)
    halves = (slice(0, n), slice(n, 2 * n))
    cot_there = moves.whole(cot_far, cot_ref)
    first = [moves.whole(*t) for t in ((o_far, o_ref), (wout_far, wout_ref), (x_far, x_ref))]
    up, down = Weight(moves, ups_far, wup_ref, 1), Weight(moves, downs_far, wdown_ref, 0)
    gs, dus = (Chunks(moves, f, b, 1, True, True) for f, b in ((g_far, g_buf), (du_far, du_buf)))
    number = 2 * up.number
    mix = weave(seq)
    cot_there()
    for r in range(rows):
        parted = dot_tn(mix, cot_ref[r]).astype(BF16)
        for i in range(2):
            dm_ref[i * n + r * seq : i * n + (r + 1) * seq] = parted[i * seq : (i + 1) * seq]
    for wait in first:
        wait()
    then = moves.whole(ho_far, ho_ref)
    start_loads(up, down)
    for i, sl in enumerate(halves):
        if i:
            then()
        h1_ref[sl] = dot(o_ref[i], wout_ref[...])
        start_norm(x_ref if i == 0 else ho_ref, h1_ref.at[pl.ds(i * n, n)], n2_ref.at[pl.ds(i * n, n)], gb_ref)
    kept = [moves.whole(*t) for t in ((n2_ref, n2_far), (dm_ref, dm_far))]
    z_ref[...] = jnp.zeros_like(z_ref)
    dn_ref[...] = jnp.zeros_like(dn_ref)

    def step(j, _):
        load_in_turn(j, up, down)

        @pl.when(j >= 2)
        def _():
            gs.wait(j - 2)
            dus.wait(j - 2)

        for sl in halves:
            u = dot(n2_ref[sl], chunk_of(wup_ref, j, 1)[...])
            dg = dot_nt(dm_ref[sl], chunk_of(wdown_ref, j, 0)[...])
            g, d = gelu_parts(u)
            g = g.astype(BF16)
            du = (dg * d).astype(BF16)
            g_buf[j % 2, sl] = g
            du_buf[j % 2, sl] = du
            z_ref[sl] += dot(g, chunk_of(wdown_ref, j, 0)[...])
            dn_ref[sl] += dot_nt(du, chunk_of(wup_ref, j, 1)[...])
        gs.start(j)
        dus.start(j)
        return 0

    lax.fori_loop(0, number, step, 0)
    for r in range(rows):
        pair = [slice(i * n + r * seq, i * n + (r + 1) * seq) for i in range(2)]
        z = jnp.concatenate([(h1_ref[s] + z_ref[s]).astype(BF16) for s in pair], axis=0)
        cot_ref[r] = dot(mix, z).astype(BF16)
    half = rows // 2
    kept += [moves.whole(cot_ref.at[pl.ds(i * half, half)], far) for i, far in enumerate((outs_far, outs2_far))]
    kept += after_norm_back(
        moves, seq, h1_ref, dn_ref, dm_ref, wout_ref, gb_ref, sums_ref, dp_ref, do_ref, dh1_far, dp_far, do_far
    )
    for wait in kept:
        wait()
    for j in range(number - 2, number):
        gs.wait(j)
        dus.wait(j)


def mlp_second(x, ho, o2, cot, wout, gb, ups, downs, seq):
    n, d = x.shape
    ff = 2 * ups[0].shape[1]
    rows = n // seq
    low, wide, full = sds((2 * n, d), BF16), sds((2 * n, ff), BF16), sds((2 * n, d), F32)
    out = sds((rows // 2, 2 * seq, d), BF16)
    return resident(
        functools.partial(mlp_second_body, rows, seq, len(ups), len(downs)),
        far_of(x, ho, o2, cot, wout) + [gb] + far_of(*ups, *downs),
        far_of(out, out, low, wide, wide, full, low, low) + [sds((2, d), F32)] + far_of(low),
        scratch=near_of(x, ho, o2, cot, wout, sds((d, ff), BF16), sds((ff, d), BF16), low, low, full, full, full, low, low)
        + [pltpu.VMEM((2, 2 * n, CHUNK), BF16)] * 2
        + [pltpu.SemaphoreType.DMA((64,))],
        vmem=60,
        name="mlp_second",
    )


def mlp_back_body(rows, seq, number_up, number_down, dy_far, h1_far, wout_far, gb_ref, d_far, *refs):
    mlp_back_work(rows, seq, dy_far, h1_far, wout_far, gb_ref, d_far, *in_pieces(refs, number_up, number_down))


def mlp_back_work(
    rows, seq, dy_far, h1_far, wout_far, gb_ref, d_far, ups_far, downs_far,
    du_far, dh1_far, dp_far, do_far, sums_ref,
    dy_ref, h1_ref, wout_ref, wup_ref, wdown_ref, d_ref, dm_ref, dn_ref, dp_ref, do_ref, du_buf, sems,
):
    moves = Moves(sems)
    first = moves.whole(dy_far, dy_ref)
    up, down = Weight(moves, ups_far, wup_ref, 1), Weight(moves, downs_far, wdown_ref, 0)
    ds, dus = Chunks(moves, d_far, d_ref, 1), Chunks(moves, du_far, du_buf, 1, True, True)
    number = 2 * up.number
    start_loads(down, up)
    for j in range(2):
        ds.start(j)
    then = [moves.later(*t) for t in ((wout_far, wout_ref), (h1_far, h1_ref))]
    first()
    dm_ref[...] = dy_ref[...].astype(BF16)
    dn_ref[...] = jnp.zeros_like(dn_ref)

    def step(j, _):
        load_in_turn(j, down, up)
        ds.wait(j)

        @pl.when(j + 2 < number)
        def _():
            ds.start(j + 2)

        @pl.when(j + 2 == number)
        def _():
            for start, _ in then:
                start()

        @pl.when(j >= 2)
        def _():
            dus.wait(j - 2)

        dg = dot_nt(dm_ref[...], chunk_of(wdown_ref, j, 0)[...])
        du = (dg * chunk_of(d_ref, j, 1)[...].astype(F32)).astype(BF16)
        du_buf[j % 2] = du
        dus.start(j)
        dn_ref[...] += dot_nt(du, chunk_of(wup_ref, j, 1)[...])
        return 0

    lax.fori_loop(0, number, step, 0)
    for _, wait in then:
        wait()
    kept = after_norm_back(
        moves, seq, h1_ref, dn_ref, dy_ref, wout_ref, gb_ref, sums_ref, dp_ref, do_ref, dh1_far, dp_far, do_far
    )
    for wait in kept:
        wait()
    for j in range(number - 2, number):
        dus.wait(j)


def mlp_back(dy, h1, wout, gb, dgelu, ups, downs, seq):
    n, d = dy.shape
    ff = dgelu.shape[1]
    low = sds((n, d), BF16)
    return resident(
        functools.partial(mlp_back_body, n // seq, seq, len(ups), len(downs)),
        far_of(dy, h1, wout) + [gb] + far_of(dgelu, *ups, *downs),
        far_of(dgelu, h1, low, low) + [sds((2, d), F32)],
        scratch=near_of(dy, h1, wout, sds((d, ff), BF16), sds((ff, d), BF16), dgelu, low, dy, low, low)
        + [pltpu.VMEM((2, n, CHUNK), BF16)]
        + [pltpu.SemaphoreType.DMA((48,))],
        vmem=48,
        name="mlp_back",
    )


def lanes_at(ref, start, size):
    return ref.at[:, pl.ds(pl.multiple_of(start, 128), size)]


def stack_rows(moves, pairs, target, start, size):
    copies, row = [], 0
    for far in pairs:
        copies.append(moves.later(lanes_at(far, start, size), target.at[pl.ds(row, far.shape[0])]))
        row += far.shape[0]
    return (lambda: [s() for s, _ in copies]), (lambda: [w() for _, w in copies])


def all_of(*parts):
    return (lambda: [s() for s, _ in parts]), (lambda: [w() for _, w in parts])


class InTurn:
    def __init__(self, *tiles):
        self.tiles, self.at = tiles, 0
        for start, _ in tiles[:2]:
            start()

    def next(self):
        self.tiles[self.at][1]()
        self.at += 1
        if self.at + 1 < len(self.tiles):
            self.tiles[self.at + 1][0]()


def place_of(quarter, y, me_ref):
    return quarter if y else 4 + (quarter ^ me_ref[1])


def packed(body, me, arrays, shape, scratch, flops, vmem, name):
    smem = pl.BlockSpec(memory_space=pltpu.SMEM)
    out = sds(shape, BF16)
    return resident(
        body,
        [(me, smem)] + far_of(*arrays),
        far_of(out, out),
        scratch=near_of(sds((2,) + shape, BF16)) + scratch + [pltpu.SemaphoreType.DMA((64,))],
        flops=flops,
        vmem=vmem,
        name=name,
    )


def grad_down_body(
    me_ref, g1_far, g2_far, dy_far, dm2_far, keep_far, go_far, out_ref, dy_ref, dm_ref, g_ref, acc_ref, sems
):
    low, group = me_ref[0] % 4, (me_ref[0] // 4) % 2
    ring, n, b = g_ref.shape[0], g1_far.shape[0], g_ref.shape[2]
    moves = Moves(sems)
    first, last = moves.take(2 * ring), moves.take(4)

    def tile(i):
        side, y, h = 1 - i // 4, (i // 2) % 2, i % 2
        quarter = ((me_ref[0] // 8) ^ side) * 2 + h
        at = jnp.where(y == 0, 4 + (quarter ^ me_ref[1]), quarter) * b
        return side, y, h, at

    def loads(i):
        at, slot = tile(i)[3], i % ring
        near = g_ref.at[slot]
        ends = ((g1_far, near.at[pl.ds(0, n)]), (g2_far, near.at[pl.ds(n, 2 * n)]))
        return [pltpu.make_async_copy(lanes_at(f, at, b), t, sems.at[first + 2 * slot + k]) for k, (f, t) in enumerate(ends)]

    def store(far, side, y):
        return pltpu.make_async_copy(out_ref.at[side, y], far.at[y], sems.at[last + side * 2 + y])

    ready = [moves.whole(dy_far, dy_ref), moves.whole(dm2_far, dm_ref.at[pl.ds(n, 2 * n)])]
    for i in range(2):
        for c in loads(i):
            c.start()
    for wait in ready:
        wait()
    dm_ref[:n] = dy_ref[...].astype(BF16)

    def step(i, _):
        side, y, h, _ = tile(i)
        for c in loads(i):
            c.wait()

        @pl.when(i + 2 < 8)
        def _():
            for c in loads(i + 2):
                c.start()

        acc_ref[...] = dot_tn(g_ref[i % ring], dm_ref[...]).reshape(acc_ref.shape)
        for s in range(4):
            out_ref[side, y, (h ^ group) * 4 + s] = acc_ref[s ^ low].astype(BF16)

        @pl.when((h == 1) & (side == 1))
        def _():
            store(go_far, 1, y).start()

        @pl.when((h == 1) & (side == 0))
        def _():
            store(keep_far, 0, y).start()

        return 0

    lax.fori_loop(0, 8, step, 0)
    for y in range(2):
        store(go_far, 1, y).wait()
        store(keep_far, 0, y).wait()


def grad_down(me, g1, g2, dy, dm2):
    n, d = dy.shape
    ff = g1.shape[1]
    b = ff // 8
    return packed(
        grad_down_body,
        me,
        (g1, g2, dy, dm2),
        (2, 8, b // 4, d),
        [
            pltpu.VMEM((n, d), F32),
            pltpu.VMEM((3 * n, d), BF16),
            pltpu.VMEM((3, 3 * n, b), BF16),
            pltpu.VMEM((4, b // 4, d), F32),
        ],
        2 * 3 * n * d * ff,
        40,
        "grad_down",
    )


CUT = 768
CUT_BACK = 1536


def swapped(s):
    return ((s >> 1) % 2) * 4 + ((s >> 2) % 2) * 2 + s % 2


def put_slots(out_ref, y, lanes, acc_ref, me):
    for s in range(16):
        out_ref[s // 8, y, s % 8, :, lanes] = acc_ref[s ^ me].astype(BF16)


def grad_up_body(
    me_ref, n1_far, n2_far, du1_far, du2_far, dp1_far, dp2_far, o1_far, o2_far, keep_far, go_far,
    out_ref, n_ref, t_ref, du_ref, dp_ref, o_ref, acc_ref, acc2_ref, sems,
):
    moves = Moves(sems)
    d, f = n_ref.shape[1], o_ref.shape[2]
    ring, c, n = du_ref.shape[0], du_ref.shape[2], du1_far.shape[0]
    first, last = moves.take(4 * ring), moves.take(4)

    def loads(i):
        y, t, slot = i // 2, i % 2, i % ring
        copies = []
        for k in range(2):
            quarter = 2 * t + k
            at = jnp.where(y == 0, 4 + (quarter ^ me_ref[1]), quarter) * f
            near = lanes_at(du_ref.at[slot], k * f, f)
            for far, rows in ((du1_far, pl.ds(0, n)), (du2_far, pl.ds(n, 2 * n))):
                copies.append((lanes_at(far, at, f), near.at[rows]))
        return [pltpu.make_async_copy(a, b, sems.at[first + 4 * slot + k]) for k, (a, b) in enumerate(copies)]

    def stores(y):
        return [
            pltpu.make_async_copy(out_ref.at[i, y], far.at[y], sems.at[last + 2 * y + i])
            for i, far in enumerate((keep_far, go_far))
        ]

    ready = stack_rows(moves, (n1_far, n2_far), n_ref, 0, d)
    ready[0]()
    for c0 in loads(0):
        c0.start()
    out_loads = [stack_rows(moves, (dp1_far, dp2_far), dp_ref, 0, d)]
    out_loads += [stack_rows(moves, (o1_far, o2_far), o_ref.at[y], (1 - y) * f, f) for y in range(2)]
    ready[1]()
    for c0 in loads(1):
        c0.start()
    t_ref[...] = n_ref[...].T

    def step(i, _):
        y, t = i // 2, i % 2
        for c0 in loads(i):
            c0.wait()

        @pl.when(i + 2 < 4)
        def _():
            for c0 in loads(i + 2):
                c0.start()

        @pl.when(i == 0)
        def _():
            for start, _ in out_loads:
                start()

        acc_ref[...] = dot(t_ref[...], du_ref[i % ring]).reshape(acc_ref.shape)
        put_slots(out_ref, y, pl.ds(pl.multiple_of(t * c, c), c), acc_ref, jnp.where(t == 0, me_ref[0], me_ref[2]))

        @pl.when(i == 1)
        def _():
            for _, wait in out_loads:
                wait()

        @pl.when(t == 1)
        def _():
            acc2_ref[...] = dot_tn(dp_ref[...], o_ref[y]).reshape(acc2_ref.shape)
            put_slots(out_ref, y, slice(2 * c, 2 * c + f), acc2_ref, me_ref[2])
            for s in stores(y):
                s.start()

        return 0

    lax.fori_loop(0, 4, step, 0)
    for y in range(2):
        for s in stores(y):
            s.wait()


def grad_up(me, n1, n2, du1, du2, dp1, dp2, o1, o2):
    n, d = n1.shape
    ff = du1.shape[1]
    f, c = o1.shape[1] // 2, ff // 4
    return packed(
        grad_up_body,
        me,
        (n1, n2, du1, du2, dp1, dp2, o1, o2),
        (2, 8, d // 16, 2 * c + f),
        [
            pltpu.VMEM((3 * n, d), BF16),
            pltpu.VMEM((d, 3 * n), BF16),
            pltpu.VMEM((3, 3 * n, c), BF16),
            pltpu.VMEM((3 * n, d), BF16),
            pltpu.VMEM((2, 3 * n, f), BF16),
            pltpu.VMEM((16, d // 16, c), F32),
            pltpu.VMEM((16, d // 16, f), F32),
        ],
        2 * 3 * n * d * (ff + d),
        56,
        "grad_up",
    )


def grad_qkv_body(me_ref, ae_far, ao_far, de_far, do_far, keep_far, go_far, out_ref, a_ref, t_ref, d_ref, acc_ref, sems):
    moves = Moves(sems)
    d = a_ref.shape[1]
    f = de_far.shape[2] // 2
    ready = stack_rows(moves, (ae_far, ao_far), a_ref, 0, d)
    n, first = ae_far.shape[0], moves.take(6)

    def loads(j):
        return [
            pltpu.make_async_copy(far.at[j], d_ref.at[j, pl.ds(k * n, n)], sems.at[first + 2 * j + k])
            for k, far in enumerate((de_far, do_far))
        ]

    ready[0]()
    for c in loads(0):
        c.start()
    ready[1]()
    for j in (1, 2):
        for c in loads(j):
            c.start()
    t_ref[...] = a_ref[...].T

    def step(j, _):
        for c in loads(j):
            c.wait()
        acc_ref[...] = dot(t_ref[...], d_ref[j]).reshape(acc_ref.shape)
        lanes = pl.ds(pl.multiple_of(j * f, f), f)
        for s in range(16):
            block = acc_ref[s ^ me_ref[0]].astype(BF16)
            out_ref[s // 8, 1, s % 8, :, lanes] = block[:, :f]
            out_ref[s // 8, 0, s % 8, :, lanes] = block[:, f:]
        return 0

    lax.fori_loop(0, 3, step, 0)
    sent = [moves.whole(out_ref.at[i], far) for i, far in ((1, go_far), (0, keep_far))]
    for wait in sent:
        wait()


def grad_qkv(me, ae, ao, dqkv_e, dqkv_o):
    n, d = ae.shape
    f = dqkv_e.shape[2] // 2
    return packed(
        grad_qkv_body,
        me,
        (ae, ao, dqkv_e, dqkv_o),
        (2, 8, d // 16, 3 * f),
        [
            pltpu.VMEM((2 * n, d), BF16),
            pltpu.VMEM((d, 2 * n), BF16),
            pltpu.VMEM((3, 2 * n, 2 * f), BF16),
            pltpu.VMEM((16, d // 16, 2 * f), F32),
        ],
        2 * 2 * 3 * n * d * 2 * f,
        40,
        "grad_qkv",
    )


def packed_call(body, grid, me, ins, outs, scratch=(), flops=0, aliases={}, name=None):
    return pl.pallas_call(
        body,
        grid_spec=pltpu.PrefetchScalarGridSpec(
            num_scalar_prefetch=1,
            grid=grid,
            in_specs=[s for _, s in ins],
            out_specs=[s for _, s in outs],
            scratch_shapes=scratch,
        ),
        out_shape=[a for a, _ in outs],
        input_output_aliases=aliases,
        compiler_params=pltpu.CompilerParams(
            dimension_semantics=("arbitrary",) * len(grid), vmem_limit_bytes=VMEM_LIMIT
        ),
        cost_estimate=pl.CostEstimate(flops=int(flops) // 16, bytes_accessed=0, transcendentals=0),
        name=name,
    )(me, *[a for a, _ in ins])


def unpack_down_body(me_ref, part_ref, *refs):
    low, rows = me_ref[0] % 8, part_ref.shape[1]
    for b in range(8):
        refs[-1][b * rows : (b + 1) * rows] = part_ref[b ^ low].astype(F32)


def unpack_down(me, side, part, into=()):
    _, r, w = part.shape
    half = 8 * r
    at = lambda me: (me[0] // 8) ^ side
    ins = [(part, pl.BlockSpec(part.shape, lambda i, me: (0, 0, 0)))]
    ins += [(t, pl.BlockSpec(memory_space=pl.ANY)) for t in into]
    return packed_call(
        unpack_down_body,
        (1,),
        me,
        ins,
        [(sds((2 * half, w), F32), pl.BlockSpec((half, w), lambda i, me: (at(me), 0)))],
        aliases={2 + i: i for i in range(len(into))},
        name="unpack_down",
    )[0]


def unpack_rest_body(side, me_ref, part_ref, *refs):
    up_far, out_far, qkv_far, up_st, wide, out_st, qkv_st, sems = refs[-8:]
    moves = Moves(sems)
    left, right = me_ref[0] % 8, me_ref[2] % 8
    rows, half = part_ref.shape[1], 8 * part_ref.shape[1]
    d, f = up_st.shape[1], wide.shape[1]
    base = ((me_ref[0] // 8) ^ side) * half
    sent = []
    for b in range(8):
        sl = slice(b * rows, (b + 1) * rows)
        up_st[sl, :CUT] = part_ref[b ^ left, :, :CUT].astype(F32)
        up_st[sl, CUT:] = part_ref[swapped(b ^ right), :, CUT:d].astype(F32)
        wide[sl] = part_ref[b ^ right, :, d : d + f].astype(F32)
        if b % 4 == 3:
            start, size = (b - 3) * rows, 4 * rows
            at = pl.ds(pl.multiple_of(base + start, 8), size)
            sent.append(moves.whole(up_st.at[pl.ds(start, size)], up_far.at[at]))
    out_st[...] = wide[...].T
    sent.append(moves.whole(out_st, lanes_at(out_far, base, half)))
    for j in range(3):
        for b in range(8):
            sl = slice(b * rows, (b + 1) * rows)
            qkv_st[j, sl] = part_ref[b ^ right, :, d + (j + 1) * f : d + (j + 2) * f].astype(F32)
        sent.append(moves.whole(qkv_st.at[j], qkv_far.at[j, pl.ds(pl.multiple_of(base, 8), half)]))
    for wait in sent:
        wait()


def unpack_rest(me, side, part, into=()):
    _, r, w = part.shape
    half = 8 * r
    d, f = CUT_BACK, (w - CUT_BACK) // 4
    smem = pl.BlockSpec(memory_space=pltpu.SMEM)
    outs = [sds((2 * half, d), F32), sds((f, 2 * half), F32), sds((3, 2 * half, f), F32)]
    stages = [sds((half, d), F32), sds((half, f), F32), sds((f, half), F32), sds((3, half, f), F32)]
    return resident(
        functools.partial(unpack_rest_body, side),
        [(me, smem), part] + far_of(*into),
        far_of(*outs),
        scratch=near_of(*stages) + [pltpu.SemaphoreType.DMA((8,))],
        vmem=24,
        aliases={2 + i: i for i in range(len(into))},
        name="unpack_rest",
    )


def fold(*parts):
    return sum(p.astype(F32) for p in parts).astype(BF16)


def after(value, *first):
    return lax.optimization_barrier((value, first))[0]


class Chunk:
    def __init__(self, keep, got):
        self.keep, self.got = keep, got
        self.sent = None

    def wait(self, *also):
        self.got, also = lax.optimization_barrier((self.got, also))
        return also

    def to_partner(self):
        total = fold(self.keep, self.got)
        self.keep, self.sent = total[1], total[0]
        self.got = lax.ppermute(self.sent, "tensor", FLIP)

    def gather_core(self):
        self.got = lax.ppermute(self.keep, "core", FLIP)


def add(k, g):
    return (k.astype(F32) + g.astype(F32)).astype(BF16)


def phase_shapes(mode, parts):
    shapes = [p[0].shape for p in parts]
    s = shapes[0]
    if mode == "half":
        out = s[:-3] + (s[-3] // 2,) + s[-2:]
        return [out, out]
    if mode == "partner":
        return [s[1:], s[1:]]
    if mode == "last":
        out = (s[0] // 2, s[1], sum(t[2] for t in shapes))
        return [out, out]
    if mode == "sum":
        return [s]
    if mode == "split":
        return [(2 * s[0], s[1], CUT_BACK), (2 * s[0], s[1], s[2] - CUT_BACK)]
    return [(2 * s[0], s[1], sum(t[2] for t in shapes))]


def phase_part(mode, parts, outs):
    if mode == "half":
        (k, g), n = parts[0], outs[0].shape[-3]
        lead = (slice(None),) * (len(k.shape) - 3)
        for i, out in enumerate(outs):
            at = lead + (slice(i * n, (i + 1) * n),)
            out[...] = add(k[at], g[at])
    elif mode == "partner":
        k, g = parts[0]
        for i, out in zip((1, 0), outs):
            out[...] = add(k[i], g[i])
    elif mode == "last":
        n, lane = outs[0].shape[0], 0
        for k, g in parts:
            for i, out in enumerate(outs):
                at = slice(i * n, (i + 1) * n)
                out[:, :, lane : lane + k.shape[2]] = add(k[at], g[at])
            lane += k.shape[2]
    elif mode == "sum":
        outs[0][...] = add(parts[0][0][...], parts[0][1][...])
    elif mode == "split":
        for i, ref in enumerate(parts[0]):
            at = slice(i * ref.shape[0], (i + 1) * ref.shape[0])
            outs[0][at] = ref[:, :, :CUT_BACK]
            outs[1][at] = ref[:, :, CUT_BACK:]
    else:
        lane = 0
        for pair in parts:
            for i, ref in enumerate(pair):
                outs[0][i * ref.shape[0] : (i + 1) * ref.shape[0], :, lane : lane + ref.shape[2]] = ref[...]
            lane += pair[0].shape[2]


def phase(*items):
    shapes = [phase_shapes(*t) for t in items]

    def body(*refs):
        at = sum(2 * len(parts) for _, parts in items)
        ins, outs = list(refs[:at]), list(refs[at:])
        for (mode, parts), made in zip(items, shapes):
            mine = [(ins.pop(0), ins.pop(0)) for _ in parts]
            phase_part(mode, mine, [outs.pop(0) for _ in made])

    flat = resident(
        body,
        [t for _, parts in items for pair in parts for t in pair],
        [sds(s, BF16) for made in shapes for s in made],
        vmem=16,
        name="phase",
    )
    flat = list(flat)
    return [[flat.pop(0) for _ in made] for made in shapes]


class Hops(Chunk):
    def __init__(self, outer, keep, got):
        super().__init__(keep, got)
        self.axes = {"x": ("x", 2, 1), "z": ("o", outer, 1), "w": ("o", outer, 2)}
        self.extra = [("o", outer, 1 << b) for b in range(2, outer.bit_length() - 1)]

    def over(self, way, t):
        return lax.ppermute(t, "tensor", FLIP) if way == "partner" else flip_bit(t, *self.axes[way])

    def send(self, *parts):
        self.keep, self.sent, self.got = [], [], []
        for total, way in parts:
            if way == "partner":
                keep, sent = total[1], total[0]
            else:
                half = total.shape[-3] // 2
                keep, sent = total[..., :half, :, :], total[..., half:, :, :]
            self.keep.append(keep)
            self.sent.append(sent)
            self.got.append(self.over(way, sent))

    def first(self):
        total = fold(self.keep, self.got)
        self.send((total[..., :CUT], "x"), (total[..., CUT:], "z"))

    def first_hop(self, way):
        self.send((fold(self.keep, self.got), way))

    def parts(self):
        return list(zip(self.keep, self.got))

    def hop(self, *ways):
        items = [("partner" if w == "partner" else "half", [p]) for w, p in zip(ways, self.parts())]

        def then(made):
            self.keep, self.sent = [m[0] for m in made], [m[1] for m in made]
            self.got = [self.over(w, s) for w, s in zip(ways, self.sent)]

        return items, then

    def absorb(self, other):
        self.keep, self.got = self.keep + other.keep, self.got + other.got

    def last_hop(self):
        def then(made):
            ((keep, sent),) = made
            self.keep, self.sent = [keep], [sent]
            self.got = [self.over("w", sent)]

        return [("last", self.parts())], then

    def back_first(self):
        def then(made):
            ((total,),) = made
            for s in self.extra:
                total = fold(total, flip_bit(total, *s))
            self.keep = self.sent = [total]
            self.got = [self.over("w", total)]

        return [("sum", self.parts())], then

    def back(self, *ways):
        if len(ways) == 2 and len(self.keep) == 1:
            items = [("split", self.parts())]
        else:
            items = [("join", [p]) for p in self.parts()]

        def then(made):
            self.keep = self.sent = [t for m in made for t in m]
            self.got = [self.over(w, t) for w, t in zip(ways, self.keep)]

        return items, then

    def back_core(self):
        def then(made):
            ((self.keep,),) = made
            self.sent = self.keep
            self.gather_core()

        return [("join", self.parts())], then


def all_steps(*steps):
    made = phase(*[item for items, _ in steps for item in items])
    for items, then in steps:
        then(made[: len(items)])
        made = made[len(items) :]


def mask_biases(seg):
    seq = seg.shape[1]
    place = jnp.arange(seq, dtype=jnp.int32)
    same = seg[:, :, None] == seg[:, None, :]
    below = (place[:, None] < place[None, :])[None]
    incl = (place[:, None] <= place[None, :])[None]
    bias = lambda m: jnp.where(same & m, 0.0, NEG).astype(F32)
    return bias(incl), bias(below)


def sync(*values):
    return lax.optimization_barrier(values)


class Link:
    def __init__(self, outer, w_qkv, w_out, w_up, w_down):
        self.outer = outer
        self.own = (w_qkv, w_out, w_up, w_down)
        self.core_at, self.x_at, o = (lax.axis_index(a) for a in ("core", "x", "o"))
        bits = {"x": self.x_at, "z": o % 2, "w": (o // 2) % 2}
        self.fetch_bits = self.core_at * 2 + self.x_at
        slots = []
        for order in ("xzw", "zxw"):
            slot = self.core_at
            for name in order:
                slot = slot * 2 + bits[name]
            slots.append(slot)
        self.me = jnp.stack([slots[0], self.fetch_bits, slots[1]]).astype(jnp.int32)
        self.me_z = self.me[2:0:-1]

    def quarter(self, own):
        flat = own.reshape(-1, own.shape[-1])
        return take_half(take_half(flat, self.core_at), self.x_at)

    def over_x(self, t):
        return lax.ppermute(t, "x", FLIP)

    def fetch(self, own_work):
        own = self.own
        size = own[2].shape[1] // 4
        part = lambda t, axis, bits: lax.dynamic_slice_in_dim(t, bits * size, size, axis)
        pieces = [
            self.quarter(own[1]),
            part(own[2], 1, self.fetch_bits),
            jnp.concatenate([part(own[3], 0, self.fetch_bits), part(own[3], 0, self.fetch_bits ^ 1)], axis=0),
        ]
        qkv = self.partner(self.quarter(own[0]))
        up, out, down = (self.partner(pieces[i]) for i in (1, 0, 2))
        qkv, own_work = sync(qkv, own_work)
        qkv, out, up = sync(ordered(self.x_at, qkv, self.over_x(qkv)).reshape(-1, qkv.shape[-1]), out, up)
        qkv_core, out_x, up_x = self.core(qkv), self.over_x(out), self.over_x(up)
        qkv = ordered(self.core_at, qkv, qkv_core).reshape(own[0].shape)

        def join_out(*work):
            nonlocal out, out_x
            work, out, out_x = sync(work, out, out_x)
            out = ordered(self.x_at, out, out_x).reshape(-1, out.shape[-1])
            out = ordered(self.core_at, out, self.core(out)).reshape(own[1].shape)
            return work, jnp.concatenate([own[1], out], axis=0)

        def pieces_of(*work):
            up_there, down_there, work = sync(up_x, down, work)
            ups = (own[2], up, up_there, self.core(up), self.core(up_there))
            return ups, (own[3], down_there, self.core(down_there)), work

        return own_work, own[0], qkv, jnp.concatenate([own[0], qkv], axis=2), join_out, pieces_of

    def partner(self, t):
        return lax.ppermute(t, "tensor", FLIP)

    def core(self, t):
        return lax.ppermute(t, "core", FLIP)

    def chunk(self, keep, got):
        return Chunk(keep, got)

    def hops(self, keep, got):
        return Hops(self.outer, keep, got)

    def small_steps(self):
        return [("core", 2, 1), ("tensor", 2, 1)] + steps_of(self.outer)

    def flip(self, t, step):
        return flip_bit(t, *step)


def local_part(x, seg, cot, gb, link):
    rows, seq = seg.shape
    n, width = x.shape
    me, me_z = link.me, link.me_z
    incl, strict = mask_biases(seg)
    normal, _ = norm_stats(x.astype(F32))
    a_e = (normal * gb[0] + gb[2]).astype(BF16)
    first = attend_first(a_e, link.own[0], incl)
    (a_e, first, cot), wq_own, fetched, wqkv, join_out, pieces_of = link.fetch((a_e, first, cot))
    second = attend_first(a_e, fetched, incl)
    qkv_e, o1 = (jnp.concatenate([s, t], axis=-1) for s, t in zip(first[:2], second[:2]))
    lse1 = jnp.concatenate([first[2], second[2]], axis=0).reshape(-1, GROUP // HD, n)
    (qkv_e, o1, lse1, wqkv), wout = join_out(qkv_e, o1, lse1, wqkv)
    h1, n2_1, g1, d1, part_one = mlp_own(x, o1, wout, gb, link.own[2], link.own[3])
    ups, downs, (n2_1, part_one) = pieces_of(n2_1, part_one)
    g1, d1, ho, a_o = mlp_other(n2_1, part_one, g1, d1, gb, ups[1:], downs[1:])
    qkv_o, o2, lse2 = attend_second(a_o, wqkv, incl, strict, qkv_e, o1, lse1)
    out, out_two, n2_2, g2, du2, dh1_2, dp2, do2, sums2, dm2 = mlp_second(x, ho, o2, cot, wout, gb, ups, downs, seq)
    out_got = link.partner(out)
    dqkv_o, part, dy, sums_o = attend_back(wqkv, incl, strict, qkv_e, qkv_o, o2, lse2, do2, dh1_2, ho, gb)
    o2_flat = o2.reshape(2 * n, width)

    out_got, dy = sync(out_got, dy)
    out_last = link.partner(after(out_two, out_got))
    down_keep, down_go = grad_down(me_z, g1, g2, dy, dm2)
    down_keep, down_go, out_last = sync(down_keep, down_go, out_last)
    down = link.hops(down_keep, link.core(down_go))
    dy = after(dy, down_go)
    du1, dh1_1, dp1, do1, sums1 = mlp_back(dy, h1, wout, gb, d1, ups, downs, seq)
    du1, dp1, do1 = down.wait(du1, dp1, do1)
    down.to_partner()
    up_keep, up_go = grad_up(me, n2_1, n2_2, after(du1, down.sent), du2, dp1, dp2, o1, o2_flat)
    do1 = after(do1, up_go)
    dqkv_e, gt, sums_e = attend_back_even(wqkv, incl, qkv_e, o1, lse1, do1, o2, lse2, do2, part, dh1_1, dh1_2, x, gb)
    dqkv_e, gt, sums_e, up_go = down.wait(dqkv_e, gt, sums_e, up_go)
    up = link.hops(up_keep, link.core(up_go))
    down.keep, down.got = [down.keep], [down.got]
    all_steps(down.hop("z"))
    small = jnp.stack([sums_e[0] + sums_o[0], sums1[0] + sums2[0], sums_e[1] + sums_o[1], sums1[1] + sums2[1], sums_o[2]])
    qkv_keep, qkv_go = grad_qkv(me_z, a_e, a_o, after(dqkv_e, *down.sent), dqkv_o)
    out = link.finish(
        jnp.concatenate([out, out_two], axis=0), jnp.concatenate([out_got, after(out_last, dqkv_e)], axis=0), link.out_shape
    )
    qkv_keep, qkv_go, down.got, out = up.wait(qkv_keep, qkv_go, down.got, out)
    qkv = link.hops(qkv_keep, link.core(qkv_go))
    small_steps = iter(link.small_steps())
    small_got = link.flip(after(small, qkv_go), next(small_steps))

    chunks = [up, qkv]

    def wait_all():
        nonlocal small, small_got
        got, small_got = sync([c.got for c in chunks], small_got)
        for c, g in zip(chunks, got):
            c.got = g
        if small_got is not None:
            small = small + small_got
            step = next(small_steps, None)
            small_got = None if step is None else link.flip(small, step)

    wait_all()
    chunks.append(down)
    up.first()
    qkv.first_hop("partner")
    all_steps(down.hop("x"))
    wait_all()
    all_steps(up.hop("partner", "x"), qkv.hop("z"), down.hop("w"))
    wait_all()
    all_steps(up.hop("z", "partner"), qkv.hop("x"), down.back_first())
    half = gt.shape[0] // 2
    gt_got = [link.partner(after(gt[:half], *up.sent))]
    wait_all()
    up.absorb(qkv)
    chunks.remove(qkv)
    all_steps(up.last_hop(), down.back("x"))
    gt_got.append(link.partner(after(gt[half:], *up.sent)))
    (gt_got[0],) = up.wait(gt_got[0])
    wait_all()
    all_steps(up.back_first(), down.back("z"))
    (gt_got[1],) = up.wait(gt_got[1])
    wait_all()
    while small_got is not None:
        wait_all()
    all_steps(up.back("z", "x"), down.back_core())
    wait_all()
    all_steps(up.back("x", "z"))
    g_down = unpack_down(me_z, 0, after(down.keep, *up.sent))
    g_down = unpack_down(me_z, 1, down.got, (g_down,))
    gt = link.finish(gt, jnp.concatenate(gt_got, axis=0), link.tokens_shape).astype(F32)
    small = (small[0:2], small[2:4], small[4])
    g_down, gt, small = up.wait(g_down, gt, small)
    all_steps(up.back_core())
    g_rest = unpack_rest(me, 0, up.keep)
    g_rest = up.wait(*g_rest)
    g_up, g_out, g_qkv = unpack_rest(me, 1, up.got, g_rest)
    return out, gt, (g_qkv, g_out, g_up, g_down), small


def shards(outer, tokens, segments, pass_embed, w_qkv, w_out, w_up, w_down, gain, bias, cotangent):
    ty = lax.axis_index("tensor")
    rows = tokens.shape[0] // 2
    width = tokens.shape[2]
    mine = lambda t: lax.dynamic_slice_in_dim(t, ty * rows, rows, 0)
    x = mine(tokens).reshape(-1, width)
    gb = jnp.concatenate([gain, bias, pass_embed[None]], axis=0)
    link = Link(outer, w_qkv, w_out, w_up, w_down)
    link.out_shape, link.tokens_shape = cotangent.shape, tokens.shape
    link.finish = lambda mine, theirs, shape: ordered(ty, mine, theirs).reshape(shape)
    out, gt, grads, small = local_part(x, mine(segments), mine(cotangent), gb, link)
    return out, gt, *grads, *small


def solution(mesh):
    outer = mesh.shape["dp"] // 4
    fine = Mesh(mesh.devices.reshape(outer, 2, 2, mesh.shape["tensor"]), ("o", "x", "core", "tensor"))
    rows = ROWS_OVER
    placed = (
        P(rows, None, None),
        P(rows, None),
        P(),
        P(None, None, "tensor"),
        P("tensor", None),
        P(None, "tensor"),
        P("tensor", None),
        P(),
        P(),
        P(rows, None, None),
    )

    def body(*args):
        return shards(outer, *args)

    return jax.shard_map(
        body,
        mesh=fine,
        in_specs=placed,
        out_specs=(
            P(rows, None, None),
            P(rows, None, None),
            P(None, None, "tensor"),
            P("tensor", None),
            P(None, "tensor"),
            P("tensor", None),
            P(),
            P(),
            P(),
        ),
        check_vma=False,
    )
```

```python
import functools

import jax
import jax.numpy as jnp
from jax import lax
from jax.experimental import pallas as pl
from jax.experimental.pallas import tpu as pltpu
from jax.sharding import Mesh
from jax.sharding import PartitionSpec as P

HD = 64
EPS = 1e-05
NEG = -1000000000.0
F32 = jnp.float32
BF16 = jnp.bfloat16
ROWS_OVER = ("o", "x", "core")
FLIP = ((0, 1), (1, 0))
VMEM_LIMIT = 16 * 1024 * 1024


def ordered(flag, mine, theirs):
    first = flag == 0
    return jnp.stack([jnp.where(first, mine, theirs), jnp.where(first, theirs, mine)])


def take_half(array, index):
    half = array.shape[0] // 2
    return lax.dynamic_slice_in_dim(array, index * half, half, 0)


def flip_bit(array, axis, size, bit):
    return lax.ppermute(array, axis, [(i, i ^ bit) for i in range(size)])


def steps_of(outer):
    steps = [("x", 2, 1)]
    bit = 1
    while bit < outer:
        steps.append(("o", outer, bit))
        bit *= 2
    return steps


def my_bit(axis, bit):
    return (lax.axis_index(axis) // bit) % 2


def dot(a, b):
    return lax.dot_general(a, b, (((1,), (0,)), ((), ())), preferred_element_type=F32)


def dot_nt(a, b):
    return lax.dot_general(a, b, (((1,), (1,)), ((), ())), preferred_element_type=F32)


def dot_tn(a, b):
    return lax.dot_general(a, b, (((0,), (0,)), ((), ())), preferred_element_type=F32)


def norm_stats(h):
    centred = h - jnp.mean(h, axis=-1, keepdims=True)
    inverse = lax.rsqrt(jnp.mean(centred * centred, axis=-1, keepdims=True) + EPS)
    return centred * inverse, inverse


def norm_back(grad, normal, inverse, gain):
    scaled = grad * gain
    centre = jnp.mean(scaled, axis=-1, keepdims=True)
    proj = jnp.mean(scaled * normal, axis=-1, keepdims=True)
    return inverse * (scaled - centre - normal * proj)


def gelu_parts(u):
    c = 0.7978845608028654
    a = 0.044715 * c
    square = u * u
    half = 0.5 + 0.5 * jnp.tanh(u * (c + a * square))
    g = u * half
    return g, half + g * (1.0 - half) * (2.0 * c + 6.0 * a * square)


def whole(shape):
    return pl.BlockSpec(shape, lambda *_: (0,) * len(shape))


def call(body, grid, ins, outs, scratch=(), cost=(0, 0), name=None, vmem=VMEM_LIMIT):
    return pl.pallas_call(
        body,
        grid=grid,
        in_specs=[s for _, s in ins],
        out_specs=[s for _, s in outs],
        out_shape=[a for a, _ in outs],
        scratch_shapes=scratch,
        compiler_params=pltpu.CompilerParams(
            dimension_semantics=("arbitrary",) * len(grid), vmem_limit_bytes=vmem
        ),
        cost_estimate=pl.CostEstimate(
            flops=int(cost[0]) // 16, bytes_accessed=int(cost[1]), transcendentals=0
        ),
        name=name,
    )(*[a for a, _ in ins])


FAR = pl.BlockSpec(memory_space=pl.ANY)


def resident(body, ins, outs, scratch=(), flops=0, vmem=16, aliases={}, name=None):
    spec = pl.BlockSpec(memory_space=pltpu.VMEM)
    ins, outs = ([o if isinstance(o, tuple) else (o, spec) for o in t] for t in (ins, outs))
    ins = [(pltpu.with_memory_space_constraint(a, pltpu.HBM) if s is FAR else a, s) for a, s in ins]
    outs = [(pltpu.HBM(a.shape, a.dtype) if s is FAR else a, s) for a, s in outs]
    return pl.pallas_call(
        body,
        in_specs=[s for _, s in ins],
        out_specs=[s for _, s in outs],
        out_shape=[a for a, _ in outs],
        scratch_shapes=scratch,
        input_output_aliases=aliases,
        compiler_params=pltpu.CompilerParams(vmem_limit_bytes=vmem * 1024 * 1024),
        cost_estimate=pl.CostEstimate(flops=int(flops) // 16, bytes_accessed=0, transcendentals=0),
        name=name,
    )(*[a for a, _ in ins])


def sds(shape, dtype):
    return jax.ShapeDtypeStruct(shape, dtype)


QB = 128
GROUP = 256


def lanes_of(ref, g):
    return ref.at[(slice(None),) * (len(ref.shape) - 1) + (pl.ds(pl.multiple_of(g * GROUP, GROUP), GROUP),)]


class Moves:
    def __init__(self, sems):
        self.sems, self.used = sems, 0

    def take(self, number):
        self.used += number
        return self.used - number

    def whole(self, source, target):
        copy = pltpu.make_async_copy(source, target, self.sems.at[self.take(1)])
        copy.start()
        return copy.wait

    def later(self, source, target):
        sem = self.sems.at[self.take(1)]
        copy = lambda: pltpu.make_async_copy(source, target, sem)
        return (lambda: copy().start()), (lambda: copy().wait())

    def groups(self, source, target):
        first = self.take(source.shape[-1] // GROUP)

        def copy(g):
            return pltpu.make_async_copy(lanes_of(source, g), lanes_of(target, g), self.sems.at[first + g])

        return (lambda g: copy(g).start()), (lambda g: copy(g).wait())


def cat_heads(t, scale=1.0):
    lane = lax.broadcasted_iota(jnp.int32, (1, 2 * HD), 1)
    parts = [t * jnp.where((lane < HD) == (h == 0), scale, 0.0).astype(t.dtype) for h in range(2)]
    return jnp.concatenate(parts, axis=0)


def own_lanes(t, scale=None):
    if scale is not None:
        t = t * scale
    return jnp.concatenate([t[:HD, :QB], t[HD:, QB:]], axis=0)


def twice(t):
    return jnp.concatenate([t, t], axis=1)


def pair_row(rows, p):
    return jnp.concatenate([rows[2 * p : 2 * p + 1], rows[2 * p + 1 : 2 * p + 2]], axis=1)


def put_pair(ref, p, cols, value):
    ref[2 * p : 2 * p + 1, cols] = value[:, :QB]
    ref[2 * p + 1 : 2 * p + 2, cols] = value[:, QB:]


def columns(t, r, seq, qb):
    return t[:, pl.ds(pl.multiple_of(r * seq + qb * QB, QB), QB)]


def rows_of(r, seq, qb):
    return pl.ds(pl.multiple_of(r * seq + qb * QB, QB), QB)


def in_turn(arrive, group, groups):
    for _, wait in arrive:
        wait(group)

    @pl.when(group + 2 < groups)
    def _():
        for start, _ in arrive:
            start(group + 2)


def attend_first_body(rows, seq, pairs, a_ref, w_ref, bias_ref, qkv_ref, o_ref, lse_ref):
    a = a_ref[...]
    for j in range(3):
        qkv_ref[j] = dot(a, w_ref[j]).astype(BF16)
    for r in range(rows):
        work = []
        for p in range(pairs):
            ln = slice(p * 2 * HD, (p + 1) * 2 * HD)
            k = qkv_ref[1, r * seq : (r + 1) * seq, ln]
            for b in range(seq // QB):
                sl, n = slice(r * seq + b * QB, r * seq + (b + 1) * QB), (b + 1) * QB
                q = cat_heads(qkv_ref[0, sl, ln], HD**-0.5)
                s = dot_nt(k[:n], q) + twice(bias_ref[r, :n, b * QB : n])
                work.append((p, ln, sl, n, s))
        done = []
        for p, ln, sl, n, s in work:
            top = jnp.max(s, axis=0, keepdims=True)
            e = jnp.exp(s - top)
            mass = jnp.sum(e, axis=0, keepdims=True)
            put_pair(lse_ref, p, sl, top + jnp.log(mass))
            done.append((e.astype(BF16), 1.0 / mass))
        for (p, ln, sl, n, _), (e, inv) in zip(work, done):
            vt = qkv_ref[2, r * seq : (r + 1) * seq, ln].T
            o_ref[sl, ln] = own_lanes(dot(vt[:, :n], e), inv).T.astype(BF16)


def attend_first(a, w, bias):
    rows, seq = bias.shape[0], bias.shape[1]
    n, d = a.shape
    f = w.shape[2]
    return resident(
        functools.partial(attend_first_body, rows, seq, f // (2 * HD)),
        (a, w, bias),
        [sds((3, n, f), BF16), sds((n, f), BF16), sds((f // HD, n), F32)],
        flops=6 * n * d * f + 16 * n * seq * f,
        name="attend_first",
    )


def attend_second_body(
    rows, seq, a_far, w_far, incl_far, strict_far, qkve_far, o1_far, lse1_ref,
    qkvo_far, o2_far, lse2_ref,
    a_ref, w_ref, incl_ref, strict_ref, qkve_ref, o1_ref, qkvo_ref, o2_ref, sems,
):
    groups = lse1_ref.shape[0]
    moves = Moves(sems)
    ready = [moves.whole(a_far, a_ref), moves.whole(w_far.at[0], w_ref.at[0])]
    arrive = [moves.groups(*t) for t in ((qkve_far, qkve_ref), (o1_far, o1_ref))]
    leave = moves.groups(o2_ref, o2_far)
    for wait in ready:
        wait()
    ready = [moves.whole(w_far.at[j], w_ref.at[j]) for j in (1, 2)]
    a = a_ref[...]
    sent = []
    for j in range(3):
        if j:
            ready[j - 1]()
        if j == 1:
            masks = [moves.whole(*t) for t in ((incl_far, incl_ref), (strict_far, strict_ref))]
            for g in range(2):
                for start, _ in arrive:
                    start(g)
        qkvo_ref[j] = dot(a, w_ref[j]).astype(BF16)
        sent.append(moves.whole(qkvo_ref.at[j], qkvo_far.at[j]))
    for wait in masks:
        wait()

    def next_group(group):
        in_turn(arrive, group, groups)

    def row(i, _):
        r, group = i % rows, i // rows
        lanes = pl.multiple_of(group * GROUP, GROUP)
        all_of = pl.ds(pl.multiple_of(r * seq, seq), seq)

        @pl.when(r == 0)
        def _():
            next_group(group)

        for p in range(GROUP // (2 * HD)):
            ln = pl.ds(lanes + p * 2 * HD, 2 * HD)
            ke, ko = qkve_ref[1, all_of, ln], qkvo_ref[1, all_of, ln]
            vte, vto = qkve_ref[2, all_of, ln].T, qkvo_ref[2, all_of, ln].T
            work = []
            for b in range(seq // QB):
                sl, n = rows_of(r, seq, b), (b + 1) * QB
                cols = slice(b * QB, n)
                incl, strict = twice(incl_ref[r, :n, cols]), twice(strict_ref[r, :n, cols])
                q = cat_heads(qkve_ref[0, sl, ln], HD**-0.5)
                work.append([dot_nt(ko[:n], q) + strict])
                q = cat_heads(qkvo_ref[0, sl, ln], HD**-0.5)
                work.append([dot_nt(ko[:n], q) + incl, dot_nt(ke[:n], q) + incl])
            for b in range(seq // QB):
                sl, n = rows_of(r, seq, b), (b + 1) * QB
                (s,), (so, se) = work[2 * b : 2 * b + 2]
                old = pair_row(lse1_ref[group, :, sl], p)
                top = jnp.maximum(old, jnp.max(s, axis=0, keepdims=True))
                e = jnp.exp(s - top)
                kept = jnp.exp(old - top)
                mass = kept + jnp.sum(e, axis=0, keepdims=True)
                work[2 * b] = (e.astype(BF16), kept, 1.0 / mass)
                put_pair(lse2_ref.at[0, group], p, sl, top + jnp.log(mass))
                top = jnp.max(jnp.maximum(se, so), axis=0, keepdims=True)
                ee, eo = jnp.exp(se - top), jnp.exp(so - top)
                mass = jnp.sum(ee + eo, axis=0, keepdims=True)
                work[2 * b + 1] = (ee.astype(BF16), eo.astype(BF16), 1.0 / mass)
                put_pair(lse2_ref.at[1, group], p, sl, top + jnp.log(mass))
            for b in range(seq // QB):
                sl, n = rows_of(r, seq, b), (b + 1) * QB
                (e, kept, inv), (ee, eo, inv2) = work[2 * b : 2 * b + 2]
                o1 = o1_ref[sl, ln].astype(F32).T
                o = own_lanes(dot(vto[:, :n], e), inv) + own_lanes(twice(o1), kept * inv)
                o2_ref[0, sl, ln] = o.T.astype(BF16)
                o = dot(vte[:, :n], ee) + dot(vto[:, :n], eo)
                o2_ref[1, sl, ln] = own_lanes(o, inv2).T.astype(BF16)

        @pl.when(r == rows - 1)
        def _():
            leave[0](group)

        return 0

    lax.fori_loop(0, rows * groups, row, 0)
    for wait in sent:
        wait()
    for g in range(groups):
        leave[1](g)


def attend_second(a, w, incl, strict, qkve, o1, lse1):
    rows, seq = incl.shape[0], incl.shape[1]
    n, d = a.shape
    f = w.shape[2]
    qkv, o2 = sds((3, n, f), BF16), sds((2, n, f), BF16)
    near = (a, w, incl, strict, qkve, o1, qkv, o2)
    return resident(
        functools.partial(attend_second_body, rows, seq),
        [(t, FAR) for t in (a, w, incl, strict, qkve, o1)] + [lse1],
        [(qkv, FAR), (o2, FAR), sds((2, *lse1.shape), F32)],
        scratch=[pltpu.VMEM(t.shape, t.dtype) for t in near] + [pltpu.SemaphoreType.DMA((64,))],
        flops=6 * n * d * f + 48 * n * seq * f,
        vmem=32,
        name="attend_second",
    )


def row_products(a, b):
    prod = cat_heads((a * b).astype(BF16))
    return dot_nt(jnp.ones((8, 2 * HD), BF16), prod)[:1]


def query_parts(sl, ln, group, p, i, qkv_ref, o_ref, lse_ref, do_ref):
    do = do_ref[i, sl, ln]
    delta = row_products(do.astype(F32), o_ref[i, sl, ln].astype(F32))
    return cat_heads(qkv_ref[0, sl, ln], HD**-0.5), cat_heads(do), pair_row(lse_ref[i, group, :, sl], p), delta


def blocks_back(tasks):
    scores = [dot_nt(k, q) + bias - lse for k, _, _, bias, q, _, lse, _ in tasks]
    moved = [dot_nt(v, do) - delta for _, v, _, _, _, do, _, delta in tasks]
    probs = [jnp.exp(s) for s in scores]
    ds = [(p * m).astype(BF16) for p, m in zip(probs, moved)]
    return [
        (dot(p.astype(BF16), do), dot(d, q), dot(kt, d))
        for (_, _, kt, _, q, do, _, _), p, d in zip(tasks, probs, ds)
    ]


def add_rows(total, part):
    if total is None:
        return part
    n = part.shape[0]
    return jnp.concatenate([total[:n] + part, total[n:]], axis=0)


def attend_back_body(
    rows, seq, w_far, incl_far, strict_far, qkve_far, qkvo_far, o2_far, lse2_ref, do_far,
    dh1_far, ho_far, gb_ref,
    dqkvo_far, dqkve_far, dy_far, sums_ref,
    w_ref, incl_ref, strict_ref, qkve_ref, qkvo_ref, o2_ref, do_ref, dh1_ref, ho_ref,
    dqkvo_ref, dqkve_ref, da_ref, dy_ref, sems,
):
    groups = lse2_ref.shape[1]
    moves = Moves(sems)
    arrive = [
        moves.groups(*t)
        for t in ((qkve_far, qkve_ref), (qkvo_far, qkvo_ref), (o2_far, o2_ref), (do_far, do_ref))
    ]
    leave = [moves.groups(*t) for t in ((dqkvo_ref, dqkvo_far), (dqkve_ref, dqkve_far))]
    for start, _ in arrive:
        start(0)
    masks = [moves.whole(*t) for t in ((incl_far, incl_ref), (strict_far, strict_ref))]
    for start, _ in arrive:
        start(1)
    odd = pl.ds(rows * seq, rows * seq)
    late = [moves.later(*t) for t in ((w_far, w_ref), (dh1_far.at[odd], dh1_ref), (ho_far, ho_ref))]
    for wait in masks:
        wait()

    def next_group(group):
        in_turn(arrive, group, groups)

        @pl.when(group == groups - 2)
        def _():
            for start, _ in late:
                start()

    sc = HD**-0.5

    def row(i, _):
        r, group = i % rows, i // rows
        lanes = pl.multiple_of(group * GROUP, GROUP)
        all_of = pl.ds(pl.multiple_of(r * seq, seq), seq)

        @pl.when(r == 0)
        def _():
            next_group(group)

        for p in range(GROUP // (2 * HD)):
            ln = pl.ds(lanes + p * 2 * HD, 2 * HD)
            ke, ve = qkve_ref[1, all_of, ln], qkve_ref[2, all_of, ln]
            ko, vo = qkvo_ref[1, all_of, ln], qkvo_ref[2, all_of, ln]
            kte, kto = ke.T, ko.T
            tasks = []
            for b in reversed(range(seq // QB)):
                sl, n = rows_of(r, seq, b), (b + 1) * QB
                cols = slice(b * QB, n)
                incl, strict = twice(incl_ref[r, :n, cols]), twice(strict_ref[r, :n, cols])
                even = query_parts(sl, ln, group, p, 0, qkve_ref, o2_ref, lse2_ref, do_ref)
                odd = query_parts(sl, ln, group, p, 1, qkvo_ref, o2_ref, lse2_ref, do_ref)
                tasks.append((ko[:n], vo[:n], kto[:, :n], strict, *even))
                tasks.append((ko[:n], vo[:n], kto[:, :n], incl, *odd))
                tasks.append((ke[:n], ve[:n], kte[:, :n], incl, *odd))
            done = blocks_back(tasks)
            dke = dve = dko = dvo = None
            for b in reversed(range(seq // QB)):
                sl = rows_of(r, seq, b)
                (dv, dk, dqe), (dv2, dk2, dqo), (dv3, dk3, dqo2) = done[:3]
                done = done[3:]
                dvo, dko = add_rows(dvo, dv + dv2), add_rows(dko, dk + dk2)
                dve, dke = add_rows(dve, dv3), add_rows(dke, dk3)
                dqkve_ref[0, sl, ln] = (own_lanes(dqe).T * sc).astype(BF16)
                dqkvo_ref[0, sl, ln] = (own_lanes(dqo + dqo2).T * sc).astype(BF16)
            dqkve_ref[1, all_of, ln] = dke.astype(BF16)
            dqkve_ref[2, all_of, ln] = dve.astype(BF16)
            dqkvo_ref[1, all_of, ln] = dko.astype(BF16)
            dqkvo_ref[2, all_of, ln] = dvo.astype(BF16)

        @pl.when(r == rows - 1)
        def _():
            for start, _ in leave:
                start(group)

        return 0

    lax.fori_loop(0, rows * groups, row, 0)
    for _, wait in late:
        wait()
    da = dot_nt(dqkvo_ref[0], w_ref[0])
    da += dot_nt(dqkvo_ref[1], w_ref[1])
    da += dot_nt(dqkvo_ref[2], w_ref[2])
    da_ref[...] = da
    sums_ref[...] = jnp.zeros_like(sums_ref)

    def finish(i, _):
        sl = pl.ds(pl.multiple_of(i * ROWS_AT_ONCE, ROWS_AT_ONCE), ROWS_AT_ONCE)
        normal, inverse = norm_stats(ho_ref[sl])
        da = da_ref[sl]
        dy = dh1_ref[sl] + norm_back(da, normal, inverse, gb_ref[0:1])
        dy_ref[sl] = dy
        for k, t in enumerate((da * normal, da, dy)):
            sums_ref[k : k + 1] += jnp.sum(t, axis=0, keepdims=True)
        return 0

    lax.fori_loop(0, rows * seq // ROWS_AT_ONCE, finish, 0)
    kept = [moves.whole(dy_ref, dy_far)]
    for g in range(groups):
        for _, wait in leave:
            wait(g)
    for wait in kept:
        wait()


def attend_back(w, incl, strict, qkve, qkvo, o2, lse2, do, dh1, ho, gb):
    rows, seq = incl.shape[0], incl.shape[1]
    n, d = ho.shape
    f = w.shape[2]
    do = do.reshape(2, n, f)
    qkv = sds((3, n, f), BF16)
    near = (w, incl, strict, qkve, qkvo, o2, do, sds((n, d), F32), ho, qkv, qkv, sds((n, d), F32))
    return resident(
        functools.partial(attend_back_body, rows, seq),
        [(t, FAR) for t in (w, incl, strict, qkve, qkvo, o2)]
        + [lse2]
        + [(t, FAR) for t in (do, dh1, ho)]
        + [gb],
        [(qkv, FAR), (qkv, FAR), (sds((n, d), F32), FAR), sds((3, d), F32)],
        scratch=[pltpu.VMEM(t.shape, t.dtype) for t in near + (sds((n, d), F32),)] + [pltpu.SemaphoreType.DMA((64,))],
        flops=6 * n * d * f + 120 * n * seq * f,
        vmem=44,
        name="attend_back",
    )


def attend_back_even_body(
    rows, seq, w_far, incl_far, qkve_far, o1_far, lse1_ref, do1_far, o2_far, lse2_ref, do2_far,
    part_far, dh1_far, dh2_far, x_far, gb_ref,
    dqkv_far, gt_ref, sums_ref,
    w_ref, incl_ref, qkve_ref, o1_ref, do1_ref, o2_ref, do2_ref, part_ref, dh1_ref, dh2_ref, x_ref,
    dqkv_ref, da_ref, sems,
):
    groups = lse1_ref.shape[0]
    moves = Moves(sems)
    even = pl.ds(0, rows * seq)
    arrive = [
        moves.groups(*t)
        for t in (
            (qkve_far, qkve_ref), (o1_far, o1_ref), (do1_far, do1_ref), (o2_far.at[0], o2_ref),
            (do2_far.at[0], do2_ref), (part_far, part_ref),
        )
    ]
    leave = [moves.groups(dqkv_ref, dqkv_far)]
    for start, _ in arrive:
        start(0)
    mask = moves.whole(incl_far, incl_ref)
    for start, _ in arrive:
        start(1)
    late = [
        moves.later(*t)
        for t in ((w_far, w_ref), (dh1_far, dh1_ref), (dh2_far.at[even], dh2_ref), (x_far, x_ref))
    ]
    mask()

    def next_group(group):
        in_turn(arrive, group, groups)

        @pl.when(group == groups - 2)
        def _():
            for start, _ in late:
                start()

    sc = HD**-0.5

    def row(i, _):
        r, group = i % rows, i // rows
        lanes = pl.multiple_of(group * GROUP, GROUP)
        all_of = pl.ds(pl.multiple_of(r * seq, seq), seq)

        @pl.when(r == 0)
        def _():
            next_group(group)

        for p in range(GROUP // (2 * HD)):
            ln = pl.ds(lanes + p * 2 * HD, 2 * HD)
            k, v = qkve_ref[1, all_of, ln], qkve_ref[2, all_of, ln]
            kt = k.T
            tasks = []
            for b in reversed(range(seq // QB)):
                sl, n = rows_of(r, seq, b), (b + 1) * QB
                incl = twice(incl_ref[r, :n, b * QB : n])
                lse1 = pair_row(lse1_ref[group, :, sl], p)
                ratio = jnp.exp(lse1 - pair_row(lse2_ref[0, group, :, sl], p))
                do1, do2 = do1_ref[sl, ln].astype(F32), do2_ref[sl, ln].astype(F32)
                delta = row_products(do1, o1_ref[sl, ln].astype(F32))
                delta += ratio * row_products(do2, o2_ref[sl, ln].astype(F32))
                both = do1 + own_lanes(twice(do2.T), ratio).T
                q, do = cat_heads(qkve_ref[0, sl, ln], sc), cat_heads(both.astype(BF16))
                tasks.append((k[:n], v[:n], kt[:, :n], incl, q, do, lse1, delta))
            dka = dva = None
            for b, (dv, dk, dq) in zip(reversed(range(seq // QB)), blocks_back(tasks)):
                sl = rows_of(r, seq, b)
                dva, dka = add_rows(dva, dv), add_rows(dka, dk)
                dqkv_ref[0, sl, ln] = (own_lanes(dq).T * sc + part_ref[0, sl, ln].astype(F32)).astype(BF16)
            dqkv_ref[1, all_of, ln] = (dka + part_ref[1, all_of, ln].astype(F32)).astype(BF16)
            dqkv_ref[2, all_of, ln] = (dva + part_ref[2, all_of, ln].astype(F32)).astype(BF16)

        @pl.when(r == rows - 1)
        def _():
            for start, _ in leave:
                start(group)

        return 0

    lax.fori_loop(0, rows * groups, row, 0)
    for _, wait in late:
        wait()
    da = dot_nt(dqkv_ref[0], w_ref[0])
    da += dot_nt(dqkv_ref[1], w_ref[1])
    da += dot_nt(dqkv_ref[2], w_ref[2])
    da_ref[...] = da
    sums_ref[...] = jnp.zeros_like(sums_ref)

    def finish(i, _):
        sl = pl.ds(pl.multiple_of(i * ROWS_AT_ONCE, ROWS_AT_ONCE), ROWS_AT_ONCE)
        normal, inverse = norm_stats(x_ref[sl].astype(F32))
        da = da_ref[sl]
        sums_ref[0:1] += jnp.sum(da * normal, axis=0, keepdims=True)
        sums_ref[1:2] += jnp.sum(da, axis=0, keepdims=True)
        back = norm_back(da, normal, inverse, gb_ref[0:1])
        gt_ref[sl] = (dh1_ref[sl] + dh2_ref[sl] + back).astype(BF16)
        return 0

    lax.fori_loop(0, rows * seq // ROWS_AT_ONCE, finish, 0)
    for g in range(groups):
        for _, wait in leave:
            wait(g)


def attend_back_even(w, incl, qkve, o1, lse1, do1, o2, lse2, do2, part, dh1, dh2, x, gb):
    rows, seq = incl.shape[0], incl.shape[1]
    n, d = x.shape
    f = w.shape[2]
    qkv, one = sds((3, n, f), BF16), sds((n, f), BF16)
    near = (w, incl, qkv, one, one, one, one, qkv, dh1, dh1, x, qkv, sds((n, d), F32))
    far = lambda *ts: [(t, FAR) for t in ts]
    return resident(
        functools.partial(attend_back_even_body, rows, seq),
        far(w, incl, qkve, o1)
        + [lse1]
        + far(do1, o2)
        + [lse2]
        + far(do2.reshape(2, n, f), part, dh1, dh2, x)
        + [gb],
        [(qkv, FAR), sds((n, d), BF16), sds((2, d), F32)],
        scratch=[pltpu.VMEM(t.shape, t.dtype) for t in near] + [pltpu.SemaphoreType.DMA((64,))],
        flops=6 * n * d * f + 40 * n * seq * f,
        vmem=40,
        name="attend_back_even",
    )


CHUNK = 512
ROWS_AT_ONCE = 256


def chunk_of(ref, j, axis):
    at = pl.ds(pl.multiple_of(j * CHUNK, CHUNK), CHUNK)
    return ref.at[:, at] if axis else ref.at[at]


class Chunks:
    def __init__(self, moves, far, near, axis, ring=False, leave=False):
        self.first = moves.take(far.shape[axis] // CHUNK)
        self.sems, self.far, self.near = moves.sems, far, near
        self.axis, self.ring, self.leave = axis, ring, leave

    def copy(self, j):
        near = self.near.at[j % self.near.shape[0]] if self.ring else chunk_of(self.near, j, self.axis)
        ends = (chunk_of(self.far, j, self.axis), near)
        return pltpu.make_async_copy(*(ends[::-1] if self.leave else ends), self.sems.at[self.first + j])

    def start(self, j):
        self.copy(j).start()

    def wait(self, j):
        self.copy(j).wait()


class Weight:
    def __init__(self, moves, pieces, near, axis):
        self.axis, self.near = axis, near
        self.own = Chunks(moves, pieces[0], near, axis) if pieces[0] is not None else None
        self.number = near.shape[axis] // CHUNK // 2
        self.others, start = [], near.shape[axis] // 2
        for far in pieces[1:]:
            at = pl.ds(start, far.shape[axis])
            self.others.append(moves.later(far, near.at[:, at] if axis else near.at[at]))
            start += far.shape[axis]

    def start_others(self):
        for start, _ in self.others:
            start()

    def wait_others(self):
        for _, wait in self.others:
            wait()


def load_in_turn(j, *weights):
    number = weights[0].number

    @pl.when(j < number)
    def _():
        for w in weights:
            w.own.wait(j)

    @pl.when(j + 2 < number)
    def _():
        for w in weights:
            w.own.start(j + 2)

    @pl.when(j + 2 == number)
    def _():
        for w in weights:
            w.start_others()

    @pl.when(j == number)
    def _():
        for w in weights:
            w.wait_others()


def start_loads(*weights):
    for j in range(2):
        for w in weights:
            w.own.start(j)


def feed_chunk(n2_ref, wup_ref, wdown_ref, j, g_buf, d_buf, ho_ref, gs, ds, first):
    @pl.when(first >= 2)
    def _():
        gs.wait(j - 2)
        ds.wait(j - 2)

    half = n2_ref.shape[0] // 2
    parts = []
    for sl in (slice(0, half), slice(half, 2 * half)):
        g, d = gelu_parts(dot(n2_ref[sl], chunk_of(wup_ref, j, 1)[...]))
        parts.append(g.astype(BF16))
        g_buf[j % 2, sl] = parts[-1]
        d_buf[j % 2, sl] = d.astype(BF16)
    gs.start(j)
    ds.start(j)
    for i, g in enumerate(parts):
        ho_ref[i * half : (i + 1) * half] += dot(g, chunk_of(wdown_ref, j, 0)[...])


def start_norm(x_ref, h1_ref, n2_ref, gb_ref, ho_ref=None):
    def part(k, _):
        sl = pl.ds(pl.multiple_of(k * ROWS_AT_ONCE, ROWS_AT_ONCE), ROWS_AT_ONCE)
        h1 = x_ref[sl].astype(F32) + h1_ref[sl]
        h1_ref[sl] = h1
        normal, _ = norm_stats(h1)
        n2_ref[sl] = (normal * gb_ref[1:2] + gb_ref[3:4]).astype(BF16)
        if ho_ref is not None:
            ho_ref[sl] = h1 + gb_ref[4:5]
        return 0

    lax.fori_loop(0, h1_ref.shape[0] // ROWS_AT_ONCE, part, 0)


def mlp_own_body(
    x_far, o_far, wout_far, gb_ref, wup_far, wdown_far,
    h1_far, n2_far, g_far, d_far, ho_far,
    x_ref, o_ref, wout_ref, wup_ref, wdown_ref, h1_ref, n2_ref, ho_ref, g_buf, d_buf, sems,
):
    moves = Moves(sems)
    first = [moves.whole(*t) for t in ((o_far, o_ref), (wout_far, wout_ref), (x_far, x_ref))]
    ups, downs = Chunks(moves, wup_far, wup_ref, 1), Chunks(moves, wdown_far, wdown_ref, 0)
    gs, ds = (Chunks(moves, f, b, 1, True, True) for f, b in ((g_far, g_buf), (d_far, d_buf)))
    number = wup_far.shape[1] // CHUNK
    for wait in first:
        wait()
    for j in range(number):
        ups.start(j)
        downs.start(j)
    h1_ref[...] = dot(o_ref[...], wout_ref[...])
    start_norm(x_ref, h1_ref, n2_ref, gb_ref, ho_ref)
    kept = [moves.whole(*t) for t in ((h1_ref, h1_far), (n2_ref, n2_far))]

    def step(j, _):
        ups.wait(j)
        downs.wait(j)
        feed_chunk(n2_ref, wup_ref, wdown_ref, j, g_buf, d_buf, ho_ref, gs, ds, j)
        return 0

    lax.fori_loop(0, number, step, 0)
    kept.append(moves.whole(ho_ref, ho_far))
    for wait in kept:
        wait()
    for j in range(number - 2, number):
        gs.wait(j)
        ds.wait(j)


def mlp_other_body(number_up, number_down, n2_far, part_far, g_in, d_in, gb_ref, *refs):
    ups_far, refs = refs[:number_up], refs[number_up:]
    downs_far, refs = refs[:number_down], refs[number_down:]
    g_far, d_far, ho_far, ao_far, n2_ref, wup_ref, wdown_ref, ho_ref, ao_ref, g_buf, d_buf, sems = refs
    moves = Moves(sems)
    up = Weight(moves, (None,) + ups_far, wup_ref, 1)
    down = Weight(moves, (None,) + downs_far, wdown_ref, 0)
    gs, ds = (Chunks(moves, f, b, 1, True, True) for f, b in ((g_far, g_buf), (d_far, d_buf)))
    ready = [moves.whole(*t) for t in ((n2_far, n2_ref), (part_far, ho_ref))]
    up.start_others()
    down.start_others()
    for wait in ready:
        wait()
    up.wait_others()
    down.wait_others()

    def step(i, _):
        feed_chunk(n2_ref, wup_ref, wdown_ref, up.number + i, g_buf, d_buf, ho_ref, gs, ds, i)
        return 0

    lax.fori_loop(0, up.number, step, 0)
    sent = moves.whole(ho_ref, ho_far)

    def norm(k, _):
        sl = pl.ds(pl.multiple_of(k * ROWS_AT_ONCE, ROWS_AT_ONCE), ROWS_AT_ONCE)
        normal, _ = norm_stats(ho_ref[sl])
        ao_ref[sl] = (normal * gb_ref[0:1] + gb_ref[2:3]).astype(BF16)
        return 0

    lax.fori_loop(0, ho_ref.shape[0] // ROWS_AT_ONCE, norm, 0)
    moves.whole(ao_ref, ao_far)()
    sent()
    for j in range(2 * up.number - 2, 2 * up.number):
        gs.wait(j)
        ds.wait(j)


def near_of(*arrays):
    return [pltpu.VMEM(t.shape, t.dtype) for t in arrays]


def far_of(*arrays):
    return [(t, FAR) for t in arrays]


def mlp_own(x, o, wout, gb, wup, wdown):
    n, d = x.shape
    ff = 2 * wup.shape[1]
    h1, low, wide = sds((n, d), F32), sds((n, d), BF16), sds((n, ff), BF16)
    return resident(
        mlp_own_body,
        far_of(x, o, wout) + [gb] + far_of(wup, wdown),
        far_of(h1, low, wide, wide, h1),
        scratch=near_of(x, o, wout, wup, wdown, h1, low, h1)
        + [pltpu.VMEM((2, n, CHUNK), BF16)] * 2
        + [pltpu.SemaphoreType.DMA((40,))],
        vmem=36,
        name="mlp_own",
    )


def mlp_other(n2, part, g, dgelu, gb, ups, downs):
    n, d = n2.shape
    ff = g.shape[1]
    return resident(
        functools.partial(mlp_other_body, len(ups), len(downs)),
        far_of(n2, part, g, dgelu) + [gb] + far_of(*ups, *downs),
        far_of(sds(g.shape, BF16), sds(g.shape, BF16), sds(part.shape, F32), sds(n2.shape, BF16)),
        scratch=near_of(n2, sds((d, ff), BF16), sds((ff, d), BF16), part, n2)
        + [pltpu.VMEM((2, n, CHUNK), BF16)] * 2
        + [pltpu.SemaphoreType.DMA((40,))],
        vmem=40,
        aliases={2: 0, 3: 1},
        name="mlp_other",
    )


def weave(seq):
    i = lax.broadcasted_iota(jnp.int32, (2 * seq, 2 * seq), 0)
    k = lax.broadcasted_iota(jnp.int32, (2 * seq, 2 * seq), 1)
    place = jnp.where(k < seq, 2 * k, 2 * (k - seq) + 1)
    return jnp.where(i == place, 1.0, 0.0).astype(BF16)


def after_norm_back(
    moves, size, h1_ref, dn_ref, db_ref, wout_ref, gb_ref, sums_ref, dp_ref, do_ref, dh1_far, dp_far, do_far
):
    gain_sum = jnp.zeros_like(gb_ref[0:1])
    bias_sum = jnp.zeros_like(gb_ref[0:1])
    waits = []
    for i in range(h1_ref.shape[0] // size):
        sl = slice(i * size, (i + 1) * size)
        normal, inverse = norm_stats(h1_ref[sl])
        dn = dn_ref[sl]
        gain_sum += jnp.sum(dn * normal, axis=0, keepdims=True)
        bias_sum += jnp.sum(dn, axis=0, keepdims=True)
        dh1 = db_ref[sl].astype(F32) + norm_back(dn, normal, inverse, gb_ref[1:2])
        dn_ref[sl] = dh1
        dp_ref[sl] = dh1.astype(BF16)
    sums_ref[0:1] = gain_sum
    sums_ref[1:2] = bias_sum
    waits += [moves.whole(dn_ref, dh1_far), moves.whole(dp_ref, dp_far)]
    do_ref[...] = dot_nt(dp_ref[...], wout_ref[...]).astype(BF16)
    return waits + [moves.whole(do_ref, do_far)]


def mlp_second_body(rows, seq, number_up, number_down, x_far, ho_far, o_far, cot_far, wout_far, gb_ref, *refs):
    mlp_second_work(rows, seq, x_far, ho_far, o_far, cot_far, wout_far, gb_ref, *in_pieces(refs, number_up, number_down))


def in_pieces(refs, *numbers):
    out = []
    for k in numbers:
        out.append(refs[:k])
        refs = refs[k:]
    return out + list(refs)


def mlp_second_work(
    rows, seq, x_far, ho_far, o_far, cot_far, wout_far, gb_ref, ups_far, downs_far,
    outs_far, outs2_far, n2_far, g_far, du_far, dh1_far, dp_far, do_far, sums_ref, dm_far,
    x_ref, ho_ref, o_ref, cot_ref, wout_ref, wup_ref, wdown_ref, n2_ref, dm_ref,
    h1_ref, z_ref, dn_ref, dp_ref, do_ref, g_buf, du_buf, sems,
):
    n = rows * seq
    moves = Moves(sems)
    halves = (slice(0, n), slice(n, 2 * n))
    cot_there = moves.whole(cot_far, cot_ref)
    first = [moves.whole(*t) for t in ((o_far, o_ref), (wout_far, wout_ref), (x_far, x_ref))]
    up, down = Weight(moves, ups_far, wup_ref, 1), Weight(moves, downs_far, wdown_ref, 0)
    gs, dus = (Chunks(moves, f, b, 1, True, True) for f, b in ((g_far, g_buf), (du_far, du_buf)))
    number = 2 * up.number
    mix = weave(seq)
    cot_there()
    for r in range(rows):
        parted = dot_tn(mix, cot_ref[r]).astype(BF16)
        for i in range(2):
            dm_ref[i * n + r * seq : i * n + (r + 1) * seq] = parted[i * seq : (i + 1) * seq]
    for wait in first:
        wait()
    then = moves.whole(ho_far, ho_ref)
    start_loads(up, down)
    for i, sl in enumerate(halves):
        if i:
            then()
        h1_ref[sl] = dot(o_ref[i], wout_ref[...])
        start_norm(x_ref if i == 0 else ho_ref, h1_ref.at[pl.ds(i * n, n)], n2_ref.at[pl.ds(i * n, n)], gb_ref)
    kept = [moves.whole(*t) for t in ((n2_ref, n2_far), (dm_ref, dm_far))]
    z_ref[...] = jnp.zeros_like(z_ref)
    dn_ref[...] = jnp.zeros_like(dn_ref)

    def step(j, _):
        load_in_turn(j, up, down)

        @pl.when(j >= 2)
        def _():
            gs.wait(j - 2)
            dus.wait(j - 2)

        for sl in halves:
            u = dot(n2_ref[sl], chunk_of(wup_ref, j, 1)[...])
            dg = dot_nt(dm_ref[sl], chunk_of(wdown_ref, j, 0)[...])
            g, d = gelu_parts(u)
            g = g.astype(BF16)
            du = (dg * d).astype(BF16)
            g_buf[j % 2, sl] = g
            du_buf[j % 2, sl] = du
            z_ref[sl] += dot(g, chunk_of(wdown_ref, j, 0)[...])
            dn_ref[sl] += dot_nt(du, chunk_of(wup_ref, j, 1)[...])
        gs.start(j)
        dus.start(j)
        return 0

    lax.fori_loop(0, number, step, 0)
    for r in range(rows):
        pair = [slice(i * n + r * seq, i * n + (r + 1) * seq) for i in range(2)]
        z = jnp.concatenate([(h1_ref[s] + z_ref[s]).astype(BF16) for s in pair], axis=0)
        cot_ref[r] = dot(mix, z).astype(BF16)
    half = rows // 2
    kept += [moves.whole(cot_ref.at[pl.ds(i * half, half)], far) for i, far in enumerate((outs_far, outs2_far))]
    kept += after_norm_back(
        moves, seq, h1_ref, dn_ref, dm_ref, wout_ref, gb_ref, sums_ref, dp_ref, do_ref, dh1_far, dp_far, do_far
    )
    for wait in kept:
        wait()
    for j in range(number - 2, number):
        gs.wait(j)
        dus.wait(j)


def mlp_second(x, ho, o2, cot, wout, gb, ups, downs, seq):
    n, d = x.shape
    ff = 2 * ups[0].shape[1]
    rows = n // seq
    low, wide, full = sds((2 * n, d), BF16), sds((2 * n, ff), BF16), sds((2 * n, d), F32)
    out = sds((rows // 2, 2 * seq, d), BF16)
    return resident(
        functools.partial(mlp_second_body, rows, seq, len(ups), len(downs)),
        far_of(x, ho, o2, cot, wout) + [gb] + far_of(*ups, *downs),
        far_of(out, out, low, wide, wide, full, low, low) + [sds((2, d), F32)] + far_of(low),
        scratch=near_of(x, ho, o2, cot, wout, sds((d, ff), BF16), sds((ff, d), BF16), low, low, full, full, full, low, low)
        + [pltpu.VMEM((2, 2 * n, CHUNK), BF16)] * 2
        + [pltpu.SemaphoreType.DMA((64,))],
        vmem=60,
        name="mlp_second",
    )


def mlp_back_body(rows, seq, number_up, number_down, dy_far, h1_far, wout_far, gb_ref, d_far, *refs):
    mlp_back_work(rows, seq, dy_far, h1_far, wout_far, gb_ref, d_far, *in_pieces(refs, number_up, number_down))


def mlp_back_work(
    rows, seq, dy_far, h1_far, wout_far, gb_ref, d_far, ups_far, downs_far,
    du_far, dh1_far, dp_far, do_far, sums_ref,
    dy_ref, h1_ref, wout_ref, wup_ref, wdown_ref, d_ref, dm_ref, dn_ref, dp_ref, do_ref, du_buf, sems,
):
    moves = Moves(sems)
    first = moves.whole(dy_far, dy_ref)
    up, down = Weight(moves, ups_far, wup_ref, 1), Weight(moves, downs_far, wdown_ref, 0)
    ds, dus = Chunks(moves, d_far, d_ref, 1), Chunks(moves, du_far, du_buf, 1, True, True)
    number = 2 * up.number
    start_loads(down, up)
    for j in range(2):
        ds.start(j)
    then = [moves.later(*t) for t in ((wout_far, wout_ref), (h1_far, h1_ref))]
    first()
    dm_ref[...] = dy_ref[...].astype(BF16)
    dn_ref[...] = jnp.zeros_like(dn_ref)

    def step(j, _):
        load_in_turn(j, down, up)
        ds.wait(j)

        @pl.when(j + 2 < number)
        def _():
            ds.start(j + 2)

        @pl.when(j + 2 == number)
        def _():
            for start, _ in then:
                start()

        @pl.when(j >= 2)
        def _():
            dus.wait(j - 2)

        dg = dot_nt(dm_ref[...], chunk_of(wdown_ref, j, 0)[...])
        du = (dg * chunk_of(d_ref, j, 1)[...].astype(F32)).astype(BF16)
        du_buf[j % 2] = du
        dus.start(j)
        dn_ref[...] += dot_nt(du, chunk_of(wup_ref, j, 1)[...])
        return 0

    lax.fori_loop(0, number, step, 0)
    for _, wait in then:
        wait()
    kept = after_norm_back(
        moves, seq, h1_ref, dn_ref, dy_ref, wout_ref, gb_ref, sums_ref, dp_ref, do_ref, dh1_far, dp_far, do_far
    )
    for wait in kept:
        wait()
    for j in range(number - 2, number):
        dus.wait(j)


def mlp_back(dy, h1, wout, gb, dgelu, ups, downs, seq):
    n, d = dy.shape
    ff = dgelu.shape[1]
    low = sds((n, d), BF16)
    return resident(
        functools.partial(mlp_back_body, n // seq, seq, len(ups), len(downs)),
        far_of(dy, h1, wout) + [gb] + far_of(dgelu, *ups, *downs),
        far_of(dgelu, h1, low, low) + [sds((2, d), F32)],
        scratch=near_of(dy, h1, wout, sds((d, ff), BF16), sds((ff, d), BF16), dgelu, low, dy, low, low)
        + [pltpu.VMEM((2, n, CHUNK), BF16)]
        + [pltpu.SemaphoreType.DMA((48,))],
        vmem=48,
        name="mlp_back",
    )


def lanes_at(ref, start, size):
    return ref.at[:, pl.ds(pl.multiple_of(start, 128), size)]


def stack_rows(moves, pairs, target, start, size):
    copies, row = [], 0
    for far in pairs:
        copies.append(moves.later(lanes_at(far, start, size), target.at[pl.ds(row, far.shape[0])]))
        row += far.shape[0]
    return (lambda: [s() for s, _ in copies]), (lambda: [w() for _, w in copies])


def all_of(*parts):
    return (lambda: [s() for s, _ in parts]), (lambda: [w() for _, w in parts])


class InTurn:
    def __init__(self, *tiles):
        self.tiles, self.at = tiles, 0
        for start, _ in tiles[:2]:
            start()

    def next(self):
        self.tiles[self.at][1]()
        self.at += 1
        if self.at + 1 < len(self.tiles):
            self.tiles[self.at + 1][0]()


def place_of(quarter, y, me_ref):
    return quarter if y else 4 + (quarter ^ me_ref[1])


def packed(body, me, arrays, shape, scratch, flops, vmem, name):
    smem = pl.BlockSpec(memory_space=pltpu.SMEM)
    out = sds(shape, BF16)
    return resident(
        body,
        [(me, smem)] + far_of(*arrays),
        far_of(out, out),
        scratch=near_of(sds((2,) + shape, BF16)) + scratch + [pltpu.SemaphoreType.DMA((64,))],
        flops=flops,
        vmem=vmem,
        name=name,
    )


def grad_down_body(
    me_ref, g1_far, g2_far, dy_far, dm2_far, keep_far, go_far, out_ref, dy_ref, dm_ref, g_ref, acc_ref, sems
):
    low, group = me_ref[0] % 4, (me_ref[0] // 4) % 2
    ring, n, b = g_ref.shape[0], g1_far.shape[0], g_ref.shape[2]
    moves = Moves(sems)
    first, last = moves.take(2 * ring), moves.take(4)

    def tile(i):
        side, y, h = 1 - i // 4, (i // 2) % 2, i % 2
        quarter = ((me_ref[0] // 8) ^ side) * 2 + h
        at = jnp.where(y == 0, 4 + (quarter ^ me_ref[1]), quarter) * b
        return side, y, h, at

    def loads(i):
        at, slot = tile(i)[3], i % ring
        near = g_ref.at[slot]
        ends = ((g1_far, near.at[pl.ds(0, n)]), (g2_far, near.at[pl.ds(n, 2 * n)]))
        return [pltpu.make_async_copy(lanes_at(f, at, b), t, sems.at[first + 2 * slot + k]) for k, (f, t) in enumerate(ends)]

    def store(far, side, y):
        return pltpu.make_async_copy(out_ref.at[side, y], far.at[y], sems.at[last + side * 2 + y])

    ready = [moves.whole(dy_far, dy_ref), moves.whole(dm2_far, dm_ref.at[pl.ds(n, 2 * n)])]
    for i in range(2):
        for c in loads(i):
            c.start()
    for wait in ready:
        wait()
    dm_ref[:n] = dy_ref[...].astype(BF16)

    def step(i, _):
        side, y, h, _ = tile(i)
        for c in loads(i):
            c.wait()

        @pl.when(i + 2 < 8)
        def _():
            for c in loads(i + 2):
                c.start()

        acc_ref[...] = dot_tn(g_ref[i % ring], dm_ref[...]).reshape(acc_ref.shape)
        for s in range(4):
            out_ref[side, y, (h ^ group) * 4 + s] = acc_ref[s ^ low].astype(BF16)

        @pl.when((h == 1) & (side == 1))
        def _():
            store(go_far, 1, y).start()

        @pl.when((h == 1) & (side == 0))
        def _():
            store(keep_far, 0, y).start()

        return 0

    lax.fori_loop(0, 8, step, 0)
    for y in range(2):
        store(go_far, 1, y).wait()
        store(keep_far, 0, y).wait()


def grad_down(me, g1, g2, dy, dm2):
    n, d = dy.shape
    ff = g1.shape[1]
    b = ff // 8
    return packed(
        grad_down_body,
        me,
        (g1, g2, dy, dm2),
        (2, 8, b // 4, d),
        [
            pltpu.VMEM((n, d), F32),
            pltpu.VMEM((3 * n, d), BF16),
            pltpu.VMEM((3, 3 * n, b), BF16),
            pltpu.VMEM((4, b // 4, d), F32),
        ],
        2 * 3 * n * d * ff,
        40,
        "grad_down",
    )


CUT = 768
CUT_BACK = 1536


def swapped(s):
    return ((s >> 1) % 2) * 4 + ((s >> 2) % 2) * 2 + s % 2


def put_slots(out_ref, y, lanes, acc_ref, me):
    for s in range(16):
        out_ref[s // 8, y, s % 8, :, lanes] = acc_ref[s ^ me].astype(BF16)


def grad_up_body(
    me_ref, n1_far, n2_far, du1_far, du2_far, dp1_far, dp2_far, o1_far, o2_far, keep_far, go_far,
    out_ref, n_ref, t_ref, du_ref, dp_ref, o_ref, acc_ref, acc2_ref, sems,
):
    moves = Moves(sems)
    d, f = n_ref.shape[1], o_ref.shape[2]
    ring, c, n = du_ref.shape[0], du_ref.shape[2], du1_far.shape[0]
    first, last = moves.take(4 * ring), moves.take(4)

    def loads(i):
        y, t, slot = i // 2, i % 2, i % ring
        copies = []
        for k in range(2):
            quarter = 2 * t + k
            at = jnp.where(y == 0, 4 + (quarter ^ me_ref[1]), quarter) * f
            near = lanes_at(du_ref.at[slot], k * f, f)
            for far, rows in ((du1_far, pl.ds(0, n)), (du2_far, pl.ds(n, 2 * n))):
                copies.append((lanes_at(far, at, f), near.at[rows]))
        return [pltpu.make_async_copy(a, b, sems.at[first + 4 * slot + k]) for k, (a, b) in enumerate(copies)]

    def stores(y):
        return [
            pltpu.make_async_copy(out_ref.at[i, y], far.at[y], sems.at[last + 2 * y + i])
            for i, far in enumerate((keep_far, go_far))
        ]

    ready = stack_rows(moves, (n1_far, n2_far), n_ref, 0, d)
    ready[0]()
    for c0 in loads(0):
        c0.start()
    out_loads = [stack_rows(moves, (dp1_far, dp2_far), dp_ref, 0, d)]
    out_loads += [stack_rows(moves, (o1_far, o2_far), o_ref.at[y], (1 - y) * f, f) for y in range(2)]
    ready[1]()
    for c0 in loads(1):
        c0.start()
    t_ref[...] = n_ref[...].T

    def step(i, _):
        y, t = i // 2, i % 2
        for c0 in loads(i):
            c0.wait()

        @pl.when(i + 2 < 4)
        def _():
            for c0 in loads(i + 2):
                c0.start()

        @pl.when(i == 0)
        def _():
            for start, _ in out_loads:
                start()

        acc_ref[...] = dot(t_ref[...], du_ref[i % ring]).reshape(acc_ref.shape)
        put_slots(out_ref, y, pl.ds(pl.multiple_of(t * c, c), c), acc_ref, jnp.where(t == 0, me_ref[0], me_ref[2]))

        @pl.when(i == 1)
        def _():
            for _, wait in out_loads:
                wait()

        @pl.when(t == 1)
        def _():
            acc2_ref[...] = dot_tn(dp_ref[...], o_ref[y]).reshape(acc2_ref.shape)
            put_slots(out_ref, y, slice(2 * c, 2 * c + f), acc2_ref, me_ref[2])
            for s in stores(y):
                s.start()

        return 0

    lax.fori_loop(0, 4, step, 0)
    for y in range(2):
        for s in stores(y):
            s.wait()


def grad_up(me, n1, n2, du1, du2, dp1, dp2, o1, o2):
    n, d = n1.shape
    ff = du1.shape[1]
    f, c = o1.shape[1] // 2, ff // 4
    return packed(
        grad_up_body,
        me,
        (n1, n2, du1, du2, dp1, dp2, o1, o2),
        (2, 8, d // 16, 2 * c + f),
        [
            pltpu.VMEM((3 * n, d), BF16),
            pltpu.VMEM((d, 3 * n), BF16),
            pltpu.VMEM((3, 3 * n, c), BF16),
            pltpu.VMEM((3 * n, d), BF16),
            pltpu.VMEM((2, 3 * n, f), BF16),
            pltpu.VMEM((16, d // 16, c), F32),
            pltpu.VMEM((16, d // 16, f), F32),
        ],
        2 * 3 * n * d * (ff + d),
        56,
        "grad_up",
    )


def grad_qkv_body(me_ref, ae_far, ao_far, de_far, do_far, keep_far, go_far, out_ref, a_ref, t_ref, d_ref, acc_ref, sems):
    moves = Moves(sems)
    d = a_ref.shape[1]
    f = de_far.shape[2] // 2
    ready = stack_rows(moves, (ae_far, ao_far), a_ref, 0, d)
    n, first = ae_far.shape[0], moves.take(6)

    def loads(j):
        return [
            pltpu.make_async_copy(far.at[j], d_ref.at[j, pl.ds(k * n, n)], sems.at[first + 2 * j + k])
            for k, far in enumerate((de_far, do_far))
        ]

    ready[0]()
    for c in loads(0):
        c.start()
    ready[1]()
    for j in (1, 2):
        for c in loads(j):
            c.start()
    t_ref[...] = a_ref[...].T

    def step(j, _):
        for c in loads(j):
            c.wait()
        acc_ref[...] = dot(t_ref[...], d_ref[j]).reshape(acc_ref.shape)
        lanes = pl.ds(pl.multiple_of(j * f, f), f)
        for s in range(16):
            block = acc_ref[s ^ me_ref[0]].astype(BF16)
            out_ref[s // 8, 1, s % 8, :, lanes] = block[:, :f]
            out_ref[s // 8, 0, s % 8, :, lanes] = block[:, f:]
        return 0

    lax.fori_loop(0, 3, step, 0)
    sent = [moves.whole(out_ref.at[i], far) for i, far in ((1, go_far), (0, keep_far))]
    for wait in sent:
        wait()


def grad_qkv(me, ae, ao, dqkv_e, dqkv_o):
    n, d = ae.shape
    f = dqkv_e.shape[2] // 2
    return packed(
        grad_qkv_body,
        me,
        (ae, ao, dqkv_e, dqkv_o),
        (2, 8, d // 16, 3 * f),
        [
            pltpu.VMEM((2 * n, d), BF16),
            pltpu.VMEM((d, 2 * n), BF16),
            pltpu.VMEM((3, 2 * n, 2 * f), BF16),
            pltpu.VMEM((16, d // 16, 2 * f), F32),
        ],
        2 * 2 * 3 * n * d * 2 * f,
        40,
        "grad_qkv",
    )


def packed_call(body, grid, me, ins, outs, scratch=(), flops=0, aliases={}, name=None):
    return pl.pallas_call(
        body,
        grid_spec=pltpu.PrefetchScalarGridSpec(
            num_scalar_prefetch=1,
            grid=grid,
            in_specs=[s for _, s in ins],
            out_specs=[s for _, s in outs],
            scratch_shapes=scratch,
        ),
        out_shape=[a for a, _ in outs],
        input_output_aliases=aliases,
        compiler_params=pltpu.CompilerParams(
            dimension_semantics=("arbitrary",) * len(grid), vmem_limit_bytes=VMEM_LIMIT
        ),
        cost_estimate=pl.CostEstimate(flops=int(flops) // 16, bytes_accessed=0, transcendentals=0),
        name=name,
    )(me, *[a for a, _ in ins])


def unpack_down_body(me_ref, part_ref, *refs):
    low, rows = me_ref[0] % 8, part_ref.shape[1]
    for b in range(8):
        refs[-1][b * rows : (b + 1) * rows] = part_ref[swapped(b ^ low)].astype(F32)


def unpack_down(me, side, part, into=()):
    _, r, w = part.shape
    half = 8 * r
    at = lambda me: (me[0] // 8) ^ side
    ins = [(part, pl.BlockSpec(part.shape, lambda i, me: (0, 0, 0)))]
    ins += [(t, pl.BlockSpec(memory_space=pl.ANY)) for t in into]
    return packed_call(
        unpack_down_body,
        (1,),
        me,
        ins,
        [(sds((2 * half, w), F32), pl.BlockSpec((half, w), lambda i, me: (at(me), 0)))],
        aliases={2 + i: i for i in range(len(into))},
        name="unpack_down",
    )[0]


def unpack_rest_body(side, me_ref, part_ref, *refs):
    up_far, out_far, qkv_far, up_st, wide, out_st, qkv_st, sems = refs[-8:]
    moves = Moves(sems)
    left, right = me_ref[0] % 8, me_ref[2] % 8
    rows, half = part_ref.shape[1], 8 * part_ref.shape[1]
    d, f = up_st.shape[1], wide.shape[1]
    base = ((me_ref[0] // 8) ^ side) * half
    sent = []
    for b in range(8):
        sl = slice(b * rows, (b + 1) * rows)
        up_st[sl, :CUT] = part_ref[b ^ left, :, :CUT].astype(F32)
        up_st[sl, CUT:] = part_ref[swapped(b ^ right), :, CUT:d].astype(F32)
        wide[sl] = part_ref[b ^ right, :, d : d + f].astype(F32)
        if b % 4 == 3:
            start, size = (b - 3) * rows, 4 * rows
            at = pl.ds(pl.multiple_of(base + start, 8), size)
            sent.append(moves.whole(up_st.at[pl.ds(start, size)], up_far.at[at]))
    out_st[...] = wide[...].T
    sent.append(moves.whole(out_st, lanes_at(out_far, base, half)))
    for j in range(3):
        for b in range(8):
            sl = slice(b * rows, (b + 1) * rows)
            qkv_st[j, sl] = part_ref[b ^ right, :, d + (j + 1) * f : d + (j + 2) * f].astype(F32)
        sent.append(moves.whole(qkv_st.at[j], qkv_far.at[j, pl.ds(pl.multiple_of(base, 8), half)]))
    for wait in sent:
        wait()


def unpack_rest(me, side, part, into=()):
    _, r, w = part.shape
    half = 8 * r
    d, f = CUT_BACK, (w - CUT_BACK) // 4
    smem = pl.BlockSpec(memory_space=pltpu.SMEM)
    outs = [sds((2 * half, d), F32), sds((f, 2 * half), F32), sds((3, 2 * half, f), F32)]
    stages = [sds((half, d), F32), sds((half, f), F32), sds((f, half), F32), sds((3, half, f), F32)]
    return resident(
        functools.partial(unpack_rest_body, side),
        [(me, smem), part] + far_of(*into),
        far_of(*outs),
        scratch=near_of(*stages) + [pltpu.SemaphoreType.DMA((8,))],
        vmem=24,
        aliases={2 + i: i for i in range(len(into))},
        name="unpack_rest",
    )


def fold(*parts):
    return sum(p.astype(F32) for p in parts).astype(BF16)


def after(value, *first):
    return lax.optimization_barrier((value, first))[0]


class Chunk:
    def __init__(self, keep, got):
        self.keep, self.got = keep, got
        self.sent = None

    def wait(self, *also):
        self.got, also = lax.optimization_barrier((self.got, also))
        return also

    def to_partner(self):
        total = fold(self.keep, self.got)
        self.keep, self.sent = total[1], total[0]
        self.got = lax.ppermute(self.sent, "tensor", FLIP)

    def gather_core(self):
        self.got = lax.ppermute(self.keep, "core", FLIP)


def add(k, g):
    return (k.astype(F32) + g.astype(F32)).astype(BF16)


def phase_shapes(mode, parts):
    shapes = [p[0].shape for p in parts]
    s = shapes[0]
    if mode == "half":
        out = s[:-3] + (s[-3] // 2,) + s[-2:]
        return [out, out]
    if mode == "partner":
        return [s[1:], s[1:]]
    if mode == "last":
        out = (s[0] // 2, s[1], sum(t[2] for t in shapes))
        return [out, out]
    if mode == "sum":
        return [s]
    if mode == "split":
        return [(2 * s[0], s[1], CUT_BACK), (2 * s[0], s[1], s[2] - CUT_BACK)]
    return [(2 * s[0], s[1], sum(t[2] for t in shapes))]


def phase_part(mode, parts, outs):
    if mode == "half":
        (k, g), n = parts[0], outs[0].shape[-3]
        lead = (slice(None),) * (len(k.shape) - 3)
        for i, out in enumerate(outs):
            at = lead + (slice(i * n, (i + 1) * n),)
            out[...] = add(k[at], g[at])
    elif mode == "partner":
        k, g = parts[0]
        for i, out in zip((1, 0), outs):
            out[...] = add(k[i], g[i])
    elif mode == "last":
        n, lane = outs[0].shape[0], 0
        for k, g in parts:
            for i, out in enumerate(outs):
                at = slice(i * n, (i + 1) * n)
                out[:, :, lane : lane + k.shape[2]] = add(k[at], g[at])
            lane += k.shape[2]
    elif mode == "sum":
        outs[0][...] = add(parts[0][0][...], parts[0][1][...])
    elif mode == "split":
        for i, ref in enumerate(parts[0]):
            at = slice(i * ref.shape[0], (i + 1) * ref.shape[0])
            outs[0][at] = ref[:, :, :CUT_BACK]
            outs[1][at] = ref[:, :, CUT_BACK:]
    else:
        lane = 0
        for pair in parts:
            for i, ref in enumerate(pair):
                outs[0][i * ref.shape[0] : (i + 1) * ref.shape[0], :, lane : lane + ref.shape[2]] = ref[...]
            lane += pair[0].shape[2]


def phase(*items):
    shapes = [phase_shapes(*t) for t in items]

    def body(*refs):
        at = sum(2 * len(parts) for _, parts in items)
        ins, outs = list(refs[:at]), list(refs[at:])
        for (mode, parts), made in zip(items, shapes):
            mine = [(ins.pop(0), ins.pop(0)) for _ in parts]
            phase_part(mode, mine, [outs.pop(0) for _ in made])

    flat = resident(
        body,
        [t for _, parts in items for pair in parts for t in pair],
        [sds(s, BF16) for made in shapes for s in made],
        vmem=16,
        name="phase",
    )
    flat = list(flat)
    return [[flat.pop(0) for _ in made] for made in shapes]


class Hops(Chunk):
    def __init__(self, outer, keep, got):
        super().__init__(keep, got)
        self.axes = {"x": ("x", 2, 1), "z": ("o", outer, 1), "w": ("o", outer, 2)}
        self.extra = [("o", outer, 1 << b) for b in range(2, outer.bit_length() - 1)]

    def over(self, way, t):
        return lax.ppermute(t, "tensor", FLIP) if way == "partner" else flip_bit(t, *self.axes[way])

    def send(self, *parts):
        self.keep, self.sent, self.got = [], [], []
        for total, way in parts:
            if way == "partner":
                keep, sent = total[1], total[0]
            else:
                half = total.shape[-3] // 2
                keep, sent = total[..., :half, :, :], total[..., half:, :, :]
            self.keep.append(keep)
            self.sent.append(sent)
            self.got.append(self.over(way, sent))

    def first(self):
        total = fold(self.keep, self.got)
        self.send((total[..., :CUT], "x"), (total[..., CUT:], "z"))

    def first_hop(self, way):
        self.send((fold(self.keep, self.got), way))

    def parts(self):
        return list(zip(self.keep, self.got))

    def hop(self, *ways):
        items = [("partner" if w == "partner" else "half", [p]) for w, p in zip(ways, self.parts())]

        def then(made):
            self.keep, self.sent = [m[0] for m in made], [m[1] for m in made]
            self.got = [self.over(w, s) for w, s in zip(ways, self.sent)]

        return items, then

    def absorb(self, other):
        self.keep, self.got = self.keep + other.keep, self.got + other.got

    def last_hop(self):
        def then(made):
            ((keep, sent),) = made
            self.keep, self.sent = [keep], [sent]
            self.got = [self.over("w", sent)]

        return [("last", self.parts())], then

    def back_first(self):
        def then(made):
            ((total,),) = made
            for s in self.extra:
                total = fold(total, flip_bit(total, *s))
            self.keep = self.sent = [total]
            self.got = [self.over("w", total)]

        return [("sum", self.parts())], then

    def back(self, *ways):
        if len(ways) == 2 and len(self.keep) == 1:
            items = [("split", self.parts())]
        else:
            items = [("join", [p]) for p in self.parts()]

        def then(made):
            self.keep = self.sent = [t for m in made for t in m]
            self.got = [self.over(w, t) for w, t in zip(ways, self.keep)]

        return items, then

    def back_core(self):
        def then(made):
            ((self.keep,),) = made
            self.sent = self.keep
            self.gather_core()

        return [("join", self.parts())], then


def all_steps(*steps):
    made = phase(*[item for items, _ in steps for item in items])
    for items, then in steps:
        then(made[: len(items)])
        made = made[len(items) :]


def mask_biases(seg):
    seq = seg.shape[1]
    place = jnp.arange(seq, dtype=jnp.int32)
    same = seg[:, :, None] == seg[:, None, :]
    below = (place[:, None] < place[None, :])[None]
    incl = (place[:, None] <= place[None, :])[None]
    bias = lambda m: jnp.where(same & m, 0.0, NEG).astype(F32)
    return bias(incl), bias(below)


def sync(*values):
    return lax.optimization_barrier(values)


class Link:
    def __init__(self, outer, w_qkv, w_out, w_up, w_down):
        self.outer = outer
        self.own = (w_qkv, w_out, w_up, w_down)
        self.core_at, self.x_at, o = (lax.axis_index(a) for a in ("core", "x", "o"))
        bits = {"x": self.x_at, "z": o % 2, "w": (o // 2) % 2}
        self.fetch_bits = self.core_at * 2 + self.x_at
        slots = []
        for order in ("xzw", "zxw"):
            slot = self.core_at
            for name in order:
                slot = slot * 2 + bits[name]
            slots.append(slot)
        self.me = jnp.stack([slots[0], self.fetch_bits, slots[1]]).astype(jnp.int32)
        self.me_z = self.me[2:0:-1]

    def quarter(self, own):
        flat = own.reshape(-1, own.shape[-1])
        return take_half(take_half(flat, self.core_at), self.x_at)

    def over_x(self, t):
        return lax.ppermute(t, "x", FLIP)

    def fetch(self, own_work):
        own = self.own
        size = own[2].shape[1] // 4
        part = lambda t, axis, bits: lax.dynamic_slice_in_dim(t, bits * size, size, axis)
        pieces = [
            self.quarter(own[1]),
            part(own[2], 1, self.fetch_bits),
            jnp.concatenate([part(own[3], 0, self.fetch_bits), part(own[3], 0, self.fetch_bits ^ 1)], axis=0),
        ]
        qkv = self.partner(self.quarter(own[0]))
        up, out, down = (self.partner(pieces[i]) for i in (1, 0, 2))
        qkv, own_work = sync(qkv, own_work)
        qkv, out, up = sync(ordered(self.x_at, qkv, self.over_x(qkv)).reshape(-1, qkv.shape[-1]), out, up)
        qkv_core, out_x, up_x = self.core(qkv), self.over_x(out), self.over_x(up)
        qkv = ordered(self.core_at, qkv, qkv_core).reshape(own[0].shape)

        def join_out(*work):
            nonlocal out, out_x
            work, out, out_x = sync(work, out, out_x)
            out = ordered(self.x_at, out, out_x).reshape(-1, out.shape[-1])
            out = ordered(self.core_at, out, self.core(out)).reshape(own[1].shape)
            return work, jnp.concatenate([own[1], out], axis=0)

        def pieces_of(*work):
            up_there, down_there, work = sync(up_x, down, work)
            ups = (own[2], up, up_there, self.core(up), self.core(up_there))
            return ups, (own[3], down_there, self.core(down_there)), work

        return own_work, own[0], qkv, jnp.concatenate([own[0], qkv], axis=2), join_out, pieces_of

    def partner(self, t):
        return lax.ppermute(t, "tensor", FLIP)

    def core(self, t):
        return lax.ppermute(t, "core", FLIP)

    def chunk(self, keep, got):
        return Chunk(keep, got)

    def hops(self, keep, got):
        return Hops(self.outer, keep, got)

    def small_steps(self):
        return [("core", 2, 1), ("tensor", 2, 1)] + steps_of(self.outer)

    def flip(self, t, step):
        return flip_bit(t, *step)


def local_part(x, seg, cot, gb, link):
    rows, seq = seg.shape
    n, width = x.shape
    me, me_z = link.me, link.me_z
    incl, strict = mask_biases(seg)
    normal, _ = norm_stats(x.astype(F32))
    a_e = (normal * gb[0] + gb[2]).astype(BF16)
    first = attend_first(a_e, link.own[0], incl)
    (a_e, first, cot), wq_own, fetched, wqkv, join_out, pieces_of = link.fetch((a_e, first, cot))
    second = attend_first(a_e, fetched, incl)
    qkv_e, o1 = (jnp.concatenate([s, t], axis=-1) for s, t in zip(first[:2], second[:2]))
    lse1 = jnp.concatenate([first[2], second[2]], axis=0).reshape(-1, GROUP // HD, n)
    (qkv_e, o1, lse1, wqkv), wout = join_out(qkv_e, o1, lse1, wqkv)
    h1, n2_1, g1, d1, part_one = mlp_own(x, o1, wout, gb, link.own[2], link.own[3])
    ups, downs, (n2_1, part_one) = pieces_of(n2_1, part_one)
    g1, d1, ho, a_o = mlp_other(n2_1, part_one, g1, d1, gb, ups[1:], downs[1:])
    qkv_o, o2, lse2 = attend_second(a_o, wqkv, incl, strict, qkv_e, o1, lse1)
    out, out_two, n2_2, g2, du2, dh1_2, dp2, do2, sums2, dm2 = mlp_second(x, ho, o2, cot, wout, gb, ups, downs, seq)
    out_got = link.partner(out)
    dqkv_o, part, dy, sums_o = attend_back(wqkv, incl, strict, qkv_e, qkv_o, o2, lse2, do2, dh1_2, ho, gb)
    o2_flat = o2.reshape(2 * n, width)

    out_got, dy = sync(out_got, dy)
    quarter = out_two.shape[1] // 2
    out_last = [link.partner(after(out_two[:, :quarter], out_got))]
    down_keep, down_go = grad_down(me_z, g1, g2, dy, dm2)
    down_keep, down_go, out_last[0] = sync(down_keep, down_go, out_last[0])
    out_last.append(link.partner(after(out_two[:, quarter:], down_go)))
    down = link.hops(down_keep, link.core(down_go))
    dy = after(dy, down_go)
    du1, dh1_1, dp1, do1, sums1 = mlp_back(dy, h1, wout, gb, d1, ups, downs, seq)
    du1, dp1, do1, out_last[1] = down.wait(du1, dp1, do1, out_last[1])
    down.to_partner()
    up_keep, up_go = grad_up(me, n2_1, n2_2, after(du1, down.sent), du2, dp1, dp2, o1, o2_flat)
    do1 = after(do1, up_go)
    dqkv_e, gt, sums_e = attend_back_even(wqkv, incl, qkv_e, o1, lse1, do1, o2, lse2, do2, part, dh1_1, dh1_2, x, gb)
    dqkv_e, gt, sums_e, up_go = down.wait(dqkv_e, gt, sums_e, up_go)
    up = link.hops(up_keep, link.core(up_go))
    down.keep, down.got = [down.keep], [down.got]
    all_steps(down.hop("z"))
    small = jnp.stack([sums_e[0] + sums_o[0], sums1[0] + sums2[0], sums_e[1] + sums_o[1], sums1[1] + sums2[1], sums_o[2]])
    qkv_keep, qkv_go = grad_qkv(me_z, a_e, a_o, after(dqkv_e, *down.sent), dqkv_o)
    out = link.finish(
        jnp.concatenate([out, out_two], axis=0), jnp.concatenate([out_got, jnp.concatenate(after(out_last, dqkv_e), axis=1)], axis=0), link.out_shape
    )
    qkv_keep, qkv_go, down.got, out = up.wait(qkv_keep, qkv_go, down.got, out)
    qkv = link.hops(qkv_keep, link.core(qkv_go))
    small_steps = iter(link.small_steps())
    small_got = link.flip(after(small, qkv_go), next(small_steps))

    chunks = [up, qkv]

    def wait_all():
        nonlocal small, small_got
        got, small_got = sync([c.got for c in chunks], small_got)
        for c, g in zip(chunks, got):
            c.got = g
        if small_got is not None:
            small = small + small_got
            step = next(small_steps, None)
            small_got = None if step is None else link.flip(small, step)

    wait_all()
    chunks.append(down)
    up.first()
    qkv.first_hop("partner")
    all_steps(down.hop("x"))
    wait_all()
    all_steps(up.hop("partner", "x"), qkv.hop("z"), down.hop("w"))
    wait_all()
    all_steps(up.hop("z", "partner"), qkv.hop("x"), down.back_first())
    half = gt.shape[0] // 2
    gt_got = [link.partner(after(gt[:half], *up.sent))]
    wait_all()
    up.absorb(qkv)
    chunks.remove(qkv)
    all_steps(up.last_hop(), down.back("z"))
    gt_got.append(link.partner(after(gt[half:], *up.sent)))
    (gt_got[0],) = up.wait(gt_got[0])
    wait_all()
    all_steps(up.back_first(), down.back("x"))
    (gt_got[1],) = up.wait(gt_got[1])
    wait_all()
    while small_got is not None:
        wait_all()
    all_steps(up.back("z", "x"), down.back_core())
    wait_all()
    all_steps(up.back("x", "z"))
    g_down = unpack_down(me_z, 0, after(down.keep, *up.sent))
    g_down = unpack_down(me_z, 1, down.got, (g_down,))
    gt = link.finish(gt, jnp.concatenate(gt_got, axis=0), link.tokens_shape).astype(F32)
    small = (small[0:2], small[2:4], small[4])
    g_down, gt, small = up.wait(g_down, gt, small)
    all_steps(up.back_core())
    g_rest = unpack_rest(me, 0, up.keep)
    g_rest = up.wait(*g_rest)
    g_up, g_out, g_qkv = unpack_rest(me, 1, up.got, g_rest)
    return out, gt, (g_qkv, g_out, g_up, g_down), small


def shards(outer, tokens, segments, pass_embed, w_qkv, w_out, w_up, w_down, gain, bias, cotangent):
    ty = lax.axis_index("tensor")
    rows = tokens.shape[0] // 2
    width = tokens.shape[2]
    mine = lambda t: lax.dynamic_slice_in_dim(t, ty * rows, rows, 0)
    x = mine(tokens).reshape(-1, width)
    gb = jnp.concatenate([gain, bias, pass_embed[None]], axis=0)
    link = Link(outer, w_qkv, w_out, w_up, w_down)
    link.out_shape, link.tokens_shape = cotangent.shape, tokens.shape
    link.finish = lambda mine, theirs, shape: ordered(ty, mine, theirs).reshape(shape)
    out, gt, grads, small = local_part(x, mine(segments), mine(cotangent), gb, link)
    return out, gt, *grads, *small


def solution(mesh):
    outer = mesh.shape["dp"] // 4
    fine = Mesh(mesh.devices.reshape(outer, 2, 2, mesh.shape["tensor"]), ("o", "x", "core", "tensor"))
    rows = ROWS_OVER
    placed = (
        P(rows, None, None),
        P(rows, None),
        P(),
        P(None, None, "tensor"),
        P("tensor", None),
        P(None, "tensor"),
        P("tensor", None),
        P(),
        P(),
        P(rows, None, None),
    )

    def body(*args):
        return shards(outer, *args)

    return jax.shard_map(
        body,
        mesh=fine,
        in_specs=placed,
        out_specs=(
            P(rows, None, None),
            P(rows, None, None),
            P(None, None, "tensor"),
            P("tensor", None),
            P(None, "tensor"),
            P("tensor", None),
            P(),
            P(),
            P(),
        ),
        check_vma=False,
    )
```

```python
import functools

import jax
import jax.numpy as jnp
from jax import lax
from jax.experimental import pallas as pl
from jax.experimental.pallas import tpu as pltpu
from jax.sharding import Mesh
from jax.sharding import PartitionSpec as P

HD = 64
EPS = 1e-05
NEG = -1000000000.0
F32 = jnp.float32
BF16 = jnp.bfloat16
ROWS_OVER = ("o", "x", "core")
FLIP = ((0, 1), (1, 0))
VMEM_LIMIT = 16 * 1024 * 1024


def ordered(flag, mine, theirs):
    first = flag == 0
    return jnp.stack([jnp.where(first, mine, theirs), jnp.where(first, theirs, mine)])


def take_half(array, index):
    half = array.shape[0] // 2
    return lax.dynamic_slice_in_dim(array, index * half, half, 0)


def flip_bit(array, axis, size, bit):
    return lax.ppermute(array, axis, [(i, i ^ bit) for i in range(size)])


def steps_of(outer):
    steps = [("x", 2, 1)]
    bit = 1
    while bit < outer:
        steps.append(("o", outer, bit))
        bit *= 2
    return steps


def my_bit(axis, bit):
    return (lax.axis_index(axis) // bit) % 2


def dot(a, b):
    return lax.dot_general(a, b, (((1,), (0,)), ((), ())), preferred_element_type=F32)


def dot_nt(a, b):
    return lax.dot_general(a, b, (((1,), (1,)), ((), ())), preferred_element_type=F32)


def dot_tn(a, b):
    return lax.dot_general(a, b, (((0,), (0,)), ((), ())), preferred_element_type=F32)


def norm_stats(h):
    centred = h - jnp.mean(h, axis=-1, keepdims=True)
    inverse = lax.rsqrt(jnp.mean(centred * centred, axis=-1, keepdims=True) + EPS)
    return centred * inverse, inverse


def norm_back(grad, normal, inverse, gain):
    scaled = grad * gain
    centre = jnp.mean(scaled, axis=-1, keepdims=True)
    proj = jnp.mean(scaled * normal, axis=-1, keepdims=True)
    return inverse * (scaled - centre - normal * proj)


def gelu_parts(u):
    c = 0.7978845608028654
    a = 0.044715 * c
    square = u * u
    half = 0.5 + 0.5 * jnp.tanh(u * (c + a * square))
    g = u * half
    return g, half + g * (1.0 - half) * (2.0 * c + 6.0 * a * square)


def whole(shape):
    return pl.BlockSpec(shape, lambda *_: (0,) * len(shape))


def call(body, grid, ins, outs, scratch=(), cost=(0, 0), name=None, vmem=VMEM_LIMIT):
    return pl.pallas_call(
        body,
        grid=grid,
        in_specs=[s for _, s in ins],
        out_specs=[s for _, s in outs],
        out_shape=[a for a, _ in outs],
        scratch_shapes=scratch,
        compiler_params=pltpu.CompilerParams(
            dimension_semantics=("arbitrary",) * len(grid), vmem_limit_bytes=vmem
        ),
        cost_estimate=pl.CostEstimate(
            flops=int(cost[0]) // 16, bytes_accessed=int(cost[1]), transcendentals=0
        ),
        name=name,
    )(*[a for a, _ in ins])


FAR = pl.BlockSpec(memory_space=pl.ANY)


def resident(body, ins, outs, scratch=(), flops=0, vmem=16, aliases={}, name=None):
    spec = pl.BlockSpec(memory_space=pltpu.VMEM)
    ins, outs = ([o if isinstance(o, tuple) else (o, spec) for o in t] for t in (ins, outs))
    ins = [(pltpu.with_memory_space_constraint(a, pltpu.HBM) if s is FAR else a, s) for a, s in ins]
    outs = [(pltpu.HBM(a.shape, a.dtype) if s is FAR else a, s) for a, s in outs]
    return pl.pallas_call(
        body,
        in_specs=[s for _, s in ins],
        out_specs=[s for _, s in outs],
        out_shape=[a for a, _ in outs],
        scratch_shapes=scratch,
        input_output_aliases=aliases,
        compiler_params=pltpu.CompilerParams(vmem_limit_bytes=vmem * 1024 * 1024),
        cost_estimate=pl.CostEstimate(flops=int(flops) // 16, bytes_accessed=0, transcendentals=0),
        name=name,
    )(*[a for a, _ in ins])


def sds(shape, dtype):
    return jax.ShapeDtypeStruct(shape, dtype)


QB = 128
GROUP = 256


def lanes_of(ref, g):
    return ref.at[(slice(None),) * (len(ref.shape) - 1) + (pl.ds(pl.multiple_of(g * GROUP, GROUP), GROUP),)]


class Moves:
    def __init__(self, sems):
        self.sems, self.used = sems, 0

    def take(self, number):
        self.used += number
        return self.used - number

    def whole(self, source, target):
        copy = pltpu.make_async_copy(source, target, self.sems.at[self.take(1)])
        copy.start()
        return copy.wait

    def later(self, source, target):
        sem = self.sems.at[self.take(1)]
        copy = lambda: pltpu.make_async_copy(source, target, sem)
        return (lambda: copy().start()), (lambda: copy().wait())

    def groups(self, source, target):
        first = self.take(source.shape[-1] // GROUP)

        def copy(g):
            return pltpu.make_async_copy(lanes_of(source, g), lanes_of(target, g), self.sems.at[first + g])

        return (lambda g: copy(g).start()), (lambda g: copy(g).wait())


def cat_heads(t, scale=1.0):
    lane = lax.broadcasted_iota(jnp.int32, (1, 2 * HD), 1)
    parts = [t * jnp.where((lane < HD) == (h == 0), scale, 0.0).astype(t.dtype) for h in range(2)]
    return jnp.concatenate(parts, axis=0)


def own_lanes(t, scale=None):
    if scale is not None:
        t = t * scale
    return jnp.concatenate([t[:HD, :QB], t[HD:, QB:]], axis=0)


def twice(t):
    return jnp.concatenate([t, t], axis=1)


def pair_row(rows, p):
    return jnp.concatenate([rows[2 * p : 2 * p + 1], rows[2 * p + 1 : 2 * p + 2]], axis=1)


def put_pair(ref, p, cols, value):
    ref[2 * p : 2 * p + 1, cols] = value[:, :QB]
    ref[2 * p + 1 : 2 * p + 2, cols] = value[:, QB:]


def columns(t, r, seq, qb):
    return t[:, pl.ds(pl.multiple_of(r * seq + qb * QB, QB), QB)]


def rows_of(r, seq, qb):
    return pl.ds(pl.multiple_of(r * seq + qb * QB, QB), QB)


def in_turn(arrive, group, groups):
    for _, wait in arrive:
        wait(group)

    @pl.when(group + 2 < groups)
    def _():
        for start, _ in arrive:
            start(group + 2)


def attend_first_body(rows, seq, pairs, a_ref, w_ref, bias_ref, qkv_ref, o_ref, lse_ref):
    a = a_ref[...]
    for j in range(3):
        qkv_ref[j] = dot(a, w_ref[j]).astype(BF16)
    for r in range(rows):
        work = []
        for p in range(pairs):
            ln = slice(p * 2 * HD, (p + 1) * 2 * HD)
            k = qkv_ref[1, r * seq : (r + 1) * seq, ln]
            for b in range(seq // QB):
                sl, n = slice(r * seq + b * QB, r * seq + (b + 1) * QB), (b + 1) * QB
                q = cat_heads(qkv_ref[0, sl, ln], HD**-0.5)
                s = dot_nt(k[:n], q) + twice(bias_ref[r, :n, b * QB : n])
                work.append((p, ln, sl, n, s))
        done = []
        for p, ln, sl, n, s in work:
            top = jnp.max(s, axis=0, keepdims=True)
            e = jnp.exp(s - top)
            mass = jnp.sum(e, axis=0, keepdims=True)
            put_pair(lse_ref, p, sl, top + jnp.log(mass))
            done.append((e.astype(BF16), 1.0 / mass))
        for (p, ln, sl, n, _), (e, inv) in zip(work, done):
            vt = qkv_ref[2, r * seq : (r + 1) * seq, ln].T
            o_ref[sl, ln] = own_lanes(dot(vt[:, :n], e), inv).T.astype(BF16)


def attend_first(a, w, bias):
    rows, seq = bias.shape[0], bias.shape[1]
    n, d = a.shape
    f = w.shape[2]
    return resident(
        functools.partial(attend_first_body, rows, seq, f // (2 * HD)),
        (a, w, bias),
        [sds((3, n, f), BF16), sds((n, f), BF16), sds((f // HD, n), F32)],
        flops=6 * n * d * f + 16 * n * seq * f,
        name="attend_first",
    )


def attend_second_body(
    rows, seq, a_far, w_far, incl_far, strict_far, qkve_far, o1_far, lse1_ref,
    qkvo_far, o2_far, lse2_ref,
    a_ref, w_ref, incl_ref, strict_ref, qkve_ref, o1_ref, qkvo_ref, o2_ref, sems,
):
    groups = lse1_ref.shape[0]
    moves = Moves(sems)
    first = moves.take(6)

    def weight(j):
        return pltpu.make_async_copy(w_far.at[j], w_ref.at[j], sems.at[first + j])

    def projected(j):
        return pltpu.make_async_copy(qkvo_ref.at[j], qkvo_far.at[j], sems.at[first + 3 + j])

    a_there = moves.whole(a_far, a_ref)
    weight(0).start()
    arrive = [moves.groups(*t) for t in ((qkve_far, qkve_ref), (o1_far, o1_ref))]
    leave = moves.groups(o2_ref, o2_far)
    a_there()
    weight(0).wait()
    weight(1).start()
    weight(2).start()
    masks = [moves.whole(*t) for t in ((incl_far, incl_ref), (strict_far, strict_ref))]
    for g in range(2):
        for start, _ in arrive:
            start(g)

    def project(j, _):
        pl.when(j > 0)(lambda: weight(j).wait())
        qkvo_ref[j] = dot(a_ref[...], w_ref[j]).astype(BF16)
        projected(j).start()
        return 0

    lax.fori_loop(0, 3, project, 0)
    for wait in masks:
        wait()

    def next_group(group):
        in_turn(arrive, group, groups)

    def row(i, _):
        r, group = i % rows, i // rows
        lanes = pl.multiple_of(group * GROUP, GROUP)
        all_of = pl.ds(pl.multiple_of(r * seq, seq), seq)

        @pl.when(r == 0)
        def _():
            next_group(group)

        for p in range(GROUP // (2 * HD)):
            ln = pl.ds(lanes + p * 2 * HD, 2 * HD)
            ke, ko = qkve_ref[1, all_of, ln], qkvo_ref[1, all_of, ln]
            vte, vto = qkve_ref[2, all_of, ln].T, qkvo_ref[2, all_of, ln].T
            work = []
            for b in range(seq // QB):
                sl, n = rows_of(r, seq, b), (b + 1) * QB
                cols = slice(b * QB, n)
                incl, strict = twice(incl_ref[r, :n, cols]), twice(strict_ref[r, :n, cols])
                q = cat_heads(qkve_ref[0, sl, ln], HD**-0.5)
                work.append([dot_nt(ko[:n], q) + strict])
                q = cat_heads(qkvo_ref[0, sl, ln], HD**-0.5)
                work.append([dot_nt(ko[:n], q) + incl, dot_nt(ke[:n], q) + incl])
            for b in range(seq // QB):
                sl, n = rows_of(r, seq, b), (b + 1) * QB
                (s,), (so, se) = work[2 * b : 2 * b + 2]
                old = pair_row(lse1_ref[group, :, sl], p)
                top = jnp.maximum(old, jnp.max(s, axis=0, keepdims=True))
                e = jnp.exp(s - top)
                kept = jnp.exp(old - top)
                mass = kept + jnp.sum(e, axis=0, keepdims=True)
                work[2 * b] = (e.astype(BF16), kept, 1.0 / mass)
                put_pair(lse2_ref.at[0, group], p, sl, top + jnp.log(mass))
                top = jnp.max(jnp.maximum(se, so), axis=0, keepdims=True)
                ee, eo = jnp.exp(se - top), jnp.exp(so - top)
                mass = jnp.sum(ee + eo, axis=0, keepdims=True)
                work[2 * b + 1] = (ee.astype(BF16), eo.astype(BF16), 1.0 / mass)
                put_pair(lse2_ref.at[1, group], p, sl, top + jnp.log(mass))
            for b in range(seq // QB):
                sl, n = rows_of(r, seq, b), (b + 1) * QB
                (e, kept, inv), (ee, eo, inv2) = work[2 * b : 2 * b + 2]
                o1 = o1_ref[sl, ln].astype(F32).T
                o = own_lanes(dot(vto[:, :n], e), inv) + own_lanes(twice(o1), kept * inv)
                o2_ref[0, sl, ln] = o.T.astype(BF16)
                o = dot(vte[:, :n], ee) + dot(vto[:, :n], eo)
                o2_ref[1, sl, ln] = own_lanes(o, inv2).T.astype(BF16)

        @pl.when(r == rows - 1)
        def _():
            leave[0](group)

        return 0

    lax.fori_loop(0, rows * groups, row, 0)
    for j in range(3):
        projected(j).wait()
    for g in range(groups):
        leave[1](g)


def attend_second(a, w, incl, strict, qkve, o1, lse1):
    rows, seq = incl.shape[0], incl.shape[1]
    n, d = a.shape
    f = w.shape[2]
    qkv, o2 = sds((3, n, f), BF16), sds((2, n, f), BF16)
    near = (a, w, incl, strict, qkve, o1, qkv, o2)
    return resident(
        functools.partial(attend_second_body, rows, seq),
        [(t, FAR) for t in (a, w, incl, strict, qkve, o1)] + [lse1],
        [(qkv, FAR), (o2, FAR), sds((2, *lse1.shape), F32)],
        scratch=[pltpu.VMEM(t.shape, t.dtype) for t in near] + [pltpu.SemaphoreType.DMA((64,))],
        flops=6 * n * d * f + 48 * n * seq * f,
        vmem=32,
        name="attend_second",
    )


def row_products(a, b):
    prod = cat_heads((a * b).astype(BF16))
    return dot_nt(jnp.ones((8, 2 * HD), BF16), prod)[:1]


def query_parts(sl, ln, group, p, i, qkv_ref, o_ref, lse_ref, do_ref):
    do = do_ref[i, sl, ln]
    delta = row_products(do.astype(F32), o_ref[i, sl, ln].astype(F32))
    return cat_heads(qkv_ref[0, sl, ln], HD**-0.5), cat_heads(do), pair_row(lse_ref[i, group, :, sl], p), delta


def blocks_back(tasks):
    scores = [dot_nt(k, q) + bias - lse for k, _, _, bias, q, _, lse, _ in tasks]
    moved = [dot_nt(v, do) - delta for _, v, _, _, _, do, _, delta in tasks]
    probs = [jnp.exp(s) for s in scores]
    ds = [(p * m).astype(BF16) for p, m in zip(probs, moved)]
    return [
        (dot(p.astype(BF16), do), dot(d, q), dot(kt, d))
        for (_, _, kt, _, q, do, _, _), p, d in zip(tasks, probs, ds)
    ]


def add_rows(total, part):
    if total is None:
        return part
    n = part.shape[0]
    return jnp.concatenate([total[:n] + part, total[n:]], axis=0)


def attend_back_body(
    rows, seq, w_far, incl_far, strict_far, qkve_far, qkvo_far, o2_far, lse2_ref, do_far,
    dh1_far, ho_far, gb_ref,
    dqkvo_far, dqkve_far, dy_far, sums_ref,
    w_ref, incl_ref, strict_ref, qkve_ref, qkvo_ref, o2_ref, do_ref, dh1_ref, ho_ref,
    dqkvo_ref, dqkve_ref, da_ref, dy_ref, sems,
):
    groups = lse2_ref.shape[1]
    moves = Moves(sems)
    arrive = [
        moves.groups(*t)
        for t in ((qkve_far, qkve_ref), (qkvo_far, qkvo_ref), (o2_far, o2_ref), (do_far, do_ref))
    ]
    leave = [moves.groups(*t) for t in ((dqkvo_ref, dqkvo_far), (dqkve_ref, dqkve_far))]
    for start, _ in arrive:
        start(0)
    masks = [moves.whole(*t) for t in ((incl_far, incl_ref), (strict_far, strict_ref))]
    for start, _ in arrive:
        start(1)
    odd = pl.ds(rows * seq, rows * seq)
    late = [moves.later(*t) for t in ((w_far, w_ref), (dh1_far.at[odd], dh1_ref), (ho_far, ho_ref))]
    for wait in masks:
        wait()

    def next_group(group):
        in_turn(arrive, group, groups)

        @pl.when(group == groups - 2)
        def _():
            for start, _ in late:
                start()

    sc = HD**-0.5

    def row(i, _):
        r, group = i % rows, i // rows
        lanes = pl.multiple_of(group * GROUP, GROUP)
        all_of = pl.ds(pl.multiple_of(r * seq, seq), seq)

        @pl.when(r == 0)
        def _():
            next_group(group)

        for p in range(GROUP // (2 * HD)):
            ln = pl.ds(lanes + p * 2 * HD, 2 * HD)
            ke, ve = qkve_ref[1, all_of, ln], qkve_ref[2, all_of, ln]
            ko, vo = qkvo_ref[1, all_of, ln], qkvo_ref[2, all_of, ln]
            kte, kto = ke.T, ko.T
            tasks = []
            for b in reversed(range(seq // QB)):
                sl, n = rows_of(r, seq, b), (b + 1) * QB
                cols = slice(b * QB, n)
                incl, strict = twice(incl_ref[r, :n, cols]), twice(strict_ref[r, :n, cols])
                even = query_parts(sl, ln, group, p, 0, qkve_ref, o2_ref, lse2_ref, do_ref)
                odd = query_parts(sl, ln, group, p, 1, qkvo_ref, o2_ref, lse2_ref, do_ref)
                tasks.append((ko[:n], vo[:n], kto[:, :n], strict, *even))
                tasks.append((ko[:n], vo[:n], kto[:, :n], incl, *odd))
                tasks.append((ke[:n], ve[:n], kte[:, :n], incl, *odd))
            done = blocks_back(tasks)
            dke = dve = dko = dvo = None
            for b in reversed(range(seq // QB)):
                sl = rows_of(r, seq, b)
                (dv, dk, dqe), (dv2, dk2, dqo), (dv3, dk3, dqo2) = done[:3]
                done = done[3:]
                dvo, dko = add_rows(dvo, dv + dv2), add_rows(dko, dk + dk2)
                dve, dke = add_rows(dve, dv3), add_rows(dke, dk3)
                dqkve_ref[0, sl, ln] = (own_lanes(dqe).T * sc).astype(BF16)
                dqkvo_ref[0, sl, ln] = (own_lanes(dqo + dqo2).T * sc).astype(BF16)
            dqkve_ref[1, all_of, ln] = dke.astype(BF16)
            dqkve_ref[2, all_of, ln] = dve.astype(BF16)
            dqkvo_ref[1, all_of, ln] = dko.astype(BF16)
            dqkvo_ref[2, all_of, ln] = dvo.astype(BF16)

        @pl.when(r == rows - 1)
        def _():
            for start, _ in leave:
                start(group)

        return 0

    lax.fori_loop(0, rows * groups, row, 0)
    for _, wait in late:
        wait()
    da = dot_nt(dqkvo_ref[0], w_ref[0])
    da += dot_nt(dqkvo_ref[1], w_ref[1])
    da += dot_nt(dqkvo_ref[2], w_ref[2])
    da_ref[...] = da
    sums_ref[...] = jnp.zeros_like(sums_ref)

    def finish(i, _):
        sl = pl.ds(pl.multiple_of(i * ROWS_AT_ONCE, ROWS_AT_ONCE), ROWS_AT_ONCE)
        normal, inverse = norm_stats(ho_ref[sl])
        da = da_ref[sl]
        dy = dh1_ref[sl] + norm_back(da, normal, inverse, gb_ref[0:1])
        dy_ref[sl] = dy
        for k, t in enumerate((da * normal, da, dy)):
            sums_ref[k : k + 1] += jnp.sum(t, axis=0, keepdims=True)
        return 0

    lax.fori_loop(0, rows * seq // ROWS_AT_ONCE, finish, 0)
    kept = [moves.whole(dy_ref, dy_far)]
    for g in range(groups):
        for _, wait in leave:
            wait(g)
    for wait in kept:
        wait()


def attend_back(w, incl, strict, qkve, qkvo, o2, lse2, do, dh1, ho, gb):
    rows, seq = incl.shape[0], incl.shape[1]
    n, d = ho.shape
    f = w.shape[2]
    do = do.reshape(2, n, f)
    qkv = sds((3, n, f), BF16)
    near = (w, incl, strict, qkve, qkvo, o2, do, sds((n, d), F32), ho, qkv, qkv, sds((n, d), F32))
    return resident(
        functools.partial(attend_back_body, rows, seq),
        [(t, FAR) for t in (w, incl, strict, qkve, qkvo, o2)]
        + [lse2]
        + [(t, FAR) for t in (do, dh1, ho)]
        + [gb],
        [(qkv, FAR), (qkv, FAR), (sds((n, d), F32), FAR), sds((3, d), F32)],
        scratch=[pltpu.VMEM(t.shape, t.dtype) for t in near + (sds((n, d), F32),)] + [pltpu.SemaphoreType.DMA((64,))],
        flops=6 * n * d * f + 120 * n * seq * f,
        vmem=44,
        name="attend_back",
    )


def attend_back_even_body(
    rows, seq, w_far, incl_far, qkve_far, o1_far, lse1_ref, do1_far, o2_far, lse2_ref, do2_far,
    part_far, dh1_far, dh2_far, x_far, gb_ref,
    dqkv_far, gt_ref, sums_ref,
    w_ref, incl_ref, qkve_ref, o1_ref, do1_ref, o2_ref, do2_ref, part_ref, dh1_ref, dh2_ref, x_ref,
    dqkv_ref, da_ref, sems,
):
    groups = lse1_ref.shape[0]
    moves = Moves(sems)
    even = pl.ds(0, rows * seq)
    arrive = [
        moves.groups(*t)
        for t in (
            (qkve_far, qkve_ref), (o1_far, o1_ref), (do1_far, do1_ref), (o2_far.at[0], o2_ref),
            (do2_far.at[0], do2_ref), (part_far, part_ref),
        )
    ]
    leave = [moves.groups(dqkv_ref, dqkv_far)]
    for start, _ in arrive:
        start(0)
    mask = moves.whole(incl_far, incl_ref)
    for start, _ in arrive:
        start(1)
    late = [
        moves.later(*t)
        for t in ((w_far, w_ref), (dh1_far, dh1_ref), (dh2_far.at[even], dh2_ref), (x_far, x_ref))
    ]
    mask()

    def next_group(group):
        in_turn(arrive, group, groups)

        @pl.when(group == groups - 2)
        def _():
            for start, _ in late:
                start()

    sc = HD**-0.5

    def row(i, _):
        r, group = i % rows, i // rows
        lanes = pl.multiple_of(group * GROUP, GROUP)
        all_of = pl.ds(pl.multiple_of(r * seq, seq), seq)

        @pl.when(r == 0)
        def _():
            next_group(group)

        for p in range(GROUP // (2 * HD)):
            ln = pl.ds(lanes + p * 2 * HD, 2 * HD)
            k, v = qkve_ref[1, all_of, ln], qkve_ref[2, all_of, ln]
            kt = k.T
            tasks = []
            for b in reversed(range(seq // QB)):
                sl, n = rows_of(r, seq, b), (b + 1) * QB
                incl = twice(incl_ref[r, :n, b * QB : n])
                lse1 = pair_row(lse1_ref[group, :, sl], p)
                ratio = jnp.exp(lse1 - pair_row(lse2_ref[0, group, :, sl], p))
                do1, do2 = do1_ref[sl, ln].astype(F32), do2_ref[sl, ln].astype(F32)
                delta = row_products(do1, o1_ref[sl, ln].astype(F32))
                delta += ratio * row_products(do2, o2_ref[sl, ln].astype(F32))
                both = do1 + own_lanes(twice(do2.T), ratio).T
                q, do = cat_heads(qkve_ref[0, sl, ln], sc), cat_heads(both.astype(BF16))
                tasks.append((k[:n], v[:n], kt[:, :n], incl, q, do, lse1, delta))
            dka = dva = None
            for b, (dv, dk, dq) in zip(reversed(range(seq // QB)), blocks_back(tasks)):
                sl = rows_of(r, seq, b)
                dva, dka = add_rows(dva, dv), add_rows(dka, dk)
                dqkv_ref[0, sl, ln] = (own_lanes(dq).T * sc + part_ref[0, sl, ln].astype(F32)).astype(BF16)
            dqkv_ref[1, all_of, ln] = (dka + part_ref[1, all_of, ln].astype(F32)).astype(BF16)
            dqkv_ref[2, all_of, ln] = (dva + part_ref[2, all_of, ln].astype(F32)).astype(BF16)

        @pl.when(r == rows - 1)
        def _():
            for start, _ in leave:
                start(group)

        return 0

    lax.fori_loop(0, rows * groups, row, 0)
    for _, wait in late:
        wait()
    da_ref[...] = jnp.zeros_like(da_ref)

    def project_back(j, _):
        da_ref[...] += dot_nt(dqkv_ref[j], w_ref[j])
        return 0

    lax.fori_loop(0, 3, project_back, 0)
    sums_ref[...] = jnp.zeros_like(sums_ref)

    def finish(i, _):
        sl = pl.ds(pl.multiple_of(i * ROWS_AT_ONCE, ROWS_AT_ONCE), ROWS_AT_ONCE)
        normal, inverse = norm_stats(x_ref[sl].astype(F32))
        da = da_ref[sl]
        sums_ref[0:1] += jnp.sum(da * normal, axis=0, keepdims=True)
        sums_ref[1:2] += jnp.sum(da, axis=0, keepdims=True)
        back = norm_back(da, normal, inverse, gb_ref[0:1])
        gt_ref[sl] = (dh1_ref[sl] + dh2_ref[sl] + back).astype(BF16)
        return 0

    lax.fori_loop(0, rows * seq // ROWS_AT_ONCE, finish, 0)
    for g in range(groups):
        for _, wait in leave:
            wait(g)


def attend_back_even(w, incl, qkve, o1, lse1, do1, o2, lse2, do2, part, dh1, dh2, x, gb):
    rows, seq = incl.shape[0], incl.shape[1]
    n, d = x.shape
    f = w.shape[2]
    qkv, one = sds((3, n, f), BF16), sds((n, f), BF16)
    near = (w, incl, qkv, one, one, one, one, qkv, dh1, dh1, x, qkv, sds((n, d), F32))
    far = lambda *ts: [(t, FAR) for t in ts]
    return resident(
        functools.partial(attend_back_even_body, rows, seq),
        far(w, incl, qkve, o1)
        + [lse1]
        + far(do1, o2)
        + [lse2]
        + far(do2.reshape(2, n, f), part, dh1, dh2, x)
        + [gb],
        [(qkv, FAR), sds((n, d), BF16), sds((2, d), F32)],
        scratch=[pltpu.VMEM(t.shape, t.dtype) for t in near] + [pltpu.SemaphoreType.DMA((64,))],
        flops=6 * n * d * f + 40 * n * seq * f,
        vmem=40,
        name="attend_back_even",
    )


CHUNK = 512
ROWS_AT_ONCE = 256


def chunk_of(ref, j, axis):
    at = pl.ds(pl.multiple_of(j * CHUNK, CHUNK), CHUNK)
    return ref.at[:, at] if axis else ref.at[at]


class Chunks:
    def __init__(self, moves, far, near, axis, ring=False, leave=False):
        self.first = moves.take(far.shape[axis] // CHUNK)
        self.sems, self.far, self.near = moves.sems, far, near
        self.axis, self.ring, self.leave = axis, ring, leave

    def copy(self, j):
        near = self.near.at[j % self.near.shape[0]] if self.ring else chunk_of(self.near, j, self.axis)
        ends = (chunk_of(self.far, j, self.axis), near)
        return pltpu.make_async_copy(*(ends[::-1] if self.leave else ends), self.sems.at[self.first + j])

    def start(self, j):
        self.copy(j).start()

    def wait(self, j):
        self.copy(j).wait()


class Weight:
    def __init__(self, moves, pieces, near, axis):
        self.axis, self.near = axis, near
        self.own = Chunks(moves, pieces[0], near, axis) if pieces[0] is not None else None
        self.number = near.shape[axis] // CHUNK // 2
        self.others, start = [], near.shape[axis] // 2
        for far in pieces[1:]:
            at = pl.ds(start, far.shape[axis])
            self.others.append(moves.later(far, near.at[:, at] if axis else near.at[at]))
            start += far.shape[axis]

    def start_others(self):
        for start, _ in self.others:
            start()

    def wait_others(self):
        for _, wait in self.others:
            wait()


def load_in_turn(j, *weights):
    number = weights[0].number

    @pl.when(j < number)
    def _():
        for w in weights:
            w.own.wait(j)

    @pl.when(j + 2 < number)
    def _():
        for w in weights:
            w.own.start(j + 2)

    @pl.when(j + 2 == number)
    def _():
        for w in weights:
            w.start_others()

    @pl.when(j == number)
    def _():
        for w in weights:
            w.wait_others()


def start_loads(*weights):
    for j in range(2):
        for w in weights:
            w.own.start(j)


def feed_chunk(n2_ref, wup_ref, wdown_ref, j, g_buf, d_buf, ho_ref, gs, ds, first):
    @pl.when(first >= 2)
    def _():
        gs.wait(j - 2)
        ds.wait(j - 2)

    half = n2_ref.shape[0] // 2
    parts = []
    for sl in (slice(0, half), slice(half, 2 * half)):
        g, d = gelu_parts(dot(n2_ref[sl], chunk_of(wup_ref, j, 1)[...]))
        parts.append(g.astype(BF16))
        g_buf[j % 2, sl] = parts[-1]
        d_buf[j % 2, sl] = d.astype(BF16)
    gs.start(j)
    ds.start(j)
    for i, g in enumerate(parts):
        ho_ref[i * half : (i + 1) * half] += dot(g, chunk_of(wdown_ref, j, 0)[...])


def start_norm(x_ref, h1_ref, n2_ref, gb_ref, ho_ref=None, normal_ref=None, inverse_ref=None):
    def part(k, _):
        sl = pl.ds(pl.multiple_of(k * ROWS_AT_ONCE, ROWS_AT_ONCE), ROWS_AT_ONCE)
        h1 = x_ref[sl].astype(F32) + h1_ref[sl]
        h1_ref[sl] = h1
        normal, inverse = norm_stats(h1)
        n2_ref[sl] = (normal * gb_ref[1:2] + gb_ref[3:4]).astype(BF16)
        if ho_ref is not None:
            ho_ref[sl] = h1 + gb_ref[4:5]
        if normal_ref is not None:
            normal_ref[sl] = normal
            inverse_ref[sl] = jnp.broadcast_to(inverse, (ROWS_AT_ONCE, inverse_ref.shape[1]))
        return 0

    lax.fori_loop(0, h1_ref.shape[0] // ROWS_AT_ONCE, part, 0)


def mlp_own_body(
    x_far, o_far, wout_far, gb_ref, wup_far, wdown_far,
    h1_far, n2_far, g_far, d_far, ho_far,
    x_ref, o_ref, wout_ref, wup_ref, wdown_ref, h1_ref, n2_ref, ho_ref, g_buf, d_buf, sems,
):
    moves = Moves(sems)
    first = [moves.whole(*t) for t in ((o_far, o_ref), (wout_far, wout_ref), (x_far, x_ref))]
    ups, downs = Chunks(moves, wup_far, wup_ref, 1), Chunks(moves, wdown_far, wdown_ref, 0)
    gs, ds = (Chunks(moves, f, b, 1, True, True) for f, b in ((g_far, g_buf), (d_far, d_buf)))
    number = wup_far.shape[1] // CHUNK
    for wait in first:
        wait()
    for j in range(number):
        ups.start(j)
        downs.start(j)
    h1_ref[...] = dot(o_ref[...], wout_ref[...])
    start_norm(x_ref, h1_ref, n2_ref, gb_ref, ho_ref)
    kept = [moves.whole(*t) for t in ((h1_ref, h1_far), (n2_ref, n2_far))]

    def step(j, _):
        ups.wait(j)
        downs.wait(j)
        feed_chunk(n2_ref, wup_ref, wdown_ref, j, g_buf, d_buf, ho_ref, gs, ds, j)
        return 0

    lax.fori_loop(0, number, step, 0)
    kept.append(moves.whole(ho_ref, ho_far))
    for wait in kept:
        wait()
    for j in range(number - 2, number):
        gs.wait(j)
        ds.wait(j)


def mlp_other_body(number_up, number_down, n2_far, part_far, g_in, d_in, gb_ref, *refs):
    ups_far, refs = refs[:number_up], refs[number_up:]
    downs_far, refs = refs[:number_down], refs[number_down:]
    g_far, d_far, ho_far, ao_far, n2_ref, wup_ref, wdown_ref, ho_ref, ao_ref, g_buf, d_buf, sems = refs
    moves = Moves(sems)
    up = Weight(moves, (None,) + ups_far, wup_ref, 1)
    down = Weight(moves, (None,) + downs_far, wdown_ref, 0)
    gs, ds = (Chunks(moves, f, b, 1, True, True) for f, b in ((g_far, g_buf), (d_far, d_buf)))
    n2_there = moves.whole(n2_far, n2_ref)
    up.start_others()
    down.start_others()
    part_there = moves.whole(part_far, ho_ref)
    number, half = up.number, n2_ref.shape[0] // 2
    n2_there()
    up.wait_others()

    def rise(i, _):
        j = number + i
        for sl in (slice(0, half), slice(half, 2 * half)):
            g, d = gelu_parts(dot(n2_ref[sl], chunk_of(wup_ref, j, 1)[...]))
            g_buf[j % number, sl] = g.astype(BF16)
            d_buf[j % number, sl] = d.astype(BF16)
        gs.start(j)
        ds.start(j)
        return 0

    lax.fori_loop(0, number, rise, 0)
    down.wait_others()
    part_there()

    def fall(i, _):
        j = number + i
        ho_ref[...] += dot(g_buf[j % number], chunk_of(wdown_ref, j, 0)[...])
        return 0

    lax.fori_loop(0, number, fall, 0)
    sent = moves.whole(ho_ref, ho_far)

    def norm(k, _):
        sl = pl.ds(pl.multiple_of(k * ROWS_AT_ONCE, ROWS_AT_ONCE), ROWS_AT_ONCE)
        normal, _ = norm_stats(ho_ref[sl])
        ao_ref[sl] = (normal * gb_ref[0:1] + gb_ref[2:3]).astype(BF16)
        return 0

    lax.fori_loop(0, ho_ref.shape[0] // ROWS_AT_ONCE, norm, 0)
    moves.whole(ao_ref, ao_far)()
    sent()
    for j in range(number, 2 * number):
        gs.wait(j)
        ds.wait(j)


def near_of(*arrays):
    return [pltpu.VMEM(t.shape, t.dtype) for t in arrays]


def far_of(*arrays):
    return [(t, FAR) for t in arrays]


def mlp_own(x, o, wout, gb, wup, wdown):
    n, d = x.shape
    ff = 2 * wup.shape[1]
    h1, low, wide = sds((n, d), F32), sds((n, d), BF16), sds((n, ff), BF16)
    return resident(
        mlp_own_body,
        far_of(x, o, wout) + [gb] + far_of(wup, wdown),
        far_of(h1, low, wide, wide, h1),
        scratch=near_of(x, o, wout, wup, wdown, h1, low, h1)
        + [pltpu.VMEM((2, n, CHUNK), BF16)] * 2
        + [pltpu.SemaphoreType.DMA((40,))],
        vmem=36,
        name="mlp_own",
    )


def mlp_other(n2, part, g, dgelu, gb, ups, downs):
    n, d = n2.shape
    ff = g.shape[1]
    return resident(
        functools.partial(mlp_other_body, len(ups), len(downs)),
        far_of(n2, part, g, dgelu) + [gb] + far_of(*ups, *downs),
        far_of(sds(g.shape, BF16), sds(g.shape, BF16), sds(part.shape, F32), sds(n2.shape, BF16)),
        scratch=near_of(n2, sds((d, ff), BF16), sds((ff, d), BF16), part, n2)
        + [pltpu.VMEM((ff // CHUNK // 2, n, CHUNK), BF16)] * 2
        + [pltpu.SemaphoreType.DMA((40,))],
        vmem=40,
        aliases={2: 0, 3: 1},
        name="mlp_other",
    )


def weave(seq):
    i = lax.broadcasted_iota(jnp.int32, (2 * seq, 2 * seq), 0)
    k = lax.broadcasted_iota(jnp.int32, (2 * seq, 2 * seq), 1)
    place = jnp.where(k < seq, 2 * k, 2 * (k - seq) + 1)
    return jnp.where(i == place, 1.0, 0.0).astype(BF16)


def after_norm_back(
    moves, size, h1_ref, dn_ref, db_ref, wout_ref, gb_ref, sums_ref, dp_ref, do_ref, dh1_far, dp_far, do_far,
    inverse_ref=None,
):
    gain_sum = jnp.zeros_like(gb_ref[0:1])
    bias_sum = jnp.zeros_like(gb_ref[0:1])
    waits = []
    for i in range(h1_ref.shape[0] // size):
        sl = slice(i * size, (i + 1) * size)
        if inverse_ref is None:
            normal, inverse = norm_stats(h1_ref[sl])
        else:
            normal, inverse = h1_ref[sl], inverse_ref[sl, :1]
        dn = dn_ref[sl]
        gain_sum += jnp.sum(dn * normal, axis=0, keepdims=True)
        bias_sum += jnp.sum(dn, axis=0, keepdims=True)
        dh1 = db_ref[sl].astype(F32) + norm_back(dn, normal, inverse, gb_ref[1:2])
        dn_ref[sl] = dh1
        dp_ref[sl] = dh1.astype(BF16)
    sums_ref[0:1] = gain_sum
    sums_ref[1:2] = bias_sum
    waits += [moves.whole(dn_ref, dh1_far), moves.whole(dp_ref, dp_far)]
    do_ref[...] = dot_nt(dp_ref[...], wout_ref[...]).astype(BF16)
    return waits + [moves.whole(do_ref, do_far)]


def mlp_second_body(rows, seq, number_up, number_down, x_far, ho_far, o_far, cot_far, wout_far, gb_ref, *refs):
    mlp_second_work(rows, seq, x_far, ho_far, o_far, cot_far, wout_far, gb_ref, *in_pieces(refs, number_up, number_down))


def in_pieces(refs, *numbers):
    out = []
    for k in numbers:
        out.append(refs[:k])
        refs = refs[k:]
    return out + list(refs)


def mlp_second_work(
    rows, seq, x_far, ho_far, o_far, cot_far, wout_far, gb_ref, ups_far, downs_far,
    outs_far, outs2_far, n2_far, g_far, du_far, dh1_far, dp_far, do_far, sums_ref, dm_far,
    x_ref, ho_ref, o_ref, cot_ref, wout_ref, wup_ref, wdown_ref, n2_ref, dm_ref,
    normal_ref, z_ref, dn_ref, dp_ref, do_ref, inverse_ref, g_buf, du_buf, sems,
):
    n = rows * seq
    moves = Moves(sems)
    halves = (slice(0, n), slice(n, 2 * n))
    cot_there = moves.whole(cot_far, cot_ref)
    first = [moves.whole(*t) for t in ((o_far, o_ref), (wout_far, wout_ref), (x_far, x_ref))]
    up, down = Weight(moves, ups_far, wup_ref, 1), Weight(moves, downs_far, wdown_ref, 0)
    gs, dus = (Chunks(moves, f, b, 1, True, True) for f, b in ((g_far, g_buf), (du_far, du_buf)))
    number = 2 * up.number
    mix = weave(seq)
    cot_there()
    for r in range(rows):
        parted = dot_tn(mix, cot_ref[r]).astype(BF16)
        for i in range(2):
            dm_ref[i * n + r * seq : i * n + (r + 1) * seq] = parted[i * seq : (i + 1) * seq]
    for wait in first:
        wait()
    then = moves.whole(ho_far, ho_ref)
    start_loads(up, down)
    for i, sl in enumerate(halves):
        if i:
            then()
        z_ref[sl] = dot(o_ref[i], wout_ref[...])
        z_at, n2_at, normal_at, inverse_at = (t.at[pl.ds(i * n, n)] for t in (z_ref, n2_ref, normal_ref, inverse_ref))
        start_norm(x_ref if i == 0 else ho_ref, z_at, n2_at, gb_ref, None, normal_at, inverse_at)
    kept = [moves.whole(*t) for t in ((n2_ref, n2_far), (dm_ref, dm_far))]
    dn_ref[...] = jnp.zeros_like(dn_ref)

    def step(j, _):
        load_in_turn(j, up, down)

        @pl.when(j >= 2)
        def _():
            gs.wait(j - 2)
            dus.wait(j - 2)

        for sl in (slice(0, 2 * n),):
            u = dot(n2_ref[sl], chunk_of(wup_ref, j, 1)[...])
            dg = dot_nt(dm_ref[sl], chunk_of(wdown_ref, j, 0)[...])
            g, d = gelu_parts(u)
            g = g.astype(BF16)
            du = (dg * d).astype(BF16)
            g_buf[j % 2, sl] = g
            du_buf[j % 2, sl] = du
            z_ref[sl] += dot(g, chunk_of(wdown_ref, j, 0)[...])
            dn_ref[sl] += dot_nt(du, chunk_of(wup_ref, j, 1)[...])
        gs.start(j)
        dus.start(j)
        return 0

    lax.fori_loop(0, number, step, 0)
    for r in range(rows):
        pair = [slice(i * n + r * seq, i * n + (r + 1) * seq) for i in range(2)]
        z = jnp.concatenate([z_ref[s].astype(BF16) for s in pair], axis=0)
        cot_ref[r] = dot(mix, z).astype(BF16)
    half = rows // 2
    kept += [moves.whole(cot_ref.at[pl.ds(i * half, half)], far) for i, far in enumerate((outs_far, outs2_far))]
    kept += after_norm_back(
        moves, seq, normal_ref, dn_ref, dm_ref, wout_ref, gb_ref, sums_ref, dp_ref, do_ref, dh1_far, dp_far, do_far,
        inverse_ref,
    )
    for wait in kept:
        wait()
    for j in range(number - 2, number):
        gs.wait(j)
        dus.wait(j)


def mlp_second(x, ho, o2, cot, wout, gb, ups, downs, seq):
    n, d = x.shape
    ff = 2 * ups[0].shape[1]
    rows = n // seq
    low, wide, full = sds((2 * n, d), BF16), sds((2 * n, ff), BF16), sds((2 * n, d), F32)
    out = sds((rows // 2, 2 * seq, d), BF16)
    return resident(
        functools.partial(mlp_second_body, rows, seq, len(ups), len(downs)),
        far_of(x, ho, o2, cot, wout) + [gb] + far_of(*ups, *downs),
        far_of(out, out, low, wide, wide, full, low, low) + [sds((2, d), F32)] + far_of(low),
        scratch=near_of(x, ho, o2, cot, wout, sds((d, ff), BF16), sds((ff, d), BF16), low, low, full, full, full, low, low, sds((2 * n, 128), F32))
        + [pltpu.VMEM((2, 2 * n, CHUNK), BF16)] * 2
        + [pltpu.SemaphoreType.DMA((64,))],
        vmem=60,
        name="mlp_second",
    )


def mlp_back_body(rows, seq, number_up, number_down, dy_far, h1_far, wout_far, gb_ref, d_far, *refs):
    mlp_back_work(rows, seq, dy_far, h1_far, wout_far, gb_ref, d_far, *in_pieces(refs, number_up, number_down))


def mlp_back_work(
    rows, seq, dy_far, h1_far, wout_far, gb_ref, d_far, ups_far, downs_far,
    du_far, dh1_far, dp_far, do_far, sums_ref,
    dy_ref, h1_ref, wout_ref, wup_ref, wdown_ref, d_ref, dm_ref, dn_ref, dp_ref, do_ref, du_buf, sems,
):
    moves = Moves(sems)
    first = moves.whole(dy_far, dy_ref)
    up, down = Weight(moves, ups_far, wup_ref, 1), Weight(moves, downs_far, wdown_ref, 0)
    ds, dus = Chunks(moves, d_far, d_ref, 1), Chunks(moves, du_far, du_buf, 1, True, True)
    number = 2 * up.number
    start_loads(down, up)
    for j in range(2):
        ds.start(j)
    then = [moves.later(*t) for t in ((wout_far, wout_ref), (h1_far, h1_ref))]
    first()
    dm_ref[...] = dy_ref[...].astype(BF16)
    dn_ref[...] = jnp.zeros_like(dn_ref)

    def step(j, _):
        load_in_turn(j, down, up)
        ds.wait(j)

        @pl.when(j + 2 < number)
        def _():
            ds.start(j + 2)

        @pl.when(j + 2 == number)
        def _():
            for start, _ in then:
                start()

        @pl.when(j >= 2)
        def _():
            dus.wait(j - 2)

        dg = dot_nt(dm_ref[...], chunk_of(wdown_ref, j, 0)[...])
        du = (dg * chunk_of(d_ref, j, 1)[...].astype(F32)).astype(BF16)
        du_buf[j % 2] = du
        dus.start(j)
        dn_ref[...] += dot_nt(du, chunk_of(wup_ref, j, 1)[...])
        return 0

    lax.fori_loop(0, number, step, 0)
    for _, wait in then:
        wait()
    kept = after_norm_back(
        moves, seq, h1_ref, dn_ref, dy_ref, wout_ref, gb_ref, sums_ref, dp_ref, do_ref, dh1_far, dp_far, do_far
    )
    for wait in kept:
        wait()
    for j in range(number - 2, number):
        dus.wait(j)


def mlp_back(dy, h1, wout, gb, dgelu, ups, downs, seq):
    n, d = dy.shape
    ff = dgelu.shape[1]
    low = sds((n, d), BF16)
    return resident(
        functools.partial(mlp_back_body, n // seq, seq, len(ups), len(downs)),
        far_of(dy, h1, wout) + [gb] + far_of(dgelu, *ups, *downs),
        far_of(dgelu, h1, low, low) + [sds((2, d), F32)],
        scratch=near_of(dy, h1, wout, sds((d, ff), BF16), sds((ff, d), BF16), dgelu, low, dy, low, low)
        + [pltpu.VMEM((2, n, CHUNK), BF16)]
        + [pltpu.SemaphoreType.DMA((48,))],
        vmem=48,
        name="mlp_back",
    )


def lanes_at(ref, start, size):
    return ref.at[:, pl.ds(pl.multiple_of(start, 128), size)]


def stack_rows(moves, pairs, target, start, size):
    copies, row = [], 0
    for far in pairs:
        copies.append(moves.later(lanes_at(far, start, size), target.at[pl.ds(row, far.shape[0])]))
        row += far.shape[0]
    return (lambda: [s() for s, _ in copies]), (lambda: [w() for _, w in copies])


def all_of(*parts):
    return (lambda: [s() for s, _ in parts]), (lambda: [w() for _, w in parts])


class InTurn:
    def __init__(self, *tiles):
        self.tiles, self.at = tiles, 0
        for start, _ in tiles[:2]:
            start()

    def next(self):
        self.tiles[self.at][1]()
        self.at += 1
        if self.at + 1 < len(self.tiles):
            self.tiles[self.at + 1][0]()


def place_of(quarter, y, me_ref):
    return quarter if y else 4 + (quarter ^ me_ref[1])


def packed(body, me, arrays, shape, scratch, flops, vmem, name):
    smem = pl.BlockSpec(memory_space=pltpu.SMEM)
    out = sds(shape, BF16)
    return resident(
        body,
        [(me, smem)] + far_of(*arrays),
        far_of(out, out),
        scratch=near_of(sds((2,) + shape, BF16)) + scratch + [pltpu.SemaphoreType.DMA((64,))],
        flops=flops,
        vmem=vmem,
        name=name,
    )


def grad_down_body(
    me_ref, g1_far, g2_far, dy_far, dm2_far, keep_far, go_far, out_ref, dy_ref, dm_ref, g_ref, acc_ref, sems
):
    low, group = me_ref[0] % 4, (me_ref[0] // 4) % 2
    ring, n, b = g_ref.shape[0], g1_far.shape[0], g_ref.shape[2]
    moves = Moves(sems)
    first, last = moves.take(2 * ring), moves.take(4)

    def tile(i):
        side, y, h = 1 - i // 4, (i // 2) % 2, i % 2
        quarter = ((me_ref[0] // 8) ^ side) * 2 + h
        at = jnp.where(y == 0, 4 + (quarter ^ me_ref[1]), quarter) * b
        return side, y, h, at

    def loads(i):
        at, slot = tile(i)[3], i % ring
        near = g_ref.at[slot]
        ends = ((g1_far, near.at[pl.ds(0, n)]), (g2_far, near.at[pl.ds(n, 2 * n)]))
        return [pltpu.make_async_copy(lanes_at(f, at, b), t, sems.at[first + 2 * slot + k]) for k, (f, t) in enumerate(ends)]

    def store(far, side, y):
        return pltpu.make_async_copy(out_ref.at[side, y], far.at[y], sems.at[last + side * 2 + y])

    ready = [moves.whole(dy_far, dy_ref), moves.whole(dm2_far, dm_ref.at[pl.ds(n, 2 * n)])]
    for i in range(2):
        for c in loads(i):
            c.start()
    for wait in ready:
        wait()
    dm_ref[:n] = dy_ref[...].astype(BF16)

    def step(i, _):
        side, y, h, _ = tile(i)
        for c in loads(i):
            c.wait()

        @pl.when(i + 2 < 8)
        def _():
            for c in loads(i + 2):
                c.start()

        acc_ref[...] = dot_tn(g_ref[i % ring], dm_ref[...]).reshape(acc_ref.shape)
        for s in range(4):
            out_ref[side, y, (h ^ group) * 4 + s] = acc_ref[s ^ low].astype(BF16)

        @pl.when((h == 1) & (side == 1))
        def _():
            store(go_far, 1, y).start()

        @pl.when((h == 1) & (side == 0))
        def _():
            store(keep_far, 0, y).start()

        return 0

    lax.fori_loop(0, 8, step, 0)
    for y in range(2):
        store(go_far, 1, y).wait()
        store(keep_far, 0, y).wait()


def grad_down(me, g1, g2, dy, dm2):
    n, d = dy.shape
    ff = g1.shape[1]
    b = ff // 8
    return packed(
        grad_down_body,
        me,
        (g1, g2, dy, dm2),
        (2, 8, b // 4, d),
        [
            pltpu.VMEM((n, d), F32),
            pltpu.VMEM((3 * n, d), BF16),
            pltpu.VMEM((3, 3 * n, b), BF16),
            pltpu.VMEM((4, b // 4, d), F32),
        ],
        2 * 3 * n * d * ff,
        40,
        "grad_down",
    )


CUT = 768
CUT_BACK = 1536


def swapped(s):
    return ((s >> 1) % 2) * 4 + ((s >> 2) % 2) * 2 + s % 2


def put_slots(out_ref, y, lanes, acc_ref, me):
    for s in range(16):
        out_ref[s // 8, y, s % 8, :, lanes] = acc_ref[s ^ me].astype(BF16)


def grad_up_body(
    me_ref, n1_far, n2_far, du1_far, du2_far, dp1_far, dp2_far, o1_far, o2_far, keep_far, go_far,
    out_ref, n_ref, t_ref, du_ref, dp_ref, o_ref, acc_ref, acc2_ref, sems,
):
    moves = Moves(sems)
    d, f = n_ref.shape[1], o_ref.shape[2]
    ring, c, n = du_ref.shape[0], du_ref.shape[2], du1_far.shape[0]
    first, last = moves.take(4 * ring), moves.take(4)

    def loads(i):
        y, t, slot = i // 2, i % 2, i % ring
        copies = []
        for k in range(2):
            quarter = 2 * t + k
            at = jnp.where(y == 0, 4 + (quarter ^ me_ref[1]), quarter) * f
            near = lanes_at(du_ref.at[slot], k * f, f)
            for far, rows in ((du1_far, pl.ds(0, n)), (du2_far, pl.ds(n, 2 * n))):
                copies.append((lanes_at(far, at, f), near.at[rows]))
        return [pltpu.make_async_copy(a, b, sems.at[first + 4 * slot + k]) for k, (a, b) in enumerate(copies)]

    def stores(y):
        return [
            pltpu.make_async_copy(out_ref.at[i, y], far.at[y], sems.at[last + 2 * y + i])
            for i, far in enumerate((keep_far, go_far))
        ]

    ready = stack_rows(moves, (n1_far, n2_far), n_ref, 0, d)
    ready[0]()
    for c0 in loads(0):
        c0.start()
    out_loads = [stack_rows(moves, (dp1_far, dp2_far), dp_ref, 0, d)]
    out_loads += [stack_rows(moves, (o1_far, o2_far), o_ref.at[y], (1 - y) * f, f) for y in range(2)]
    ready[1]()
    for c0 in loads(1):
        c0.start()
    t_ref[...] = n_ref[...].T

    def step(i, _):
        y, t = i // 2, i % 2
        for c0 in loads(i):
            c0.wait()

        @pl.when(i + 2 < 4)
        def _():
            for c0 in loads(i + 2):
                c0.start()

        @pl.when(i == 0)
        def _():
            for start, _ in out_loads:
                start()

        acc_ref[...] = dot(t_ref[...], du_ref[i % ring]).reshape(acc_ref.shape)
        put_slots(out_ref, y, pl.ds(pl.multiple_of(t * c, c), c), acc_ref, jnp.where(t == 0, me_ref[0], me_ref[2]))

        @pl.when(i == 1)
        def _():
            for _, wait in out_loads:
                wait()

        @pl.when(t == 1)
        def _():
            acc2_ref[...] = dot_tn(dp_ref[...], o_ref[y]).reshape(acc2_ref.shape)
            put_slots(out_ref, y, slice(2 * c, 2 * c + f), acc2_ref, me_ref[2])
            for s in stores(y):
                s.start()

        return 0

    lax.fori_loop(0, 4, step, 0)
    for y in range(2):
        for s in stores(y):
            s.wait()


def grad_up(me, n1, n2, du1, du2, dp1, dp2, o1, o2):
    n, d = n1.shape
    ff = du1.shape[1]
    f, c = o1.shape[1] // 2, ff // 4
    return packed(
        grad_up_body,
        me,
        (n1, n2, du1, du2, dp1, dp2, o1, o2),
        (2, 8, d // 16, 2 * c + f),
        [
            pltpu.VMEM((3 * n, d), BF16),
            pltpu.VMEM((d, 3 * n), BF16),
            pltpu.VMEM((3, 3 * n, c), BF16),
            pltpu.VMEM((3 * n, d), BF16),
            pltpu.VMEM((2, 3 * n, f), BF16),
            pltpu.VMEM((16, d // 16, c), F32),
            pltpu.VMEM((16, d // 16, f), F32),
        ],
        2 * 3 * n * d * (ff + d),
        56,
        "grad_up",
    )


def grad_qkv_body(me_ref, ae_far, ao_far, de_far, do_far, keep_far, go_far, out_ref, a_ref, t_ref, d_ref, acc_ref, sems):
    moves = Moves(sems)
    d = a_ref.shape[1]
    f = de_far.shape[2] // 2
    ready = stack_rows(moves, (ae_far, ao_far), a_ref, 0, d)
    n, first = ae_far.shape[0], moves.take(6)

    def loads(j):
        return [
            pltpu.make_async_copy(far.at[j], d_ref.at[j, pl.ds(k * n, n)], sems.at[first + 2 * j + k])
            for k, far in enumerate((de_far, do_far))
        ]

    ready[0]()
    for c in loads(0):
        c.start()
    ready[1]()
    for j in (1, 2):
        for c in loads(j):
            c.start()
    t_ref[...] = a_ref[...].T

    def step(j, _):
        for c in loads(j):
            c.wait()
        acc_ref[...] = dot(t_ref[...], d_ref[j]).reshape(acc_ref.shape)
        lanes = pl.ds(pl.multiple_of(j * f, f), f)
        for s in range(16):
            block = acc_ref[s ^ me_ref[0]].astype(BF16)
            out_ref[s // 8, 1, s % 8, :, lanes] = block[:, :f]
            out_ref[s // 8, 0, s % 8, :, lanes] = block[:, f:]
        return 0

    lax.fori_loop(0, 3, step, 0)
    sent = [moves.whole(out_ref.at[i], far) for i, far in ((1, go_far), (0, keep_far))]
    for wait in sent:
        wait()


def grad_qkv(me, ae, ao, dqkv_e, dqkv_o):
    n, d = ae.shape
    f = dqkv_e.shape[2] // 2
    return packed(
        grad_qkv_body,
        me,
        (ae, ao, dqkv_e, dqkv_o),
        (2, 8, d // 16, 3 * f),
        [
            pltpu.VMEM((2 * n, d), BF16),
            pltpu.VMEM((d, 2 * n), BF16),
            pltpu.VMEM((3, 2 * n, 2 * f), BF16),
            pltpu.VMEM((16, d // 16, 2 * f), F32),
        ],
        2 * 2 * 3 * n * d * 2 * f,
        40,
        "grad_qkv",
    )


def packed_call(body, grid, me, ins, outs, scratch=(), flops=0, aliases={}, name=None):
    return pl.pallas_call(
        body,
        grid_spec=pltpu.PrefetchScalarGridSpec(
            num_scalar_prefetch=1,
            grid=grid,
            in_specs=[s for _, s in ins],
            out_specs=[s for _, s in outs],
            scratch_shapes=scratch,
        ),
        out_shape=[a for a, _ in outs],
        input_output_aliases=aliases,
        compiler_params=pltpu.CompilerParams(
            dimension_semantics=("arbitrary",) * len(grid), vmem_limit_bytes=VMEM_LIMIT
        ),
        cost_estimate=pl.CostEstimate(flops=int(flops) // 16, bytes_accessed=0, transcendentals=0),
        name=name,
    )(me, *[a for a, _ in ins])


def unpack_down_body(me_ref, part_ref, *refs):
    low, rows = me_ref[0] % 8, part_ref.shape[1]
    for b in range(8):
        refs[-1][b * rows : (b + 1) * rows] = part_ref[swapped(b ^ low)].astype(F32)


def unpack_down(me, side, part, into=()):
    _, r, w = part.shape
    half = 8 * r
    at = lambda me: (me[0] // 8) ^ side
    ins = [(part, pl.BlockSpec(part.shape, lambda i, me: (0, 0, 0)))]
    ins += [(t, pl.BlockSpec(memory_space=pl.ANY)) for t in into]
    return packed_call(
        unpack_down_body,
        (1,),
        me,
        ins,
        [(sds((2 * half, w), F32), pl.BlockSpec((half, w), lambda i, me: (at(me), 0)))],
        aliases={2 + i: i for i in range(len(into))},
        name="unpack_down",
    )[0]


def unpack_rest_body(side, me_ref, part_ref, *refs):
    up_far, out_far, qkv_far, up_st, wide, out_st, qkv_st, sems = refs[-8:]
    moves = Moves(sems)
    left, right = me_ref[0] % 8, me_ref[2] % 8
    rows, half = part_ref.shape[1], 8 * part_ref.shape[1]
    d, f = up_st.shape[1], wide.shape[1]
    base = ((me_ref[0] // 8) ^ side) * half
    sent = []
    for b in range(8):
        sl = slice(b * rows, (b + 1) * rows)
        up_st[sl, :CUT] = part_ref[b ^ left, :, :CUT].astype(F32)
        up_st[sl, CUT:] = part_ref[swapped(b ^ right), :, CUT:d].astype(F32)
        wide[sl] = part_ref[b ^ right, :, d : d + f].astype(F32)
        if b % 4 == 3:
            start, size = (b - 3) * rows, 4 * rows
            at = pl.ds(pl.multiple_of(base + start, 8), size)
            sent.append(moves.whole(up_st.at[pl.ds(start, size)], up_far.at[at]))
    out_st[...] = wide[...].T
    sent.append(moves.whole(out_st, lanes_at(out_far, base, half)))
    for j in range(3):
        for b in range(8):
            sl = slice(b * rows, (b + 1) * rows)
            qkv_st[j, sl] = part_ref[b ^ right, :, d + (j + 1) * f : d + (j + 2) * f].astype(F32)
        sent.append(moves.whole(qkv_st.at[j], qkv_far.at[j, pl.ds(pl.multiple_of(base, 8), half)]))
    for wait in sent:
        wait()


def unpack_rest(me, side, part, into=()):
    _, r, w = part.shape
    half = 8 * r
    d, f = CUT_BACK, (w - CUT_BACK) // 4
    smem = pl.BlockSpec(memory_space=pltpu.SMEM)
    outs = [sds((2 * half, d), F32), sds((f, 2 * half), F32), sds((3, 2 * half, f), F32)]
    stages = [sds((half, d), F32), sds((half, f), F32), sds((f, half), F32), sds((3, half, f), F32)]
    return resident(
        functools.partial(unpack_rest_body, side),
        [(me, smem), part] + far_of(*into),
        far_of(*outs),
        scratch=near_of(*stages) + [pltpu.SemaphoreType.DMA((8,))],
        vmem=24,
        aliases={2 + i: i for i in range(len(into))},
        name="unpack_rest",
    )


def fold(*parts):
    return sum(p.astype(F32) for p in parts).astype(BF16)


def after(value, *first):
    return lax.optimization_barrier((value, first))[0]


class Chunk:
    def __init__(self, keep, got):
        self.keep, self.got = keep, got
        self.sent = None

    def wait(self, *also):
        self.got, also = lax.optimization_barrier((self.got, also))
        return also

    def to_partner(self):
        total = fold(self.keep, self.got)
        self.keep, self.sent = total[1], total[0]
        self.got = lax.ppermute(self.sent, "tensor", FLIP)

    def gather_core(self):
        self.got = lax.ppermute(self.keep, "core", FLIP)


def add(k, g):
    return (k.astype(F32) + g.astype(F32)).astype(BF16)


def phase_shapes(mode, parts):
    shapes = [p[0].shape for p in parts]
    s = shapes[0]
    if mode == "half":
        out = s[:-3] + (s[-3] // 2,) + s[-2:]
        return [out, out]
    if mode == "partner":
        return [s[1:], s[1:]]
    if mode == "last":
        out = (s[0] // 2, s[1], sum(t[2] for t in shapes))
        return [out, out]
    if mode == "sum":
        return [s]
    if mode == "split":
        return [(2 * s[0], s[1], CUT_BACK), (2 * s[0], s[1], s[2] - CUT_BACK)]
    return [(2 * s[0], s[1], sum(t[2] for t in shapes))]


def phase_part(mode, parts, outs):
    if mode == "half":
        (k, g), n = parts[0], outs[0].shape[-3]
        lead = (slice(None),) * (len(k.shape) - 3)
        for i, out in enumerate(outs):
            at = lead + (slice(i * n, (i + 1) * n),)
            out[...] = add(k[at], g[at])
    elif mode == "partner":
        k, g = parts[0]
        for i, out in zip((1, 0), outs):
            out[...] = add(k[i], g[i])
    elif mode == "last":
        n, lane = outs[0].shape[0], 0
        for k, g in parts:
            for i, out in enumerate(outs):
                at = slice(i * n, (i + 1) * n)
                out[:, :, lane : lane + k.shape[2]] = add(k[at], g[at])
            lane += k.shape[2]
    elif mode == "sum":
        outs[0][...] = add(parts[0][0][...], parts[0][1][...])
    elif mode == "split":
        for i, ref in enumerate(parts[0]):
            at = slice(i * ref.shape[0], (i + 1) * ref.shape[0])
            outs[0][at] = ref[:, :, :CUT_BACK]
            outs[1][at] = ref[:, :, CUT_BACK:]
    else:
        lane = 0
        for pair in parts:
            for i, ref in enumerate(pair):
                outs[0][i * ref.shape[0] : (i + 1) * ref.shape[0], :, lane : lane + ref.shape[2]] = ref[...]
            lane += pair[0].shape[2]


def phase(*items):
    shapes = [phase_shapes(*t) for t in items]

    def body(*refs):
        at = sum(2 * len(parts) for _, parts in items)
        ins, outs = list(refs[:at]), list(refs[at:])
        for (mode, parts), made in zip(items, shapes):
            mine = [(ins.pop(0), ins.pop(0)) for _ in parts]
            phase_part(mode, mine, [outs.pop(0) for _ in made])

    flat = resident(
        body,
        [t for _, parts in items for pair in parts for t in pair],
        [sds(s, BF16) for made in shapes for s in made],
        vmem=16,
        name="phase",
    )
    flat = list(flat)
    return [[flat.pop(0) for _ in made] for made in shapes]


class Hops(Chunk):
    def __init__(self, outer, keep, got):
        super().__init__(keep, got)
        self.axes = {"x": ("x", 2, 1), "z": ("o", outer, 1), "w": ("o", outer, 2)}
        self.extra = [("o", outer, 1 << b) for b in range(2, outer.bit_length() - 1)]

    def over(self, way, t):
        return lax.ppermute(t, "tensor", FLIP) if way == "partner" else flip_bit(t, *self.axes[way])

    def send(self, *parts):
        self.keep, self.sent, self.got = [], [], []
        for total, way in parts:
            if way == "partner":
                keep, sent = total[1], total[0]
            else:
                half = total.shape[-3] // 2
                keep, sent = total[..., :half, :, :], total[..., half:, :, :]
            self.keep.append(keep)
            self.sent.append(sent)
            self.got.append(self.over(way, sent))

    def fold_first(self):
        total = fold(self.keep, self.got)
        half = total.shape[1] // 2
        return [part for lanes in (total[..., :CUT], total[..., CUT:]) for part in (lanes[:, :half], lanes[:, half:])]

    def first(self, parts):
        self.keep, self.sent = [parts[0], parts[2]], [parts[1], parts[3]]
        self.got = [self.over("x", parts[1]), self.over("z", parts[3])]

    def first_hop(self, way):
        self.send((fold(self.keep, self.got), way))

    def parts(self):
        return list(zip(self.keep, self.got))

    def hop(self, *ways):
        items = [("partner" if w == "partner" else "half", [p]) for w, p in zip(ways, self.parts())]

        def then(made):
            self.keep, self.sent = [m[0] for m in made], [m[1] for m in made]
            self.got = [self.over(w, s) for w, s in zip(ways, self.sent)]

        return items, then

    def absorb(self, other):
        self.keep, self.got = self.keep + other.keep, self.got + other.got

    def last_hop(self):
        def then(made):
            ((keep, sent),) = made
            self.keep, self.sent = [keep], [sent]
            self.got = [self.over("w", sent)]

        return [("last", self.parts())], then

    def back_first(self):
        def then(made):
            ((total,),) = made
            for s in self.extra:
                total = fold(total, flip_bit(total, *s))
            self.keep = self.sent = [total]
            self.got = [self.over("w", total)]

        return [("sum", self.parts())], then

    def back(self, *ways):
        if len(ways) == 2 and len(self.keep) == 1:
            items = [("split", self.parts())]
        else:
            items = [("join", [p]) for p in self.parts()]

        def then(made):
            self.keep = self.sent = [t for m in made for t in m]
            self.got = [self.over(w, t) for w, t in zip(ways, self.keep)]

        return items, then

    def back_core(self):
        def then(made):
            ((self.keep,),) = made
            self.sent = self.keep
            self.gather_core()

        return [("join", self.parts())], then


def all_steps(*steps):
    made = phase(*[item for items, _ in steps for item in items])
    for items, then in steps:
        then(made[: len(items)])
        made = made[len(items) :]


def mask_biases(seg):
    seq = seg.shape[1]
    place = jnp.arange(seq, dtype=jnp.int32)
    same = seg[:, :, None] == seg[:, None, :]
    below = (place[:, None] < place[None, :])[None]
    incl = (place[:, None] <= place[None, :])[None]
    bias = lambda m: jnp.where(same & m, 0.0, NEG).astype(F32)
    return bias(incl), bias(below)


def sync(*values):
    return lax.optimization_barrier(values)


class Link:
    def __init__(self, outer, w_qkv, w_out, w_up, w_down):
        self.outer = outer
        self.own = (w_qkv, w_out, w_up, w_down)
        self.core_at, self.x_at, o = (lax.axis_index(a) for a in ("core", "x", "o"))
        bits = {"x": self.x_at, "z": o % 2, "w": (o // 2) % 2}
        self.fetch_bits = self.core_at * 2 + self.x_at
        slots = []
        for order in ("xzw", "zxw"):
            slot = self.core_at
            for name in order:
                slot = slot * 2 + bits[name]
            slots.append(slot)
        self.me = jnp.stack([slots[0], self.fetch_bits, slots[1]]).astype(jnp.int32)
        self.me_z = self.me[2:0:-1]

    def quarter(self, own):
        flat = own.reshape(-1, own.shape[-1])
        return take_half(take_half(flat, self.core_at), self.x_at)

    def over_x(self, t):
        return lax.ppermute(t, "x", FLIP)

    def fetch(self, own_work):
        own = self.own
        size = own[2].shape[1] // 4
        part = lambda t, axis, bits: lax.dynamic_slice_in_dim(t, bits * size, size, axis)
        pieces = [
            self.quarter(own[1]),
            part(own[2], 1, self.fetch_bits),
            jnp.concatenate([part(own[3], 0, self.fetch_bits), part(own[3], 0, self.fetch_bits ^ 1)], axis=0),
        ]
        qkv = self.partner(self.quarter(own[0]))
        up, out, down = (self.partner(pieces[i]) for i in (1, 0, 2))
        qkv, own_work = sync(qkv, own_work)
        qkv, out, up = sync(ordered(self.x_at, qkv, self.over_x(qkv)).reshape(-1, qkv.shape[-1]), out, up)
        qkv_core, out_x, up_x = self.core(qkv), self.over_x(out), self.over_x(up)
        qkv = ordered(self.core_at, qkv, qkv_core).reshape(own[0].shape)

        def join_out(*work):
            nonlocal out, out_x
            work, out, out_x = sync(work, out, out_x)
            out = ordered(self.x_at, out, out_x).reshape(-1, out.shape[-1])
            out = ordered(self.core_at, out, self.core(out)).reshape(own[1].shape)
            return work, jnp.concatenate([own[1], out], axis=0)

        def pieces_of(*work):
            up_there, down_there, work = sync(up_x, down, work)
            ups = (own[2], up, up_there, self.core(up), self.core(up_there))
            return ups, (own[3], down_there, self.core(down_there)), work

        return own_work, own[0], qkv, jnp.concatenate([own[0], qkv], axis=2), join_out, pieces_of

    def partner(self, t):
        return lax.ppermute(t, "tensor", FLIP)

    def core(self, t):
        return lax.ppermute(t, "core", FLIP)

    def chunk(self, keep, got):
        return Chunk(keep, got)

    def hops(self, keep, got):
        return Hops(self.outer, keep, got)

    def small_steps(self):
        return [("core", 2, 1), ("tensor", 2, 1)] + steps_of(self.outer)

    def flip(self, t, step):
        return flip_bit(t, *step)


def local_part(x, seg, cot, gb, link):
    rows, seq = seg.shape
    n, width = x.shape
    me, me_z = link.me, link.me_z
    incl, strict = mask_biases(seg)
    normal, _ = norm_stats(x.astype(F32))
    a_e = (normal * gb[0] + gb[2]).astype(BF16)
    first = attend_first(a_e, link.own[0], incl)
    (a_e, first, cot), wq_own, fetched, wqkv, join_out, pieces_of = link.fetch((a_e, first, cot))
    second = attend_first(a_e, fetched, incl)
    qkv_e, o1 = (jnp.concatenate([s, t], axis=-1) for s, t in zip(first[:2], second[:2]))
    lse1 = jnp.concatenate([first[2], second[2]], axis=0).reshape(-1, GROUP // HD, n)
    (qkv_e, o1, lse1, wqkv), wout = join_out(qkv_e, o1, lse1, wqkv)
    h1, n2_1, g1, d1, part_one = mlp_own(x, o1, wout, gb, link.own[2], link.own[3])
    ups, downs, (n2_1, part_one) = pieces_of(n2_1, part_one)
    g1, d1, ho, a_o = mlp_other(n2_1, part_one, g1, d1, gb, ups[1:], downs[1:])
    qkv_o, o2, lse2 = attend_second(a_o, wqkv, incl, strict, qkv_e, o1, lse1)
    out, out_two, n2_2, g2, du2, dh1_2, dp2, do2, sums2, dm2 = mlp_second(x, ho, o2, cot, wout, gb, ups, downs, seq)
    out_got = link.partner(out)
    dqkv_o, part, dy, sums_o = attend_back(wqkv, incl, strict, qkv_e, qkv_o, o2, lse2, do2, dh1_2, ho, gb)
    o2_flat = o2.reshape(2 * n, width)

    out_got, dy = sync(out_got, dy)
    quarter = out_two.shape[1] // 2
    out_last = [link.partner(after(out_two[:, :quarter], out_got))]
    down_keep, down_go = grad_down(me_z, g1, g2, dy, dm2)
    down_keep, down_go, out_last[0] = sync(down_keep, down_go, out_last[0])
    out_last.append(link.partner(after(out_two[:, quarter:], down_go)))
    down = link.hops(down_keep, link.core(down_go))
    dy = after(dy, down_go)
    du1, dh1_1, dp1, do1, sums1 = mlp_back(dy, h1, wout, gb, d1, ups, downs, seq)
    du1, dp1, do1, out_last[1] = down.wait(du1, dp1, do1, out_last[1])
    down.to_partner()
    up_keep, up_go = grad_up(me, n2_1, n2_2, after(du1, down.sent), du2, dp1, dp2, o1, o2_flat)
    do1 = after(do1, up_go)
    dqkv_e, gt, sums_e = attend_back_even(wqkv, incl, qkv_e, o1, lse1, do1, o2, lse2, do2, part, dh1_1, dh1_2, x, gb)
    dqkv_e, gt, sums_e, up_go = down.wait(dqkv_e, gt, sums_e, up_go)
    up = link.hops(up_keep, link.core(up_go))
    down.keep, down.got = [down.keep], [down.got]
    all_steps(down.hop("z"))
    small = jnp.stack([sums_e[0] + sums_o[0], sums1[0] + sums2[0], sums_e[1] + sums_o[1], sums1[1] + sums2[1], sums_o[2]])
    qkv_keep, qkv_go = grad_qkv(me_z, a_e, a_o, after(dqkv_e, *down.sent), dqkv_o)
    up_parts = up.fold_first()
    qkv_keep, qkv_go, down.got, up_parts = sync(qkv_keep, qkv_go, down.got, up_parts)
    out = link.finish(
        jnp.concatenate([out, out_two], axis=0),
        jnp.concatenate([out_got, jnp.concatenate(after(out_last, up_parts), axis=1)], axis=0),
        link.out_shape,
    )
    qkv = link.hops(qkv_keep, link.core(qkv_go))
    small_steps = iter(link.small_steps())
    small_got = link.flip(after(small, qkv_go), next(small_steps))

    chunks = [up, qkv]

    def wait_all():
        nonlocal small, small_got
        got, small_got = sync([c.got for c in chunks], small_got)
        for c, g in zip(chunks, got):
            c.got = g
        if small_got is not None:
            small = small + small_got
            step = next(small_steps, None)
            small_got = None if step is None else link.flip(small, step)

    chunks.remove(up)
    wait_all()
    up.first(up_parts)
    qkv.first_hop("partner")
    all_steps(down.hop("x"))
    chunks += [up, down]
    (out,) = up.wait(out)
    wait_all()
    all_steps(up.hop("partner", "x"), qkv.hop("z"), down.hop("w"))
    wait_all()
    all_steps(up.hop("z", "partner"), qkv.hop("x"), down.back_first())
    half = gt.shape[0] // 2
    gt_got = [link.partner(after(gt[:half], *up.sent))]
    wait_all()
    up.absorb(qkv)
    chunks.remove(qkv)
    all_steps(up.last_hop(), down.back("z"))
    gt_got.append(link.partner(after(gt[half:], *up.sent)))
    (gt_got[0],) = up.wait(gt_got[0])
    wait_all()
    all_steps(up.back_first(), down.back("x"))
    (gt_got[1],) = up.wait(gt_got[1])
    wait_all()
    while small_got is not None:
        wait_all()
    all_steps(up.back("z", "x"), down.back_core())
    wait_all()
    all_steps(up.back("x", "z"))
    g_down = unpack_down(me_z, 0, after(down.keep, *up.sent))
    g_down = unpack_down(me_z, 1, down.got, (g_down,))
    gt = link.finish(gt, jnp.concatenate(gt_got, axis=0), link.tokens_shape).astype(F32)
    small = (small[0:2], small[2:4], small[4])
    g_down, gt, small = up.wait(g_down, gt, small)
    all_steps(up.back_core())
    g_rest = unpack_rest(me, 0, up.keep)
    g_rest = up.wait(*g_rest)
    g_up, g_out, g_qkv = unpack_rest(me, 1, up.got, g_rest)
    return out, gt, (g_qkv, g_out, g_up, g_down), small


def shards(outer, tokens, segments, pass_embed, w_qkv, w_out, w_up, w_down, gain, bias, cotangent):
    ty = lax.axis_index("tensor")
    rows = tokens.shape[0] // 2
    width = tokens.shape[2]
    mine = lambda t: lax.dynamic_slice_in_dim(t, ty * rows, rows, 0)
    x = mine(tokens).reshape(-1, width)
    gb = jnp.concatenate([gain, bias, pass_embed[None]], axis=0)
    link = Link(outer, w_qkv, w_out, w_up, w_down)
    link.out_shape, link.tokens_shape = cotangent.shape, tokens.shape
    link.finish = lambda mine, theirs, shape: ordered(ty, mine, theirs).reshape(shape)
    out, gt, grads, small = local_part(x, mine(segments), mine(cotangent), gb, link)
    return out, gt, *grads, *small


def solution(mesh):
    outer = mesh.shape["dp"] // 4
    fine = Mesh(mesh.devices.reshape(outer, 2, 2, mesh.shape["tensor"]), ("o", "x", "core", "tensor"))
    rows = ROWS_OVER
    placed = (
        P(rows, None, None),
        P(rows, None),
        P(),
        P(None, None, "tensor"),
        P("tensor", None),
        P(None, "tensor"),
        P("tensor", None),
        P(),
        P(),
        P(rows, None, None),
    )

    def body(*args):
        return shards(outer, *args)

    return jax.shard_map(
        body,
        mesh=fine,
        in_specs=placed,
        out_specs=(
            P(rows, None, None),
            P(rows, None, None),
            P(None, None, "tensor"),
            P("tensor", None),
            P(None, "tensor"),
            P("tensor", None),
            P(),
            P(),
            P(),
        ),
        check_vma=False,
    )
```

```python
import functools

import jax
import jax.numpy as jnp
from jax import lax
from jax.experimental import pallas as pl
from jax.experimental.pallas import tpu as pltpu
from jax.sharding import Mesh
from jax.sharding import PartitionSpec as P

HD = 64
EPS = 1e-05
NEG = -1000000000.0
F32 = jnp.float32
BF16 = jnp.bfloat16
ROWS_OVER = ("o", "x", "core")
FLIP = ((0, 1), (1, 0))
VMEM_LIMIT = 16 * 1024 * 1024


def ordered(flag, mine, theirs):
    first = flag == 0
    return jnp.stack([jnp.where(first, mine, theirs), jnp.where(first, theirs, mine)])


def take_half(array, index):
    half = array.shape[0] // 2
    return lax.dynamic_slice_in_dim(array, index * half, half, 0)


def flip_bit(array, axis, size, bit):
    return lax.ppermute(array, axis, [(i, i ^ bit) for i in range(size)])


def steps_of(outer):
    steps = [("x", 2, 1)]
    bit = 1
    while bit < outer:
        steps.append(("o", outer, bit))
        bit *= 2
    return steps


def my_bit(axis, bit):
    return (lax.axis_index(axis) // bit) % 2


def dot(a, b):
    return lax.dot_general(a, b, (((1,), (0,)), ((), ())), preferred_element_type=F32)


def dot_nt(a, b):
    return lax.dot_general(a, b, (((1,), (1,)), ((), ())), preferred_element_type=F32)


def dot_tn(a, b):
    return lax.dot_general(a, b, (((0,), (0,)), ((), ())), preferred_element_type=F32)


def norm_stats(h):
    centred = h - jnp.mean(h, axis=-1, keepdims=True)
    inverse = lax.rsqrt(jnp.mean(centred * centred, axis=-1, keepdims=True) + EPS)
    return centred * inverse, inverse


def norm_back(grad, normal, inverse, gain):
    scaled = grad * gain
    centre = jnp.mean(scaled, axis=-1, keepdims=True)
    proj = jnp.mean(scaled * normal, axis=-1, keepdims=True)
    return inverse * (scaled - centre - normal * proj)


def gelu_parts(u):
    c = 0.7978845608028654
    a = 0.044715 * c
    square = u * u
    half = 0.5 + 0.5 * jnp.tanh(u * (c + a * square))
    g = u * half
    return g, half + g * (1.0 - half) * (2.0 * c + 6.0 * a * square)


def whole(shape):
    return pl.BlockSpec(shape, lambda *_: (0,) * len(shape))


def call(body, grid, ins, outs, scratch=(), cost=(0, 0), name=None, vmem=VMEM_LIMIT):
    return pl.pallas_call(
        body,
        grid=grid,
        in_specs=[s for _, s in ins],
        out_specs=[s for _, s in outs],
        out_shape=[a for a, _ in outs],
        scratch_shapes=scratch,
        compiler_params=pltpu.CompilerParams(
            dimension_semantics=("arbitrary",) * len(grid), vmem_limit_bytes=vmem
        ),
        cost_estimate=pl.CostEstimate(
            flops=int(cost[0]) // 16, bytes_accessed=int(cost[1]), transcendentals=0
        ),
        name=name,
    )(*[a for a, _ in ins])


FAR = pl.BlockSpec(memory_space=pl.ANY)


def resident(body, ins, outs, scratch=(), flops=0, vmem=16, aliases={}, name=None):
    spec = pl.BlockSpec(memory_space=pltpu.VMEM)
    ins, outs = ([o if isinstance(o, tuple) else (o, spec) for o in t] for t in (ins, outs))
    ins = [(pltpu.with_memory_space_constraint(a, pltpu.HBM) if s is FAR else a, s) for a, s in ins]
    outs = [(pltpu.HBM(a.shape, a.dtype) if s is FAR else a, s) for a, s in outs]
    return pl.pallas_call(
        body,
        in_specs=[s for _, s in ins],
        out_specs=[s for _, s in outs],
        out_shape=[a for a, _ in outs],
        scratch_shapes=scratch,
        input_output_aliases=aliases,
        compiler_params=pltpu.CompilerParams(vmem_limit_bytes=vmem * 1024 * 1024),
        cost_estimate=pl.CostEstimate(flops=int(flops) // 16, bytes_accessed=0, transcendentals=0),
        name=name,
    )(*[a for a, _ in ins])


def sds(shape, dtype):
    return jax.ShapeDtypeStruct(shape, dtype)


QB = 128
GROUP = 256


def lanes_of(ref, g):
    return ref.at[(slice(None),) * (len(ref.shape) - 1) + (pl.ds(pl.multiple_of(g * GROUP, GROUP), GROUP),)]


class Moves:
    def __init__(self, sems):
        self.sems, self.used = sems, 0

    def take(self, number):
        self.used += number
        return self.used - number

    def whole(self, source, target):
        copy = pltpu.make_async_copy(source, target, self.sems.at[self.take(1)])
        copy.start()
        return copy.wait

    def later(self, source, target):
        sem = self.sems.at[self.take(1)]
        copy = lambda: pltpu.make_async_copy(source, target, sem)
        return (lambda: copy().start()), (lambda: copy().wait())

    def groups(self, source, target):
        first = self.take(source.shape[-1] // GROUP)

        def copy(g):
            return pltpu.make_async_copy(lanes_of(source, g), lanes_of(target, g), self.sems.at[first + g])

        return (lambda g: copy(g).start()), (lambda g: copy(g).wait())


def cat_heads(t, scale=1.0):
    lane = lax.broadcasted_iota(jnp.int32, (1, 2 * HD), 1)
    parts = [t * jnp.where((lane < HD) == (h == 0), scale, 0.0).astype(t.dtype) for h in range(2)]
    return jnp.concatenate(parts, axis=0)


def own_lanes(t, scale=None):
    if scale is not None:
        t = t * scale
    return jnp.concatenate([t[:HD, :QB], t[HD:, QB:]], axis=0)


def twice(t):
    return jnp.concatenate([t, t], axis=1)


def pair_row(rows, p):
    return jnp.concatenate([rows[2 * p : 2 * p + 1], rows[2 * p + 1 : 2 * p + 2]], axis=1)


def put_pair(ref, p, cols, value):
    ref[2 * p : 2 * p + 1, cols] = value[:, :QB]
    ref[2 * p + 1 : 2 * p + 2, cols] = value[:, QB:]


def columns(t, r, seq, qb):
    return t[:, pl.ds(pl.multiple_of(r * seq + qb * QB, QB), QB)]


def rows_of(r, seq, qb):
    return pl.ds(pl.multiple_of(r * seq + qb * QB, QB), QB)


def in_turn(arrive, group, groups):
    for _, wait in arrive:
        wait(group)

    @pl.when(group + 2 < groups)
    def _():
        for start, _ in arrive:
            start(group + 2)


def attend_first_body(rows, seq, pairs, a_ref, w_ref, bias_ref, qkv_ref, o_ref, lse_ref):
    a = a_ref[...]
    for j in range(3):
        qkv_ref[j] = dot(a, w_ref[j]).astype(BF16)
    for r in range(rows):
        work = []
        for p in range(pairs):
            ln = slice(p * 2 * HD, (p + 1) * 2 * HD)
            k = qkv_ref[1, r * seq : (r + 1) * seq, ln]
            for b in range(seq // QB):
                sl, n = slice(r * seq + b * QB, r * seq + (b + 1) * QB), (b + 1) * QB
                q = cat_heads(qkv_ref[0, sl, ln], HD**-0.5)
                s = dot_nt(k[:n], q) + twice(bias_ref[r, :n, b * QB : n])
                work.append((p, ln, sl, n, s))
        done = []
        for p, ln, sl, n, s in work:
            top = jnp.max(s, axis=0, keepdims=True)
            e = jnp.exp(s - top)
            mass = jnp.sum(e, axis=0, keepdims=True)
            put_pair(lse_ref, p, sl, top + jnp.log(mass))
            done.append((e.astype(BF16), 1.0 / mass))
        for (p, ln, sl, n, _), (e, inv) in zip(work, done):
            vt = qkv_ref[2, r * seq : (r + 1) * seq, ln].T
            o_ref[sl, ln] = own_lanes(dot(vt[:, :n], e), inv).T.astype(BF16)


def attend_first(a, w, bias):
    rows, seq = bias.shape[0], bias.shape[1]
    n, d = a.shape
    f = w.shape[2]
    return resident(
        functools.partial(attend_first_body, rows, seq, f // (2 * HD)),
        (a, w, bias),
        [sds((3, n, f), BF16), sds((n, f), BF16), sds((f // HD, n), F32)],
        flops=6 * n * d * f + 16 * n * seq * f,
        name="attend_first",
    )


def attend_second_body(
    rows, seq, a_far, w_far, incl_far, strict_far, qkve_far, o1_far, lse1_ref,
    qkvo_far, o2_far, lse2_ref,
    a_ref, w_ref, incl_ref, strict_ref, qkve_ref, o1_ref, qkvo_ref, o2_ref, sems,
):
    groups = lse1_ref.shape[0]
    moves = Moves(sems)
    first = moves.take(6)

    def weight(j):
        return pltpu.make_async_copy(w_far.at[j], w_ref.at[j], sems.at[first + j])

    def projected(j):
        return pltpu.make_async_copy(qkvo_ref.at[j], qkvo_far.at[j], sems.at[first + 3 + j])

    a_there = moves.whole(a_far, a_ref)
    weight(0).start()
    arrive = [moves.groups(*t) for t in ((qkve_far, qkve_ref), (o1_far, o1_ref))]
    leave = moves.groups(o2_ref, o2_far)
    a_there()
    weight(0).wait()
    weight(1).start()
    weight(2).start()
    masks = [moves.whole(*t) for t in ((incl_far, incl_ref), (strict_far, strict_ref))]
    for g in range(2):
        for start, _ in arrive:
            start(g)

    def project(j, _):
        pl.when(j > 0)(lambda: weight(j).wait())
        qkvo_ref[j] = dot(a_ref[...], w_ref[j]).astype(BF16)
        projected(j).start()
        return 0

    lax.fori_loop(0, 3, project, 0)
    for wait in masks:
        wait()

    def next_group(group):
        in_turn(arrive, group, groups)

    def row(i, _):
        r, group = i % rows, i // rows
        lanes = pl.multiple_of(group * GROUP, GROUP)
        all_of = pl.ds(pl.multiple_of(r * seq, seq), seq)

        @pl.when(r == 0)
        def _():
            next_group(group)

        for p in range(GROUP // (2 * HD)):
            ln = pl.ds(lanes + p * 2 * HD, 2 * HD)
            ke, ko = qkve_ref[1, all_of, ln], qkvo_ref[1, all_of, ln]
            vte, vto = qkve_ref[2, all_of, ln].T, qkvo_ref[2, all_of, ln].T
            work = []
            for b in range(seq // QB):
                sl, n = rows_of(r, seq, b), (b + 1) * QB
                cols = slice(b * QB, n)
                incl, strict = twice(incl_ref[r, :n, cols]), twice(strict_ref[r, :n, cols])
                q = cat_heads(qkve_ref[0, sl, ln], HD**-0.5)
                work.append([dot_nt(ko[:n], q) + strict])
                q = cat_heads(qkvo_ref[0, sl, ln], HD**-0.5)
                work.append([dot_nt(ko[:n], q) + incl, dot_nt(ke[:n], q) + incl])
            for b in range(seq // QB):
                sl, n = rows_of(r, seq, b), (b + 1) * QB
                (s,), (so, se) = work[2 * b : 2 * b + 2]
                old = pair_row(lse1_ref[group, :, sl], p)
                top = jnp.maximum(old, jnp.max(s, axis=0, keepdims=True))
                e = jnp.exp(s - top)
                kept = jnp.exp(old - top)
                mass = kept + jnp.sum(e, axis=0, keepdims=True)
                work[2 * b] = (e.astype(BF16), kept, 1.0 / mass)
                put_pair(lse2_ref.at[0, group], p, sl, top + jnp.log(mass))
                top = jnp.max(jnp.maximum(se, so), axis=0, keepdims=True)
                ee, eo = jnp.exp(se - top), jnp.exp(so - top)
                mass = jnp.sum(ee + eo, axis=0, keepdims=True)
                work[2 * b + 1] = (ee.astype(BF16), eo.astype(BF16), 1.0 / mass)
                put_pair(lse2_ref.at[1, group], p, sl, top + jnp.log(mass))
            for b in range(seq // QB):
                sl, n = rows_of(r, seq, b), (b + 1) * QB
                (e, kept, inv), (ee, eo, inv2) = work[2 * b : 2 * b + 2]
                o1 = o1_ref[sl, ln].astype(F32).T
                o = own_lanes(dot(vto[:, :n], e), inv) + own_lanes(twice(o1), kept * inv)
                o2_ref[0, sl, ln] = o.T.astype(BF16)
                o = dot(vte[:, :n], ee) + dot(vto[:, :n], eo)
                o2_ref[1, sl, ln] = own_lanes(o, inv2).T.astype(BF16)

        @pl.when(r == rows - 1)
        def _():
            leave[0](group)

        return 0

    lax.fori_loop(0, rows * groups, row, 0)
    for j in range(3):
        projected(j).wait()
    for g in range(groups):
        leave[1](g)


def attend_second(a, w, incl, strict, qkve, o1, lse1):
    rows, seq = incl.shape[0], incl.shape[1]
    n, d = a.shape
    f = w.shape[2]
    qkv, o2 = sds((3, n, f), BF16), sds((2, n, f), BF16)
    near = (a, w, incl, strict, qkve, o1, qkv, o2)
    return resident(
        functools.partial(attend_second_body, rows, seq),
        [(t, FAR) for t in (a, w, incl, strict, qkve, o1)] + [lse1],
        [(qkv, FAR), (o2, FAR), sds((2, *lse1.shape), F32)],
        scratch=[pltpu.VMEM(t.shape, t.dtype) for t in near] + [pltpu.SemaphoreType.DMA((64,))],
        flops=6 * n * d * f + 48 * n * seq * f,
        vmem=32,
        name="attend_second",
    )


def row_products(a, b):
    prod = cat_heads((a * b).astype(BF16))
    return dot_nt(jnp.ones((8, 2 * HD), BF16), prod)[:1]


def query_parts(sl, ln, group, p, i, qkv_ref, o_ref, lse_ref, do_ref):
    do = do_ref[i, sl, ln]
    delta = row_products(do.astype(F32), o_ref[i, sl, ln].astype(F32))
    return cat_heads(qkv_ref[0, sl, ln], HD**-0.5), cat_heads(do), pair_row(lse_ref[i, group, :, sl], p), delta


def blocks_back(tasks):
    scores = [dot_nt(k, q) + bias - lse for k, _, _, bias, q, _, lse, _ in tasks]
    moved = [dot_nt(v, do) - delta for _, v, _, _, _, do, _, delta in tasks]
    probs = [jnp.exp(s) for s in scores]
    ds = [(p * m).astype(BF16) for p, m in zip(probs, moved)]
    return [
        (dot(p.astype(BF16), do), dot(d, q), dot(kt, d))
        for (_, _, kt, _, q, do, _, _), p, d in zip(tasks, probs, ds)
    ]


def add_rows(total, part):
    if total is None:
        return part
    n = part.shape[0]
    return jnp.concatenate([total[:n] + part, total[n:]], axis=0)


def attend_back_body(
    rows, seq, w_far, incl_far, strict_far, qkve_far, qkvo_far, o2_far, lse2_ref, do_far,
    dh1_far, ho_far, gb_ref,
    dqkvo_far, dqkve_far, dy_far, sums_ref,
    w_ref, incl_ref, strict_ref, qkve_ref, qkvo_ref, o2_ref, do_ref, dh1_ref, ho_ref,
    dqkvo_ref, dqkve_ref, da_ref, dy_ref, sems,
):
    groups = lse2_ref.shape[1]
    moves = Moves(sems)
    arrive = [
        moves.groups(*t)
        for t in ((qkve_far, qkve_ref), (qkvo_far, qkvo_ref), (o2_far, o2_ref), (do_far, do_ref))
    ]
    leave = [moves.groups(*t) for t in ((dqkvo_ref, dqkvo_far), (dqkve_ref, dqkve_far))]
    for start, _ in arrive:
        start(0)
    masks = [moves.whole(*t) for t in ((incl_far, incl_ref), (strict_far, strict_ref))]
    for start, _ in arrive:
        start(1)
    odd = pl.ds(rows * seq, rows * seq)
    late = [moves.later(*t) for t in ((w_far, w_ref), (dh1_far.at[odd], dh1_ref), (ho_far, ho_ref))]
    for wait in masks:
        wait()

    def next_group(group):
        in_turn(arrive, group, groups)

        @pl.when(group == groups - 2)
        def _():
            for start, _ in late:
                start()

    sc = HD**-0.5

    def row(i, _):
        r, group = i % rows, i // rows
        lanes = pl.multiple_of(group * GROUP, GROUP)
        all_of = pl.ds(pl.multiple_of(r * seq, seq), seq)

        @pl.when(r == 0)
        def _():
            next_group(group)

        for p in range(GROUP // (2 * HD)):
            ln = pl.ds(lanes + p * 2 * HD, 2 * HD)
            ke, ve = qkve_ref[1, all_of, ln], qkve_ref[2, all_of, ln]
            ko, vo = qkvo_ref[1, all_of, ln], qkvo_ref[2, all_of, ln]
            kte, kto = ke.T, ko.T
            tasks = []
            for b in reversed(range(seq // QB)):
                sl, n = rows_of(r, seq, b), (b + 1) * QB
                cols = slice(b * QB, n)
                incl, strict = twice(incl_ref[r, :n, cols]), twice(strict_ref[r, :n, cols])
                even = query_parts(sl, ln, group, p, 0, qkve_ref, o2_ref, lse2_ref, do_ref)
                odd = query_parts(sl, ln, group, p, 1, qkvo_ref, o2_ref, lse2_ref, do_ref)
                tasks.append((ko[:n], vo[:n], kto[:, :n], strict, *even))
                tasks.append((ko[:n], vo[:n], kto[:, :n], incl, *odd))
                tasks.append((ke[:n], ve[:n], kte[:, :n], incl, *odd))
            done = blocks_back(tasks)
            dke = dve = dko = dvo = None
            for b in reversed(range(seq // QB)):
                sl = rows_of(r, seq, b)
                (dv, dk, dqe), (dv2, dk2, dqo), (dv3, dk3, dqo2) = done[:3]
                done = done[3:]
                dvo, dko = add_rows(dvo, dv + dv2), add_rows(dko, dk + dk2)
                dve, dke = add_rows(dve, dv3), add_rows(dke, dk3)
                dqkve_ref[0, sl, ln] = (own_lanes(dqe).T * sc).astype(BF16)
                dqkvo_ref[0, sl, ln] = (own_lanes(dqo + dqo2).T * sc).astype(BF16)
            dqkve_ref[1, all_of, ln] = dke.astype(BF16)
            dqkve_ref[2, all_of, ln] = dve.astype(BF16)
            dqkvo_ref[1, all_of, ln] = dko.astype(BF16)
            dqkvo_ref[2, all_of, ln] = dvo.astype(BF16)

        @pl.when(r == rows - 1)
        def _():
            for start, _ in leave:
                start(group)

        return 0

    lax.fori_loop(0, rows * groups, row, 0)
    for _, wait in late:
        wait()
    da = dot_nt(dqkvo_ref[0], w_ref[0])
    da += dot_nt(dqkvo_ref[1], w_ref[1])
    da += dot_nt(dqkvo_ref[2], w_ref[2])
    da_ref[...] = da
    sums_ref[...] = jnp.zeros_like(sums_ref)

    def finish(i, _):
        sl = pl.ds(pl.multiple_of(i * ROWS_AT_ONCE, ROWS_AT_ONCE), ROWS_AT_ONCE)
        normal, inverse = norm_stats(ho_ref[sl])
        da = da_ref[sl]
        dy = dh1_ref[sl] + norm_back(da, normal, inverse, gb_ref[0:1])
        dy_ref[sl] = dy
        for k, t in enumerate((da * normal, da, dy)):
            sums_ref[k : k + 1] += jnp.sum(t, axis=0, keepdims=True)
        return 0

    lax.fori_loop(0, rows * seq // ROWS_AT_ONCE, finish, 0)
    kept = [moves.whole(dy_ref, dy_far)]
    for g in range(groups):
        for _, wait in leave:
            wait(g)
    for wait in kept:
        wait()


def attend_back(w, incl, strict, qkve, qkvo, o2, lse2, do, dh1, ho, gb):
    rows, seq = incl.shape[0], incl.shape[1]
    n, d = ho.shape
    f = w.shape[2]
    do = do.reshape(2, n, f)
    qkv = sds((3, n, f), BF16)
    near = (w, incl, strict, qkve, qkvo, o2, do, sds((n, d), F32), ho, qkv, qkv, sds((n, d), F32))
    return resident(
        functools.partial(attend_back_body, rows, seq),
        [(t, FAR) for t in (w, incl, strict, qkve, qkvo, o2)]
        + [lse2]
        + [(t, FAR) for t in (do, dh1, ho)]
        + [gb],
        [(qkv, FAR), (qkv, FAR), (sds((n, d), F32), FAR), sds((3, d), F32)],
        scratch=[pltpu.VMEM(t.shape, t.dtype) for t in near + (sds((n, d), F32),)] + [pltpu.SemaphoreType.DMA((64,))],
        flops=6 * n * d * f + 120 * n * seq * f,
        vmem=44,
        name="attend_back",
    )


def attend_back_even_body(
    rows, seq, w_far, incl_far, qkve_far, o1_far, lse1_ref, do1_far, o2_far, lse2_ref, do2_far,
    part_far, dh1_far, dh2_far, x_far, gb_ref,
    dqkv_far, gt_ref, sums_ref,
    w_ref, incl_ref, qkve_ref, o1_ref, do1_ref, o2_ref, do2_ref, part_ref, dh1_ref, dh2_ref, x_ref,
    dqkv_ref, da_ref, sems,
):
    groups = lse1_ref.shape[0]
    moves = Moves(sems)
    even = pl.ds(0, rows * seq)
    arrive = [
        moves.groups(*t)
        for t in (
            (qkve_far, qkve_ref), (o1_far, o1_ref), (do1_far, do1_ref), (o2_far.at[0], o2_ref),
            (do2_far.at[0], do2_ref), (part_far, part_ref),
        )
    ]
    leave = [moves.groups(dqkv_ref, dqkv_far)]
    for start, _ in arrive:
        start(0)
    mask = moves.whole(incl_far, incl_ref)
    for start, _ in arrive:
        start(1)
    late = [
        moves.later(*t)
        for t in ((w_far, w_ref), (dh1_far, dh1_ref), (dh2_far.at[even], dh2_ref), (x_far, x_ref))
    ]
    mask()

    def next_group(group):
        in_turn(arrive, group, groups)

        @pl.when(group == groups - 2)
        def _():
            for start, _ in late:
                start()

    sc = HD**-0.5

    def row(i, _):
        r, group = i % rows, i // rows
        lanes = pl.multiple_of(group * GROUP, GROUP)
        all_of = pl.ds(pl.multiple_of(r * seq, seq), seq)

        @pl.when(r == 0)
        def _():
            next_group(group)

        for p in range(GROUP // (2 * HD)):
            ln = pl.ds(lanes + p * 2 * HD, 2 * HD)
            k, v = qkve_ref[1, all_of, ln], qkve_ref[2, all_of, ln]
            kt = k.T
            tasks = []
            for b in reversed(range(seq // QB)):
                sl, n = rows_of(r, seq, b), (b + 1) * QB
                incl = twice(incl_ref[r, :n, b * QB : n])
                lse1 = pair_row(lse1_ref[group, :, sl], p)
                ratio = jnp.exp(lse1 - pair_row(lse2_ref[0, group, :, sl], p))
                do1, do2 = do1_ref[sl, ln].astype(F32), do2_ref[sl, ln].astype(F32)
                delta = row_products(do1, o1_ref[sl, ln].astype(F32))
                delta += ratio * row_products(do2, o2_ref[sl, ln].astype(F32))
                both = do1 + own_lanes(twice(do2.T), ratio).T
                q, do = cat_heads(qkve_ref[0, sl, ln], sc), cat_heads(both.astype(BF16))
                tasks.append((k[:n], v[:n], kt[:, :n], incl, q, do, lse1, delta))
            dka = dva = None
            for b, (dv, dk, dq) in zip(reversed(range(seq // QB)), blocks_back(tasks)):
                sl = rows_of(r, seq, b)
                dva, dka = add_rows(dva, dv), add_rows(dka, dk)
                dqkv_ref[0, sl, ln] = (own_lanes(dq).T * sc + part_ref[0, sl, ln].astype(F32)).astype(BF16)
            dqkv_ref[1, all_of, ln] = (dka + part_ref[1, all_of, ln].astype(F32)).astype(BF16)
            dqkv_ref[2, all_of, ln] = (dva + part_ref[2, all_of, ln].astype(F32)).astype(BF16)

        @pl.when(r == rows - 1)
        def _():
            for start, _ in leave:
                start(group)

        return 0

    lax.fori_loop(0, rows * groups, row, 0)
    for _, wait in late:
        wait()
    da_ref[...] = jnp.zeros_like(da_ref)

    def project_back(j, _):
        da_ref[...] += dot_nt(dqkv_ref[j], w_ref[j])
        return 0

    lax.fori_loop(0, 3, project_back, 0)
    sums_ref[...] = jnp.zeros_like(sums_ref)

    def finish(i, _):
        sl = pl.ds(pl.multiple_of(i * ROWS_AT_ONCE, ROWS_AT_ONCE), ROWS_AT_ONCE)
        normal, inverse = norm_stats(x_ref[sl].astype(F32))
        da = da_ref[sl]
        sums_ref[0:1] += jnp.sum(da * normal, axis=0, keepdims=True)
        sums_ref[1:2] += jnp.sum(da, axis=0, keepdims=True)
        back = norm_back(da, normal, inverse, gb_ref[0:1])
        gt_ref[sl] = (dh1_ref[sl] + dh2_ref[sl] + back).astype(BF16)
        return 0

    lax.fori_loop(0, rows * seq // ROWS_AT_ONCE, finish, 0)
    for g in range(groups):
        for _, wait in leave:
            wait(g)


def attend_back_even(w, incl, qkve, o1, lse1, do1, o2, lse2, do2, part, dh1, dh2, x, gb):
    rows, seq = incl.shape[0], incl.shape[1]
    n, d = x.shape
    f = w.shape[2]
    qkv, one = sds((3, n, f), BF16), sds((n, f), BF16)
    near = (w, incl, qkv, one, one, one, one, qkv, dh1, dh1, x, qkv, sds((n, d), F32))
    far = lambda *ts: [(t, FAR) for t in ts]
    return resident(
        functools.partial(attend_back_even_body, rows, seq),
        far(w, incl, qkve, o1)
        + [lse1]
        + far(do1, o2)
        + [lse2]
        + far(do2.reshape(2, n, f), part, dh1, dh2, x)
        + [gb],
        [(qkv, FAR), sds((n, d), BF16), sds((2, d), F32)],
        scratch=[pltpu.VMEM(t.shape, t.dtype) for t in near] + [pltpu.SemaphoreType.DMA((64,))],
        flops=6 * n * d * f + 40 * n * seq * f,
        vmem=40,
        name="attend_back_even",
    )


CHUNK = 512
ROWS_AT_ONCE = 256


def chunk_of(ref, j, axis):
    at = pl.ds(pl.multiple_of(j * CHUNK, CHUNK), CHUNK)
    return ref.at[:, at] if axis else ref.at[at]


class Chunks:
    def __init__(self, moves, far, near, axis, ring=False, leave=False):
        self.first = moves.take(far.shape[axis] // CHUNK)
        self.sems, self.far, self.near = moves.sems, far, near
        self.axis, self.ring, self.leave = axis, ring, leave

    def copy(self, j):
        near = self.near.at[j % self.near.shape[0]] if self.ring else chunk_of(self.near, j, self.axis)
        ends = (chunk_of(self.far, j, self.axis), near)
        return pltpu.make_async_copy(*(ends[::-1] if self.leave else ends), self.sems.at[self.first + j])

    def start(self, j):
        self.copy(j).start()

    def wait(self, j):
        self.copy(j).wait()


class Weight:
    def __init__(self, moves, pieces, near, axis):
        self.axis, self.near = axis, near
        self.own = Chunks(moves, pieces[0], near, axis) if pieces[0] is not None else None
        self.number = near.shape[axis] // CHUNK // 2
        self.others, start = [], near.shape[axis] // 2
        for far in pieces[1:]:
            at = pl.ds(start, far.shape[axis])
            self.others.append(moves.later(far, near.at[:, at] if axis else near.at[at]))
            start += far.shape[axis]

    def start_others(self):
        for start, _ in self.others:
            start()

    def wait_others(self):
        for _, wait in self.others:
            wait()


def load_in_turn(j, *weights):
    number = weights[0].number

    @pl.when(j < number)
    def _():
        for w in weights:
            w.own.wait(j)

    @pl.when(j + 2 < number)
    def _():
        for w in weights:
            w.own.start(j + 2)

    @pl.when(j + 2 == number)
    def _():
        for w in weights:
            w.start_others()

    @pl.when(j == number)
    def _():
        for w in weights:
            w.wait_others()


def start_loads(*weights):
    for j in range(2):
        for w in weights:
            w.own.start(j)


def feed_chunk(n2_ref, wup_ref, wdown_ref, j, g_buf, d_buf, ho_ref, gs, ds, first):
    @pl.when(first >= 2)
    def _():
        gs.wait(j - 2)
        ds.wait(j - 2)

    half = n2_ref.shape[0] // 2
    parts = []
    for sl in (slice(0, half), slice(half, 2 * half)):
        g, d = gelu_parts(dot(n2_ref[sl], chunk_of(wup_ref, j, 1)[...]))
        parts.append(g.astype(BF16))
        g_buf[j % 2, sl] = parts[-1]
        d_buf[j % 2, sl] = d.astype(BF16)
    gs.start(j)
    ds.start(j)
    for i, g in enumerate(parts):
        ho_ref[i * half : (i + 1) * half] += dot(g, chunk_of(wdown_ref, j, 0)[...])


def start_norm(x_ref, h1_ref, n2_ref, gb_ref, ho_ref=None, normal_ref=None, inverse_ref=None):
    def part(k, _):
        sl = pl.ds(pl.multiple_of(k * ROWS_AT_ONCE, ROWS_AT_ONCE), ROWS_AT_ONCE)
        h1 = x_ref[sl].astype(F32) + h1_ref[sl]
        h1_ref[sl] = h1
        normal, inverse = norm_stats(h1)
        n2_ref[sl] = (normal * gb_ref[1:2] + gb_ref[3:4]).astype(BF16)
        if ho_ref is not None:
            ho_ref[sl] = h1 + gb_ref[4:5]
        if normal_ref is not None:
            normal_ref[sl] = normal
            inverse_ref[sl] = jnp.broadcast_to(inverse, (ROWS_AT_ONCE, inverse_ref.shape[1]))
        return 0

    lax.fori_loop(0, h1_ref.shape[0] // ROWS_AT_ONCE, part, 0)


def weave(seq):
    i = lax.broadcasted_iota(jnp.int32, (2 * seq, 2 * seq), 0)
    k = lax.broadcasted_iota(jnp.int32, (2 * seq, 2 * seq), 1)
    place = jnp.where(k < seq, 2 * k, 2 * (k - seq) + 1)
    return jnp.where(i == place, 1.0, 0.0).astype(BF16)


def mlp_own_body(
    x_far, o_far, wout_far, gb_ref, wup_far, wdown_far, cot_far,
    h1_far, n2_far, g_far, d_far, ho_far, dm_far,
    x_ref, o_ref, wout_ref, wup_ref, wdown_ref, h1_ref, n2_ref, ho_ref, cot_ref, dm_ref, g_buf, d_buf, sems,
):
    moves = Moves(sems)
    first = [moves.whole(*t) for t in ((o_far, o_ref), (wout_far, wout_ref), (x_far, x_ref))]
    ups, downs = Chunks(moves, wup_far, wup_ref, 1), Chunks(moves, wdown_far, wdown_ref, 0)
    gs, ds = (Chunks(moves, f, b, 1, True, True) for f, b in ((g_far, g_buf), (d_far, d_buf)))
    number = wup_far.shape[1] // CHUNK
    for wait in first:
        wait()
    for j in range(number):
        ups.start(j)
        downs.start(j)
    cot_there = moves.whole(cot_far, cot_ref)
    h1_ref[...] = dot(o_ref[...], wout_ref[...])
    start_norm(x_ref, h1_ref, n2_ref, gb_ref, ho_ref)
    kept = [moves.whole(*t) for t in ((h1_ref, h1_far), (n2_ref, n2_far))]

    def step(j, _):
        ups.wait(j)
        downs.wait(j)
        feed_chunk(n2_ref, wup_ref, wdown_ref, j, g_buf, d_buf, ho_ref, gs, ds, j)
        return 0

    lax.fori_loop(0, number, step, 0)
    kept.append(moves.whole(ho_ref, ho_far))
    cot_there()
    rows, seq = cot_ref.shape[0], cot_ref.shape[1] // 2
    mix = weave(seq)
    for r in range(rows):
        parted = dot_tn(mix, cot_ref[r]).astype(BF16)
        for i in range(2):
            at = (i * rows + r) * seq
            dm_ref[at : at + seq] = parted[i * seq : (i + 1) * seq]
    kept.append(moves.whole(dm_ref, dm_far))
    for wait in kept:
        wait()
    for j in range(number - 2, number):
        gs.wait(j)
        ds.wait(j)


def mlp_other_body(number_up, number_down, n2_far, part_far, g_in, d_in, gb_ref, *refs):
    ups_far, refs = refs[:number_up], refs[number_up:]
    downs_far, refs = refs[:number_down], refs[number_down:]
    g_far, d_far, ho_far, ao_far, n2_ref, wup_ref, wdown_ref, ho_ref, ao_ref, g_buf, d_buf, sems = refs
    moves = Moves(sems)
    up = Weight(moves, (None,) + ups_far, wup_ref, 1)
    down = Weight(moves, (None,) + downs_far, wdown_ref, 0)
    gs, ds = (Chunks(moves, f, b, 1, True, True) for f, b in ((g_far, g_buf), (d_far, d_buf)))
    n2_there = moves.whole(n2_far, n2_ref)
    up.start_others()
    down.start_others()
    part_there = moves.whole(part_far, ho_ref)
    number, half = up.number, n2_ref.shape[0] // 2
    n2_there()
    up.wait_others()

    def rise(i, _):
        j = number + i
        for sl in (slice(0, half), slice(half, 2 * half)):
            g, d = gelu_parts(dot(n2_ref[sl], chunk_of(wup_ref, j, 1)[...]))
            g_buf[j % number, sl] = g.astype(BF16)
            d_buf[j % number, sl] = d.astype(BF16)
        gs.start(j)
        ds.start(j)
        return 0

    lax.fori_loop(0, number, rise, 0)
    down.wait_others()
    part_there()

    def fall(i, _):
        j = number + i
        ho_ref[...] += dot(g_buf[j % number], chunk_of(wdown_ref, j, 0)[...])
        return 0

    lax.fori_loop(0, number, fall, 0)
    sent = moves.whole(ho_ref, ho_far)

    def norm(k, _):
        sl = pl.ds(pl.multiple_of(k * ROWS_AT_ONCE, ROWS_AT_ONCE), ROWS_AT_ONCE)
        normal, _ = norm_stats(ho_ref[sl])
        ao_ref[sl] = (normal * gb_ref[0:1] + gb_ref[2:3]).astype(BF16)
        return 0

    lax.fori_loop(0, ho_ref.shape[0] // ROWS_AT_ONCE, norm, 0)
    moves.whole(ao_ref, ao_far)()
    sent()
    for j in range(number, 2 * number):
        gs.wait(j)
        ds.wait(j)


def near_of(*arrays):
    return [pltpu.VMEM(t.shape, t.dtype) for t in arrays]


def far_of(*arrays):
    return [(t, FAR) for t in arrays]


def mlp_own(x, o, wout, gb, wup, wdown, cot):
    n, d = x.shape
    ff = 2 * wup.shape[1]
    h1, low, wide = sds((n, d), F32), sds((n, d), BF16), sds((n, ff), BF16)
    return resident(
        mlp_own_body,
        far_of(x, o, wout) + [gb] + far_of(wup, wdown, cot),
        far_of(h1, low, wide, wide, h1, sds((2 * n, d), BF16)),
        scratch=near_of(x, o, wout, wup, wdown, h1, low, h1, cot, sds((2 * n, d), BF16))
        + [pltpu.VMEM((2, n, CHUNK), BF16)] * 2
        + [pltpu.SemaphoreType.DMA((40,))],
        vmem=44,
        name="mlp_own",
    )


def mlp_other(n2, part, g, dgelu, gb, ups, downs):
    n, d = n2.shape
    ff = g.shape[1]
    return resident(
        functools.partial(mlp_other_body, len(ups), len(downs)),
        far_of(n2, part, g, dgelu) + [gb] + far_of(*ups, *downs),
        far_of(sds(g.shape, BF16), sds(g.shape, BF16), sds(part.shape, F32), sds(n2.shape, BF16)),
        scratch=near_of(n2, sds((d, ff), BF16), sds((ff, d), BF16), part, n2)
        + [pltpu.VMEM((ff // CHUNK // 2, n, CHUNK), BF16)] * 2
        + [pltpu.SemaphoreType.DMA((40,))],
        vmem=40,
        aliases={2: 0, 3: 1},
        name="mlp_other",
    )


def after_norm_back(
    moves, size, h1_ref, dn_ref, db_ref, wout_ref, gb_ref, sums_ref, dp_ref, do_ref, dh1_far, dp_far, do_far,
    inverse_ref=None,
):
    gain_sum = jnp.zeros_like(gb_ref[0:1])
    bias_sum = jnp.zeros_like(gb_ref[0:1])
    waits = []
    for i in range(h1_ref.shape[0] // size):
        sl = slice(i * size, (i + 1) * size)
        if inverse_ref is None:
            normal, inverse = norm_stats(h1_ref[sl])
        else:
            normal, inverse = h1_ref[sl], inverse_ref[sl, :1]
        dn = dn_ref[sl]
        gain_sum += jnp.sum(dn * normal, axis=0, keepdims=True)
        bias_sum += jnp.sum(dn, axis=0, keepdims=True)
        dh1 = db_ref[sl].astype(F32) + norm_back(dn, normal, inverse, gb_ref[1:2])
        dn_ref[sl] = dh1
        dp_ref[sl] = dh1.astype(BF16)
        at = pl.ds(i * size, size)
        waits += [moves.whole(a.at[at], b.at[at]) for a, b in ((dn_ref, dh1_far), (dp_ref, dp_far))]
        if i % 2:
            both = pl.ds((i - 1) * size, 2 * size)
            do_ref[both] = dot_nt(dp_ref[both], wout_ref[...]).astype(BF16)
            waits.append(moves.whole(do_ref.at[both], do_far.at[both]))
    sums_ref[0:1] = gain_sum
    sums_ref[1:2] = bias_sum
    return waits


def mlp_second_body(rows, seq, number_up, number_down, x_far, ho_far, o_far, dm_far, wout_far, gb_ref, *refs):
    mlp_second_work(rows, seq, x_far, ho_far, o_far, dm_far, wout_far, gb_ref, *in_pieces(refs, number_up, number_down))


def in_pieces(refs, *numbers):
    out = []
    for k in numbers:
        out.append(refs[:k])
        refs = refs[k:]
    return out + list(refs)


def mlp_second_work(
    rows, seq, x_far, ho_far, o_far, dm_far, wout_far, gb_ref, ups_far, downs_far,
    outs_far, outs2_far, n2_far, g_far, du_far, dh1_far, dp_far, do_far, sums_ref,
    x_ref, ho_ref, o_ref, cot_ref, wout_ref, wup_ref, wdown_ref, n2_ref, dm_ref,
    normal_ref, z_ref, dn_ref, dp_ref, do_ref, inverse_ref, g_buf, du_buf, sems,
):
    n = rows * seq
    moves = Moves(sems)
    halves = (slice(0, n), slice(n, 2 * n))
    first = [moves.whole(*t) for t in ((o_far.at[0], o_ref.at[0]), (wout_far, wout_ref))]
    up, down = Weight(moves, ups_far, wup_ref, 1), Weight(moves, downs_far, wdown_ref, 0)
    gs, dus = (Chunks(moves, f, b, 1, True, True) for f, b in ((g_far, g_buf), (du_far, du_buf)))
    number = 2 * up.number
    for wait in first:
        wait()
    x_there = moves.whole(x_far, x_ref)
    then = [moves.whole(*t) for t in ((o_far.at[1], o_ref.at[1]), (ho_far, ho_ref))]
    start_loads(up, down)
    dm_there = moves.whole(dm_far, dm_ref)
    for i, sl in enumerate(halves):
        if i:
            for wait in then:
                wait()
        z_ref[sl] = dot(o_ref[i], wout_ref[...])
        if i == 0:
            x_there()
        z_at, n2_at, normal_at, inverse_at = (t.at[pl.ds(i * n, n)] for t in (z_ref, n2_ref, normal_ref, inverse_ref))
        start_norm(x_ref if i == 0 else ho_ref, z_at, n2_at, gb_ref, None, normal_at, inverse_at)
    dm_there()
    mix = weave(seq)
    kept = [moves.whole(n2_ref, n2_far)]
    dn_ref[...] = jnp.zeros_like(dn_ref)

    def step(j, _):
        load_in_turn(j, up, down)

        @pl.when(j >= 2)
        def _():
            gs.wait(j - 2)
            dus.wait(j - 2)

        for sl in (slice(0, 2 * n),):
            u = dot(n2_ref[sl], chunk_of(wup_ref, j, 1)[...])
            dg = dot_nt(dm_ref[sl], chunk_of(wdown_ref, j, 0)[...])
            g, d = gelu_parts(u)
            g = g.astype(BF16)
            du = (dg * d).astype(BF16)
            g_buf[j % 2, sl] = g
            du_buf[j % 2, sl] = du
            z_ref[sl] += dot(g, chunk_of(wdown_ref, j, 0)[...])
            dn_ref[sl] += dot_nt(du, chunk_of(wup_ref, j, 1)[...])
        gs.start(j)
        dus.start(j)
        return 0

    lax.fori_loop(0, number, step, 0)
    for r in range(rows):
        pair = [slice(i * n + r * seq, i * n + (r + 1) * seq) for i in range(2)]
        z = jnp.concatenate([z_ref[s].astype(BF16) for s in pair], axis=0)
        cot_ref[r] = dot(mix, z).astype(BF16)
    half = rows // 2
    kept += [moves.whole(cot_ref.at[pl.ds(i * half, half)], far) for i, far in enumerate((outs_far, outs2_far))]
    kept += after_norm_back(
        moves, seq, normal_ref, dn_ref, dm_ref, wout_ref, gb_ref, sums_ref, dp_ref, do_ref, dh1_far, dp_far, do_far,
        inverse_ref,
    )
    for wait in kept:
        wait()
    for j in range(number - 2, number):
        gs.wait(j)
        dus.wait(j)


def mlp_second(x, ho, o2, dm, wout, gb, ups, downs, seq):
    n, d = x.shape
    ff = 2 * ups[0].shape[1]
    rows = n // seq
    low, wide, full = sds((2 * n, d), BF16), sds((2 * n, ff), BF16), sds((2 * n, d), F32)
    out = sds((rows // 2, 2 * seq, d), BF16)
    return resident(
        functools.partial(mlp_second_body, rows, seq, len(ups), len(downs)),
        far_of(x, ho, o2, dm, wout) + [gb] + far_of(*ups, *downs),
        far_of(out, out, low, wide, wide, full, low, low) + [sds((2, d), F32)],
        scratch=near_of(x, ho, o2, sds((rows, 2 * seq, d), BF16), wout, sds((d, ff), BF16), sds((ff, d), BF16), low, low, full, full, full, low, low, sds((2 * n, 128), F32))
        + [pltpu.VMEM((2, 2 * n, CHUNK), BF16)] * 2
        + [pltpu.SemaphoreType.DMA((64,))],
        vmem=60,
        name="mlp_second",
    )


def mlp_back_body(rows, seq, number_up, number_down, dy_far, h1_far, wout_far, gb_ref, d_far, *refs):
    mlp_back_work(rows, seq, dy_far, h1_far, wout_far, gb_ref, d_far, *in_pieces(refs, number_up, number_down))


def mlp_back_work(
    rows, seq, dy_far, h1_far, wout_far, gb_ref, d_far, ups_far, downs_far,
    du_far, dh1_far, dp_far, do_far, sums_ref,
    dy_ref, h1_ref, wout_ref, wup_ref, wdown_ref, d_ref, dm_ref, dn_ref, dp_ref, do_ref, du_buf, sems,
):
    moves = Moves(sems)
    first = moves.whole(dy_far, dy_ref)
    up, down = Weight(moves, ups_far, wup_ref, 1), Weight(moves, downs_far, wdown_ref, 0)
    ds, dus = Chunks(moves, d_far, d_ref, 1), Chunks(moves, du_far, du_buf, 1, True, True)
    number = 2 * up.number
    start_loads(down, up)
    for j in range(2):
        ds.start(j)
    then = [moves.later(*t) for t in ((wout_far, wout_ref), (h1_far, h1_ref))]
    first()
    dm_ref[...] = dy_ref[...].astype(BF16)
    dn_ref[...] = jnp.zeros_like(dn_ref)

    def step(j, _):
        load_in_turn(j, down, up)
        ds.wait(j)

        @pl.when(j + 2 < number)
        def _():
            ds.start(j + 2)

        @pl.when(j + 2 == number)
        def _():
            for start, _ in then:
                start()

        @pl.when(j >= 2)
        def _():
            dus.wait(j - 2)

        dg = dot_nt(dm_ref[...], chunk_of(wdown_ref, j, 0)[...])
        du = (dg * chunk_of(d_ref, j, 1)[...].astype(F32)).astype(BF16)
        du_buf[j % 2] = du
        dus.start(j)
        dn_ref[...] += dot_nt(du, chunk_of(wup_ref, j, 1)[...])
        return 0

    lax.fori_loop(0, number, step, 0)
    for _, wait in then:
        wait()
    kept = after_norm_back(
        moves, seq, h1_ref, dn_ref, dy_ref, wout_ref, gb_ref, sums_ref, dp_ref, do_ref, dh1_far, dp_far, do_far
    )
    for wait in kept:
        wait()
    for j in range(number - 2, number):
        dus.wait(j)


def mlp_back(dy, h1, wout, gb, dgelu, ups, downs, seq):
    n, d = dy.shape
    ff = dgelu.shape[1]
    low = sds((n, d), BF16)
    return resident(
        functools.partial(mlp_back_body, n // seq, seq, len(ups), len(downs)),
        far_of(dy, h1, wout) + [gb] + far_of(dgelu, *ups, *downs),
        far_of(dgelu, h1, low, low) + [sds((2, d), F32)],
        scratch=near_of(dy, h1, wout, sds((d, ff), BF16), sds((ff, d), BF16), dgelu, low, dy, low, low)
        + [pltpu.VMEM((2, n, CHUNK), BF16)]
        + [pltpu.SemaphoreType.DMA((48,))],
        vmem=48,
        name="mlp_back",
    )


def lanes_at(ref, start, size):
    return ref.at[:, pl.ds(pl.multiple_of(start, 128), size)]


def stack_rows(moves, pairs, target, start, size):
    copies, row = [], 0
    for far in pairs:
        copies.append(moves.later(lanes_at(far, start, size), target.at[pl.ds(row, far.shape[0])]))
        row += far.shape[0]
    return (lambda: [s() for s, _ in copies]), (lambda: [w() for _, w in copies])


def all_of(*parts):
    return (lambda: [s() for s, _ in parts]), (lambda: [w() for _, w in parts])


class InTurn:
    def __init__(self, *tiles):
        self.tiles, self.at = tiles, 0
        for start, _ in tiles[:2]:
            start()

    def next(self):
        self.tiles[self.at][1]()
        self.at += 1
        if self.at + 1 < len(self.tiles):
            self.tiles[self.at + 1][0]()


def place_of(quarter, y, me_ref):
    return quarter if y else 4 + (quarter ^ me_ref[1])


def packed(body, me, arrays, shape, scratch, flops, vmem, name):
    smem = pl.BlockSpec(memory_space=pltpu.SMEM)
    out = sds(shape, BF16)
    return resident(
        body,
        [(me, smem)] + far_of(*arrays),
        far_of(out, out),
        scratch=near_of(sds((2,) + shape, BF16)) + scratch + [pltpu.SemaphoreType.DMA((64,))],
        flops=flops,
        vmem=vmem,
        name=name,
    )


def grad_down_body(
    me_ref, g1_far, g2_far, dy_far, dm2_far, keep_far, go_far, out_ref, dy_ref, dm_ref, g_ref, acc_ref, sems
):
    low, group = me_ref[0] % 4, (me_ref[0] // 4) % 2
    ring, n, b = g_ref.shape[0], g1_far.shape[0], g_ref.shape[2]
    moves = Moves(sems)
    first, last = moves.take(2 * ring), moves.take(4)

    def tile(i):
        side, y, h = 1 - i // 4, (i // 2) % 2, i % 2
        quarter = ((me_ref[0] // 8) ^ side) * 2 + h
        at = jnp.where(y == 0, 4 + (quarter ^ me_ref[1]), quarter) * b
        return side, y, h, at

    def loads(i):
        at, slot = tile(i)[3], i % ring
        near = g_ref.at[slot]
        ends = ((g1_far, near.at[pl.ds(0, n)]), (g2_far, near.at[pl.ds(n, 2 * n)]))
        return [pltpu.make_async_copy(lanes_at(f, at, b), t, sems.at[first + 2 * slot + k]) for k, (f, t) in enumerate(ends)]

    def store(far, side, y):
        return pltpu.make_async_copy(out_ref.at[side, y], far.at[y], sems.at[last + side * 2 + y])

    ready = [moves.whole(dy_far, dy_ref), moves.whole(dm2_far, dm_ref.at[pl.ds(n, 2 * n)])]
    for i in range(2):
        for c in loads(i):
            c.start()
    for wait in ready:
        wait()
    dm_ref[:n] = dy_ref[...].astype(BF16)

    def step(i, _):
        side, y, h, _ = tile(i)
        for c in loads(i):
            c.wait()

        @pl.when(i + 2 < 8)
        def _():
            for c in loads(i + 2):
                c.start()

        acc_ref[...] = dot_tn(g_ref[i % ring], dm_ref[...]).reshape(acc_ref.shape)
        for s in range(4):
            out_ref[side, y, (h ^ group) * 4 + s] = acc_ref[s ^ low].astype(BF16)

        @pl.when((h == 1) & (side == 1))
        def _():
            store(go_far, 1, y).start()

        @pl.when((h == 1) & (side == 0))
        def _():
            store(keep_far, 0, y).start()

        return 0

    lax.fori_loop(0, 8, step, 0)
    for y in range(2):
        store(go_far, 1, y).wait()
        store(keep_far, 0, y).wait()


def grad_down(me, g1, g2, dy, dm2):
    n, d = dy.shape
    ff = g1.shape[1]
    b = ff // 8
    return packed(
        grad_down_body,
        me,
        (g1, g2, dy, dm2),
        (2, 8, b // 4, d),
        [
            pltpu.VMEM((n, d), F32),
            pltpu.VMEM((3 * n, d), BF16),
            pltpu.VMEM((3, 3 * n, b), BF16),
            pltpu.VMEM((4, b // 4, d), F32),
        ],
        2 * 3 * n * d * ff,
        40,
        "grad_down",
    )


CUT = 768
CUT_BACK = 1536


def swapped(s):
    return ((s >> 1) % 2) * 4 + ((s >> 2) % 2) * 2 + s % 2


def put_slots(out_ref, y, lanes, acc_ref, me):
    for s in range(16):
        out_ref[s // 8, y, s % 8, :, lanes] = acc_ref[s ^ me].astype(BF16)


def grad_up_body(
    me_ref, n1_far, n2_far, du1_far, du2_far, dp1_far, dp2_far, o1_far, o2_far, keep_far, go_far,
    out_ref, n_ref, t_ref, du_ref, dp_ref, o_ref, acc_ref, acc2_ref, sems,
):
    moves = Moves(sems)
    d, f = n_ref.shape[1], o_ref.shape[2]
    ring, c, n = du_ref.shape[0], du_ref.shape[2], du1_far.shape[0]
    first, last = moves.take(4 * ring), moves.take(4)

    def loads(i):
        y, t, slot = i // 2, i % 2, i % ring
        copies = []
        for k in range(2):
            quarter = 2 * t + k
            at = jnp.where(y == 0, 4 + (quarter ^ me_ref[1]), quarter) * f
            near = lanes_at(du_ref.at[slot], k * f, f)
            for far, rows in ((du1_far, pl.ds(0, n)), (du2_far, pl.ds(n, 2 * n))):
                copies.append((lanes_at(far, at, f), near.at[rows]))
        return [pltpu.make_async_copy(a, b, sems.at[first + 4 * slot + k]) for k, (a, b) in enumerate(copies)]

    def stores(y):
        return [
            pltpu.make_async_copy(out_ref.at[i, y], far.at[y], sems.at[last + 2 * y + i])
            for i, far in enumerate((keep_far, go_far))
        ]

    ready = stack_rows(moves, (n1_far, n2_far), n_ref, 0, d)
    ready[0]()
    for c0 in loads(0):
        c0.start()
    out_loads = [stack_rows(moves, (dp1_far, dp2_far), dp_ref, 0, d)]
    out_loads += [stack_rows(moves, (o1_far, o2_far), o_ref.at[y], (1 - y) * f, f) for y in range(2)]
    ready[1]()
    for c0 in loads(1):
        c0.start()
    t_ref[...] = n_ref[...].T

    def step(i, _):
        y, t = i // 2, i % 2
        for c0 in loads(i):
            c0.wait()

        @pl.when(i + 2 < 4)
        def _():
            for c0 in loads(i + 2):
                c0.start()

        @pl.when(i == 0)
        def _():
            for start, _ in out_loads:
                start()

        acc_ref[...] = dot(t_ref[...], du_ref[i % ring]).reshape(acc_ref.shape)
        put_slots(out_ref, y, pl.ds(pl.multiple_of(t * c, c), c), acc_ref, jnp.where(t == 0, me_ref[0], me_ref[2]))

        @pl.when(i == 1)
        def _():
            for _, wait in out_loads:
                wait()

        @pl.when(t == 1)
        def _():
            acc2_ref[...] = dot_tn(dp_ref[...], o_ref[y]).reshape(acc2_ref.shape)
            put_slots(out_ref, y, slice(2 * c, 2 * c + f), acc2_ref, me_ref[2])
            for s in stores(y):
                s.start()

        return 0

    lax.fori_loop(0, 4, step, 0)
    for y in range(2):
        for s in stores(y):
            s.wait()


def grad_up(me, n1, n2, du1, du2, dp1, dp2, o1, o2):
    n, d = n1.shape
    ff = du1.shape[1]
    f, c = o1.shape[1] // 2, ff // 4
    return packed(
        grad_up_body,
        me,
        (n1, n2, du1, du2, dp1, dp2, o1, o2),
        (2, 8, d // 16, 2 * c + f),
        [
            pltpu.VMEM((3 * n, d), BF16),
            pltpu.VMEM((d, 3 * n), BF16),
            pltpu.VMEM((3, 3 * n, c), BF16),
            pltpu.VMEM((3 * n, d), BF16),
            pltpu.VMEM((2, 3 * n, f), BF16),
            pltpu.VMEM((16, d // 16, c), F32),
            pltpu.VMEM((16, d // 16, f), F32),
        ],
        2 * 3 * n * d * (ff + d),
        56,
        "grad_up",
    )


def grad_qkv_body(me_ref, ae_far, ao_far, de_far, do_far, keep_far, go_far, out_ref, a_ref, t_ref, d_ref, acc_ref, sems):
    moves = Moves(sems)
    d = a_ref.shape[1]
    f = de_far.shape[2] // 2
    ready = stack_rows(moves, (ae_far, ao_far), a_ref, 0, d)
    n, first = ae_far.shape[0], moves.take(6)

    def loads(j):
        return [
            pltpu.make_async_copy(far.at[j], d_ref.at[j, pl.ds(k * n, n)], sems.at[first + 2 * j + k])
            for k, far in enumerate((de_far, do_far))
        ]

    ready[0]()
    for c in loads(0):
        c.start()
    ready[1]()
    for j in (1, 2):
        for c in loads(j):
            c.start()
    t_ref[...] = a_ref[...].T

    def step(j, _):
        for c in loads(j):
            c.wait()
        acc_ref[...] = dot(t_ref[...], d_ref[j]).reshape(acc_ref.shape)
        lanes = pl.ds(pl.multiple_of(j * f, f), f)
        for s in range(16):
            block = acc_ref[s ^ me_ref[0]].astype(BF16)
            out_ref[s // 8, 1, s % 8, :, lanes] = block[:, :f]
            out_ref[s // 8, 0, s % 8, :, lanes] = block[:, f:]
        return 0

    lax.fori_loop(0, 3, step, 0)
    sent = [moves.whole(out_ref.at[i], far) for i, far in ((1, go_far), (0, keep_far))]
    for wait in sent:
        wait()


def grad_qkv(me, ae, ao, dqkv_e, dqkv_o):
    n, d = ae.shape
    f = dqkv_e.shape[2] // 2
    return packed(
        grad_qkv_body,
        me,
        (ae, ao, dqkv_e, dqkv_o),
        (2, 8, d // 16, 3 * f),
        [
            pltpu.VMEM((2 * n, d), BF16),
            pltpu.VMEM((d, 2 * n), BF16),
            pltpu.VMEM((3, 2 * n, 2 * f), BF16),
            pltpu.VMEM((16, d // 16, 2 * f), F32),
        ],
        2 * 2 * 3 * n * d * 2 * f,
        40,
        "grad_qkv",
    )


def packed_call(body, grid, me, ins, outs, scratch=(), flops=0, aliases={}, name=None):
    return pl.pallas_call(
        body,
        grid_spec=pltpu.PrefetchScalarGridSpec(
            num_scalar_prefetch=1,
            grid=grid,
            in_specs=[s for _, s in ins],
            out_specs=[s for _, s in outs],
            scratch_shapes=scratch,
        ),
        out_shape=[a for a, _ in outs],
        input_output_aliases=aliases,
        compiler_params=pltpu.CompilerParams(
            dimension_semantics=("arbitrary",) * len(grid), vmem_limit_bytes=VMEM_LIMIT
        ),
        cost_estimate=pl.CostEstimate(flops=int(flops) // 16, bytes_accessed=0, transcendentals=0),
        name=name,
    )(me, *[a for a, _ in ins])


def unpack_down_body(me_ref, part_ref, *refs):
    low, rows = me_ref[0] % 8, part_ref.shape[1]
    for b in range(8):
        refs[-1][b * rows : (b + 1) * rows] = part_ref[swapped(b ^ low)].astype(F32)


def unpack_down(me, side, part, into=()):
    _, r, w = part.shape
    half = 8 * r
    at = lambda me: (me[0] // 8) ^ side
    ins = [(part, pl.BlockSpec(part.shape, lambda i, me: (0, 0, 0)))]
    ins += [(t, pl.BlockSpec(memory_space=pl.ANY)) for t in into]
    return packed_call(
        unpack_down_body,
        (1,),
        me,
        ins,
        [(sds((2 * half, w), F32), pl.BlockSpec((half, w), lambda i, me: (at(me), 0)))],
        aliases={2 + i: i for i in range(len(into))},
        name="unpack_down",
    )[0]


def unpack_rest_body(side, me_ref, part_ref, *refs):
    up_far, out_far, qkv_far, up_st, wide, out_st, qkv_st, sems = refs[-8:]
    moves = Moves(sems)
    left, right = me_ref[0] % 8, me_ref[2] % 8
    rows, half = part_ref.shape[1], 8 * part_ref.shape[1]
    d, f = up_st.shape[1], wide.shape[1]
    base = ((me_ref[0] // 8) ^ side) * half
    sent = []
    for b in range(8):
        sl = slice(b * rows, (b + 1) * rows)
        up_st[sl, :CUT] = part_ref[b ^ left, :, :CUT].astype(F32)
        up_st[sl, CUT:] = part_ref[swapped(b ^ right), :, CUT:d].astype(F32)
        wide[sl] = part_ref[b ^ right, :, d : d + f].astype(F32)
        if b % 4 == 3:
            start, size = (b - 3) * rows, 4 * rows
            at = pl.ds(pl.multiple_of(base + start, 8), size)
            sent.append(moves.whole(up_st.at[pl.ds(start, size)], up_far.at[at]))
    out_st[...] = wide[...].T
    sent.append(moves.whole(out_st, lanes_at(out_far, base, half)))
    for j in range(3):
        for b in range(8):
            sl = slice(b * rows, (b + 1) * rows)
            qkv_st[j, sl] = part_ref[b ^ right, :, d + (j + 1) * f : d + (j + 2) * f].astype(F32)
        sent.append(moves.whole(qkv_st.at[j], qkv_far.at[j, pl.ds(pl.multiple_of(base, 8), half)]))
    for wait in sent:
        wait()


def unpack_rest(me, side, part, into=()):
    _, r, w = part.shape
    half = 8 * r
    d, f = CUT_BACK, (w - CUT_BACK) // 4
    smem = pl.BlockSpec(memory_space=pltpu.SMEM)
    outs = [sds((2 * half, d), F32), sds((f, 2 * half), F32), sds((3, 2 * half, f), F32)]
    stages = [sds((half, d), F32), sds((half, f), F32), sds((f, half), F32), sds((3, half, f), F32)]
    return resident(
        functools.partial(unpack_rest_body, side),
        [(me, smem), part] + far_of(*into),
        far_of(*outs),
        scratch=near_of(*stages) + [pltpu.SemaphoreType.DMA((8,))],
        vmem=24,
        aliases={2 + i: i for i in range(len(into))},
        name="unpack_rest",
    )


def fold(*parts):
    return sum(p.astype(F32) for p in parts).astype(BF16)


def after(value, *first):
    return lax.optimization_barrier((value, first))[0]


class Chunk:
    def __init__(self, keep, got):
        self.keep, self.got = keep, got
        self.sent = None

    def wait(self, *also):
        self.got, also = lax.optimization_barrier((self.got, also))
        return also

    def to_partner(self):
        total = fold(self.keep, self.got)
        self.keep, self.sent = total[1], total[0]
        self.got = lax.ppermute(self.sent, "tensor", FLIP)

    def gather_core(self):
        self.got = lax.ppermute(self.keep, "core", FLIP)


def add(k, g):
    return (k.astype(F32) + g.astype(F32)).astype(BF16)


def phase_shapes(mode, parts):
    shapes = [p[0].shape for p in parts]
    s = shapes[0]
    if mode == "half":
        out = s[:-3] + (s[-3] // 2,) + s[-2:]
        return [out, out]
    if mode == "partner":
        return [s[1:], s[1:]]
    if mode == "last":
        out = (s[0] // 2, s[1], sum(t[2] for t in shapes))
        return [out, out]
    if mode == "sum":
        return [s]
    if mode == "split":
        return [(2 * s[0], s[1], CUT_BACK), (2 * s[0], s[1], s[2] - CUT_BACK)]
    return [(2 * s[0], s[1], sum(t[2] for t in shapes))]


def phase_part(mode, parts, outs):
    if mode == "half":
        (k, g), n = parts[0], outs[0].shape[-3]
        lead = (slice(None),) * (len(k.shape) - 3)
        for i, out in enumerate(outs):
            at = lead + (slice(i * n, (i + 1) * n),)
            out[...] = add(k[at], g[at])
    elif mode == "partner":
        k, g = parts[0]
        for i, out in zip((1, 0), outs):
            out[...] = add(k[i], g[i])
    elif mode == "last":
        n, lane = outs[0].shape[0], 0
        for k, g in parts:
            for i, out in enumerate(outs):
                at = slice(i * n, (i + 1) * n)
                out[:, :, lane : lane + k.shape[2]] = add(k[at], g[at])
            lane += k.shape[2]
    elif mode == "sum":
        outs[0][...] = add(parts[0][0][...], parts[0][1][...])
    elif mode == "split":
        for i, ref in enumerate(parts[0]):
            at = slice(i * ref.shape[0], (i + 1) * ref.shape[0])
            outs[0][at] = ref[:, :, :CUT_BACK]
            outs[1][at] = ref[:, :, CUT_BACK:]
    else:
        lane = 0
        for pair in parts:
            for i, ref in enumerate(pair):
                outs[0][i * ref.shape[0] : (i + 1) * ref.shape[0], :, lane : lane + ref.shape[2]] = ref[...]
            lane += pair[0].shape[2]


def phase(*items):
    shapes = [phase_shapes(*t) for t in items]

    def body(*refs):
        at = sum(2 * len(parts) for _, parts in items)
        ins, outs = list(refs[:at]), list(refs[at:])
        for (mode, parts), made in zip(items, shapes):
            mine = [(ins.pop(0), ins.pop(0)) for _ in parts]
            phase_part(mode, mine, [outs.pop(0) for _ in made])

    flat = resident(
        body,
        [t for _, parts in items for pair in parts for t in pair],
        [sds(s, BF16) for made in shapes for s in made],
        vmem=16,
        name="phase",
    )
    flat = list(flat)
    return [[flat.pop(0) for _ in made] for made in shapes]


class Hops(Chunk):
    def __init__(self, outer, keep, got):
        super().__init__(keep, got)
        self.axes = {"x": ("x", 2, 1), "z": ("o", outer, 1), "w": ("o", outer, 2)}
        self.extra = [("o", outer, 1 << b) for b in range(2, outer.bit_length() - 1)]

    def over(self, way, t):
        return lax.ppermute(t, "tensor", FLIP) if way == "partner" else flip_bit(t, *self.axes[way])

    def send(self, *parts):
        self.keep, self.sent, self.got = [], [], []
        for total, way in parts:
            if way == "partner":
                keep, sent = total[1], total[0]
            else:
                half = total.shape[-3] // 2
                keep, sent = total[..., :half, :, :], total[..., half:, :, :]
            self.keep.append(keep)
            self.sent.append(sent)
            self.got.append(self.over(way, sent))

    def fold_first(self):
        total = fold(self.keep, self.got)
        half = total.shape[1] // 2
        return [part for lanes in (total[..., :CUT], total[..., CUT:]) for part in (lanes[:, :half], lanes[:, half:])]

    def first(self, parts):
        self.keep, self.sent = [parts[0], parts[2]], [parts[1], parts[3]]
        self.got = [self.over("x", parts[1]), self.over("z", parts[3])]

    def first_hop(self, way):
        self.send((fold(self.keep, self.got), way))

    def parts(self):
        return list(zip(self.keep, self.got))

    def hop(self, *ways):
        items = [("partner" if w == "partner" else "half", [p]) for w, p in zip(ways, self.parts())]

        def then(made):
            self.keep, self.sent = [m[0] for m in made], [m[1] for m in made]
            self.got = [self.over(w, s) for w, s in zip(ways, self.sent)]

        return items, then

    def absorb(self, other):
        self.keep, self.got = self.keep + other.keep, self.got + other.got

    def last_hop(self):
        def then(made):
            ((keep, sent),) = made
            self.keep, self.sent = [keep], [sent]
            self.got = [self.over("w", sent)]

        return [("last", self.parts())], then

    def back_first(self):
        def then(made):
            ((total,),) = made
            for s in self.extra:
                total = fold(total, flip_bit(total, *s))
            self.keep = self.sent = [total]
            self.got = [self.over("w", total)]

        return [("sum", self.parts())], then

    def back(self, *ways):
        if len(ways) == 2 and len(self.keep) == 1:
            items = [("split", self.parts())]
        else:
            items = [("join", [p]) for p in self.parts()]

        def then(made):
            self.keep = self.sent = [t for m in made for t in m]
            self.got = [self.over(w, t) for w, t in zip(ways, self.keep)]

        return items, then

    def back_core(self):
        def then(made):
            ((self.keep,),) = made
            self.sent = self.keep
            self.gather_core()

        return [("join", self.parts())], then


def all_steps(*steps):
    made = phase(*[item for items, _ in steps for item in items])
    for items, then in steps:
        then(made[: len(items)])
        made = made[len(items) :]


def mask_biases(seg):
    seq = seg.shape[1]
    place = jnp.arange(seq, dtype=jnp.int32)
    same = seg[:, :, None] == seg[:, None, :]
    below = (place[:, None] < place[None, :])[None]
    incl = (place[:, None] <= place[None, :])[None]
    bias = lambda m: jnp.where(same & m, 0.0, NEG).astype(F32)
    return bias(incl), bias(below)


def sync(*values):
    return lax.optimization_barrier(values)


class Link:
    def __init__(self, outer, w_qkv, w_out, w_up, w_down):
        self.outer = outer
        self.own = (w_qkv, w_out, w_up, w_down)
        self.core_at, self.x_at, o = (lax.axis_index(a) for a in ("core", "x", "o"))
        bits = {"x": self.x_at, "z": o % 2, "w": (o // 2) % 2}
        self.fetch_bits = self.core_at * 2 + self.x_at
        slots = []
        for order in ("xzw", "zxw"):
            slot = self.core_at
            for name in order:
                slot = slot * 2 + bits[name]
            slots.append(slot)
        self.me = jnp.stack([slots[0], self.fetch_bits, slots[1]]).astype(jnp.int32)
        self.me_z = self.me[2:0:-1]

    def quarter(self, own):
        flat = own.reshape(-1, own.shape[-1])
        return take_half(take_half(flat, self.core_at), self.x_at)

    def over_x(self, t):
        return lax.ppermute(t, "x", FLIP)

    def fetch(self, own_work):
        own = self.own
        size = own[2].shape[1] // 4
        part = lambda t, axis, bits: lax.dynamic_slice_in_dim(t, bits * size, size, axis)
        pieces = [
            self.quarter(own[1]),
            part(own[2], 1, self.fetch_bits),
            jnp.concatenate([part(own[3], 0, self.fetch_bits), part(own[3], 0, self.fetch_bits ^ 1)], axis=0),
        ]
        qkv = self.partner(self.quarter(own[0]))
        up, out, down = (self.partner(pieces[i]) for i in (1, 0, 2))
        qkv, own_work = sync(qkv, own_work)
        qkv, out, up = sync(ordered(self.x_at, qkv, self.over_x(qkv)).reshape(-1, qkv.shape[-1]), out, up)
        qkv_core, out_x, up_x = self.core(qkv), self.over_x(out), self.over_x(up)
        qkv = ordered(self.core_at, qkv, qkv_core).reshape(own[0].shape)

        def join_out(*work):
            nonlocal out, out_x
            work, out, out_x = sync(work, out, out_x)
            out = ordered(self.x_at, out, out_x).reshape(-1, out.shape[-1])
            out = ordered(self.core_at, out, self.core(out)).reshape(own[1].shape)
            return work, jnp.concatenate([own[1], out], axis=0)

        def pieces_of(*work):
            up_there, down_there, work = sync(up_x, down, work)
            ups = (own[2], up, up_there, self.core(up), self.core(up_there))
            return ups, (own[3], down_there, self.core(down_there)), work

        return own_work, own[0], qkv, jnp.concatenate([own[0], qkv], axis=2), join_out, pieces_of

    def partner(self, t):
        return lax.ppermute(t, "tensor", FLIP)

    def core(self, t):
        return lax.ppermute(t, "core", FLIP)

    def chunk(self, keep, got):
        return Chunk(keep, got)

    def hops(self, keep, got):
        return Hops(self.outer, keep, got)

    def small_steps(self):
        return [("core", 2, 1), ("tensor", 2, 1)] + steps_of(self.outer)

    def flip(self, t, step):
        return flip_bit(t, *step)


def local_part(x, seg, cot, gb, link):
    rows, seq = seg.shape
    n, width = x.shape
    me, me_z = link.me, link.me_z
    incl, strict = mask_biases(seg)
    normal, _ = norm_stats(x.astype(F32))
    a_e = (normal * gb[0] + gb[2]).astype(BF16)
    first = attend_first(a_e, link.own[0], incl)
    (a_e, first, cot, me, me_z), wq_own, fetched, wqkv, join_out, pieces_of = link.fetch((a_e, first, cot, me, me_z))
    second = attend_first(a_e, fetched, incl)
    qkv_e, o1 = (jnp.concatenate([s, t], axis=-1) for s, t in zip(first[:2], second[:2]))
    lse1 = jnp.concatenate([first[2], second[2]], axis=0).reshape(-1, GROUP // HD, n)
    (qkv_e, o1, lse1, wqkv), wout = join_out(qkv_e, o1, lse1, wqkv)
    h1, n2_1, g1, d1, part_one, dm2 = mlp_own(x, o1, wout, gb, link.own[2], link.own[3], cot)
    ups, downs, (n2_1, part_one) = pieces_of(n2_1, part_one)
    g1, d1, ho, a_o = mlp_other(n2_1, part_one, g1, d1, gb, ups[1:], downs[1:])
    qkv_o, o2, lse2 = attend_second(a_o, wqkv, incl, strict, qkv_e, o1, lse1)
    out, out_two, n2_2, g2, du2, dh1_2, dp2, do2, sums2 = mlp_second(x, ho, o2, dm2, wout, gb, ups, downs, seq)
    out_got = link.partner(out)
    dqkv_o, part, dy, sums_o = attend_back(wqkv, incl, strict, qkv_e, qkv_o, o2, lse2, do2, dh1_2, ho, gb)
    o2_flat = o2.reshape(2 * n, width)

    out_got, dy = sync(out_got, dy)
    quarter = out_two.shape[1] // 2
    out_last = [link.partner(after(out_two[:, :quarter], out_got))]
    down_keep, down_go = grad_down(me_z, g1, g2, dy, dm2)
    down_keep, down_go, out_last[0] = sync(down_keep, down_go, out_last[0])
    out_last.append(link.partner(after(out_two[:, quarter:], down_go)))
    down = link.hops(down_keep, link.core(down_go))
    dy = after(dy, down_go)
    du1, dh1_1, dp1, do1, sums1 = mlp_back(dy, h1, wout, gb, d1, ups, downs, seq)
    du1, dp1, do1, out_last[1] = down.wait(du1, dp1, do1, out_last[1])
    down.to_partner()
    up_keep, up_go = grad_up(me, n2_1, n2_2, after(du1, down.sent), du2, dp1, dp2, o1, o2_flat)
    do1 = after(do1, up_go)
    dqkv_e, gt, sums_e = attend_back_even(wqkv, incl, qkv_e, o1, lse1, do1, o2, lse2, do2, part, dh1_1, dh1_2, x, gb)
    dqkv_e, gt, sums_e, up_go = down.wait(dqkv_e, gt, sums_e, up_go)
    up = link.hops(up_keep, link.core(up_go))
    down.keep, down.got = [down.keep], [down.got]
    all_steps(down.hop("z"))
    small = jnp.stack([sums_e[0] + sums_o[0], sums1[0] + sums2[0], sums_e[1] + sums_o[1], sums1[1] + sums2[1], sums_o[2]])
    qkv_keep, qkv_go = grad_qkv(me_z, a_e, a_o, after(dqkv_e, *down.sent), dqkv_o)
    up_parts = up.fold_first()
    qkv_keep, qkv_go, down.got, up_parts = sync(qkv_keep, qkv_go, down.got, up_parts)
    out = link.finish(
        jnp.concatenate([out, out_two], axis=0),
        jnp.concatenate([out_got, jnp.concatenate(after(out_last, up_parts), axis=1)], axis=0),
        link.out_shape,
    )
    qkv = link.hops(qkv_keep, link.core(qkv_go))
    small_steps = iter(link.small_steps())
    small_got = link.flip(after(small, qkv_go), next(small_steps))

    chunks = [up, qkv]

    def wait_all():
        nonlocal small, small_got
        got, small_got = sync([c.got for c in chunks], small_got)
        for c, g in zip(chunks, got):
            c.got = g
        if small_got is not None:
            small = small + small_got
            step = next(small_steps, None)
            small_got = None if step is None else link.flip(small, step)

    chunks.remove(up)
    wait_all()
    up.first(up_parts)
    qkv.first_hop("partner")
    all_steps(down.hop("x"))
    chunks += [up, down]
    (out,) = up.wait(out)
    wait_all()
    all_steps(up.hop("partner", "x"), qkv.hop("z"), down.hop("w"))
    wait_all()
    all_steps(up.hop("z", "partner"), qkv.hop("x"), down.back_first())
    half = gt.shape[0] // 2
    gt_got = [link.partner(after(gt[:half], *up.sent))]
    wait_all()
    up.absorb(qkv)
    chunks.remove(qkv)
    all_steps(up.last_hop(), down.back("z"))
    gt_got.append(link.partner(after(gt[half:], *up.sent)))
    (gt_got[0],) = up.wait(gt_got[0])
    wait_all()
    all_steps(up.back_first(), down.back("x"))
    (gt_got[1],) = up.wait(gt_got[1])
    wait_all()
    while small_got is not None:
        wait_all()
    all_steps(up.back("z", "x"), down.back_core())
    wait_all()
    all_steps(up.back("x", "z"))
    g_down = unpack_down(me_z, 0, after(down.keep, *up.sent))
    g_down = unpack_down(me_z, 1, down.got, (g_down,))
    gt = link.finish(gt, jnp.concatenate(gt_got, axis=0), link.tokens_shape).astype(F32)
    small = (small[0:2], small[2:4], small[4])
    g_down, gt, small = up.wait(g_down, gt, small)
    all_steps(up.back_core())
    g_rest = unpack_rest(me, 0, up.keep)
    g_rest = up.wait(*g_rest)
    g_up, g_out, g_qkv = unpack_rest(me, 1, up.got, g_rest)
    return out, gt, (g_qkv, g_out, g_up, g_down), small


def shards(outer, tokens, segments, pass_embed, w_qkv, w_out, w_up, w_down, gain, bias, cotangent):
    ty = lax.axis_index("tensor")
    rows = tokens.shape[0] // 2
    width = tokens.shape[2]
    mine = lambda t: lax.dynamic_slice_in_dim(t, ty * rows, rows, 0)
    x = mine(tokens).reshape(-1, width)
    gb = jnp.concatenate([gain, bias, pass_embed[None]], axis=0)
    link = Link(outer, w_qkv, w_out, w_up, w_down)
    link.out_shape, link.tokens_shape = cotangent.shape, tokens.shape
    link.finish = lambda mine, theirs, shape: ordered(ty, mine, theirs).reshape(shape)
    out, gt, grads, small = local_part(x, mine(segments), mine(cotangent), gb, link)
    return out, gt, *grads, *small


def solution(mesh):
    outer = mesh.shape["dp"] // 4
    fine = Mesh(mesh.devices.reshape(outer, 2, 2, mesh.shape["tensor"]), ("o", "x", "core", "tensor"))
    rows = ROWS_OVER
    placed = (
        P(rows, None, None),
        P(rows, None),
        P(),
        P(None, None, "tensor"),
        P("tensor", None),
        P(None, "tensor"),
        P("tensor", None),
        P(),
        P(),
        P(rows, None, None),
    )

    def body(*args):
        return shards(outer, *args)

    return jax.shard_map(
        body,
        mesh=fine,
        in_specs=placed,
        out_specs=(
            P(rows, None, None),
            P(rows, None, None),
            P(None, None, "tensor"),
            P("tensor", None),
            P(None, "tensor"),
            P("tensor", None),
            P(),
            P(),
            P(),
        ),
        check_vma=False,
    )
```

```python
import functools

import jax
import jax.numpy as jnp
from jax import lax
from jax.experimental import pallas as pl
from jax.experimental.pallas import tpu as pltpu
from jax.sharding import Mesh
from jax.sharding import PartitionSpec as P

HD = 64
EPS = 1e-05
NEG = -1000000000.0
F32 = jnp.float32
BF16 = jnp.bfloat16
ROWS_OVER = ("o", "x", "core")
FLIP = ((0, 1), (1, 0))
VMEM_LIMIT = 16 * 1024 * 1024


def ordered(flag, mine, theirs):
    first = flag == 0
    return jnp.stack([jnp.where(first, mine, theirs), jnp.where(first, theirs, mine)])


def take_half(array, index):
    half = array.shape[0] // 2
    return lax.dynamic_slice_in_dim(array, index * half, half, 0)


def flip_bit(array, axis, size, bit):
    return lax.ppermute(array, axis, [(i, i ^ bit) for i in range(size)])


def steps_of(outer):
    steps = [("x", 2, 1)]
    bit = 1
    while bit < outer:
        steps.append(("o", outer, bit))
        bit *= 2
    return steps


def my_bit(axis, bit):
    return (lax.axis_index(axis) // bit) % 2


def dot(a, b):
    return lax.dot_general(a, b, (((1,), (0,)), ((), ())), preferred_element_type=F32)


def dot_nt(a, b):
    return lax.dot_general(a, b, (((1,), (1,)), ((), ())), preferred_element_type=F32)


def dot_tn(a, b):
    return lax.dot_general(a, b, (((0,), (0,)), ((), ())), preferred_element_type=F32)


def norm_stats(h):
    centred = h - jnp.mean(h, axis=-1, keepdims=True)
    inverse = lax.rsqrt(jnp.mean(centred * centred, axis=-1, keepdims=True) + EPS)
    return centred * inverse, inverse


def norm_back(grad, normal, inverse, gain):
    scaled = grad * gain
    centre = jnp.mean(scaled, axis=-1, keepdims=True)
    proj = jnp.mean(scaled * normal, axis=-1, keepdims=True)
    return inverse * (scaled - centre - normal * proj)


def gelu_parts(u):
    c = 0.7978845608028654
    a = 0.044715 * c
    square = u * u
    half = 0.5 + 0.5 * jnp.tanh(u * (c + a * square))
    g = u * half
    return g, half + g * (1.0 - half) * (2.0 * c + 6.0 * a * square)


def whole(shape):
    return pl.BlockSpec(shape, lambda *_: (0,) * len(shape))


def call(body, grid, ins, outs, scratch=(), cost=(0, 0), name=None, vmem=VMEM_LIMIT):
    return pl.pallas_call(
        body,
        grid=grid,
        in_specs=[s for _, s in ins],
        out_specs=[s for _, s in outs],
        out_shape=[a for a, _ in outs],
        scratch_shapes=scratch,
        compiler_params=pltpu.CompilerParams(
            dimension_semantics=("arbitrary",) * len(grid), vmem_limit_bytes=vmem
        ),
        cost_estimate=pl.CostEstimate(
            flops=int(cost[0]) // 16, bytes_accessed=int(cost[1]), transcendentals=0
        ),
        name=name,
    )(*[a for a, _ in ins])


FAR = pl.BlockSpec(memory_space=pl.ANY)


def resident(body, ins, outs, scratch=(), flops=0, vmem=16, aliases={}, name=None):
    spec = pl.BlockSpec(memory_space=pltpu.VMEM)
    ins, outs = ([o if isinstance(o, tuple) else (o, spec) for o in t] for t in (ins, outs))
    ins = [(pltpu.with_memory_space_constraint(a, pltpu.HBM) if s is FAR else a, s) for a, s in ins]
    outs = [(pltpu.HBM(a.shape, a.dtype) if s is FAR else a, s) for a, s in outs]
    return pl.pallas_call(
        body,
        in_specs=[s for _, s in ins],
        out_specs=[s for _, s in outs],
        out_shape=[a for a, _ in outs],
        scratch_shapes=scratch,
        input_output_aliases=aliases,
        compiler_params=pltpu.CompilerParams(vmem_limit_bytes=vmem * 1024 * 1024),
        cost_estimate=pl.CostEstimate(flops=int(flops) // 16, bytes_accessed=0, transcendentals=0),
        name=name,
    )(*[a for a, _ in ins])


def sds(shape, dtype):
    return jax.ShapeDtypeStruct(shape, dtype)


QB = 128
GROUP = 256


def lanes_of(ref, g):
    return ref.at[(slice(None),) * (len(ref.shape) - 1) + (pl.ds(pl.multiple_of(g * GROUP, GROUP), GROUP),)]


class Moves:
    def __init__(self, sems):
        self.sems, self.used = sems, 0

    def take(self, number):
        self.used += number
        return self.used - number

    def whole(self, source, target):
        copy = pltpu.make_async_copy(source, target, self.sems.at[self.take(1)])
        copy.start()
        return copy.wait

    def later(self, source, target):
        sem = self.sems.at[self.take(1)]
        copy = lambda: pltpu.make_async_copy(source, target, sem)
        return (lambda: copy().start()), (lambda: copy().wait())

    def groups(self, source, target):
        first = self.take(source.shape[-1] // GROUP)

        def copy(g):
            return pltpu.make_async_copy(lanes_of(source, g), lanes_of(target, g), self.sems.at[first + g])

        return (lambda g: copy(g).start()), (lambda g: copy(g).wait())


def cat_heads(t, scale=1.0):
    lane = lax.broadcasted_iota(jnp.int32, (1, 2 * HD), 1)
    parts = [t * jnp.where((lane < HD) == (h == 0), scale, 0.0).astype(t.dtype) for h in range(2)]
    return jnp.concatenate(parts, axis=0)


def own_lanes(t, scale=None):
    if scale is not None:
        t = t * scale
    return jnp.concatenate([t[:HD, :QB], t[HD:, QB:]], axis=0)


def twice(t):
    return jnp.concatenate([t, t], axis=1)


def pair_row(rows, p):
    return jnp.concatenate([rows[2 * p : 2 * p + 1], rows[2 * p + 1 : 2 * p + 2]], axis=1)


def put_pair(ref, p, cols, value):
    ref[2 * p : 2 * p + 1, cols] = value[:, :QB]
    ref[2 * p + 1 : 2 * p + 2, cols] = value[:, QB:]


def columns(t, r, seq, qb):
    return t[:, pl.ds(pl.multiple_of(r * seq + qb * QB, QB), QB)]


def rows_of(r, seq, qb):
    return pl.ds(pl.multiple_of(r * seq + qb * QB, QB), QB)


def in_turn(arrive, group, groups):
    for _, wait in arrive:
        wait(group)

    @pl.when(group + 2 < groups)
    def _():
        for start, _ in arrive:
            start(group + 2)


def attend_first_body(rows, seq, pairs, a_ref, w_ref, bias_ref, qkv_ref, o_ref, lse_ref):
    a = a_ref[...]
    for j in range(3):
        qkv_ref[j] = dot(a, w_ref[j]).astype(BF16)
    for r in range(rows):
        work = []
        for p in range(pairs):
            ln = slice(p * 2 * HD, (p + 1) * 2 * HD)
            k = qkv_ref[1, r * seq : (r + 1) * seq, ln]
            for b in range(seq // QB):
                sl, n = slice(r * seq + b * QB, r * seq + (b + 1) * QB), (b + 1) * QB
                q = cat_heads(qkv_ref[0, sl, ln], HD**-0.5)
                s = dot_nt(k[:n], q) + twice(bias_ref[r, :n, b * QB : n])
                work.append((p, ln, sl, n, s))
        done = []
        for p, ln, sl, n, s in work:
            top = jnp.max(s, axis=0, keepdims=True)
            e = jnp.exp(s - top)
            mass = jnp.sum(e, axis=0, keepdims=True)
            put_pair(lse_ref, p, sl, top + jnp.log(mass))
            done.append((e.astype(BF16), 1.0 / mass))
        for (p, ln, sl, n, _), (e, inv) in zip(work, done):
            vt = qkv_ref[2, r * seq : (r + 1) * seq, ln].T
            o_ref[sl, ln] = own_lanes(dot(vt[:, :n], e), inv).T.astype(BF16)


def attend_first(a, w, bias):
    rows, seq = bias.shape[0], bias.shape[1]
    n, d = a.shape
    f = w.shape[2]
    return resident(
        functools.partial(attend_first_body, rows, seq, f // (2 * HD)),
        (a, w, bias),
        [sds((3, n, f), BF16), sds((n, f), BF16), sds((f // HD, n), F32)],
        flops=6 * n * d * f + 16 * n * seq * f,
        name="attend_first",
    )


def attend_second_body(
    rows, seq, a_far, w_far, incl_far, strict_far, qkve_far, o1_far, lse1_ref,
    qkvo_far, o2_far, lse2_ref,
    a_ref, w_ref, incl_ref, strict_ref, qkve_ref, o1_ref, qkvo_ref, o2_ref, sems,
):
    groups = lse1_ref.shape[0]
    moves = Moves(sems)
    first = moves.take(6)

    def weight(j):
        return pltpu.make_async_copy(w_far.at[j], w_ref.at[j], sems.at[first + j])

    def projected(j):
        return pltpu.make_async_copy(qkvo_ref.at[j], qkvo_far.at[j], sems.at[first + 3 + j])

    a_there = moves.whole(a_far, a_ref)
    weight(0).start()
    arrive = [moves.groups(*t) for t in ((qkve_far, qkve_ref), (o1_far, o1_ref))]
    leave = moves.groups(o2_ref, o2_far)
    a_there()
    weight(0).wait()
    weight(1).start()
    weight(2).start()
    masks = [moves.whole(*t) for t in ((incl_far, incl_ref), (strict_far, strict_ref))]
    for g in range(2):
        for start, _ in arrive:
            start(g)

    def project(j, _):
        pl.when(j > 0)(lambda: weight(j).wait())
        qkvo_ref[j] = dot(a_ref[...], w_ref[j]).astype(BF16)
        projected(j).start()
        return 0

    lax.fori_loop(0, 3, project, 0)
    for wait in masks:
        wait()

    def next_group(group):
        in_turn(arrive, group, groups)

    def row(i, _):
        r, group = i % rows, i // rows
        lanes = pl.multiple_of(group * GROUP, GROUP)
        all_of = pl.ds(pl.multiple_of(r * seq, seq), seq)

        @pl.when(r == 0)
        def _():
            next_group(group)

        for p in range(GROUP // (2 * HD)):
            ln = pl.ds(lanes + p * 2 * HD, 2 * HD)
            ke, ko = qkve_ref[1, all_of, ln], qkvo_ref[1, all_of, ln]
            vte, vto = qkve_ref[2, all_of, ln].T, qkvo_ref[2, all_of, ln].T
            work = []
            for b in range(seq // QB):
                sl, n = rows_of(r, seq, b), (b + 1) * QB
                cols = slice(b * QB, n)
                incl, strict = twice(incl_ref[r, :n, cols]), twice(strict_ref[r, :n, cols])
                q = cat_heads(qkve_ref[0, sl, ln], HD**-0.5)
                work.append([dot_nt(ko[:n], q) + strict])
                q = cat_heads(qkvo_ref[0, sl, ln], HD**-0.5)
                work.append([dot_nt(ko[:n], q) + incl, dot_nt(ke[:n], q) + incl])
            for b in range(seq // QB):
                sl, n = rows_of(r, seq, b), (b + 1) * QB
                (s,), (so, se) = work[2 * b : 2 * b + 2]
                old = pair_row(lse1_ref[group, :, sl], p)
                top = jnp.maximum(old, jnp.max(s, axis=0, keepdims=True))
                e = jnp.exp(s - top)
                kept = jnp.exp(old - top)
                mass = kept + jnp.sum(e, axis=0, keepdims=True)
                work[2 * b] = (e.astype(BF16), kept, 1.0 / mass)
                put_pair(lse2_ref.at[0, group], p, sl, top + jnp.log(mass))
                top = jnp.max(jnp.maximum(se, so), axis=0, keepdims=True)
                ee, eo = jnp.exp(se - top), jnp.exp(so - top)
                mass = jnp.sum(ee + eo, axis=0, keepdims=True)
                work[2 * b + 1] = (ee.astype(BF16), eo.astype(BF16), 1.0 / mass)
                put_pair(lse2_ref.at[1, group], p, sl, top + jnp.log(mass))
            for b in range(seq // QB):
                sl, n = rows_of(r, seq, b), (b + 1) * QB
                (e, kept, inv), (ee, eo, inv2) = work[2 * b : 2 * b + 2]
                o1 = o1_ref[sl, ln].astype(F32).T
                o = own_lanes(dot(vto[:, :n], e), inv) + own_lanes(twice(o1), kept * inv)
                o2_ref[0, sl, ln] = o.T.astype(BF16)
                o = dot(vte[:, :n], ee) + dot(vto[:, :n], eo)
                o2_ref[1, sl, ln] = own_lanes(o, inv2).T.astype(BF16)

        @pl.when(r == rows - 1)
        def _():
            leave[0](group)

        return 0

    lax.fori_loop(0, rows * groups, row, 0)
    for j in range(3):
        projected(j).wait()
    for g in range(groups):
        leave[1](g)


def attend_second(a, w, incl, strict, qkve, o1, lse1):
    rows, seq = incl.shape[0], incl.shape[1]
    n, d = a.shape
    f = w.shape[2]
    qkv, o2 = sds((3, n, f), BF16), sds((2, n, f), BF16)
    near = (a, w, incl, strict, qkve, o1, qkv, o2)
    return resident(
        functools.partial(attend_second_body, rows, seq),
        [(t, FAR) for t in (a, w, incl, strict, qkve, o1)] + [lse1],
        [(qkv, FAR), (o2, FAR), sds((2, *lse1.shape), F32)],
        scratch=[pltpu.VMEM(t.shape, t.dtype) for t in near] + [pltpu.SemaphoreType.DMA((64,))],
        flops=6 * n * d * f + 48 * n * seq * f,
        vmem=32,
        name="attend_second",
    )


def row_products(a, b):
    prod = cat_heads((a * b).astype(BF16))
    return dot_nt(jnp.ones((8, 2 * HD), BF16), prod)[:1]


def query_parts(sl, ln, group, p, i, qkv_ref, o_ref, lse_ref, do_ref):
    do = do_ref[i, sl, ln]
    delta = row_products(do.astype(F32), o_ref[i, sl, ln].astype(F32))
    return cat_heads(qkv_ref[0, sl, ln], HD**-0.5), cat_heads(do), pair_row(lse_ref[i, group, :, sl], p), delta


def blocks_back(tasks):
    scores = [dot_nt(k, q) + bias - lse for k, _, _, bias, q, _, lse, _ in tasks]
    moved = [dot_nt(v, do) - delta for _, v, _, _, _, do, _, delta in tasks]
    probs = [jnp.exp(s) for s in scores]
    ds = [(p * m).astype(BF16) for p, m in zip(probs, moved)]
    return [
        (dot(p.astype(BF16), do), dot(d, q), dot(kt, d))
        for (_, _, kt, _, q, do, _, _), p, d in zip(tasks, probs, ds)
    ]


def add_rows(total, part):
    if total is None:
        return part
    n = part.shape[0]
    return jnp.concatenate([total[:n] + part, total[n:]], axis=0)


def attend_back_body(
    rows, seq, w_far, incl_far, strict_far, qkve_far, qkvo_far, o2_far, lse2_ref, do_far,
    dh1_far, ho_far, gb_ref,
    dqkvo_far, dqkve_far, dy_far, sums_ref,
    w_ref, incl_ref, strict_ref, qkve_ref, qkvo_ref, o2_ref, do_ref, dh1_ref, ho_ref,
    dqkvo_ref, dqkve_ref, da_ref, dy_ref, sems,
):
    groups = lse2_ref.shape[1]
    moves = Moves(sems)
    arrive = [
        moves.groups(*t)
        for t in ((qkve_far, qkve_ref), (qkvo_far, qkvo_ref), (o2_far, o2_ref), (do_far, do_ref))
    ]
    leave = [moves.groups(*t) for t in ((dqkvo_ref, dqkvo_far), (dqkve_ref, dqkve_far))]
    for start, _ in arrive:
        start(0)
    masks = [moves.whole(*t) for t in ((incl_far, incl_ref), (strict_far, strict_ref))]
    for start, _ in arrive:
        start(1)
    odd = pl.ds(rows * seq, rows * seq)
    late = [moves.later(*t) for t in ((w_far, w_ref), (dh1_far.at[odd], dh1_ref), (ho_far, ho_ref))]
    for wait in masks:
        wait()

    def next_group(group):
        in_turn(arrive, group, groups)

        @pl.when(group == groups - 2)
        def _():
            for start, _ in late:
                start()

    sc = HD**-0.5

    def row(i, _):
        r, group = i % rows, i // rows
        lanes = pl.multiple_of(group * GROUP, GROUP)
        all_of = pl.ds(pl.multiple_of(r * seq, seq), seq)

        @pl.when(r == 0)
        def _():
            next_group(group)

        for p in range(GROUP // (2 * HD)):
            ln = pl.ds(lanes + p * 2 * HD, 2 * HD)
            ke, ve = qkve_ref[1, all_of, ln], qkve_ref[2, all_of, ln]
            ko, vo = qkvo_ref[1, all_of, ln], qkvo_ref[2, all_of, ln]
            kte, kto = ke.T, ko.T
            tasks = []
            for b in reversed(range(seq // QB)):
                sl, n = rows_of(r, seq, b), (b + 1) * QB
                cols = slice(b * QB, n)
                incl, strict = twice(incl_ref[r, :n, cols]), twice(strict_ref[r, :n, cols])
                even = query_parts(sl, ln, group, p, 0, qkve_ref, o2_ref, lse2_ref, do_ref)
                odd = query_parts(sl, ln, group, p, 1, qkvo_ref, o2_ref, lse2_ref, do_ref)
                tasks.append((ko[:n], vo[:n], kto[:, :n], strict, *even))
                tasks.append((ko[:n], vo[:n], kto[:, :n], incl, *odd))
                tasks.append((ke[:n], ve[:n], kte[:, :n], incl, *odd))
            done = blocks_back(tasks)
            dke = dve = dko = dvo = None
            for b in reversed(range(seq // QB)):
                sl = rows_of(r, seq, b)
                (dv, dk, dqe), (dv2, dk2, dqo), (dv3, dk3, dqo2) = done[:3]
                done = done[3:]
                dvo, dko = add_rows(dvo, dv + dv2), add_rows(dko, dk + dk2)
                dve, dke = add_rows(dve, dv3), add_rows(dke, dk3)
                dqkve_ref[0, sl, ln] = (own_lanes(dqe).T * sc).astype(BF16)
                dqkvo_ref[0, sl, ln] = (own_lanes(dqo + dqo2).T * sc).astype(BF16)
            dqkve_ref[1, all_of, ln] = dke.astype(BF16)
            dqkve_ref[2, all_of, ln] = dve.astype(BF16)
            dqkvo_ref[1, all_of, ln] = dko.astype(BF16)
            dqkvo_ref[2, all_of, ln] = dvo.astype(BF16)

        @pl.when(r == rows - 1)
        def _():
            for start, _ in leave:
                start(group)

        return 0

    lax.fori_loop(0, rows * groups, row, 0)
    for _, wait in late:
        wait()
    da = dot_nt(dqkvo_ref[0], w_ref[0])
    da += dot_nt(dqkvo_ref[1], w_ref[1])
    da += dot_nt(dqkvo_ref[2], w_ref[2])
    da_ref[...] = da
    sums_ref[...] = jnp.zeros_like(sums_ref)

    def finish(i, _):
        sl = pl.ds(pl.multiple_of(i * ROWS_AT_ONCE, ROWS_AT_ONCE), ROWS_AT_ONCE)
        normal, inverse = norm_stats(ho_ref[sl])
        da = da_ref[sl]
        dy = dh1_ref[sl] + norm_back(da, normal, inverse, gb_ref[0:1])
        dy_ref[sl] = dy
        for k, t in enumerate((da * normal, da, dy)):
            sums_ref[k : k + 1] += jnp.sum(t, axis=0, keepdims=True)
        return 0

    lax.fori_loop(0, rows * seq // ROWS_AT_ONCE, finish, 0)
    kept = [moves.whole(dy_ref, dy_far)]
    for g in range(groups):
        for _, wait in leave:
            wait(g)
    for wait in kept:
        wait()


def attend_back(w, incl, strict, qkve, qkvo, o2, lse2, do, dh1, ho, gb):
    rows, seq = incl.shape[0], incl.shape[1]
    n, d = ho.shape
    f = w.shape[2]
    do = do.reshape(2, n, f)
    qkv = sds((3, n, f), BF16)
    near = (w, incl, strict, qkve, qkvo, o2, do, sds((n, d), F32), ho, qkv, qkv, sds((n, d), F32))
    return resident(
        functools.partial(attend_back_body, rows, seq),
        [(t, FAR) for t in (w, incl, strict, qkve, qkvo, o2)]
        + [lse2]
        + [(t, FAR) for t in (do, dh1, ho)]
        + [gb],
        [(qkv, FAR), (qkv, FAR), (sds((n, d), F32), FAR), sds((3, d), F32)],
        scratch=[pltpu.VMEM(t.shape, t.dtype) for t in near + (sds((n, d), F32),)] + [pltpu.SemaphoreType.DMA((64,))],
        flops=6 * n * d * f + 120 * n * seq * f,
        vmem=44,
        name="attend_back",
    )


def attend_back_even_body(
    rows, seq, w_far, incl_far, qkve_far, o1_far, lse1_ref, do1_far, o2_far, lse2_ref, do2_far,
    part_far, dh1_far, dh2_far, x_far, gb_ref,
    dqkv_far, gt_ref, sums_ref,
    w_ref, incl_ref, qkve_ref, o1_ref, do1_ref, o2_ref, do2_ref, part_ref, dh1_ref, dh2_ref, x_ref,
    dqkv_ref, da_ref, sems,
):
    groups = lse1_ref.shape[0]
    moves = Moves(sems)
    even = pl.ds(0, rows * seq)
    arrive = [
        moves.groups(*t)
        for t in (
            (qkve_far, qkve_ref), (o1_far, o1_ref), (do1_far, do1_ref), (o2_far.at[0], o2_ref),
            (do2_far.at[0], do2_ref), (part_far, part_ref),
        )
    ]
    leave = [moves.groups(dqkv_ref, dqkv_far)]
    for start, _ in arrive:
        start(0)
    mask = moves.whole(incl_far, incl_ref)
    for start, _ in arrive:
        start(1)
    late = [
        moves.later(*t)
        for t in ((w_far, w_ref), (dh1_far, dh1_ref), (dh2_far.at[even], dh2_ref), (x_far, x_ref))
    ]
    mask()

    def next_group(group):
        in_turn(arrive, group, groups)

        @pl.when(group == groups - 2)
        def _():
            for start, _ in late:
                start()

    sc = HD**-0.5

    def row(i, _):
        r, group = i % rows, i // rows
        lanes = pl.multiple_of(group * GROUP, GROUP)
        all_of = pl.ds(pl.multiple_of(r * seq, seq), seq)

        @pl.when(r == 0)
        def _():
            next_group(group)

        for p in range(GROUP // (2 * HD)):
            ln = pl.ds(lanes + p * 2 * HD, 2 * HD)
            k, v = qkve_ref[1, all_of, ln], qkve_ref[2, all_of, ln]
            kt = k.T
            tasks = []
            for b in reversed(range(seq // QB)):
                sl, n = rows_of(r, seq, b), (b + 1) * QB
                incl = twice(incl_ref[r, :n, b * QB : n])
                lse1 = pair_row(lse1_ref[group, :, sl], p)
                ratio = jnp.exp(lse1 - pair_row(lse2_ref[0, group, :, sl], p))
                do1, do2 = do1_ref[sl, ln].astype(F32), do2_ref[sl, ln].astype(F32)
                delta = row_products(do1, o1_ref[sl, ln].astype(F32))
                delta += ratio * row_products(do2, o2_ref[sl, ln].astype(F32))
                both = do1 + own_lanes(twice(do2.T), ratio).T
                q, do = cat_heads(qkve_ref[0, sl, ln], sc), cat_heads(both.astype(BF16))
                tasks.append((k[:n], v[:n], kt[:, :n], incl, q, do, lse1, delta))
            dka = dva = None
            for b, (dv, dk, dq) in zip(reversed(range(seq // QB)), blocks_back(tasks)):
                sl = rows_of(r, seq, b)
                dva, dka = add_rows(dva, dv), add_rows(dka, dk)
                dqkv_ref[0, sl, ln] = (own_lanes(dq).T * sc + part_ref[0, sl, ln].astype(F32)).astype(BF16)
            dqkv_ref[1, all_of, ln] = (dka + part_ref[1, all_of, ln].astype(F32)).astype(BF16)
            dqkv_ref[2, all_of, ln] = (dva + part_ref[2, all_of, ln].astype(F32)).astype(BF16)

        @pl.when(r == rows - 1)
        def _():
            for start, _ in leave:
                start(group)

        return 0

    lax.fori_loop(0, rows * groups, row, 0)
    for _, wait in late:
        wait()
    da_ref[...] = jnp.zeros_like(da_ref)

    def project_back(j, _):
        da_ref[...] += dot_nt(dqkv_ref[j], w_ref[j])
        return 0

    lax.fori_loop(0, 3, project_back, 0)
    sums_ref[...] = jnp.zeros_like(sums_ref)

    def finish(i, _):
        sl = pl.ds(pl.multiple_of(i * ROWS_AT_ONCE, ROWS_AT_ONCE), ROWS_AT_ONCE)
        normal, inverse = norm_stats(x_ref[sl].astype(F32))
        da = da_ref[sl]
        sums_ref[0:1] += jnp.sum(da * normal, axis=0, keepdims=True)
        sums_ref[1:2] += jnp.sum(da, axis=0, keepdims=True)
        back = norm_back(da, normal, inverse, gb_ref[0:1])
        gt_ref[sl] = (dh1_ref[sl] + dh2_ref[sl] + back).astype(BF16)
        return 0

    lax.fori_loop(0, rows * seq // ROWS_AT_ONCE, finish, 0)
    for g in range(groups):
        for _, wait in leave:
            wait(g)


def attend_back_even(w, incl, qkve, o1, lse1, do1, o2, lse2, do2, part, dh1, dh2, x, gb):
    rows, seq = incl.shape[0], incl.shape[1]
    n, d = x.shape
    f = w.shape[2]
    qkv, one = sds((3, n, f), BF16), sds((n, f), BF16)
    near = (w, incl, qkv, one, one, one, one, qkv, dh1, dh1, x, qkv, sds((n, d), F32))
    far = lambda *ts: [(t, FAR) for t in ts]
    return resident(
        functools.partial(attend_back_even_body, rows, seq),
        far(w, incl, qkve, o1)
        + [lse1]
        + far(do1, o2)
        + [lse2]
        + far(do2.reshape(2, n, f), part, dh1, dh2, x)
        + [gb],
        [(qkv, FAR), sds((n, d), BF16), sds((2, d), F32)],
        scratch=[pltpu.VMEM(t.shape, t.dtype) for t in near] + [pltpu.SemaphoreType.DMA((64,))],
        flops=6 * n * d * f + 40 * n * seq * f,
        vmem=40,
        name="attend_back_even",
    )


CHUNK = 512
ROWS_AT_ONCE = 256


def chunk_of(ref, j, axis):
    at = pl.ds(pl.multiple_of(j * CHUNK, CHUNK), CHUNK)
    return ref.at[:, at] if axis else ref.at[at]


class Chunks:
    def __init__(self, moves, far, near, axis, ring=False, leave=False):
        self.first = moves.take(far.shape[axis] // CHUNK)
        self.sems, self.far, self.near = moves.sems, far, near
        self.axis, self.ring, self.leave = axis, ring, leave

    def copy(self, j):
        near = self.near.at[j % self.near.shape[0]] if self.ring else chunk_of(self.near, j, self.axis)
        ends = (chunk_of(self.far, j, self.axis), near)
        return pltpu.make_async_copy(*(ends[::-1] if self.leave else ends), self.sems.at[self.first + j])

    def start(self, j):
        self.copy(j).start()

    def wait(self, j):
        self.copy(j).wait()


class Weight:
    def __init__(self, moves, pieces, near, axis):
        self.axis, self.near = axis, near
        self.own = Chunks(moves, pieces[0], near, axis) if pieces[0] is not None else None
        self.number = near.shape[axis] // CHUNK // 2
        self.others, start = [], near.shape[axis] // 2
        for far in pieces[1:]:
            at = pl.ds(start, far.shape[axis])
            self.others.append(moves.later(far, near.at[:, at] if axis else near.at[at]))
            start += far.shape[axis]

    def start_others(self):
        for start, _ in self.others:
            start()

    def wait_others(self):
        for _, wait in self.others:
            wait()


def load_in_turn(j, *weights):
    number = weights[0].number

    @pl.when(j < number)
    def _():
        for w in weights:
            w.own.wait(j)

    @pl.when(j + 2 < number)
    def _():
        for w in weights:
            w.own.start(j + 2)

    @pl.when(j + 2 == number)
    def _():
        for w in weights:
            w.start_others()

    @pl.when(j == number)
    def _():
        for w in weights:
            w.wait_others()


def start_loads(*weights):
    for j in range(2):
        for w in weights:
            w.own.start(j)


def feed_chunk(n2_ref, wup_ref, wdown_ref, j, g_buf, d_buf, ho_ref, gs, ds, first):
    @pl.when(first >= 2)
    def _():
        gs.wait(j - 2)
        ds.wait(j - 2)

    half = n2_ref.shape[0] // 2
    parts = []
    for sl in (slice(0, half), slice(half, 2 * half)):
        g, d = gelu_parts(dot(n2_ref[sl], chunk_of(wup_ref, j, 1)[...]))
        parts.append(g.astype(BF16))
        g_buf[j % 2, sl] = parts[-1]
        d_buf[j % 2, sl] = d.astype(BF16)
    gs.start(j)
    ds.start(j)
    for i, g in enumerate(parts):
        ho_ref[i * half : (i + 1) * half] += dot(g, chunk_of(wdown_ref, j, 0)[...])


def start_norm(x_ref, h1_ref, n2_ref, gb_ref, ho_ref=None, normal_ref=None, inverse_ref=None):
    def part(k, _):
        sl = pl.ds(pl.multiple_of(k * ROWS_AT_ONCE, ROWS_AT_ONCE), ROWS_AT_ONCE)
        h1 = x_ref[sl].astype(F32) + h1_ref[sl]
        h1_ref[sl] = h1
        normal, inverse = norm_stats(h1)
        n2_ref[sl] = (normal * gb_ref[1:2] + gb_ref[3:4]).astype(BF16)
        if ho_ref is not None:
            ho_ref[sl] = h1 + gb_ref[4:5]
        if normal_ref is not None:
            normal_ref[sl] = normal
            inverse_ref[sl] = jnp.broadcast_to(inverse, (ROWS_AT_ONCE, inverse_ref.shape[1]))
        return 0

    lax.fori_loop(0, h1_ref.shape[0] // ROWS_AT_ONCE, part, 0)


def weave(seq):
    i = lax.broadcasted_iota(jnp.int32, (2 * seq, 2 * seq), 0)
    k = lax.broadcasted_iota(jnp.int32, (2 * seq, 2 * seq), 1)
    place = jnp.where(k < seq, 2 * k, 2 * (k - seq) + 1)
    return jnp.where(i == place, 1.0, 0.0).astype(BF16)


def mlp_own_body(
    x_far, o_far, wout_far, gb_ref, wup_far, wdown_far, cot_far,
    h1_far, n2_far, g_far, d_far, ho_far, dm_far,
    x_ref, o_ref, wout_ref, wup_ref, wdown_ref, h1_ref, n2_ref, ho_ref, cot_ref, dm_ref, g_buf, d_buf, sems,
):
    moves = Moves(sems)
    first = [moves.whole(*t) for t in ((o_far, o_ref), (wout_far, wout_ref), (x_far, x_ref))]
    ups, downs = Chunks(moves, wup_far, wup_ref, 1), Chunks(moves, wdown_far, wdown_ref, 0)
    gs, ds = (Chunks(moves, f, b, 1, True, True) for f, b in ((g_far, g_buf), (d_far, d_buf)))
    number = wup_far.shape[1] // CHUNK
    for wait in first:
        wait()
    for j in range(number):
        ups.start(j)
        downs.start(j)
    cot_there = moves.whole(cot_far, cot_ref)
    h1_ref[...] = dot(o_ref[...], wout_ref[...])
    start_norm(x_ref, h1_ref, n2_ref, gb_ref, ho_ref)
    kept = [moves.whole(*t) for t in ((h1_ref, h1_far), (n2_ref, n2_far))]

    def step(j, _):
        ups.wait(j)
        downs.wait(j)
        feed_chunk(n2_ref, wup_ref, wdown_ref, j, g_buf, d_buf, ho_ref, gs, ds, j)
        return 0

    lax.fori_loop(0, number, step, 0)
    kept.append(moves.whole(ho_ref, ho_far))
    cot_there()
    rows, seq = cot_ref.shape[0], cot_ref.shape[1] // 2
    mix = weave(seq)
    for r in range(rows):
        parted = dot_tn(mix, cot_ref[r]).astype(BF16)
        for i in range(2):
            at = (i * rows + r) * seq
            dm_ref[at : at + seq] = parted[i * seq : (i + 1) * seq]
    kept.append(moves.whole(dm_ref, dm_far))
    for wait in kept:
        wait()
    for j in range(number - 2, number):
        gs.wait(j)
        ds.wait(j)


def mlp_other_body(number_up, number_down, n2_far, part_far, g_in, d_in, gb_ref, *refs):
    ups_far, refs = refs[:number_up], refs[number_up:]
    downs_far, refs = refs[:number_down], refs[number_down:]
    g_far, d_far, ho_far, ao_far, n2_ref, wup_ref, wdown_ref, ho_ref, ao_ref, g_buf, d_buf, sems = refs
    moves = Moves(sems)
    up = Weight(moves, (None,) + ups_far, wup_ref, 1)
    down = Weight(moves, (None,) + downs_far, wdown_ref, 0)
    gs, ds = (Chunks(moves, f, b, 1, True, True) for f, b in ((g_far, g_buf), (d_far, d_buf)))
    n2_there = moves.whole(n2_far, n2_ref)
    up.start_others()
    down.start_others()
    part_there = moves.whole(part_far, ho_ref)
    number, half = up.number, n2_ref.shape[0] // 2
    n2_there()
    up.wait_others()

    def rise(i, _):
        j = number + i
        for sl in (slice(0, half), slice(half, 2 * half)):
            g, d = gelu_parts(dot(n2_ref[sl], chunk_of(wup_ref, j, 1)[...]))
            g_buf[j % number, sl] = g.astype(BF16)
            d_buf[j % number, sl] = d.astype(BF16)
        gs.start(j)
        ds.start(j)
        return 0

    lax.fori_loop(0, number, rise, 0)
    down.wait_others()
    part_there()

    def fall(i, _):
        j = number + i
        ho_ref[...] += dot(g_buf[j % number], chunk_of(wdown_ref, j, 0)[...])
        return 0

    lax.fori_loop(0, number, fall, 0)
    sent = moves.whole(ho_ref, ho_far)

    def norm(k, _):
        sl = pl.ds(pl.multiple_of(k * ROWS_AT_ONCE, ROWS_AT_ONCE), ROWS_AT_ONCE)
        normal, _ = norm_stats(ho_ref[sl])
        ao_ref[sl] = (normal * gb_ref[0:1] + gb_ref[2:3]).astype(BF16)
        return 0

    lax.fori_loop(0, ho_ref.shape[0] // ROWS_AT_ONCE, norm, 0)
    moves.whole(ao_ref, ao_far)()
    sent()
    for j in range(number, 2 * number):
        gs.wait(j)
        ds.wait(j)


def near_of(*arrays):
    return [pltpu.VMEM(t.shape, t.dtype) for t in arrays]


def far_of(*arrays):
    return [(t, FAR) for t in arrays]


def mlp_own(x, o, wout, gb, wup, wdown, cot):
    n, d = x.shape
    ff = 2 * wup.shape[1]
    h1, low, wide = sds((n, d), F32), sds((n, d), BF16), sds((n, ff), BF16)
    return resident(
        mlp_own_body,
        far_of(x, o, wout) + [gb] + far_of(wup, wdown, cot),
        far_of(h1, low, wide, wide, h1, sds((2 * n, d), BF16)),
        scratch=near_of(x, o, wout, wup, wdown, h1, low, h1, cot, sds((2 * n, d), BF16))
        + [pltpu.VMEM((2, n, CHUNK), BF16)] * 2
        + [pltpu.SemaphoreType.DMA((40,))],
        vmem=44,
        name="mlp_own",
    )


def mlp_other(n2, part, g, dgelu, gb, ups, downs):
    n, d = n2.shape
    ff = g.shape[1]
    return resident(
        functools.partial(mlp_other_body, len(ups), len(downs)),
        far_of(n2, part, g, dgelu) + [gb] + far_of(*ups, *downs),
        far_of(sds(g.shape, BF16), sds(g.shape, BF16), sds(part.shape, F32), sds(n2.shape, BF16)),
        scratch=near_of(n2, sds((d, ff), BF16), sds((ff, d), BF16), part, n2)
        + [pltpu.VMEM((ff // CHUNK // 2, n, CHUNK), BF16)] * 2
        + [pltpu.SemaphoreType.DMA((40,))],
        vmem=40,
        aliases={2: 0, 3: 1},
        name="mlp_other",
    )


def after_norm_back(
    moves, size, h1_ref, dn_ref, db_ref, wout_ref, gb_ref, sums_ref, dp_ref, do_ref, dh1_far, dp_far, do_far,
    inverse_ref=None,
):
    gain_sum = jnp.zeros_like(gb_ref[0:1])
    bias_sum = jnp.zeros_like(gb_ref[0:1])
    waits = []
    for i in range(h1_ref.shape[0] // size):
        sl = slice(i * size, (i + 1) * size)
        if inverse_ref is None:
            normal, inverse = norm_stats(h1_ref[sl])
        else:
            normal, inverse = h1_ref[sl], inverse_ref[sl, :1]
        dn = dn_ref[sl]
        gain_sum += jnp.sum(dn * normal, axis=0, keepdims=True)
        bias_sum += jnp.sum(dn, axis=0, keepdims=True)
        dh1 = db_ref[sl].astype(F32) + norm_back(dn, normal, inverse, gb_ref[1:2])
        dn_ref[sl] = dh1
        dp_ref[sl] = dh1.astype(BF16)
        at = pl.ds(i * size, size)
        waits += [moves.whole(a.at[at], b.at[at]) for a, b in ((dn_ref, dh1_far), (dp_ref, dp_far))]
        if i % 2:
            both = pl.ds((i - 1) * size, 2 * size)
            do_ref[both] = dot_nt(dp_ref[both], wout_ref[...]).astype(BF16)
            waits.append(moves.whole(do_ref.at[both], do_far.at[both]))
    sums_ref[0:1] = gain_sum
    sums_ref[1:2] = bias_sum
    return waits


def mlp_second_body(rows, seq, number_up, number_down, x_far, ho_far, o_far, dm_far, wout_far, gb_ref, *refs):
    mlp_second_work(rows, seq, x_far, ho_far, o_far, dm_far, wout_far, gb_ref, *in_pieces(refs, number_up, number_down))


def in_pieces(refs, *numbers):
    out = []
    for k in numbers:
        out.append(refs[:k])
        refs = refs[k:]
    return out + list(refs)


def mlp_second_work(
    rows, seq, x_far, ho_far, o_far, dm_far, wout_far, gb_ref, ups_far, downs_far,
    outs_far, outs2_far, n2_far, g_far, du_far, dh1_far, dp_far, do_far, sums_ref,
    x_ref, ho_ref, o_ref, cot_ref, wout_ref, wup_ref, wdown_ref, n2_ref, dm_ref,
    normal_ref, z_ref, dn_ref, dp_ref, do_ref, inverse_ref, g_buf, du_buf, sems,
):
    n = rows * seq
    moves = Moves(sems)
    halves = (slice(0, n), slice(n, 2 * n))
    first = [moves.whole(*t) for t in ((o_far.at[0], o_ref.at[0]), (wout_far, wout_ref))]
    up, down = Weight(moves, ups_far, wup_ref, 1), Weight(moves, downs_far, wdown_ref, 0)
    gs, dus = (Chunks(moves, f, b, 1, True, True) for f, b in ((g_far, g_buf), (du_far, du_buf)))
    number = 2 * up.number
    for wait in first:
        wait()
    x_there = moves.whole(x_far, x_ref)
    then = [moves.whole(*t) for t in ((o_far.at[1], o_ref.at[1]), (ho_far, ho_ref))]
    start_loads(up, down)
    dm_there = moves.whole(dm_far, dm_ref)
    for i, sl in enumerate(halves):
        if i:
            for wait in then:
                wait()
        z_ref[sl] = dot(o_ref[i], wout_ref[...])
        if i == 0:
            x_there()
        z_at, n2_at, normal_at, inverse_at = (t.at[pl.ds(i * n, n)] for t in (z_ref, n2_ref, normal_ref, inverse_ref))
        start_norm(x_ref if i == 0 else ho_ref, z_at, n2_at, gb_ref, None, normal_at, inverse_at)
    dm_there()
    mix = weave(seq)
    kept = [moves.whole(n2_ref, n2_far)]
    dn_ref[...] = jnp.zeros_like(dn_ref)

    def step(j, _):
        load_in_turn(j, up, down)

        @pl.when(j >= 2)
        def _():
            gs.wait(j - 2)
            dus.wait(j - 2)

        for sl in (slice(0, 2 * n),):
            u = dot(n2_ref[sl], chunk_of(wup_ref, j, 1)[...])
            dg = dot_nt(dm_ref[sl], chunk_of(wdown_ref, j, 0)[...])
            g, d = gelu_parts(u)
            g = g.astype(BF16)
            du = (dg * d).astype(BF16)
            g_buf[j % 2, sl] = g
            du_buf[j % 2, sl] = du
            z_ref[sl] += dot(g, chunk_of(wdown_ref, j, 0)[...])
            dn_ref[sl] += dot_nt(du, chunk_of(wup_ref, j, 1)[...])
        gs.start(j)
        dus.start(j)
        return 0

    lax.fori_loop(0, number, step, 0)
    for r in range(rows):
        pair = [slice(i * n + r * seq, i * n + (r + 1) * seq) for i in range(2)]
        z = jnp.concatenate([z_ref[s].astype(BF16) for s in pair], axis=0)
        cot_ref[r] = dot(mix, z).astype(BF16)
    half = rows // 2
    kept += [moves.whole(cot_ref.at[pl.ds(i * half, half)], far) for i, far in enumerate((outs_far, outs2_far))]
    kept += after_norm_back(
        moves, seq, normal_ref, dn_ref, dm_ref, wout_ref, gb_ref, sums_ref, dp_ref, do_ref, dh1_far, dp_far, do_far,
        inverse_ref,
    )
    for wait in kept:
        wait()
    for j in range(number - 2, number):
        gs.wait(j)
        dus.wait(j)


def mlp_second(x, ho, o2, dm, wout, gb, ups, downs, seq):
    n, d = x.shape
    ff = 2 * ups[0].shape[1]
    rows = n // seq
    low, wide, full = sds((2 * n, d), BF16), sds((2 * n, ff), BF16), sds((2 * n, d), F32)
    out = sds((rows // 2, 2 * seq, d), BF16)
    return resident(
        functools.partial(mlp_second_body, rows, seq, len(ups), len(downs)),
        far_of(x, ho, o2, dm, wout) + [gb] + far_of(*ups, *downs),
        far_of(out, out, low, wide, wide, full, low, low) + [sds((2, d), F32)],
        scratch=near_of(x, ho, o2, sds((rows, 2 * seq, d), BF16), wout, sds((d, ff), BF16), sds((ff, d), BF16), low, low, full, full, full, low, low, sds((2 * n, 128), F32))
        + [pltpu.VMEM((2, 2 * n, CHUNK), BF16)] * 2
        + [pltpu.SemaphoreType.DMA((64,))],
        vmem=60,
        name="mlp_second",
    )


def mlp_back_body(rows, seq, number_up, number_down, dy_far, h1_far, wout_far, gb_ref, d_far, *refs):
    mlp_back_work(rows, seq, dy_far, h1_far, wout_far, gb_ref, d_far, *in_pieces(refs, number_up, number_down))


def mlp_back_work(
    rows, seq, dy_far, h1_far, wout_far, gb_ref, d_far, ups_far, downs_far,
    du_far, dh1_far, dp_far, do_far, sums_ref,
    dy_ref, h1_ref, wout_ref, wup_ref, wdown_ref, d_ref, dm_ref, dn_ref, dp_ref, do_ref, du_buf, sems,
):
    moves = Moves(sems)
    first = moves.whole(dy_far, dy_ref)
    up, down = Weight(moves, ups_far, wup_ref, 1), Weight(moves, downs_far, wdown_ref, 0)
    ds, dus = Chunks(moves, d_far, d_ref, 1), Chunks(moves, du_far, du_buf, 1, True, True)
    number = 2 * up.number
    start_loads(down, up)
    for j in range(2):
        ds.start(j)
    then = [moves.later(*t) for t in ((wout_far, wout_ref), (h1_far, h1_ref))]
    first()
    dm_ref[...] = dy_ref[...].astype(BF16)
    dn_ref[...] = jnp.zeros_like(dn_ref)

    def step(j, _):
        load_in_turn(j, down, up)
        ds.wait(j)

        @pl.when(j + 2 < number)
        def _():
            ds.start(j + 2)

        @pl.when(j + 2 == number)
        def _():
            for start, _ in then:
                start()

        @pl.when(j >= 2)
        def _():
            dus.wait(j - 2)

        dg = dot_nt(dm_ref[...], chunk_of(wdown_ref, j, 0)[...])
        du = (dg * chunk_of(d_ref, j, 1)[...].astype(F32)).astype(BF16)
        du_buf[j % 2] = du
        dus.start(j)
        dn_ref[...] += dot_nt(du, chunk_of(wup_ref, j, 1)[...])
        return 0

    lax.fori_loop(0, number, step, 0)
    for _, wait in then:
        wait()
    kept = after_norm_back(
        moves, seq, h1_ref, dn_ref, dy_ref, wout_ref, gb_ref, sums_ref, dp_ref, do_ref, dh1_far, dp_far, do_far
    )
    for wait in kept:
        wait()
    for j in range(number - 2, number):
        dus.wait(j)


def mlp_back(dy, h1, wout, gb, dgelu, ups, downs, seq):
    n, d = dy.shape
    ff = dgelu.shape[1]
    low = sds((n, d), BF16)
    return resident(
        functools.partial(mlp_back_body, n // seq, seq, len(ups), len(downs)),
        far_of(dy, h1, wout) + [gb] + far_of(dgelu, *ups, *downs),
        far_of(dgelu, h1, low, low) + [sds((2, d), F32)],
        scratch=near_of(dy, h1, wout, sds((d, ff), BF16), sds((ff, d), BF16), dgelu, low, dy, low, low)
        + [pltpu.VMEM((2, n, CHUNK), BF16)]
        + [pltpu.SemaphoreType.DMA((48,))],
        vmem=48,
        name="mlp_back",
    )


def lanes_at(ref, start, size):
    return ref.at[:, pl.ds(pl.multiple_of(start, 128), size)]


def stack_rows(moves, pairs, target, start, size):
    copies, row = [], 0
    for far in pairs:
        copies.append(moves.later(lanes_at(far, start, size), target.at[pl.ds(row, far.shape[0])]))
        row += far.shape[0]
    return (lambda: [s() for s, _ in copies]), (lambda: [w() for _, w in copies])


def all_of(*parts):
    return (lambda: [s() for s, _ in parts]), (lambda: [w() for _, w in parts])


class InTurn:
    def __init__(self, *tiles):
        self.tiles, self.at = tiles, 0
        for start, _ in tiles[:2]:
            start()

    def next(self):
        self.tiles[self.at][1]()
        self.at += 1
        if self.at + 1 < len(self.tiles):
            self.tiles[self.at + 1][0]()


def place_of(quarter, y, me_ref):
    return quarter if y else 4 + (quarter ^ me_ref[1])


def packed(body, me, arrays, shape, scratch, flops, vmem, name):
    smem = pl.BlockSpec(memory_space=pltpu.SMEM)
    out = sds(shape, BF16)
    return resident(
        body,
        [(me, smem)] + far_of(*arrays),
        far_of(out, out),
        scratch=near_of(sds((2,) + shape, BF16)) + scratch + [pltpu.SemaphoreType.DMA((64,))],
        flops=flops,
        vmem=vmem,
        name=name,
    )


def grad_down_body(
    me_ref, g1_far, g2_far, dy_far, dm2_far, keep_far, go_far, out_ref, dy_ref, dm_ref, g_ref, acc_ref, sems
):
    low, group = me_ref[0] % 4, (me_ref[0] // 4) % 2
    ring, n, b = g_ref.shape[0], g1_far.shape[0], g_ref.shape[2]
    moves = Moves(sems)
    first, last = moves.take(2 * ring), moves.take(4)

    def tile(i):
        side, y, h = 1 - i // 4, (i // 2) % 2, i % 2
        quarter = ((me_ref[0] // 8) ^ side) * 2 + h
        at = jnp.where(y == 0, 4 + (quarter ^ me_ref[1]), quarter) * b
        return side, y, h, at

    def loads(i):
        at, slot = tile(i)[3], i % ring
        near = g_ref.at[slot]
        ends = ((g1_far, near.at[pl.ds(0, n)]), (g2_far, near.at[pl.ds(n, 2 * n)]))
        return [pltpu.make_async_copy(lanes_at(f, at, b), t, sems.at[first + 2 * slot + k]) for k, (f, t) in enumerate(ends)]

    def store(far, side, y):
        return pltpu.make_async_copy(out_ref.at[side, y], far.at[y], sems.at[last + side * 2 + y])

    ready = [moves.whole(dy_far, dy_ref), moves.whole(dm2_far, dm_ref.at[pl.ds(n, 2 * n)])]
    for i in range(2):
        for c in loads(i):
            c.start()
    for wait in ready:
        wait()
    dm_ref[:n] = dy_ref[...].astype(BF16)

    def step(i, _):
        side, y, h, _ = tile(i)
        for c in loads(i):
            c.wait()

        @pl.when(i + 2 < 8)
        def _():
            for c in loads(i + 2):
                c.start()

        acc_ref[...] = dot_tn(g_ref[i % ring], dm_ref[...]).reshape(acc_ref.shape)
        for s in range(4):
            out_ref[side, y, (h ^ group) * 4 + s] = acc_ref[s ^ low].astype(BF16)

        @pl.when((h == 1) & (side == 1))
        def _():
            store(go_far, 1, y).start()

        @pl.when((h == 1) & (side == 0))
        def _():
            store(keep_far, 0, y).start()

        return 0

    lax.fori_loop(0, 8, step, 0)
    for y in range(2):
        store(go_far, 1, y).wait()
        store(keep_far, 0, y).wait()


def grad_down(me, g1, g2, dy, dm2):
    n, d = dy.shape
    ff = g1.shape[1]
    b = ff // 8
    return packed(
        grad_down_body,
        me,
        (g1, g2, dy, dm2),
        (2, 8, b // 4, d),
        [
            pltpu.VMEM((n, d), F32),
            pltpu.VMEM((3 * n, d), BF16),
            pltpu.VMEM((3, 3 * n, b), BF16),
            pltpu.VMEM((4, b // 4, d), F32),
        ],
        2 * 3 * n * d * ff,
        40,
        "grad_down",
    )


CUT = 768
CUT_BACK = 1536


def swapped(s):
    return ((s >> 1) % 2) * 4 + ((s >> 2) % 2) * 2 + s % 2


def put_slots(out_ref, y, lanes, acc_ref, me):
    for s in range(16):
        out_ref[s // 8, y, s % 8, :, lanes] = acc_ref[s ^ me].astype(BF16)


def grad_up_body(
    me_ref, n1_far, n2_far, du1_far, du2_far, dp1_far, dp2_far, o1_far, o2_far, keep_far, go_far,
    out_ref, n_ref, t_ref, du_ref, dp_ref, o_ref, acc_ref, acc2_ref, sems,
):
    moves = Moves(sems)
    d, f = n_ref.shape[1], o_ref.shape[2]
    ring, c, n = du_ref.shape[0], du_ref.shape[2], du1_far.shape[0]
    first, last = moves.take(4 * ring), moves.take(4)

    def loads(i):
        y, t, slot = i // 2, i % 2, i % ring
        copies = []
        for k in range(2):
            quarter = 2 * t + k
            at = jnp.where(y == 0, 4 + (quarter ^ me_ref[1]), quarter) * f
            near = lanes_at(du_ref.at[slot], k * f, f)
            for far, rows in ((du1_far, pl.ds(0, n)), (du2_far, pl.ds(n, 2 * n))):
                copies.append((lanes_at(far, at, f), near.at[rows]))
        return [pltpu.make_async_copy(a, b, sems.at[first + 4 * slot + k]) for k, (a, b) in enumerate(copies)]

    def stores(y):
        return [
            pltpu.make_async_copy(out_ref.at[i, y], far.at[y], sems.at[last + 2 * y + i])
            for i, far in enumerate((keep_far, go_far))
        ]

    ready = stack_rows(moves, (n1_far, n2_far), n_ref, 0, d)
    ready[0]()
    for c0 in loads(0):
        c0.start()
    out_loads = [stack_rows(moves, (dp1_far, dp2_far), dp_ref, 0, d)]
    out_loads += [stack_rows(moves, (o1_far, o2_far), o_ref.at[y], (1 - y) * f, f) for y in range(2)]
    ready[1]()
    for c0 in loads(1):
        c0.start()
    t_ref[...] = n_ref[...].T

    def step(i, _):
        y, t = i // 2, i % 2
        for c0 in loads(i):
            c0.wait()

        @pl.when(i + 2 < 4)
        def _():
            for c0 in loads(i + 2):
                c0.start()

        @pl.when(i == 0)
        def _():
            for start, _ in out_loads:
                start()

        acc_ref[...] = dot(t_ref[...], du_ref[i % ring]).reshape(acc_ref.shape)
        put_slots(out_ref, y, pl.ds(pl.multiple_of(t * c, c), c), acc_ref, jnp.where(t == 0, me_ref[0], me_ref[2]))

        @pl.when(i == 1)
        def _():
            for _, wait in out_loads:
                wait()

        @pl.when(t == 1)
        def _():
            acc2_ref[...] = dot_tn(dp_ref[...], o_ref[y]).reshape(acc2_ref.shape)
            put_slots(out_ref, y, slice(2 * c, 2 * c + f), acc2_ref, me_ref[2])
            for s in stores(y):
                s.start()

        return 0

    lax.fori_loop(0, 4, step, 0)
    for y in range(2):
        for s in stores(y):
            s.wait()


def grad_up(me, n1, n2, du1, du2, dp1, dp2, o1, o2):
    n, d = n1.shape
    ff = du1.shape[1]
    f, c = o1.shape[1] // 2, ff // 4
    return packed(
        grad_up_body,
        me,
        (n1, n2, du1, du2, dp1, dp2, o1, o2),
        (2, 8, d // 16, 2 * c + f),
        [
            pltpu.VMEM((3 * n, d), BF16),
            pltpu.VMEM((d, 3 * n), BF16),
            pltpu.VMEM((3, 3 * n, c), BF16),
            pltpu.VMEM((3 * n, d), BF16),
            pltpu.VMEM((2, 3 * n, f), BF16),
            pltpu.VMEM((16, d // 16, c), F32),
            pltpu.VMEM((16, d // 16, f), F32),
        ],
        2 * 3 * n * d * (ff + d),
        56,
        "grad_up",
    )


def grad_qkv_body(me_ref, ae_far, ao_far, de_far, do_far, keep_far, go_far, out_ref, a_ref, t_ref, d_ref, acc_ref, sems):
    moves = Moves(sems)
    d = a_ref.shape[1]
    f = de_far.shape[2] // 2
    ready = stack_rows(moves, (ae_far, ao_far), a_ref, 0, d)
    n, first = ae_far.shape[0], moves.take(6)

    def loads(j):
        return [
            pltpu.make_async_copy(far.at[j], d_ref.at[j, pl.ds(k * n, n)], sems.at[first + 2 * j + k])
            for k, far in enumerate((de_far, do_far))
        ]

    ready[0]()
    for c in loads(0):
        c.start()
    ready[1]()
    for j in (1, 2):
        for c in loads(j):
            c.start()
    t_ref[...] = a_ref[...].T

    def step(j, _):
        for c in loads(j):
            c.wait()
        acc_ref[...] = dot(t_ref[...], d_ref[j]).reshape(acc_ref.shape)
        lanes = pl.ds(pl.multiple_of(j * f, f), f)
        for s in range(16):
            block = acc_ref[s ^ me_ref[0]].astype(BF16)
            out_ref[s // 8, 1, s % 8, :, lanes] = block[:, :f]
            out_ref[s // 8, 0, s % 8, :, lanes] = block[:, f:]
        return 0

    lax.fori_loop(0, 3, step, 0)
    sent = [moves.whole(out_ref.at[i], far) for i, far in ((1, go_far), (0, keep_far))]
    for wait in sent:
        wait()


def grad_qkv(me, ae, ao, dqkv_e, dqkv_o):
    n, d = ae.shape
    f = dqkv_e.shape[2] // 2
    return packed(
        grad_qkv_body,
        me,
        (ae, ao, dqkv_e, dqkv_o),
        (2, 8, d // 16, 3 * f),
        [
            pltpu.VMEM((2 * n, d), BF16),
            pltpu.VMEM((d, 2 * n), BF16),
            pltpu.VMEM((3, 2 * n, 2 * f), BF16),
            pltpu.VMEM((16, d // 16, 2 * f), F32),
        ],
        2 * 2 * 3 * n * d * 2 * f,
        40,
        "grad_qkv",
    )


def packed_call(body, grid, me, ins, outs, scratch=(), flops=0, aliases={}, name=None):
    return pl.pallas_call(
        body,
        grid_spec=pltpu.PrefetchScalarGridSpec(
            num_scalar_prefetch=1,
            grid=grid,
            in_specs=[s for _, s in ins],
            out_specs=[s for _, s in outs],
            scratch_shapes=scratch,
        ),
        out_shape=[a for a, _ in outs],
        input_output_aliases=aliases,
        compiler_params=pltpu.CompilerParams(
            dimension_semantics=("arbitrary",) * len(grid), vmem_limit_bytes=VMEM_LIMIT
        ),
        cost_estimate=pl.CostEstimate(flops=int(flops) // 16, bytes_accessed=0, transcendentals=0),
        name=name,
    )(me, *[a for a, _ in ins])


def unpack_down_body(me_ref, part_ref, *refs):
    low, rows = me_ref[0] % 8, part_ref.shape[1]
    for b in range(8):
        refs[-1][b * rows : (b + 1) * rows] = part_ref[swapped(b ^ low)].astype(F32)


def unpack_down(me, side, part, into=()):
    _, r, w = part.shape
    half = 8 * r
    at = lambda me: (me[0] // 8) ^ side
    ins = [(part, pl.BlockSpec(part.shape, lambda i, me: (0, 0, 0)))]
    ins += [(t, pl.BlockSpec(memory_space=pl.ANY)) for t in into]
    return packed_call(
        unpack_down_body,
        (1,),
        me,
        ins,
        [(sds((2 * half, w), F32), pl.BlockSpec((half, w), lambda i, me: (at(me), 0)))],
        aliases={2 + i: i for i in range(len(into))},
        name="unpack_down",
    )[0]


def unpack_rest_body(side, me_ref, part_ref, *refs):
    up_far, out_far, qkv_far, up_st, wide, out_st, qkv_st, sems = refs[-8:]
    moves = Moves(sems)
    left, right = me_ref[0] % 8, me_ref[2] % 8
    rows, half = part_ref.shape[1], 8 * part_ref.shape[1]
    d, f = up_st.shape[1], wide.shape[1]
    base = ((me_ref[0] // 8) ^ side) * half
    sent = []
    for b in range(8):
        sl = slice(b * rows, (b + 1) * rows)
        up_st[sl, :CUT] = part_ref[b ^ left, :, :CUT].astype(F32)
        up_st[sl, CUT:] = part_ref[swapped(b ^ right), :, CUT:d].astype(F32)
        wide[sl] = part_ref[b ^ right, :, d : d + f].astype(F32)
        if b % 4 == 3:
            start, size = (b - 3) * rows, 4 * rows
            at = pl.ds(pl.multiple_of(base + start, 8), size)
            sent.append(moves.whole(up_st.at[pl.ds(start, size)], up_far.at[at]))
    out_st[...] = wide[...].T
    sent.append(moves.whole(out_st, lanes_at(out_far, base, half)))
    for j in range(3):
        for b in range(8):
            sl = slice(b * rows, (b + 1) * rows)
            qkv_st[j, sl] = part_ref[swapped(b ^ left), :, d + (j + 1) * f : d + (j + 2) * f].astype(F32)
        sent.append(moves.whole(qkv_st.at[j], qkv_far.at[j, pl.ds(pl.multiple_of(base, 8), half)]))
    for wait in sent:
        wait()


def unpack_rest(me, side, part, into=()):
    _, r, w = part.shape
    half = 8 * r
    d, f = CUT_BACK, (w - CUT_BACK) // 4
    smem = pl.BlockSpec(memory_space=pltpu.SMEM)
    outs = [sds((2 * half, d), F32), sds((f, 2 * half), F32), sds((3, 2 * half, f), F32)]
    stages = [sds((half, d), F32), sds((half, f), F32), sds((f, half), F32), sds((3, half, f), F32)]
    return resident(
        functools.partial(unpack_rest_body, side),
        [(me, smem), part] + far_of(*into),
        far_of(*outs),
        scratch=near_of(*stages) + [pltpu.SemaphoreType.DMA((8,))],
        vmem=24,
        aliases={2 + i: i for i in range(len(into))},
        name="unpack_rest",
    )


def fold(*parts):
    return sum(p.astype(F32) for p in parts).astype(BF16)


def after(value, *first):
    return lax.optimization_barrier((value, first))[0]


class Chunk:
    def __init__(self, keep, got):
        self.keep, self.got = keep, got
        self.sent = None

    def wait(self, *also):
        self.got, also = lax.optimization_barrier((self.got, also))
        return also

    def to_partner(self):
        total = fold(self.keep, self.got)
        self.keep, self.sent = total[1], total[0]
        self.got = lax.ppermute(self.sent, "tensor", FLIP)

    def gather_core(self):
        self.got = lax.ppermute(self.keep, "core", FLIP)


def add(k, g):
    return (k.astype(F32) + g.astype(F32)).astype(BF16)


def phase_shapes(mode, parts):
    shapes = [p[0].shape for p in parts]
    s = shapes[0]
    if mode == "half":
        out = s[:-3] + (s[-3] // 2,) + s[-2:]
        return [out, out]
    if mode == "partner":
        return [s[1:], s[1:]]
    if mode == "last":
        out = (s[0] // 2, s[1], sum(t[2] for t in shapes))
        return [out, out]
    if mode == "sum":
        return [s]
    if mode == "split":
        return [(2 * s[0], s[1], CUT_BACK), (2 * s[0], s[1], s[2] - CUT_BACK)]
    return [(2 * s[0], s[1], sum(t[2] for t in shapes))]


def phase_part(mode, parts, outs):
    if mode == "half":
        (k, g), n = parts[0], outs[0].shape[-3]
        lead = (slice(None),) * (len(k.shape) - 3)
        for i, out in enumerate(outs):
            at = lead + (slice(i * n, (i + 1) * n),)
            out[...] = add(k[at], g[at])
    elif mode == "partner":
        k, g = parts[0]
        for i, out in zip((1, 0), outs):
            out[...] = add(k[i], g[i])
    elif mode == "last":
        n, lane = outs[0].shape[0], 0
        for k, g in parts:
            for i, out in enumerate(outs):
                at = slice(i * n, (i + 1) * n)
                out[:, :, lane : lane + k.shape[2]] = add(k[at], g[at])
            lane += k.shape[2]
    elif mode == "sum":
        outs[0][...] = add(parts[0][0][...], parts[0][1][...])
    elif mode == "split":
        for i, ref in enumerate(parts[0]):
            at = slice(i * ref.shape[0], (i + 1) * ref.shape[0])
            outs[0][at] = ref[:, :, :CUT_BACK]
            outs[1][at] = ref[:, :, CUT_BACK:]
    else:
        lane = 0
        for pair in parts:
            for i, ref in enumerate(pair):
                outs[0][i * ref.shape[0] : (i + 1) * ref.shape[0], :, lane : lane + ref.shape[2]] = ref[...]
            lane += pair[0].shape[2]


def phase(*items):
    shapes = [phase_shapes(*t) for t in items]

    def body(*refs):
        at = sum(2 * len(parts) for _, parts in items)
        ins, outs = list(refs[:at]), list(refs[at:])
        for (mode, parts), made in zip(items, shapes):
            mine = [(ins.pop(0), ins.pop(0)) for _ in parts]
            phase_part(mode, mine, [outs.pop(0) for _ in made])

    flat = resident(
        body,
        [t for _, parts in items for pair in parts for t in pair],
        [sds(s, BF16) for made in shapes for s in made],
        vmem=16,
        name="phase",
    )
    flat = list(flat)
    return [[flat.pop(0) for _ in made] for made in shapes]


class Hops(Chunk):
    def __init__(self, outer, keep, got):
        super().__init__(keep, got)
        self.axes = {"x": ("x", 2, 1), "z": ("o", outer, 1), "w": ("o", outer, 2)}
        self.extra = [("o", outer, 1 << b) for b in range(2, outer.bit_length() - 1)]

    def over(self, way, t):
        return lax.ppermute(t, "tensor", FLIP) if way == "partner" else flip_bit(t, *self.axes[way])

    def send(self, *parts):
        self.keep, self.sent, self.got = [], [], []
        for total, way in parts:
            if way == "partner":
                keep, sent = total[1], total[0]
            else:
                half = total.shape[-3] // 2
                keep, sent = total[..., :half, :, :], total[..., half:, :, :]
            self.keep.append(keep)
            self.sent.append(sent)
            self.got.append(self.over(way, sent))

    def fold_first(self):
        total = fold(self.keep, self.got)
        half = total.shape[1] // 2
        return [part for lanes in (total[..., :CUT], total[..., CUT:]) for part in (lanes[:, :half], lanes[:, half:])]

    def first(self, parts):
        self.keep, self.sent = [parts[0], parts[2]], [parts[1], parts[3]]
        self.got = [self.over("x", parts[1]), self.over("z", parts[3])]

    def first_hop(self, way):
        self.send((fold(self.keep, self.got), way))

    def parts(self):
        return list(zip(self.keep, self.got))

    def hop(self, *ways):
        items = [("partner" if w == "partner" else "half", [p]) for w, p in zip(ways, self.parts())]

        def then(made):
            self.keep, self.sent = [m[0] for m in made], [m[1] for m in made]
            self.got = [self.over(w, s) for w, s in zip(ways, self.sent)]

        return items, then

    def absorb(self, other):
        self.keep, self.got = self.keep + other.keep, self.got + other.got

    def last_hop(self):
        def then(made):
            ((keep, sent),) = made
            self.keep, self.sent = [keep], [sent]
            self.got = [self.over("w", sent)]

        return [("last", self.parts())], then

    def back_first(self):
        def then(made):
            ((total,),) = made
            for s in self.extra:
                total = fold(total, flip_bit(total, *s))
            self.keep = self.sent = [total]
            self.got = [self.over("w", total)]

        return [("sum", self.parts())], then

    def back(self, *ways):
        if len(ways) == 2 and len(self.keep) == 1:
            items = [("split", self.parts())]
        else:
            items = [("join", [p]) for p in self.parts()]

        def then(made):
            self.keep = self.sent = [t for m in made for t in m]
            self.got = [self.over(w, t) for w, t in zip(ways, self.keep)]

        return items, then

    def back_core(self):
        def then(made):
            ((self.keep,),) = made
            self.sent = self.keep
            self.gather_core()

        return [("join", self.parts())], then


def all_steps(*steps):
    made = phase(*[item for items, _ in steps for item in items])
    for items, then in steps:
        then(made[: len(items)])
        made = made[len(items) :]


def mask_biases(seg):
    seq = seg.shape[1]
    place = jnp.arange(seq, dtype=jnp.int32)
    same = seg[:, :, None] == seg[:, None, :]
    below = (place[:, None] < place[None, :])[None]
    incl = (place[:, None] <= place[None, :])[None]
    bias = lambda m: jnp.where(same & m, 0.0, NEG).astype(F32)
    return bias(incl), bias(below)


def sync(*values):
    return lax.optimization_barrier(values)


class Link:
    def __init__(self, outer, w_qkv, w_out, w_up, w_down):
        self.outer = outer
        self.own = (w_qkv, w_out, w_up, w_down)
        self.core_at, self.x_at, o = (lax.axis_index(a) for a in ("core", "x", "o"))
        bits = {"x": self.x_at, "z": o % 2, "w": (o // 2) % 2}
        self.fetch_bits = self.core_at * 2 + self.x_at
        slots = []
        for order in ("xzw", "zxw"):
            slot = self.core_at
            for name in order:
                slot = slot * 2 + bits[name]
            slots.append(slot)
        self.me = jnp.stack([slots[0], self.fetch_bits, slots[1]]).astype(jnp.int32)
        self.me_z = self.me[2:0:-1]

    def quarter(self, own):
        flat = own.reshape(-1, own.shape[-1])
        return take_half(take_half(flat, self.core_at), self.x_at)

    def over_x(self, t):
        return lax.ppermute(t, "x", FLIP)

    def fetch(self, own_work):
        own = self.own
        size = own[2].shape[1] // 4
        part = lambda t, axis, bits: lax.dynamic_slice_in_dim(t, bits * size, size, axis)
        pieces = [
            self.quarter(own[1]),
            part(own[2], 1, self.fetch_bits),
            jnp.concatenate([part(own[3], 0, self.fetch_bits), part(own[3], 0, self.fetch_bits ^ 1)], axis=0),
        ]
        qkv = self.partner(self.quarter(own[0]))
        up, out, down = (self.partner(pieces[i]) for i in (1, 0, 2))
        qkv, own_work = sync(qkv, own_work)
        qkv, out, up = sync(ordered(self.x_at, qkv, self.over_x(qkv)).reshape(-1, qkv.shape[-1]), out, up)
        qkv_core, out_x, up_x = self.core(qkv), self.over_x(out), self.over_x(up)
        qkv = ordered(self.core_at, qkv, qkv_core).reshape(own[0].shape)

        def join_out(*work):
            nonlocal out, out_x
            work, out, out_x = sync(work, out, out_x)
            out = ordered(self.x_at, out, out_x).reshape(-1, out.shape[-1])
            out = ordered(self.core_at, out, self.core(out)).reshape(own[1].shape)
            return work, jnp.concatenate([own[1], out], axis=0)

        def pieces_of(*work):
            up_there, down_there, work = sync(up_x, down, work)
            ups = (own[2], up, up_there, self.core(up), self.core(up_there))
            return ups, (own[3], down_there, self.core(down_there)), work

        return own_work, own[0], qkv, jnp.concatenate([own[0], qkv], axis=2), join_out, pieces_of

    def partner(self, t):
        return lax.ppermute(t, "tensor", FLIP)

    def core(self, t):
        return lax.ppermute(t, "core", FLIP)

    def chunk(self, keep, got):
        return Chunk(keep, got)

    def hops(self, keep, got):
        return Hops(self.outer, keep, got)

    def small_steps(self):
        return [("core", 2, 1), ("tensor", 2, 1)] + steps_of(self.outer)

    def flip(self, t, step):
        return flip_bit(t, *step)


def local_part(x, seg, cot, gb, link):
    rows, seq = seg.shape
    n, width = x.shape
    me, me_z = link.me, link.me_z
    incl, strict = mask_biases(seg)
    normal, _ = norm_stats(x.astype(F32))
    a_e = (normal * gb[0] + gb[2]).astype(BF16)
    first = attend_first(a_e, link.own[0], incl)
    (a_e, first, cot, me, me_z), wq_own, fetched, wqkv, join_out, pieces_of = link.fetch((a_e, first, cot, me, me_z))
    second = attend_first(a_e, fetched, incl)
    qkv_e, o1 = (jnp.concatenate([s, t], axis=-1) for s, t in zip(first[:2], second[:2]))
    lse1 = jnp.concatenate([first[2], second[2]], axis=0).reshape(-1, GROUP // HD, n)
    (qkv_e, o1, lse1, wqkv), wout = join_out(qkv_e, o1, lse1, wqkv)
    h1, n2_1, g1, d1, part_one, dm2 = mlp_own(x, o1, wout, gb, link.own[2], link.own[3], cot)
    ups, downs, (n2_1, part_one) = pieces_of(n2_1, part_one)
    g1, d1, ho, a_o = mlp_other(n2_1, part_one, g1, d1, gb, ups[1:], downs[1:])
    qkv_o, o2, lse2 = attend_second(a_o, wqkv, incl, strict, qkv_e, o1, lse1)
    out, out_two, n2_2, g2, du2, dh1_2, dp2, do2, sums2 = mlp_second(x, ho, o2, dm2, wout, gb, ups, downs, seq)
    out_got = link.partner(out)
    dqkv_o, part, dy, sums_o = attend_back(wqkv, incl, strict, qkv_e, qkv_o, o2, lse2, do2, dh1_2, ho, gb)
    o2_flat = o2.reshape(2 * n, width)

    out_got, dy = sync(out_got, dy)
    quarter = out_two.shape[1] // 2
    out_last = [link.partner(after(out_two[:, :quarter], out_got))]
    down_keep, down_go = grad_down(me_z, g1, g2, dy, dm2)
    down_keep, down_go, out_last[0] = sync(down_keep, down_go, out_last[0])
    out_last.append(link.partner(after(out_two[:, quarter:], down_go)))
    down = link.hops(down_keep, link.core(down_go))
    dy = after(dy, down_go)
    du1, dh1_1, dp1, do1, sums1 = mlp_back(dy, h1, wout, gb, d1, ups, downs, seq)
    du1, dp1, do1, out_last[1] = down.wait(du1, dp1, do1, out_last[1])
    down.to_partner()
    up_keep, up_go = grad_up(me, n2_1, n2_2, after(du1, down.sent), du2, dp1, dp2, o1, o2_flat)
    do1 = after(do1, up_go)
    dqkv_e, gt, sums_e = attend_back_even(wqkv, incl, qkv_e, o1, lse1, do1, o2, lse2, do2, part, dh1_1, dh1_2, x, gb)
    dqkv_e, gt, sums_e, up_go = down.wait(dqkv_e, gt, sums_e, up_go)
    up = link.hops(up_keep, link.core(up_go))
    down.keep, down.got = [down.keep], [down.got]
    all_steps(down.hop("z"))
    small = jnp.stack([sums_e[0] + sums_o[0], sums1[0] + sums2[0], sums_e[1] + sums_o[1], sums1[1] + sums2[1], sums_o[2]])
    qkv_keep, qkv_go = grad_qkv(me, a_e, a_o, after(dqkv_e, *down.sent), dqkv_o)
    up_parts = up.fold_first()
    qkv_keep, qkv_go, down.got, up_parts = sync(qkv_keep, qkv_go, down.got, up_parts)
    out = link.finish(
        jnp.concatenate([out, out_two], axis=0),
        jnp.concatenate([out_got, jnp.concatenate(after(out_last, up_parts), axis=1)], axis=0),
        link.out_shape,
    )
    qkv = link.hops(qkv_keep, link.core(qkv_go))
    small_steps = iter(link.small_steps())
    small_got = link.flip(after(small, qkv_go), next(small_steps))

    chunks = [up, qkv]

    def wait_all():
        nonlocal small, small_got
        got, small_got = sync([c.got for c in chunks], small_got)
        for c, g in zip(chunks, got):
            c.got = g
        if small_got is not None:
            small = small + small_got
            step = next(small_steps, None)
            small_got = None if step is None else link.flip(small, step)

    chunks.remove(up)
    wait_all()
    up.first(up_parts)
    qkv.first_hop("partner")
    all_steps(down.hop("x"))
    chunks += [up, down]
    (out,) = up.wait(out)
    wait_all()
    all_steps(up.hop("z", "partner"), qkv.hop("x"), down.hop("w"))
    wait_all()
    all_steps(up.hop("partner", "x"), qkv.hop("z"), down.back_first())
    half = gt.shape[0] // 2
    gt_got = [link.partner(after(gt[:half], *up.sent))]
    wait_all()
    up.absorb(qkv)
    chunks.remove(qkv)
    all_steps(up.last_hop(), down.back("z"))
    gt_got.append(link.partner(after(gt[half:], *up.sent)))
    (gt_got[0],) = up.wait(gt_got[0])
    wait_all()
    all_steps(up.back_first(), down.back("x"))
    (gt_got[1],) = up.wait(gt_got[1])
    wait_all()
    while small_got is not None:
        wait_all()
    all_steps(up.back("z", "x"), down.back_core())
    wait_all()
    all_steps(up.back("x", "z"))
    g_down = unpack_down(me_z, 0, after(down.keep, *up.sent))
    g_down = unpack_down(me_z, 1, down.got, (g_down,))
    gt = link.finish(gt, jnp.concatenate(gt_got, axis=0), link.tokens_shape).astype(F32)
    small = (small[0:2], small[2:4], small[4])
    g_down, gt, small = up.wait(g_down, gt, small)
    all_steps(up.back_core())
    g_rest = unpack_rest(me, 0, up.keep)
    g_rest = up.wait(*g_rest)
    g_up, g_out, g_qkv = unpack_rest(me, 1, up.got, g_rest)
    return out, gt, (g_qkv, g_out, g_up, g_down), small


def shards(outer, tokens, segments, pass_embed, w_qkv, w_out, w_up, w_down, gain, bias, cotangent):
    ty = lax.axis_index("tensor")
    rows = tokens.shape[0] // 2
    width = tokens.shape[2]
    mine = lambda t: lax.dynamic_slice_in_dim(t, ty * rows, rows, 0)
    x = mine(tokens).reshape(-1, width)
    gb = jnp.concatenate([gain, bias, pass_embed[None]], axis=0)
    link = Link(outer, w_qkv, w_out, w_up, w_down)
    link.out_shape, link.tokens_shape = cotangent.shape, tokens.shape
    link.finish = lambda mine, theirs, shape: ordered(ty, mine, theirs).reshape(shape)
    out, gt, grads, small = local_part(x, mine(segments), mine(cotangent), gb, link)
    return out, gt, *grads, *small


def solution(mesh):
    outer = mesh.shape["dp"] // 4
    fine = Mesh(mesh.devices.reshape(outer, 2, 2, mesh.shape["tensor"]), ("o", "x", "core", "tensor"))
    rows = ROWS_OVER
    placed = (
        P(rows, None, None),
        P(rows, None),
        P(),
        P(None, None, "tensor"),
        P("tensor", None),
        P(None, "tensor"),
        P("tensor", None),
        P(),
        P(),
        P(rows, None, None),
    )

    def body(*args):
        return shards(outer, *args)

    return jax.shard_map(
        body,
        mesh=fine,
        in_specs=placed,
        out_specs=(
            P(rows, None, None),
            P(rows, None, None),
            P(None, None, "tensor"),
            P("tensor", None),
            P(None, "tensor"),
            P("tensor", None),
            P(),
            P(),
            P(),
        ),
        check_vma=False,
    )
```

```python
import functools

import jax
import jax.numpy as jnp
from jax import lax
from jax.experimental import pallas as pl
from jax.experimental.pallas import tpu as pltpu
from jax.sharding import Mesh
from jax.sharding import PartitionSpec as P

HD = 64
EPS = 1e-05
NEG = -1000000000.0
F32 = jnp.float32
BF16 = jnp.bfloat16
ROWS_OVER = ("o", "x", "core")
FLIP = ((0, 1), (1, 0))
VMEM_LIMIT = 16 * 1024 * 1024


def ordered(flag, mine, theirs):
    first = flag == 0
    return jnp.stack([jnp.where(first, mine, theirs), jnp.where(first, theirs, mine)])


def take_half(array, index):
    half = array.shape[0] // 2
    return lax.dynamic_slice_in_dim(array, index * half, half, 0)


def flip_bit(array, axis, size, bit):
    return lax.ppermute(array, axis, [(i, i ^ bit) for i in range(size)])


def steps_of(outer):
    steps = [("x", 2, 1)]
    bit = 1
    while bit < outer:
        steps.append(("o", outer, bit))
        bit *= 2
    return steps


def my_bit(axis, bit):
    return (lax.axis_index(axis) // bit) % 2


def dot(a, b):
    return lax.dot_general(a, b, (((1,), (0,)), ((), ())), preferred_element_type=F32)


def dot_nt(a, b):
    return lax.dot_general(a, b, (((1,), (1,)), ((), ())), preferred_element_type=F32)


def dot_tn(a, b):
    return lax.dot_general(a, b, (((0,), (0,)), ((), ())), preferred_element_type=F32)


def norm_stats(h):
    centred = h - jnp.mean(h, axis=-1, keepdims=True)
    inverse = lax.rsqrt(jnp.mean(centred * centred, axis=-1, keepdims=True) + EPS)
    return centred * inverse, inverse


def norm_back(grad, normal, inverse, gain):
    scaled = grad * gain
    centre = jnp.mean(scaled, axis=-1, keepdims=True)
    proj = jnp.mean(scaled * normal, axis=-1, keepdims=True)
    return inverse * (scaled - centre - normal * proj)


def gelu_parts(u):
    c = 0.7978845608028654
    a = 0.044715 * c
    square = u * u
    half = 0.5 + 0.5 * jnp.tanh(u * (c + a * square))
    g = u * half
    return g, half + g * (1.0 - half) * (2.0 * c + 6.0 * a * square)


def whole(shape):
    return pl.BlockSpec(shape, lambda *_: (0,) * len(shape))


def call(body, grid, ins, outs, scratch=(), cost=(0, 0), name=None, vmem=VMEM_LIMIT):
    return pl.pallas_call(
        body,
        grid=grid,
        in_specs=[s for _, s in ins],
        out_specs=[s for _, s in outs],
        out_shape=[a for a, _ in outs],
        scratch_shapes=scratch,
        compiler_params=pltpu.CompilerParams(
            dimension_semantics=("arbitrary",) * len(grid), vmem_limit_bytes=vmem
        ),
        cost_estimate=pl.CostEstimate(
            flops=int(cost[0]) // 16, bytes_accessed=int(cost[1]), transcendentals=0
        ),
        name=name,
    )(*[a for a, _ in ins])


FAR = pl.BlockSpec(memory_space=pl.ANY)


def resident(body, ins, outs, scratch=(), flops=0, vmem=16, aliases={}, name=None):
    spec = pl.BlockSpec(memory_space=pltpu.VMEM)
    ins, outs = ([o if isinstance(o, tuple) else (o, spec) for o in t] for t in (ins, outs))
    ins = [(pltpu.with_memory_space_constraint(a, pltpu.HBM) if s is FAR else a, s) for a, s in ins]
    outs = [(pltpu.HBM(a.shape, a.dtype) if s is FAR else a, s) for a, s in outs]
    return pl.pallas_call(
        body,
        in_specs=[s for _, s in ins],
        out_specs=[s for _, s in outs],
        out_shape=[a for a, _ in outs],
        scratch_shapes=scratch,
        input_output_aliases=aliases,
        compiler_params=pltpu.CompilerParams(vmem_limit_bytes=vmem * 1024 * 1024),
        cost_estimate=pl.CostEstimate(flops=int(flops) // 16, bytes_accessed=0, transcendentals=0),
        name=name,
    )(*[a for a, _ in ins])


def sds(shape, dtype):
    return jax.ShapeDtypeStruct(shape, dtype)


QB = 128
GROUP = 256


def lanes_of(ref, g):
    return ref.at[(slice(None),) * (len(ref.shape) - 1) + (pl.ds(pl.multiple_of(g * GROUP, GROUP), GROUP),)]


class Moves:
    def __init__(self, sems):
        self.sems, self.used = sems, 0

    def take(self, number):
        self.used += number
        return self.used - number

    def whole(self, source, target):
        copy = pltpu.make_async_copy(source, target, self.sems.at[self.take(1)])
        copy.start()
        return copy.wait

    def later(self, source, target):
        sem = self.sems.at[self.take(1)]
        copy = lambda: pltpu.make_async_copy(source, target, sem)
        return (lambda: copy().start()), (lambda: copy().wait())

    def groups(self, source, target):
        first = self.take(source.shape[-1] // GROUP)

        def copy(g):
            return pltpu.make_async_copy(lanes_of(source, g), lanes_of(target, g), self.sems.at[first + g])

        return (lambda g: copy(g).start()), (lambda g: copy(g).wait())


def cat_heads(t, scale=1.0):
    lane = lax.broadcasted_iota(jnp.int32, (1, 2 * HD), 1)
    parts = [t * jnp.where((lane < HD) == (h == 0), scale, 0.0).astype(t.dtype) for h in range(2)]
    return jnp.concatenate(parts, axis=0)


def own_lanes(t, scale=None):
    if scale is not None:
        t = t * scale
    return jnp.concatenate([t[:HD, :QB], t[HD:, QB:]], axis=0)


def twice(t):
    return jnp.concatenate([t, t], axis=1)


def pair_row(rows, p):
    return jnp.concatenate([rows[2 * p : 2 * p + 1], rows[2 * p + 1 : 2 * p + 2]], axis=1)


def put_pair(ref, p, cols, value):
    ref[2 * p : 2 * p + 1, cols] = value[:, :QB]
    ref[2 * p + 1 : 2 * p + 2, cols] = value[:, QB:]


def columns(t, r, seq, qb):
    return t[:, pl.ds(pl.multiple_of(r * seq + qb * QB, QB), QB)]


def rows_of(r, seq, qb):
    return pl.ds(pl.multiple_of(r * seq + qb * QB, QB), QB)


def in_turn(arrive, group, groups):
    for _, wait in arrive:
        wait(group)

    @pl.when(group + 2 < groups)
    def _():
        for start, _ in arrive:
            start(group + 2)


def attend_first_body(rows, seq, pairs, a_ref, w_ref, bias_ref, qkv_ref, o_ref, lse_ref):
    a = a_ref[...]
    for j in range(3):
        qkv_ref[j] = dot(a, w_ref[j]).astype(BF16)
    for r in range(rows):
        work = []
        for p in range(pairs):
            ln = slice(p * 2 * HD, (p + 1) * 2 * HD)
            k = qkv_ref[1, r * seq : (r + 1) * seq, ln]
            for b in range(seq // QB):
                sl, n = slice(r * seq + b * QB, r * seq + (b + 1) * QB), (b + 1) * QB
                q = cat_heads(qkv_ref[0, sl, ln], HD**-0.5)
                s = dot_nt(k[:n], q) + twice(bias_ref[r, :n, b * QB : n])
                work.append((p, ln, sl, n, s))
        done = []
        for p, ln, sl, n, s in work:
            top = jnp.max(s, axis=0, keepdims=True)
            e = jnp.exp(s - top)
            mass = jnp.sum(e, axis=0, keepdims=True)
            put_pair(lse_ref, p, sl, top + jnp.log(mass))
            done.append((e.astype(BF16), 1.0 / mass))
        for (p, ln, sl, n, _), (e, inv) in zip(work, done):
            vt = qkv_ref[2, r * seq : (r + 1) * seq, ln].T
            o_ref[sl, ln] = own_lanes(dot(vt[:, :n], e), inv).T.astype(BF16)


def attend_first(a, w, bias):
    rows, seq = bias.shape[0], bias.shape[1]
    n, d = a.shape
    f = w.shape[2]
    return resident(
        functools.partial(attend_first_body, rows, seq, f // (2 * HD)),
        (a, w, bias),
        [sds((3, n, f), BF16), sds((n, f), BF16), sds((f // HD, n), F32)],
        flops=6 * n * d * f + 16 * n * seq * f,
        name="attend_first",
    )


def attend_second_body(
    rows, seq, a_far, w_far, incl_far, strict_far, qkve_far, o1_far, lse1_ref,
    qkvo_far, o2_far, lse2_ref,
    a_ref, w_ref, incl_ref, strict_ref, qkve_ref, o1_ref, qkvo_ref, o2_ref, sems,
):
    groups = lse1_ref.shape[0]
    moves = Moves(sems)
    first = moves.take(6)

    def weight(j):
        return pltpu.make_async_copy(w_far.at[j], w_ref.at[j], sems.at[first + j])

    def projected(j):
        return pltpu.make_async_copy(qkvo_ref.at[j], qkvo_far.at[j], sems.at[first + 3 + j])

    a_there = moves.whole(a_far, a_ref)
    weight(0).start()
    arrive = [moves.groups(*t) for t in ((qkve_far, qkve_ref), (o1_far, o1_ref))]
    leave = moves.groups(o2_ref, o2_far)
    a_there()
    weight(0).wait()
    weight(1).start()
    weight(2).start()
    masks = [moves.whole(*t) for t in ((incl_far, incl_ref), (strict_far, strict_ref))]
    for g in range(2):
        for start, _ in arrive:
            start(g)

    def project(j, _):
        pl.when(j > 0)(lambda: weight(j).wait())
        qkvo_ref[j] = dot(a_ref[...], w_ref[j]).astype(BF16)
        projected(j).start()
        return 0

    lax.fori_loop(0, 3, project, 0)
    for wait in masks:
        wait()

    def next_group(group):
        in_turn(arrive, group, groups)

    def row(i, _):
        r, group = i % rows, i // rows
        lanes = pl.multiple_of(group * GROUP, GROUP)
        all_of = pl.ds(pl.multiple_of(r * seq, seq), seq)

        @pl.when(r == 0)
        def _():
            next_group(group)

        for p in range(GROUP // (2 * HD)):
            ln = pl.ds(lanes + p * 2 * HD, 2 * HD)
            ke, ko = qkve_ref[1, all_of, ln], qkvo_ref[1, all_of, ln]
            vte, vto = qkve_ref[2, all_of, ln].T, qkvo_ref[2, all_of, ln].T
            work = []
            for b in range(seq // QB):
                sl, n = rows_of(r, seq, b), (b + 1) * QB
                cols = slice(b * QB, n)
                incl, strict = twice(incl_ref[r, :n, cols]), twice(strict_ref[r, :n, cols])
                q = cat_heads(qkve_ref[0, sl, ln], HD**-0.5)
                work.append([dot_nt(ko[:n], q) + strict])
                q = cat_heads(qkvo_ref[0, sl, ln], HD**-0.5)
                work.append([dot_nt(ko[:n], q) + incl, dot_nt(ke[:n], q) + incl])
            for b in range(seq // QB):
                sl, n = rows_of(r, seq, b), (b + 1) * QB
                (s,), (so, se) = work[2 * b : 2 * b + 2]
                old = pair_row(lse1_ref[group, :, sl], p)
                top = jnp.maximum(old, jnp.max(s, axis=0, keepdims=True))
                e = jnp.exp(s - top)
                kept = jnp.exp(old - top)
                mass = kept + jnp.sum(e, axis=0, keepdims=True)
                work[2 * b] = (e.astype(BF16), kept, 1.0 / mass)
                put_pair(lse2_ref.at[0, group], p, sl, top + jnp.log(mass))
                top = jnp.max(jnp.maximum(se, so), axis=0, keepdims=True)
                ee, eo = jnp.exp(se - top), jnp.exp(so - top)
                mass = jnp.sum(ee + eo, axis=0, keepdims=True)
                work[2 * b + 1] = (ee.astype(BF16), eo.astype(BF16), 1.0 / mass)
                put_pair(lse2_ref.at[1, group], p, sl, top + jnp.log(mass))
            for b in range(seq // QB):
                sl, n = rows_of(r, seq, b), (b + 1) * QB
                (e, kept, inv), (ee, eo, inv2) = work[2 * b : 2 * b + 2]
                o1 = o1_ref[sl, ln].astype(F32).T
                o = own_lanes(dot(vto[:, :n], e), inv) + own_lanes(twice(o1), kept * inv)
                o2_ref[0, sl, ln] = o.T.astype(BF16)
                o = dot(vte[:, :n], ee) + dot(vto[:, :n], eo)
                o2_ref[1, sl, ln] = own_lanes(o, inv2).T.astype(BF16)

        @pl.when(r == rows - 1)
        def _():
            leave[0](group)

        return 0

    lax.fori_loop(0, rows * groups, row, 0)
    for j in range(3):
        projected(j).wait()
    for g in range(groups):
        leave[1](g)


def attend_second(a, w, incl, strict, qkve, o1, lse1):
    rows, seq = incl.shape[0], incl.shape[1]
    n, d = a.shape
    f = w.shape[2]
    qkv, o2 = sds((3, n, f), BF16), sds((2, n, f), BF16)
    near = (a, w, incl, strict, qkve, o1, qkv, o2)
    return resident(
        functools.partial(attend_second_body, rows, seq),
        [(t, FAR) for t in (a, w, incl, strict, qkve, o1)] + [lse1],
        [(qkv, FAR), (o2, FAR), sds((2, *lse1.shape), F32)],
        scratch=[pltpu.VMEM(t.shape, t.dtype) for t in near] + [pltpu.SemaphoreType.DMA((64,))],
        flops=6 * n * d * f + 48 * n * seq * f,
        vmem=32,
        name="attend_second",
    )


def row_products(a, b):
    prod = cat_heads((a * b).astype(BF16))
    return dot_nt(jnp.ones((8, 2 * HD), BF16), prod)[:1]


def query_parts(sl, ln, group, p, i, qkv_ref, o_ref, lse_ref, do_ref):
    do = do_ref[i, sl, ln]
    delta = row_products(do.astype(F32), o_ref[i, sl, ln].astype(F32))
    return cat_heads(qkv_ref[0, sl, ln], HD**-0.5), cat_heads(do), pair_row(lse_ref[i, group, :, sl], p), delta


def blocks_back(tasks):
    scores = [dot_nt(k, q) + bias - lse for k, _, _, bias, q, _, lse, _ in tasks]
    moved = [dot_nt(v, do) - delta for _, v, _, _, _, do, _, delta in tasks]
    probs = [jnp.exp(s) for s in scores]
    ds = [(p * m).astype(BF16) for p, m in zip(probs, moved)]
    return [
        (dot(p.astype(BF16), do), dot(d, q), dot(kt, d))
        for (_, _, kt, _, q, do, _, _), p, d in zip(tasks, probs, ds)
    ]


def add_rows(total, part):
    if total is None:
        return part
    n = part.shape[0]
    return jnp.concatenate([total[:n] + part, total[n:]], axis=0)


def attend_back_body(
    rows, seq, w_far, incl_far, strict_far, qkve_far, qkvo_far, o2_far, lse2_ref, do_far,
    dh1_far, ho_far, gb_ref,
    dqkvo_far, dqkve_far, dy_far, sums_ref,
    w_ref, incl_ref, strict_ref, qkve_ref, qkvo_ref, o2_ref, do_ref, dh1_ref, ho_ref,
    dqkvo_ref, dqkve_ref, da_ref, dy_ref, sems,
):
    groups = lse2_ref.shape[1]
    moves = Moves(sems)
    arrive = [
        moves.groups(*t)
        for t in ((qkve_far, qkve_ref), (qkvo_far, qkvo_ref), (o2_far, o2_ref), (do_far, do_ref))
    ]
    leave = [moves.groups(*t) for t in ((dqkvo_ref, dqkvo_far), (dqkve_ref, dqkve_far))]
    for start, _ in arrive:
        start(0)
    masks = [moves.whole(*t) for t in ((incl_far, incl_ref), (strict_far, strict_ref))]
    for start, _ in arrive:
        start(1)
    odd = pl.ds(rows * seq, rows * seq)
    late = [moves.later(*t) for t in ((w_far, w_ref), (dh1_far.at[odd], dh1_ref), (ho_far, ho_ref))]
    for wait in masks:
        wait()

    def next_group(group):
        in_turn(arrive, group, groups)

        @pl.when(group == groups - 2)
        def _():
            for start, _ in late:
                start()

    sc = HD**-0.5

    def row(i, _):
        r, group = i % rows, i // rows
        lanes = pl.multiple_of(group * GROUP, GROUP)
        all_of = pl.ds(pl.multiple_of(r * seq, seq), seq)

        @pl.when(r == 0)
        def _():
            next_group(group)

        for p in range(GROUP // (2 * HD)):
            ln = pl.ds(lanes + p * 2 * HD, 2 * HD)
            ke, ve = qkve_ref[1, all_of, ln], qkve_ref[2, all_of, ln]
            ko, vo = qkvo_ref[1, all_of, ln], qkvo_ref[2, all_of, ln]
            kte, kto = ke.T, ko.T
            tasks = []
            for b in reversed(range(seq // QB)):
                sl, n = rows_of(r, seq, b), (b + 1) * QB
                cols = slice(b * QB, n)
                incl, strict = twice(incl_ref[r, :n, cols]), twice(strict_ref[r, :n, cols])
                even = query_parts(sl, ln, group, p, 0, qkve_ref, o2_ref, lse2_ref, do_ref)
                odd = query_parts(sl, ln, group, p, 1, qkvo_ref, o2_ref, lse2_ref, do_ref)
                tasks.append((ko[:n], vo[:n], kto[:, :n], strict, *even))
                tasks.append((ko[:n], vo[:n], kto[:, :n], incl, *odd))
                tasks.append((ke[:n], ve[:n], kte[:, :n], incl, *odd))
            done = blocks_back(tasks)
            dke = dve = dko = dvo = None
            for b in reversed(range(seq // QB)):
                sl = rows_of(r, seq, b)
                (dv, dk, dqe), (dv2, dk2, dqo), (dv3, dk3, dqo2) = done[:3]
                done = done[3:]
                dvo, dko = add_rows(dvo, dv + dv2), add_rows(dko, dk + dk2)
                dve, dke = add_rows(dve, dv3), add_rows(dke, dk3)
                dqkve_ref[0, sl, ln] = (own_lanes(dqe).T * sc).astype(BF16)
                dqkvo_ref[0, sl, ln] = (own_lanes(dqo + dqo2).T * sc).astype(BF16)
            dqkve_ref[1, all_of, ln] = dke.astype(BF16)
            dqkve_ref[2, all_of, ln] = dve.astype(BF16)
            dqkvo_ref[1, all_of, ln] = dko.astype(BF16)
            dqkvo_ref[2, all_of, ln] = dvo.astype(BF16)

        @pl.when(r == rows - 1)
        def _():
            for start, _ in leave:
                start(group)

        return 0

    lax.fori_loop(0, rows * groups, row, 0)
    for _, wait in late:
        wait()
    da = dot_nt(dqkvo_ref[0], w_ref[0])
    da += dot_nt(dqkvo_ref[1], w_ref[1])
    da += dot_nt(dqkvo_ref[2], w_ref[2])
    da_ref[...] = da
    sums_ref[...] = jnp.zeros_like(sums_ref)

    def finish(i, _):
        sl = pl.ds(pl.multiple_of(i * ROWS_AT_ONCE, ROWS_AT_ONCE), ROWS_AT_ONCE)
        normal, inverse = norm_stats(ho_ref[sl])
        da = da_ref[sl]
        dy = dh1_ref[sl] + norm_back(da, normal, inverse, gb_ref[0:1])
        dy_ref[sl] = dy
        for k, t in enumerate((da * normal, da, dy)):
            sums_ref[k : k + 1] += jnp.sum(t, axis=0, keepdims=True)
        return 0

    lax.fori_loop(0, rows * seq // ROWS_AT_ONCE, finish, 0)
    kept = [moves.whole(dy_ref, dy_far)]
    for g in range(groups):
        for _, wait in leave:
            wait(g)
    for wait in kept:
        wait()


def attend_back(w, incl, strict, qkve, qkvo, o2, lse2, do, dh1, ho, gb):
    rows, seq = incl.shape[0], incl.shape[1]
    n, d = ho.shape
    f = w.shape[2]
    do = do.reshape(2, n, f)
    qkv = sds((3, n, f), BF16)
    near = (w, incl, strict, qkve, qkvo, o2, do, sds((n, d), F32), ho, qkv, qkv, sds((n, d), F32))
    return resident(
        functools.partial(attend_back_body, rows, seq),
        [(t, FAR) for t in (w, incl, strict, qkve, qkvo, o2)]
        + [lse2]
        + [(t, FAR) for t in (do, dh1, ho)]
        + [gb],
        [(qkv, FAR), (qkv, FAR), (sds((n, d), F32), FAR), sds((3, d), F32)],
        scratch=[pltpu.VMEM(t.shape, t.dtype) for t in near + (sds((n, d), F32),)] + [pltpu.SemaphoreType.DMA((64,))],
        flops=6 * n * d * f + 120 * n * seq * f,
        vmem=44,
        name="attend_back",
    )


def attend_back_even_body(
    rows, seq, w_far, incl_far, qkve_far, o1_far, lse1_ref, do1_far, o2_far, lse2_ref, do2_far,
    part_far, dh1_far, dh2_far, x_far, gb_ref,
    dqkv_far, gt_ref, sums_ref,
    w_ref, incl_ref, qkve_ref, o1_ref, do1_ref, o2_ref, do2_ref, part_ref, dh1_ref, dh2_ref, x_ref,
    dqkv_ref, da_ref, sems,
):
    groups = lse1_ref.shape[0]
    moves = Moves(sems)
    even = pl.ds(0, rows * seq)
    arrive = [
        moves.groups(*t)
        for t in (
            (qkve_far, qkve_ref), (o1_far, o1_ref), (do1_far, do1_ref), (o2_far.at[0], o2_ref),
            (do2_far.at[0], do2_ref), (part_far, part_ref),
        )
    ]
    leave = [moves.groups(dqkv_ref, dqkv_far)]
    for start, _ in arrive:
        start(0)
    mask = moves.whole(incl_far, incl_ref)
    for start, _ in arrive:
        start(1)
    late = [
        moves.later(*t)
        for t in ((w_far, w_ref), (dh1_far, dh1_ref), (dh2_far.at[even], dh2_ref), (x_far, x_ref))
    ]
    mask()

    def next_group(group):
        in_turn(arrive, group, groups)

        @pl.when(group == groups - 2)
        def _():
            for start, _ in late:
                start()

    sc = HD**-0.5

    def row(i, _):
        r, group = i % rows, i // rows
        lanes = pl.multiple_of(group * GROUP, GROUP)
        all_of = pl.ds(pl.multiple_of(r * seq, seq), seq)

        @pl.when(r == 0)
        def _():
            next_group(group)

        for p in range(GROUP // (2 * HD)):
            ln = pl.ds(lanes + p * 2 * HD, 2 * HD)
            k, v = qkve_ref[1, all_of, ln], qkve_ref[2, all_of, ln]
            kt = k.T
            tasks = []
            for b in reversed(range(seq // QB)):
                sl, n = rows_of(r, seq, b), (b + 1) * QB
                incl = twice(incl_ref[r, :n, b * QB : n])
                lse1 = pair_row(lse1_ref[group, :, sl], p)
                ratio = jnp.exp(lse1 - pair_row(lse2_ref[0, group, :, sl], p))
                do1, do2 = do1_ref[sl, ln].astype(F32), do2_ref[sl, ln].astype(F32)
                delta = row_products(do1, o1_ref[sl, ln].astype(F32))
                delta += ratio * row_products(do2, o2_ref[sl, ln].astype(F32))
                both = do1 + own_lanes(twice(do2.T), ratio).T
                q, do = cat_heads(qkve_ref[0, sl, ln], sc), cat_heads(both.astype(BF16))
                tasks.append((k[:n], v[:n], kt[:, :n], incl, q, do, lse1, delta))
            dka = dva = None
            for b, (dv, dk, dq) in zip(reversed(range(seq // QB)), blocks_back(tasks)):
                sl = rows_of(r, seq, b)
                dva, dka = add_rows(dva, dv), add_rows(dka, dk)
                dqkv_ref[0, sl, ln] = (own_lanes(dq).T * sc + part_ref[0, sl, ln].astype(F32)).astype(BF16)
            dqkv_ref[1, all_of, ln] = (dka + part_ref[1, all_of, ln].astype(F32)).astype(BF16)
            dqkv_ref[2, all_of, ln] = (dva + part_ref[2, all_of, ln].astype(F32)).astype(BF16)

        @pl.when(r == rows - 1)
        def _():
            for start, _ in leave:
                start(group)

        return 0

    lax.fori_loop(0, rows * groups, row, 0)
    for _, wait in late:
        wait()
    da_ref[...] = jnp.zeros_like(da_ref)

    def project_back(j, _):
        da_ref[...] += dot_nt(dqkv_ref[j], w_ref[j])
        return 0

    lax.fori_loop(0, 3, project_back, 0)
    sums_ref[...] = jnp.zeros_like(sums_ref)

    def finish(i, _):
        sl = pl.ds(pl.multiple_of(i * ROWS_AT_ONCE, ROWS_AT_ONCE), ROWS_AT_ONCE)
        normal, inverse = norm_stats(x_ref[sl].astype(F32))
        da = da_ref[sl]
        sums_ref[0:1] += jnp.sum(da * normal, axis=0, keepdims=True)
        sums_ref[1:2] += jnp.sum(da, axis=0, keepdims=True)
        back = norm_back(da, normal, inverse, gb_ref[0:1])
        gt_ref[sl] = (dh1_ref[sl] + dh2_ref[sl] + back).astype(BF16)
        return 0

    lax.fori_loop(0, rows * seq // ROWS_AT_ONCE, finish, 0)
    for g in range(groups):
        for _, wait in leave:
            wait(g)


def attend_back_even(w, incl, qkve, o1, lse1, do1, o2, lse2, do2, part, dh1, dh2, x, gb):
    rows, seq = incl.shape[0], incl.shape[1]
    n, d = x.shape
    f = w.shape[2]
    qkv, one = sds((3, n, f), BF16), sds((n, f), BF16)
    near = (w, incl, qkv, one, one, one, one, qkv, dh1, dh1, x, qkv, sds((n, d), F32))
    far = lambda *ts: [(t, FAR) for t in ts]
    return resident(
        functools.partial(attend_back_even_body, rows, seq),
        far(w, incl, qkve, o1)
        + [lse1]
        + far(do1, o2)
        + [lse2]
        + far(do2.reshape(2, n, f), part, dh1, dh2, x)
        + [gb],
        [(qkv, FAR), sds((n, d), BF16), sds((2, d), F32)],
        scratch=[pltpu.VMEM(t.shape, t.dtype) for t in near] + [pltpu.SemaphoreType.DMA((64,))],
        flops=6 * n * d * f + 40 * n * seq * f,
        vmem=40,
        name="attend_back_even",
    )


CHUNK = 512
ROWS_AT_ONCE = 256


def chunk_of(ref, j, axis):
    at = pl.ds(pl.multiple_of(j * CHUNK, CHUNK), CHUNK)
    return ref.at[:, at] if axis else ref.at[at]


class Chunks:
    def __init__(self, moves, far, near, axis, ring=False, leave=False):
        self.first = moves.take(far.shape[axis] // CHUNK)
        self.sems, self.far, self.near = moves.sems, far, near
        self.axis, self.ring, self.leave = axis, ring, leave

    def copy(self, j):
        near = self.near.at[j % self.near.shape[0]] if self.ring else chunk_of(self.near, j, self.axis)
        ends = (chunk_of(self.far, j, self.axis), near)
        return pltpu.make_async_copy(*(ends[::-1] if self.leave else ends), self.sems.at[self.first + j])

    def start(self, j):
        self.copy(j).start()

    def wait(self, j):
        self.copy(j).wait()


class Weight:
    def __init__(self, moves, pieces, near, axis):
        self.axis, self.near = axis, near
        self.own = Chunks(moves, pieces[0], near, axis) if pieces[0] is not None else None
        self.number = near.shape[axis] // CHUNK // 2
        self.others, start = [], near.shape[axis] // 2
        for far in pieces[1:]:
            at = pl.ds(start, far.shape[axis])
            self.others.append(moves.later(far, near.at[:, at] if axis else near.at[at]))
            start += far.shape[axis]

    def start_others(self):
        for start, _ in self.others:
            start()

    def wait_others(self):
        for _, wait in self.others:
            wait()


def load_in_turn(j, *weights):
    number = weights[0].number

    @pl.when(j < number)
    def _():
        for w in weights:
            w.own.wait(j)

    @pl.when(j + 2 < number)
    def _():
        for w in weights:
            w.own.start(j + 2)

    @pl.when(j + 2 == number)
    def _():
        for w in weights:
            w.start_others()

    @pl.when(j == number)
    def _():
        for w in weights:
            w.wait_others()


def start_loads(*weights):
    for j in range(2):
        for w in weights:
            w.own.start(j)


def feed_chunk(n2_ref, wup_ref, wdown_ref, j, g_buf, d_buf, ho_ref, gs, ds, first):
    @pl.when(first >= 2)
    def _():
        gs.wait(j - 2)
        ds.wait(j - 2)

    half = n2_ref.shape[0] // 2
    parts = []
    for sl in (slice(0, half), slice(half, 2 * half)):
        g, d = gelu_parts(dot(n2_ref[sl], chunk_of(wup_ref, j, 1)[...]))
        parts.append(g.astype(BF16))
        g_buf[j % 2, sl] = parts[-1]
        d_buf[j % 2, sl] = d.astype(BF16)
    gs.start(j)
    ds.start(j)
    for i, g in enumerate(parts):
        ho_ref[i * half : (i + 1) * half] += dot(g, chunk_of(wdown_ref, j, 0)[...])


def start_norm(x_ref, h1_ref, n2_ref, gb_ref, ho_ref=None, normal_ref=None, inverse_ref=None):
    def part(k, _):
        sl = pl.ds(pl.multiple_of(k * ROWS_AT_ONCE, ROWS_AT_ONCE), ROWS_AT_ONCE)
        h1 = x_ref[sl].astype(F32) + h1_ref[sl]
        h1_ref[sl] = h1
        normal, inverse = norm_stats(h1)
        n2_ref[sl] = (normal * gb_ref[1:2] + gb_ref[3:4]).astype(BF16)
        if ho_ref is not None:
            ho_ref[sl] = h1 + gb_ref[4:5]
        if normal_ref is not None:
            normal_ref[sl] = normal
            inverse_ref[sl] = jnp.broadcast_to(inverse, (ROWS_AT_ONCE, inverse_ref.shape[1]))
        return 0

    lax.fori_loop(0, h1_ref.shape[0] // ROWS_AT_ONCE, part, 0)


def weave(seq):
    i = lax.broadcasted_iota(jnp.int32, (2 * seq, 2 * seq), 0)
    k = lax.broadcasted_iota(jnp.int32, (2 * seq, 2 * seq), 1)
    place = jnp.where(k < seq, 2 * k, 2 * (k - seq) + 1)
    return jnp.where(i == place, 1.0, 0.0).astype(BF16)


def mlp_own_body(
    x_far, o_far, wout_far, gb_ref, wup_far, wdown_far, cot_far,
    h1_far, n2_far, g_far, d_far, ho_far, dm_far,
    x_ref, o_ref, wout_ref, wup_ref, wdown_ref, h1_ref, n2_ref, ho_ref, cot_ref, dm_ref, g_buf, d_buf, sems,
):
    moves = Moves(sems)
    first = [moves.whole(*t) for t in ((o_far, o_ref), (wout_far, wout_ref), (x_far, x_ref))]
    ups, downs = Chunks(moves, wup_far, wup_ref, 1), Chunks(moves, wdown_far, wdown_ref, 0)
    gs, ds = (Chunks(moves, f, b, 1, True, True) for f, b in ((g_far, g_buf), (d_far, d_buf)))
    number = wup_far.shape[1] // CHUNK
    for wait in first:
        wait()
    for j in range(number):
        ups.start(j)
        downs.start(j)
    cot_there = moves.whole(cot_far, cot_ref)
    h1_ref[...] = dot(o_ref[...], wout_ref[...])
    start_norm(x_ref, h1_ref, n2_ref, gb_ref, ho_ref)
    kept = [moves.whole(*t) for t in ((h1_ref, h1_far), (n2_ref, n2_far))]

    def step(j, _):
        ups.wait(j)
        downs.wait(j)
        feed_chunk(n2_ref, wup_ref, wdown_ref, j, g_buf, d_buf, ho_ref, gs, ds, j)
        return 0

    lax.fori_loop(0, number, step, 0)
    kept.append(moves.whole(ho_ref, ho_far))
    cot_there()
    rows, seq = cot_ref.shape[0], cot_ref.shape[1] // 2
    mix = weave(seq)
    for r in range(rows):
        parted = dot_tn(mix, cot_ref[r]).astype(BF16)
        for i in range(2):
            at = (i * rows + r) * seq
            dm_ref[at : at + seq] = parted[i * seq : (i + 1) * seq]
    kept.append(moves.whole(dm_ref, dm_far))
    for wait in kept:
        wait()
    for j in range(number - 2, number):
        gs.wait(j)
        ds.wait(j)


def mlp_other_body(number_up, number_down, n2_far, part_far, g_in, d_in, gb_ref, *refs):
    ups_far, refs = refs[:number_up], refs[number_up:]
    downs_far, refs = refs[:number_down], refs[number_down:]
    g_far, d_far, ho_far, ao_far, n2_ref, wup_ref, wdown_ref, ho_ref, ao_ref, g_buf, d_buf, sems = refs
    moves = Moves(sems)
    up = Weight(moves, (None,) + ups_far, wup_ref, 1)
    down = Weight(moves, (None,) + downs_far, wdown_ref, 0)
    gs, ds = (Chunks(moves, f, b, 1, True, True) for f, b in ((g_far, g_buf), (d_far, d_buf)))
    n2_there = moves.whole(n2_far, n2_ref)
    up.start_others()
    down.start_others()
    part_there = moves.whole(part_far, ho_ref)
    number, half = up.number, n2_ref.shape[0] // 2
    n2_there()
    up.wait_others()

    def rise(i, _):
        j = number + i
        for sl in (slice(0, half), slice(half, 2 * half)):
            g, d = gelu_parts(dot(n2_ref[sl], chunk_of(wup_ref, j, 1)[...]))
            g_buf[j % number, sl] = g.astype(BF16)
            d_buf[j % number, sl] = d.astype(BF16)
        gs.start(j)
        ds.start(j)
        return 0

    lax.fori_loop(0, number, rise, 0)
    down.wait_others()
    part_there()

    def fall(i, _):
        j = number + i
        ho_ref[...] += dot(g_buf[j % number], chunk_of(wdown_ref, j, 0)[...])
        return 0

    lax.fori_loop(0, number, fall, 0)
    sent = moves.whole(ho_ref, ho_far)

    def norm(k, _):
        sl = pl.ds(pl.multiple_of(k * ROWS_AT_ONCE, ROWS_AT_ONCE), ROWS_AT_ONCE)
        normal, _ = norm_stats(ho_ref[sl])
        ao_ref[sl] = (normal * gb_ref[0:1] + gb_ref[2:3]).astype(BF16)
        return 0

    lax.fori_loop(0, ho_ref.shape[0] // ROWS_AT_ONCE, norm, 0)
    moves.whole(ao_ref, ao_far)()
    sent()
    for j in range(number, 2 * number):
        gs.wait(j)
        ds.wait(j)


def near_of(*arrays):
    return [pltpu.VMEM(t.shape, t.dtype) for t in arrays]


def far_of(*arrays):
    return [(t, FAR) for t in arrays]


def mlp_own(x, o, wout, gb, wup, wdown, cot):
    n, d = x.shape
    ff = 2 * wup.shape[1]
    h1, low, wide = sds((n, d), F32), sds((n, d), BF16), sds((n, ff), BF16)
    return resident(
        mlp_own_body,
        far_of(x, o, wout) + [gb] + far_of(wup, wdown, cot),
        far_of(h1, low, wide, wide, h1, sds((2 * n, d), BF16)),
        scratch=near_of(x, o, wout, wup, wdown, h1, low, h1, cot, sds((2 * n, d), BF16))
        + [pltpu.VMEM((2, n, CHUNK), BF16)] * 2
        + [pltpu.SemaphoreType.DMA((40,))],
        vmem=44,
        name="mlp_own",
    )


def mlp_other(n2, part, g, dgelu, gb, ups, downs):
    n, d = n2.shape
    ff = g.shape[1]
    return resident(
        functools.partial(mlp_other_body, len(ups), len(downs)),
        far_of(n2, part, g, dgelu) + [gb] + far_of(*ups, *downs),
        far_of(sds(g.shape, BF16), sds(g.shape, BF16), sds(part.shape, F32), sds(n2.shape, BF16)),
        scratch=near_of(n2, sds((d, ff), BF16), sds((ff, d), BF16), part, n2)
        + [pltpu.VMEM((ff // CHUNK // 2, n, CHUNK), BF16)] * 2
        + [pltpu.SemaphoreType.DMA((40,))],
        vmem=40,
        aliases={2: 0, 3: 1},
        name="mlp_other",
    )


def after_norm_back(
    moves, size, h1_ref, dn_ref, db_ref, wout_ref, gb_ref, sums_ref, dp_ref, do_ref, dh1_far, dp_far, do_far,
    inverse_ref=None,
):
    gain_sum = jnp.zeros_like(gb_ref[0:1])
    bias_sum = jnp.zeros_like(gb_ref[0:1])
    waits = []
    for i in range(h1_ref.shape[0] // size):
        sl = slice(i * size, (i + 1) * size)
        if inverse_ref is None:
            normal, inverse = norm_stats(h1_ref[sl])
        else:
            normal, inverse = h1_ref[sl], inverse_ref[sl, :1]
        dn = dn_ref[sl]
        gain_sum += jnp.sum(dn * normal, axis=0, keepdims=True)
        bias_sum += jnp.sum(dn, axis=0, keepdims=True)
        dh1 = db_ref[sl].astype(F32) + norm_back(dn, normal, inverse, gb_ref[1:2])
        dn_ref[sl] = dh1
        dp_ref[sl] = dh1.astype(BF16)
        at = pl.ds(i * size, size)
        waits += [moves.whole(a.at[at], b.at[at]) for a, b in ((dn_ref, dh1_far), (dp_ref, dp_far))]
        if i % 2:
            both = pl.ds((i - 1) * size, 2 * size)
            do_ref[both] = dot_nt(dp_ref[both], wout_ref[...]).astype(BF16)
            waits.append(moves.whole(do_ref.at[both], do_far.at[both]))
    sums_ref[0:1] = gain_sum
    sums_ref[1:2] = bias_sum
    return waits


def mlp_second_body(rows, seq, number_up, number_down, x_far, ho_far, o_far, dm_far, wout_far, gb_ref, *refs):
    mlp_second_work(rows, seq, x_far, ho_far, o_far, dm_far, wout_far, gb_ref, *in_pieces(refs, number_up, number_down))


def in_pieces(refs, *numbers):
    out = []
    for k in numbers:
        out.append(refs[:k])
        refs = refs[k:]
    return out + list(refs)


def mlp_second_work(
    rows, seq, x_far, ho_far, o_far, dm_far, wout_far, gb_ref, ups_far, downs_far,
    outs_far, outs2_far, n2_far, g_far, du_far, dh1_far, dp_far, do_far, sums_ref,
    x_ref, ho_ref, o_ref, cot_ref, wout_ref, wup_ref, wdown_ref, n2_ref, dm_ref,
    normal_ref, z_ref, dn_ref, dp_ref, do_ref, inverse_ref, g_buf, du_buf, sems,
):
    n = rows * seq
    moves = Moves(sems)
    halves = (slice(0, n), slice(n, 2 * n))
    first = [moves.whole(*t) for t in ((o_far.at[0], o_ref.at[0]), (wout_far, wout_ref))]
    up, down = Weight(moves, ups_far, wup_ref, 1), Weight(moves, downs_far, wdown_ref, 0)
    gs, dus = (Chunks(moves, f, b, 1, True, True) for f, b in ((g_far, g_buf), (du_far, du_buf)))
    number = 2 * up.number
    for wait in first:
        wait()
    x_there = moves.whole(x_far, x_ref)
    then = [moves.whole(*t) for t in ((o_far.at[1], o_ref.at[1]), (ho_far, ho_ref))]
    start_loads(up, down)
    dm_there = moves.whole(dm_far, dm_ref)
    for i, sl in enumerate(halves):
        if i:
            for wait in then:
                wait()
        z_ref[sl] = dot(o_ref[i], wout_ref[...])
        if i == 0:
            x_there()
        z_at, n2_at, normal_at, inverse_at = (t.at[pl.ds(i * n, n)] for t in (z_ref, n2_ref, normal_ref, inverse_ref))
        start_norm(x_ref if i == 0 else ho_ref, z_at, n2_at, gb_ref, None, normal_at, inverse_at)
    dm_there()
    mix = weave(seq)
    kept = [moves.whole(n2_ref, n2_far)]
    dn_ref[...] = jnp.zeros_like(dn_ref)

    def step(j, _):
        load_in_turn(j, up, down)

        @pl.when(j >= 2)
        def _():
            gs.wait(j - 2)
            dus.wait(j - 2)

        for sl in (slice(0, 2 * n),):
            u = dot(n2_ref[sl], chunk_of(wup_ref, j, 1)[...])
            dg = dot_nt(dm_ref[sl], chunk_of(wdown_ref, j, 0)[...])
            g, d = gelu_parts(u)
            g = g.astype(BF16)
            du = (dg * d).astype(BF16)
            g_buf[j % 2, sl] = g
            du_buf[j % 2, sl] = du
            z_ref[sl] += dot(g, chunk_of(wdown_ref, j, 0)[...])
            dn_ref[sl] += dot_nt(du, chunk_of(wup_ref, j, 1)[...])
        gs.start(j)
        dus.start(j)
        return 0

    lax.fori_loop(0, number, step, 0)
    for r in range(rows):
        pair = [slice(i * n + r * seq, i * n + (r + 1) * seq) for i in range(2)]
        z = jnp.concatenate([z_ref[s].astype(BF16) for s in pair], axis=0)
        cot_ref[r] = dot(mix, z).astype(BF16)
    half = rows // 2
    kept += [moves.whole(cot_ref.at[pl.ds(i * half, half)], far) for i, far in enumerate((outs_far, outs2_far))]
    kept += after_norm_back(
        moves, seq, normal_ref, dn_ref, dm_ref, wout_ref, gb_ref, sums_ref, dp_ref, do_ref, dh1_far, dp_far, do_far,
        inverse_ref,
    )
    for wait in kept:
        wait()
    for j in range(number - 2, number):
        gs.wait(j)
        dus.wait(j)


def mlp_second(x, ho, o2, dm, wout, gb, ups, downs, seq):
    n, d = x.shape
    ff = 2 * ups[0].shape[1]
    rows = n // seq
    low, wide, full = sds((2 * n, d), BF16), sds((2 * n, ff), BF16), sds((2 * n, d), F32)
    out = sds((rows // 2, 2 * seq, d), BF16)
    return resident(
        functools.partial(mlp_second_body, rows, seq, len(ups), len(downs)),
        far_of(x, ho, o2, dm, wout) + [gb] + far_of(*ups, *downs),
        far_of(out, out, low, wide, wide, full, low, low) + [sds((2, d), F32)],
        scratch=near_of(x, ho, o2, sds((rows, 2 * seq, d), BF16), wout, sds((d, ff), BF16), sds((ff, d), BF16), low, low, full, full, full, low, low, sds((2 * n, 128), F32))
        + [pltpu.VMEM((2, 2 * n, CHUNK), BF16)] * 2
        + [pltpu.SemaphoreType.DMA((64,))],
        vmem=60,
        name="mlp_second",
    )


def mlp_back_body(rows, seq, number_up, number_down, dy_far, h1_far, wout_far, gb_ref, d_far, *refs):
    mlp_back_work(rows, seq, dy_far, h1_far, wout_far, gb_ref, d_far, *in_pieces(refs, number_up, number_down))


def mlp_back_work(
    rows, seq, dy_far, h1_far, wout_far, gb_ref, d_far, ups_far, downs_far,
    du_far, dh1_far, dp_far, do_far, sums_ref,
    dy_ref, h1_ref, wout_ref, wup_ref, wdown_ref, d_ref, dm_ref, dn_ref, dp_ref, do_ref, du_buf, sems,
):
    moves = Moves(sems)
    first = moves.whole(dy_far, dy_ref)
    up, down = Weight(moves, ups_far, wup_ref, 1), Weight(moves, downs_far, wdown_ref, 0)
    ds, dus = Chunks(moves, d_far, d_ref, 1), Chunks(moves, du_far, du_buf, 1, True, True)
    number = 2 * up.number
    for chunks in (down.own, ds, up.own):
        chunks.start(0)
    then = [moves.later(*t) for t in ((wout_far, wout_ref), (h1_far, h1_ref))]
    first()
    for chunks in (down.own, ds, up.own):
        chunks.start(1)
    dm_ref[...] = dy_ref[...].astype(BF16)
    dn_ref[...] = jnp.zeros_like(dn_ref)

    def step(j, _):
        load_in_turn(j, down, up)
        ds.wait(j)

        @pl.when(j + 2 < number)
        def _():
            ds.start(j + 2)

        @pl.when(j + 2 == number)
        def _():
            for start, _ in then:
                start()

        @pl.when(j >= 2)
        def _():
            dus.wait(j - 2)

        dg = dot_nt(dm_ref[...], chunk_of(wdown_ref, j, 0)[...])
        du = (dg * chunk_of(d_ref, j, 1)[...].astype(F32)).astype(BF16)
        du_buf[j % 2] = du
        dus.start(j)
        dn_ref[...] += dot_nt(du, chunk_of(wup_ref, j, 1)[...])
        return 0

    lax.fori_loop(0, number, step, 0)
    for _, wait in then:
        wait()
    kept = after_norm_back(
        moves, seq, h1_ref, dn_ref, dy_ref, wout_ref, gb_ref, sums_ref, dp_ref, do_ref, dh1_far, dp_far, do_far
    )
    for wait in kept:
        wait()
    for j in range(number - 2, number):
        dus.wait(j)


def mlp_back(dy, h1, wout, gb, dgelu, ups, downs, seq):
    n, d = dy.shape
    ff = dgelu.shape[1]
    low = sds((n, d), BF16)
    return resident(
        functools.partial(mlp_back_body, n // seq, seq, len(ups), len(downs)),
        far_of(dy, h1, wout) + [gb] + far_of(dgelu, *ups, *downs),
        far_of(dgelu, h1, low, low) + [sds((2, d), F32)],
        scratch=near_of(dy, h1, wout, sds((d, ff), BF16), sds((ff, d), BF16), dgelu, low, dy, low, low)
        + [pltpu.VMEM((2, n, CHUNK), BF16)]
        + [pltpu.SemaphoreType.DMA((48,))],
        vmem=48,
        name="mlp_back",
    )


def lanes_at(ref, start, size):
    return ref.at[:, pl.ds(pl.multiple_of(start, 128), size)]


def stack_rows(moves, pairs, target, start, size):
    copies, row = [], 0
    for far in pairs:
        copies.append(moves.later(lanes_at(far, start, size), target.at[pl.ds(row, far.shape[0])]))
        row += far.shape[0]
    return (lambda: [s() for s, _ in copies]), (lambda: [w() for _, w in copies])


def all_of(*parts):
    return (lambda: [s() for s, _ in parts]), (lambda: [w() for _, w in parts])


class InTurn:
    def __init__(self, *tiles):
        self.tiles, self.at = tiles, 0
        for start, _ in tiles[:2]:
            start()

    def next(self):
        self.tiles[self.at][1]()
        self.at += 1
        if self.at + 1 < len(self.tiles):
            self.tiles[self.at + 1][0]()


def place_of(quarter, y, me_ref):
    return quarter if y else 4 + (quarter ^ me_ref[1])


def packed(body, me, arrays, shape, scratch, flops, vmem, name):
    smem = pl.BlockSpec(memory_space=pltpu.SMEM)
    out = sds(shape, BF16)
    return resident(
        body,
        [(me, smem)] + far_of(*arrays),
        far_of(out, out),
        scratch=near_of(sds((2,) + shape, BF16)) + scratch + [pltpu.SemaphoreType.DMA((64,))],
        flops=flops,
        vmem=vmem,
        name=name,
    )


def grad_down_body(
    me_ref, g1_far, g2_far, dy_far, dm2_far, keep_far, go_far, out_ref, dy_ref, dm_ref, g_ref, acc_ref, sems
):
    low, group = me_ref[0] % 4, (me_ref[0] // 4) % 2
    ring, n, b = g_ref.shape[0], g1_far.shape[0], g_ref.shape[2]
    moves = Moves(sems)
    first, last = moves.take(2 * ring), moves.take(4)

    def tile(i):
        side, y, h = 1 - i // 4, (i // 2) % 2, i % 2
        quarter = ((me_ref[0] // 8) ^ side) * 2 + h
        at = jnp.where(y == 0, 4 + (quarter ^ me_ref[1]), quarter) * b
        return side, y, h, at

    def loads(i):
        at, slot = tile(i)[3], i % ring
        near = g_ref.at[slot]
        ends = ((g1_far, near.at[pl.ds(0, n)]), (g2_far, near.at[pl.ds(n, 2 * n)]))
        return [pltpu.make_async_copy(lanes_at(f, at, b), t, sems.at[first + 2 * slot + k]) for k, (f, t) in enumerate(ends)]

    def store(far, side, y):
        return pltpu.make_async_copy(out_ref.at[side, y], far.at[y], sems.at[last + side * 2 + y])

    ready = [moves.whole(dy_far, dy_ref), moves.whole(dm2_far, dm_ref.at[pl.ds(n, 2 * n)])]
    for c in loads(0):
        c.start()
    for wait in ready:
        wait()
    for c in loads(1):
        c.start()
    dm_ref[:n] = dy_ref[...].astype(BF16)

    def step(i, _):
        side, y, h, _ = tile(i)
        for c in loads(i):
            c.wait()

        @pl.when(i + 2 < 8)
        def _():
            for c in loads(i + 2):
                c.start()

        acc_ref[...] = dot_tn(g_ref[i % ring], dm_ref[...]).reshape(acc_ref.shape)
        for s in range(4):
            out_ref[side, y, (h ^ group) * 4 + s] = acc_ref[s ^ low].astype(BF16)

        @pl.when((h == 1) & (side == 1))
        def _():
            store(go_far, 1, y).start()

        @pl.when((h == 1) & (side == 0))
        def _():
            store(keep_far, 0, y).start()

        return 0

    lax.fori_loop(0, 8, step, 0)
    for y in range(2):
        store(go_far, 1, y).wait()
        store(keep_far, 0, y).wait()


def grad_down(me, g1, g2, dy, dm2):
    n, d = dy.shape
    ff = g1.shape[1]
    b = ff // 8
    return packed(
        grad_down_body,
        me,
        (g1, g2, dy, dm2),
        (2, 8, b // 4, d),
        [
            pltpu.VMEM((n, d), F32),
            pltpu.VMEM((3 * n, d), BF16),
            pltpu.VMEM((3, 3 * n, b), BF16),
            pltpu.VMEM((4, b // 4, d), F32),
        ],
        2 * 3 * n * d * ff,
        40,
        "grad_down",
    )


CUT = 768
CUT_BACK = 1536


def swapped(s):
    return ((s >> 1) % 2) * 4 + ((s >> 2) % 2) * 2 + s % 2


def put_slots(out_ref, y, lanes, acc_ref, me):
    for s in range(16):
        out_ref[s // 8, y, s % 8, :, lanes] = acc_ref[s ^ me].astype(BF16)


def grad_up_body(
    me_ref, n1_far, n2_far, du1_far, du2_far, dp1_far, dp2_far, o1_far, o2_far, keep_far, go_far,
    out_ref, n_ref, t_ref, du_ref, dp_ref, o_ref, acc_ref, acc2_ref, sems,
):
    moves = Moves(sems)
    d, f = n_ref.shape[1], o_ref.shape[2]
    ring, c, n = du_ref.shape[0], du_ref.shape[2], du1_far.shape[0]
    first, last = moves.take(4 * ring), moves.take(4)

    def loads(i):
        y, t, slot = i // 2, i % 2, i % ring
        copies = []
        for k in range(2):
            quarter = 2 * t + k
            at = jnp.where(y == 0, 4 + (quarter ^ me_ref[1]), quarter) * f
            near = lanes_at(du_ref.at[slot], k * f, f)
            for far, rows in ((du1_far, pl.ds(0, n)), (du2_far, pl.ds(n, 2 * n))):
                copies.append((lanes_at(far, at, f), near.at[rows]))
        return [pltpu.make_async_copy(a, b, sems.at[first + 4 * slot + k]) for k, (a, b) in enumerate(copies)]

    def stores(y):
        return [
            pltpu.make_async_copy(out_ref.at[i, y], far.at[y], sems.at[last + 2 * y + i])
            for i, far in enumerate((keep_far, go_far))
        ]

    ready = stack_rows(moves, (n1_far, n2_far), n_ref, 0, d)
    ready[0]()
    for c0 in loads(0):
        c0.start()
    out_loads = [stack_rows(moves, (dp1_far, dp2_far), dp_ref, 0, d)]
    out_loads += [stack_rows(moves, (o1_far, o2_far), o_ref.at[y], (1 - y) * f, f) for y in range(2)]
    ready[1]()
    for c0 in loads(1):
        c0.start()
    t_ref[...] = n_ref[...].T

    def step(i, _):
        y, t = i // 2, i % 2
        for c0 in loads(i):
            c0.wait()

        @pl.when(i + 2 < 4)
        def _():
            for c0 in loads(i + 2):
                c0.start()

        @pl.when(i == 0)
        def _():
            for start, _ in out_loads:
                start()

        acc_ref[...] = dot(t_ref[...], du_ref[i % ring]).reshape(acc_ref.shape)
        put_slots(out_ref, y, pl.ds(pl.multiple_of(t * c, c), c), acc_ref, jnp.where(t == 0, me_ref[0], me_ref[2]))

        @pl.when(i == 1)
        def _():
            for _, wait in out_loads:
                wait()

        @pl.when(t == 1)
        def _():
            acc2_ref[...] = dot_tn(dp_ref[...], o_ref[y]).reshape(acc2_ref.shape)
            put_slots(out_ref, y, slice(2 * c, 2 * c + f), acc2_ref, me_ref[2])
            for s in stores(y):
                s.start()

        return 0

    lax.fori_loop(0, 4, step, 0)
    for y in range(2):
        for s in stores(y):
            s.wait()


def grad_up(me, n1, n2, du1, du2, dp1, dp2, o1, o2):
    n, d = n1.shape
    ff = du1.shape[1]
    f, c = o1.shape[1] // 2, ff // 4
    return packed(
        grad_up_body,
        me,
        (n1, n2, du1, du2, dp1, dp2, o1, o2),
        (2, 8, d // 16, 2 * c + f),
        [
            pltpu.VMEM((3 * n, d), BF16),
            pltpu.VMEM((d, 3 * n), BF16),
            pltpu.VMEM((3, 3 * n, c), BF16),
            pltpu.VMEM((3 * n, d), BF16),
            pltpu.VMEM((2, 3 * n, f), BF16),
            pltpu.VMEM((16, d // 16, c), F32),
            pltpu.VMEM((16, d // 16, f), F32),
        ],
        2 * 3 * n * d * (ff + d),
        56,
        "grad_up",
    )


def grad_qkv_body(me_ref, ae_far, ao_far, de_far, do_far, keep_far, go_far, out_ref, a_ref, t_ref, d_ref, acc_ref, sems):
    moves = Moves(sems)
    d = a_ref.shape[1]
    f = de_far.shape[2] // 2
    ready = stack_rows(moves, (ae_far, ao_far), a_ref, 0, d)
    n, first = ae_far.shape[0], moves.take(6)

    def loads(j):
        return [
            pltpu.make_async_copy(far.at[j], d_ref.at[j, pl.ds(k * n, n)], sems.at[first + 2 * j + k])
            for k, far in enumerate((de_far, do_far))
        ]

    ready[0]()
    for c in loads(0):
        c.start()
    ready[1]()
    for j in (1, 2):
        for c in loads(j):
            c.start()
    t_ref[...] = a_ref[...].T

    def step(j, _):
        for c in loads(j):
            c.wait()
        acc_ref[...] = dot(t_ref[...], d_ref[j]).reshape(acc_ref.shape)
        lanes = pl.ds(pl.multiple_of(j * f, f), f)
        for s in range(16):
            block = acc_ref[s ^ me_ref[0]].astype(BF16)
            out_ref[s // 8, 1, s % 8, :, lanes] = block[:, :f]
            out_ref[s // 8, 0, s % 8, :, lanes] = block[:, f:]
        return 0

    lax.fori_loop(0, 3, step, 0)
    sent = [moves.whole(out_ref.at[i], far) for i, far in ((1, go_far), (0, keep_far))]
    for wait in sent:
        wait()


def grad_qkv(me, ae, ao, dqkv_e, dqkv_o):
    n, d = ae.shape
    f = dqkv_e.shape[2] // 2
    return packed(
        grad_qkv_body,
        me,
        (ae, ao, dqkv_e, dqkv_o),
        (2, 8, d // 16, 3 * f),
        [
            pltpu.VMEM((2 * n, d), BF16),
            pltpu.VMEM((d, 2 * n), BF16),
            pltpu.VMEM((3, 2 * n, 2 * f), BF16),
            pltpu.VMEM((16, d // 16, 2 * f), F32),
        ],
        2 * 2 * 3 * n * d * 2 * f,
        40,
        "grad_qkv",
    )


def packed_call(body, grid, me, ins, outs, scratch=(), flops=0, aliases={}, name=None):
    return pl.pallas_call(
        body,
        grid_spec=pltpu.PrefetchScalarGridSpec(
            num_scalar_prefetch=1,
            grid=grid,
            in_specs=[s for _, s in ins],
            out_specs=[s for _, s in outs],
            scratch_shapes=scratch,
        ),
        out_shape=[a for a, _ in outs],
        input_output_aliases=aliases,
        compiler_params=pltpu.CompilerParams(
            dimension_semantics=("arbitrary",) * len(grid), vmem_limit_bytes=VMEM_LIMIT
        ),
        cost_estimate=pl.CostEstimate(flops=int(flops) // 16, bytes_accessed=0, transcendentals=0),
        name=name,
    )(me, *[a for a, _ in ins])


def unpack_down_body(me_ref, part_ref, *refs):
    low, rows = me_ref[0] % 8, part_ref.shape[1]
    for b in range(8):
        refs[-1][b * rows : (b + 1) * rows] = part_ref[swapped(b ^ low)].astype(F32)


def unpack_down(me, side, part, into=()):
    _, r, w = part.shape
    half = 8 * r
    at = lambda me: (me[0] // 8) ^ side
    ins = [(part, pl.BlockSpec(part.shape, lambda i, me: (0, 0, 0)))]
    ins += [(t, pl.BlockSpec(memory_space=pl.ANY)) for t in into]
    return packed_call(
        unpack_down_body,
        (1,),
        me,
        ins,
        [(sds((2 * half, w), F32), pl.BlockSpec((half, w), lambda i, me: (at(me), 0)))],
        aliases={2 + i: i for i in range(len(into))},
        name="unpack_down",
    )[0]


def unpack_rest_body(side, me_ref, part_ref, *refs):
    up_far, out_far, qkv_far, up_st, wide, out_st, qkv_st, sems = refs[-8:]
    moves = Moves(sems)
    left, right = me_ref[0] % 8, me_ref[2] % 8
    rows, half = part_ref.shape[1], 8 * part_ref.shape[1]
    d, f = up_st.shape[1], wide.shape[1]
    base = ((me_ref[0] // 8) ^ side) * half
    sent = []
    for b in range(8):
        sl = slice(b * rows, (b + 1) * rows)
        up_st[sl, :CUT] = part_ref[b ^ left, :, :CUT].astype(F32)
        up_st[sl, CUT:] = part_ref[swapped(b ^ right), :, CUT:d].astype(F32)
        wide[sl] = part_ref[b ^ right, :, d : d + f].astype(F32)
        if b % 4 == 3:
            start, size = (b - 3) * rows, 4 * rows
            at = pl.ds(pl.multiple_of(base + start, 8), size)
            sent.append(moves.whole(up_st.at[pl.ds(start, size)], up_far.at[at]))
    out_st[...] = wide[...].T
    sent.append(moves.whole(out_st, lanes_at(out_far, base, half)))
    for j in range(3):
        for b in range(8):
            sl = slice(b * rows, (b + 1) * rows)
            qkv_st[j, sl] = part_ref[swapped(b ^ left), :, d + (j + 1) * f : d + (j + 2) * f].astype(F32)
        sent.append(moves.whole(qkv_st.at[j], qkv_far.at[j, pl.ds(pl.multiple_of(base, 8), half)]))
    for wait in sent:
        wait()


def unpack_rest(me, side, part, into=()):
    _, r, w = part.shape
    half = 8 * r
    d, f = CUT_BACK, (w - CUT_BACK) // 4
    smem = pl.BlockSpec(memory_space=pltpu.SMEM)
    outs = [sds((2 * half, d), F32), sds((f, 2 * half), F32), sds((3, 2 * half, f), F32)]
    stages = [sds((half, d), F32), sds((half, f), F32), sds((f, half), F32), sds((3, half, f), F32)]
    return resident(
        functools.partial(unpack_rest_body, side),
        [(me, smem), part] + far_of(*into),
        far_of(*outs),
        scratch=near_of(*stages) + [pltpu.SemaphoreType.DMA((8,))],
        vmem=24,
        aliases={2 + i: i for i in range(len(into))},
        name="unpack_rest",
    )


def fold(*parts):
    return sum(p.astype(F32) for p in parts).astype(BF16)


def after(value, *first):
    return lax.optimization_barrier((value, first))[0]


class Chunk:
    def __init__(self, keep, got):
        self.keep, self.got = keep, got
        self.sent = None

    def wait(self, *also):
        self.got, also = lax.optimization_barrier((self.got, also))
        return also

    def to_partner(self):
        total = fold(self.keep, self.got)
        self.keep, self.sent = total[1], total[0]
        self.got = lax.ppermute(self.sent, "tensor", FLIP)

    def gather_core(self):
        self.got = lax.ppermute(self.keep, "core", FLIP)


def add(k, g):
    return (k.astype(F32) + g.astype(F32)).astype(BF16)


def phase_shapes(mode, parts):
    shapes = [p[0].shape for p in parts]
    s = shapes[0]
    if mode == "half":
        out = s[:-3] + (s[-3] // 2,) + s[-2:]
        return [out, out]
    if mode == "partner":
        return [s[1:], s[1:]]
    if mode == "last":
        out = (s[0] // 2, s[1], sum(t[2] for t in shapes))
        return [out, out]
    if mode == "sum":
        return [s]
    if mode == "split":
        return [(2 * s[0], s[1], CUT_BACK), (2 * s[0], s[1], s[2] - CUT_BACK)]
    return [(2 * s[0], s[1], sum(t[2] for t in shapes))]


def phase_part(mode, parts, outs):
    if mode == "half":
        (k, g), n = parts[0], outs[0].shape[-3]
        lead = (slice(None),) * (len(k.shape) - 3)
        for i, out in enumerate(outs):
            at = lead + (slice(i * n, (i + 1) * n),)
            out[...] = add(k[at], g[at])
    elif mode == "partner":
        k, g = parts[0]
        for i, out in zip((1, 0), outs):
            out[...] = add(k[i], g[i])
    elif mode == "last":
        n, lane = outs[0].shape[0], 0
        for k, g in parts:
            for i, out in enumerate(outs):
                at = slice(i * n, (i + 1) * n)
                out[:, :, lane : lane + k.shape[2]] = add(k[at], g[at])
            lane += k.shape[2]
    elif mode == "sum":
        outs[0][...] = add(parts[0][0][...], parts[0][1][...])
    elif mode == "split":
        for i, ref in enumerate(parts[0]):
            at = slice(i * ref.shape[0], (i + 1) * ref.shape[0])
            outs[0][at] = ref[:, :, :CUT_BACK]
            outs[1][at] = ref[:, :, CUT_BACK:]
    else:
        lane = 0
        for pair in parts:
            for i, ref in enumerate(pair):
                outs[0][i * ref.shape[0] : (i + 1) * ref.shape[0], :, lane : lane + ref.shape[2]] = ref[...]
            lane += pair[0].shape[2]


def phase(*items):
    shapes = [phase_shapes(*t) for t in items]

    def body(*refs):
        at = sum(2 * len(parts) for _, parts in items)
        ins, outs = list(refs[:at]), list(refs[at:])
        for (mode, parts), made in zip(items, shapes):
            mine = [(ins.pop(0), ins.pop(0)) for _ in parts]
            phase_part(mode, mine, [outs.pop(0) for _ in made])

    flat = resident(
        body,
        [t for _, parts in items for pair in parts for t in pair],
        [sds(s, BF16) for made in shapes for s in made],
        vmem=16,
        name="phase",
    )
    flat = list(flat)
    return [[flat.pop(0) for _ in made] for made in shapes]


class Hops(Chunk):
    def __init__(self, outer, keep, got):
        super().__init__(keep, got)
        self.axes = {"x": ("x", 2, 1), "z": ("o", outer, 1), "w": ("o", outer, 2)}
        self.extra = [("o", outer, 1 << b) for b in range(2, outer.bit_length() - 1)]

    def over(self, way, t):
        return lax.ppermute(t, "tensor", FLIP) if way == "partner" else flip_bit(t, *self.axes[way])

    def send(self, *parts):
        self.keep, self.sent, self.got = [], [], []
        for total, way in parts:
            if way == "partner":
                keep, sent = total[1], total[0]
            else:
                half = total.shape[-3] // 2
                keep, sent = total[..., :half, :, :], total[..., half:, :, :]
            self.keep.append(keep)
            self.sent.append(sent)
            self.got.append(self.over(way, sent))

    def fold_first(self):
        total = fold(self.keep, self.got)
        half = total.shape[1] // 2
        return [part for lanes in (total[..., :CUT], total[..., CUT:]) for part in (lanes[:, :half], lanes[:, half:])]

    def first(self, parts):
        self.keep, self.sent = [parts[0], parts[2]], [parts[1], parts[3]]
        self.got = [self.over("x", parts[1]), self.over("z", parts[3])]

    def first_hop(self, way):
        self.send((fold(self.keep, self.got), way))

    def parts(self):
        return list(zip(self.keep, self.got))

    def hop(self, *ways):
        items = [("partner" if w == "partner" else "half", [p]) for w, p in zip(ways, self.parts())]

        def then(made):
            self.keep, self.sent = [m[0] for m in made], [m[1] for m in made]
            self.got = [self.over(w, s) for w, s in zip(ways, self.sent)]

        return items, then

    def absorb(self, other):
        self.keep, self.got = self.keep + other.keep, self.got + other.got

    def last_hop(self):
        def then(made):
            ((keep, sent),) = made
            self.keep, self.sent = [keep], [sent]
            self.got = [self.over("w", sent)]

        return [("last", self.parts())], then

    def back_first(self):
        def then(made):
            ((total,),) = made
            for s in self.extra:
                total = fold(total, flip_bit(total, *s))
            self.keep = self.sent = [total]
            self.got = [self.over("w", total)]

        return [("sum", self.parts())], then

    def back(self, *ways):
        if len(ways) == 2 and len(self.keep) == 1:
            items = [("split", self.parts())]
        else:
            items = [("join", [p]) for p in self.parts()]

        def then(made):
            self.keep = self.sent = [t for m in made for t in m]
            self.got = [self.over(w, t) for w, t in zip(ways, self.keep)]

        return items, then

    def back_core(self):
        def then(made):
            ((self.keep,),) = made
            self.sent = self.keep
            self.gather_core()

        return [("join", self.parts())], then


def all_steps(*steps):
    made = phase(*[item for items, _ in steps for item in items])
    for items, then in steps:
        then(made[: len(items)])
        made = made[len(items) :]


def mask_biases(seg):
    seq = seg.shape[1]
    place = jnp.arange(seq, dtype=jnp.int32)
    same = seg[:, :, None] == seg[:, None, :]
    below = (place[:, None] < place[None, :])[None]
    incl = (place[:, None] <= place[None, :])[None]
    bias = lambda m: jnp.where(same & m, 0.0, NEG).astype(F32)
    return bias(incl), bias(below)


def sync(*values):
    return lax.optimization_barrier(values)


class Link:
    def __init__(self, outer, w_qkv, w_out, w_up, w_down):
        self.outer = outer
        self.own = (w_qkv, w_out, w_up, w_down)
        self.core_at, self.x_at, o = (lax.axis_index(a) for a in ("core", "x", "o"))
        bits = {"x": self.x_at, "z": o % 2, "w": (o // 2) % 2}
        self.fetch_bits = self.core_at * 2 + self.x_at
        slots = []
        for order in ("xzw", "zxw"):
            slot = self.core_at
            for name in order:
                slot = slot * 2 + bits[name]
            slots.append(slot)
        self.me = jnp.stack([slots[0], self.fetch_bits, slots[1]]).astype(jnp.int32)
        self.me_z = self.me[2:0:-1]

    def quarter(self, own):
        flat = own.reshape(-1, own.shape[-1])
        return take_half(take_half(flat, self.core_at), self.x_at)

    def over_x(self, t):
        return lax.ppermute(t, "x", FLIP)

    def fetch(self, own_work):
        own = self.own
        size = own[2].shape[1] // 4
        part = lambda t, axis, bits: lax.dynamic_slice_in_dim(t, bits * size, size, axis)
        pieces = [
            self.quarter(own[1]),
            part(own[2], 1, self.fetch_bits),
            jnp.concatenate([part(own[3], 0, self.fetch_bits), part(own[3], 0, self.fetch_bits ^ 1)], axis=0),
        ]
        qkv = self.partner(self.quarter(own[0]))
        up, out, down = (self.partner(pieces[i]) for i in (1, 0, 2))
        qkv, own_work = sync(qkv, own_work)
        qkv, out, up = sync(ordered(self.x_at, qkv, self.over_x(qkv)).reshape(-1, qkv.shape[-1]), out, up)
        qkv_core, out_x, up_x = self.core(qkv), self.over_x(out), self.over_x(up)
        qkv = ordered(self.core_at, qkv, qkv_core).reshape(own[0].shape)

        def join_out(*work):
            nonlocal out, out_x
            work, out, out_x = sync(work, out, out_x)
            out = ordered(self.x_at, out, out_x).reshape(-1, out.shape[-1])
            out = ordered(self.core_at, out, self.core(out)).reshape(own[1].shape)
            return work, jnp.concatenate([own[1], out], axis=0)

        def pieces_of(*work):
            up_there, down_there, work = sync(up_x, down, work)
            ups = (own[2], up, up_there, self.core(up), self.core(up_there))
            return ups, (own[3], down_there, self.core(down_there)), work

        return own_work, own[0], qkv, jnp.concatenate([own[0], qkv], axis=2), join_out, pieces_of

    def partner(self, t):
        return lax.ppermute(t, "tensor", FLIP)

    def core(self, t):
        return lax.ppermute(t, "core", FLIP)

    def chunk(self, keep, got):
        return Chunk(keep, got)

    def hops(self, keep, got):
        return Hops(self.outer, keep, got)

    def small_steps(self):
        return [("core", 2, 1), ("tensor", 2, 1)] + steps_of(self.outer)

    def flip(self, t, step):
        return flip_bit(t, *step)


def local_part(x, seg, cot, gb, link):
    rows, seq = seg.shape
    n, width = x.shape
    me, me_z = link.me, link.me_z
    incl, strict = mask_biases(seg)
    normal, _ = norm_stats(x.astype(F32))
    a_e = (normal * gb[0] + gb[2]).astype(BF16)
    first = attend_first(a_e, link.own[0], incl)
    (a_e, first, cot, me, me_z), wq_own, fetched, wqkv, join_out, pieces_of = link.fetch((a_e, first, cot, me, me_z))
    second = attend_first(a_e, fetched, incl)
    qkv_e, o1 = (jnp.concatenate([s, t], axis=-1) for s, t in zip(first[:2], second[:2]))
    lse1 = jnp.concatenate([first[2], second[2]], axis=0).reshape(-1, GROUP // HD, n)
    (qkv_e, o1, lse1, wqkv), wout = join_out(qkv_e, o1, lse1, wqkv)
    h1, n2_1, g1, d1, part_one, dm2 = mlp_own(x, o1, wout, gb, link.own[2], link.own[3], cot)
    ups, downs, (n2_1, part_one) = pieces_of(n2_1, part_one)
    g1, d1, ho, a_o = mlp_other(n2_1, part_one, g1, d1, gb, ups[1:], downs[1:])
    qkv_o, o2, lse2 = attend_second(a_o, wqkv, incl, strict, qkv_e, o1, lse1)
    out, out_two, n2_2, g2, du2, dh1_2, dp2, do2, sums2 = mlp_second(x, ho, o2, dm2, wout, gb, ups, downs, seq)
    out_got = link.partner(out)
    dqkv_o, part, dy, sums_o = attend_back(wqkv, incl, strict, qkv_e, qkv_o, o2, lse2, do2, dh1_2, ho, gb)
    o2_flat = o2.reshape(2 * n, width)

    out_got, dy = sync(out_got, dy)
    quarter = out_two.shape[1] // 2
    out_last = [link.partner(after(out_two[:, :quarter], out_got))]
    down_keep, down_go = grad_down(me_z, g1, g2, dy, dm2)
    down_keep, down_go, out_last[0] = sync(down_keep, down_go, out_last[0])
    out_last.append(link.partner(after(out_two[:, quarter:], down_go)))
    down = link.hops(down_keep, link.core(down_go))
    dy = after(dy, down_go)
    du1, dh1_1, dp1, do1, sums1 = mlp_back(dy, h1, wout, gb, d1, ups, downs, seq)
    du1, dp1, do1, out_last[1] = down.wait(du1, dp1, do1, out_last[1])
    down.to_partner()
    up_keep, up_go = grad_up(me, n2_1, n2_2, after(du1, down.sent), du2, dp1, dp2, o1, o2_flat)
    do1 = after(do1, up_go)
    dqkv_e, gt, sums_e = attend_back_even(wqkv, incl, qkv_e, o1, lse1, do1, o2, lse2, do2, part, dh1_1, dh1_2, x, gb)
    dqkv_e, gt, sums_e, up_go = down.wait(dqkv_e, gt, sums_e, up_go)
    up = link.hops(up_keep, link.core(up_go))
    down.keep, down.got = [down.keep], [down.got]
    all_steps(down.hop("z"))
    small = jnp.stack([sums_e[0] + sums_o[0], sums1[0] + sums2[0], sums_e[1] + sums_o[1], sums1[1] + sums2[1], sums_o[2]])
    qkv_keep, qkv_go = grad_qkv(me, a_e, a_o, after(dqkv_e, *down.sent), dqkv_o)
    up_parts = up.fold_first()
    qkv_keep, qkv_go, down.got, up_parts = sync(qkv_keep, qkv_go, down.got, up_parts)
    out = link.finish(
        jnp.concatenate([out, out_two], axis=0),
        jnp.concatenate([out_got, jnp.concatenate(after(out_last, up_parts), axis=1)], axis=0),
        link.out_shape,
    )
    qkv = link.hops(qkv_keep, link.core(qkv_go))
    small_steps = iter(link.small_steps())
    small_got = link.flip(after(small, qkv_go), next(small_steps))

    chunks = [up, qkv]

    def wait_all():
        nonlocal small, small_got
        got, small_got = sync([c.got for c in chunks], small_got)
        for c, g in zip(chunks, got):
            c.got = g
        if small_got is not None:
            small = small + small_got
            step = next(small_steps, None)
            small_got = None if step is None else link.flip(small, step)

    chunks.remove(up)
    wait_all()
    up.first(up_parts)
    qkv.first_hop("partner")
    all_steps(down.hop("x"))
    chunks += [up, down]
    (out,) = up.wait(out)
    wait_all()
    all_steps(up.hop("z", "partner"), qkv.hop("x"), down.hop("w"))
    wait_all()
    all_steps(up.hop("partner", "x"), qkv.hop("z"), down.back_first())
    half = gt.shape[0] // 2
    gt_got = [link.partner(after(gt[:half], *up.sent))]
    wait_all()
    up.absorb(qkv)
    chunks.remove(qkv)
    all_steps(up.last_hop(), down.back("z"))
    gt_got.append(link.partner(after(gt[half:], *up.sent)))
    (gt_got[0],) = up.wait(gt_got[0])
    wait_all()
    all_steps(up.back_first(), down.back("x"))
    (gt_got[1],) = up.wait(gt_got[1])
    wait_all()
    while small_got is not None:
        wait_all()
    all_steps(up.back("z", "x"), down.back_core())
    wait_all()
    all_steps(up.back("x", "z"))
    g_down = unpack_down(me_z, 0, after(down.keep, *up.sent))
    g_down = unpack_down(me_z, 1, down.got, (g_down,))
    gt = link.finish(gt, jnp.concatenate(gt_got, axis=0), link.tokens_shape).astype(F32)
    small = (small[0:2], small[2:4], small[4])
    g_down, gt, small = up.wait(g_down, gt, small)
    all_steps(up.back_core())
    g_rest = unpack_rest(me, 0, up.keep)
    g_rest = up.wait(*g_rest)
    g_up, g_out, g_qkv = unpack_rest(me, 1, up.got, g_rest)
    return out, gt, (g_qkv, g_out, g_up, g_down), small


def shards(outer, tokens, segments, pass_embed, w_qkv, w_out, w_up, w_down, gain, bias, cotangent):
    ty = lax.axis_index("tensor")
    rows = tokens.shape[0] // 2
    width = tokens.shape[2]
    mine = lambda t: lax.dynamic_slice_in_dim(t, ty * rows, rows, 0)
    x = mine(tokens).reshape(-1, width)
    gb = jnp.concatenate([gain, bias, pass_embed[None]], axis=0)
    link = Link(outer, w_qkv, w_out, w_up, w_down)
    link.out_shape, link.tokens_shape = cotangent.shape, tokens.shape
    link.finish = lambda mine, theirs, shape: ordered(ty, mine, theirs).reshape(shape)
    out, gt, grads, small = local_part(x, mine(segments), mine(cotangent), gb, link)
    return out, gt, *grads, *small


def solution(mesh):
    outer = mesh.shape["dp"] // 4
    fine = Mesh(mesh.devices.reshape(outer, 2, 2, mesh.shape["tensor"]), ("o", "x", "core", "tensor"))
    rows = ROWS_OVER
    placed = (
        P(rows, None, None),
        P(rows, None),
        P(),
        P(None, None, "tensor"),
        P("tensor", None),
        P(None, "tensor"),
        P("tensor", None),
        P(),
        P(),
        P(rows, None, None),
    )

    def body(*args):
        return shards(outer, *args)

    return jax.shard_map(
        body,
        mesh=fine,
        in_specs=placed,
        out_specs=(
            P(rows, None, None),
            P(rows, None, None),
            P(None, None, "tensor"),
            P("tensor", None),
            P(None, "tensor"),
            P("tensor", None),
            P(),
            P(),
            P(),
        ),
        check_vma=False,
    )
```
